32 devices in a mesh: bucket: 4 (over y, x), dp: 8 (over z, core).
Axes of the slice: x: 2, y: 2, z: 4, core: 2. Of those that a mesh axis runs over, the one named last changes fastest.
Arguments:
- tokens: bfloat16 [32768, 384], P(('bucket', 'dp')), may hold values from -6 to 6
- cotangent: bfloat16 [32768, 384], P(('bucket', 'dp')), may hold values from -6 to 6
- segment_ids: int32 [32768], P(('bucket', 'dp')), may hold values from 0 to 6, as said below
- keep_mask: int32 [32768], P(('bucket', 'dp')), may hold values from 0 to 1, as said below
- bucket_patches: int32 [4], replicated, may hold values from 64 to 576
- master: float32 [1771776], P(('bucket', 'dp')), may hold values from -3 to 3
- first_moment: float32 [1771776], P(('bucket', 'dp')), may hold values from -90.50967 to 90.50967
- second_moment: float32 [1771776], P(('bucket', 'dp')), may hold values from 3.2768 to 68.8128, as said below
Outputs:
- block_output: bfloat16 [32768, 384], P(('bucket', 'dp'))
- input_grad: float32 [32768, 384], P(('bucket', 'dp'))
- new_first: float32 [1771776], P(('bucket', 'dp'))
- new_second: float32 [1771776], P(('bucket', 'dp'))
- new_master: float32 [1771776], P(('bucket', 'dp'))
- norms: float32 [2, 10], replicated
- trust: float32 [10], replicated
The draws below stay inside these ranges and needn't reach their ends.
Inputs may be any that keep to these rules, and one draw needn't show every extreme that they name: `segment_ids`: within each sequence (aligned blocks of 1024 rows) ids start at 0 and never fall; in buckets 0 to 1 no id occurs in both halves of a sequence. `keep_mask`: the first row of every sequence (aligned blocks of 1024 rows) is 1. `second_moment`: no entry is zero.
All inputs are finite; a program needn't handle non-finite values.
Results may differ from the reference program's by a relative error of at most 0.0085.
The reference program's roundings to bfloat16 on the way count: a program that leaves them out, or rounds other values in their place, can miss the bound.
Values may be sent and summed in bfloat16 or wider, within the bound.
No kernel may reach another device: no remote copies, remote signals or barrier semaphores. Data moves between devices by JAX's collectives and lax.ppermute only.
A program may use at most 128 MiB of HBM per device.

```python
import math
import jax
import jax.numpy as jnp
from jax import lax

D = 384
HEADS = 6
HD = 64
FF = 1536
SEQ = 1024
STEP = 10
MATS = 10
HALF = 512
BUCKETS = 4
TOK_BUCKET = 8192
TOKENS = 32768
PARAMS = 1771776
N_BUCKET = 4


def flat_layout():
    position = jnp.arange(PARAMS, dtype=jnp.int32)
    matrix_end = 4 * D * D + 2 * D * FF
    bounds = [0, 3 * D * D, 4 * D * D, 4 * D * D + D * FF, matrix_end] + [matrix_end + (j + 1) * D for j in range(6)]
    owners = jnp.zeros((PARAMS,), jnp.int32)
    lowest = jnp.zeros((PARAMS,), jnp.int32)
    extent = jnp.zeros((PARAMS,), jnp.int32) + bounds[1]
    for j in range(1, len(bounds) - 1):
        inside = position >= bounds[j]
        owners = owners + inside.astype(jnp.int32)
        lowest = jnp.where(inside, bounds[j], lowest)
        extent = jnp.where(inside, bounds[j + 1] - bounds[j], extent)
    fraction = (position - lowest).astype(jnp.float32) / extent.astype(jnp.float32)
    return (owners, fraction)


def draw_master(key, part):
    key = jax.random.fold_in(key, 11)
    owners, fraction = flat_layout()
    noise = jnp.clip(jax.random.normal(key, (PARAMS,), jnp.float32), -4.0, 4.0)
    rising = 0.75 + 0.75 * fraction
    scales = jnp.where(owners == 0, D ** (-0.5), jnp.where(owners == 1, 5.0 * D ** (-0.5), jnp.where(owners == 2, D ** (-0.5), jnp.where(owners == 3, FF ** (-0.5), 0.2))))
    matrices = noise * scales * rising
    gain_mask = (owners == 4) | (owners == 6) | (owners == 7) | (owners == 8)
    gain_values = (0.6 + 0.9 * fraction) * (1.0 + 0.1 * noise)
    return jnp.where(gain_mask, gain_values, matrices)


def draw_first_moment(key, part):
    key = jax.random.fold_in(key, 12)
    owners, fraction = flat_layout()
    noise = jnp.clip(jax.random.normal(key, (PARAMS,), jnp.float32), -4.0, 4.0)
    rising = 1.0 + 0.8 * fraction
    return 0.055 * TOKENS ** 0.5 * rising * noise


def draw_second_moment(key, part):
    key = jax.random.fold_in(key, 13)
    factor = jnp.exp(jax.random.uniform(key, (PARAMS,), jnp.float32, jnp.log(0.0005), jnp.log(0.008)))
    return factor * (0.25 * TOKENS)


def draw_segment_ids(key, part):
    key = jax.random.fold_in(key, 14)
    position = jnp.arange(TOKENS, dtype=jnp.int32)
    bucket_index = position // TOK_BUCKET
    within = position % SEQ
    spacing = jnp.maximum(SEQ // jnp.power(2, BUCKETS - bucket_index), 2)
    picks = jax.random.randint(key, (TOKENS,), 0, 1048576)
    fresh = picks % spacing == 0
    middle = (bucket_index < BUCKETS // 2) & (within == HALF)
    in_half = within % HALF
    placed = (in_half % (HALF // 4) == 0) & (in_half != 0)
    starts = (fresh | middle | placed | (within == 0)).astype(jnp.int32).reshape(TOKENS // SEQ, SEQ)
    first_ids = jnp.minimum(jnp.cumsum(starts[:, :HALF], axis=1) - 1, 3)
    second_ids = first_ids[:, HALF - 1:HALF] + jnp.minimum(jnp.cumsum(starts[:, HALF:], axis=1), 3)
    return jnp.concatenate([first_ids, second_ids], axis=1).reshape(TOKENS).astype(jnp.int32)


def draw_keep_mask(key, part):
    key = jax.random.fold_in(key, 15)
    position = jnp.arange(TOKENS, dtype=jnp.int32)
    local_rows = position % TOK_BUCKET
    limit = 300 + 600 * local_rows // TOK_BUCKET
    drawn = jax.random.randint(key, (TOKENS,), 0, 1000) < limit
    return (drawn | (position % SEQ == 0)).astype(jnp.int32)


def with_ends(values, stream_key, least, top_value):
    shape = values.shape
    place = [jax.random.randint(jax.random.fold_in(stream_key, axis), (), 0, shape[axis]) for axis in range(len(shape))]
    values = values.at[tuple(place)].set(least)
    longest = shape.index(max(shape))
    place[longest] = (place[longest] + 1) % shape[longest]
    return values.at[tuple(place)].set(top_value)


def block_levels(rng, shape, cuts, low, top_value):
    factor_of = 1.0
    for dim, blocks in cuts:
        heights = jax.random.uniform(jax.random.fold_in(jax.random.fold_in(rng, 6), dim), (blocks,), jnp.float32, low / len(cuts), top_value / len(cuts))
        factor_of = factor_of * jnp.repeat(jnp.exp(heights), shape[dim] // blocks).reshape((-1,) + (1,) * (len(shape) - 1 - dim))
    return factor_of


def scatter_about(own_key, shape, spread, most, cuts=(), kind=jnp.bfloat16):
    level = block_levels(own_key, shape, cuts, -0.22, 0.18) if cuts else 1.0
    array = jax.random.normal(own_key, shape, jnp.float32) * spread * level
    return jnp.minimum(jnp.maximum(array, -most), most).astype(kind)


def setup_inputs(seed: int = 0) -> dict:
    key_of = jax.random.split(jax.random.key(seed), 9)
    return {
        "tokens": scatter_about(key_of[0], (TOKENS, D), 1.0, 6.0, ((0, 32),)),
        "cotangent": scatter_about(key_of[1], (TOKENS, D), 1.0, 6.0, ((0, 32),)),
        "segment_ids": draw_segment_ids(jax.random.fold_in(key_of[8], 71), 0),
        "keep_mask": draw_keep_mask(jax.random.fold_in(key_of[8], 71), 0),
        "bucket_patches": with_ends(jax.random.randint(key_of[4], (BUCKETS,), 64, 577), jax.random.fold_in(key_of[4], 1), 64, 576).astype(jnp.int32),
        "master": draw_master(jax.random.fold_in(key_of[8], 71), 0),
        "first_moment": draw_first_moment(jax.random.fold_in(key_of[8], 71), 0),
        "second_moment": draw_second_moment(jax.random.fold_in(key_of[8], 71), 0),
    }


@jax.custom_vjp
def low(v):
    return lax.optimization_barrier(v.astype(jnp.bfloat16)).astype(jnp.float32)

@jax.custom_vjp
def low_back(v):
    return v

def low_keep(v):
    return (low(v), None)

def low_pass(kept, grad):
    return (grad,)

def back_keep(v):
    return (v, None)

def back_low(kept, grad):
    return (low(grad),)
low.defvjp(low_keep, low_pass)
low_back.defvjp(back_keep, back_low)
norm_epsilon = 1e-06
adam_epsilon = 1e-06
beta_one = 0.9
beta_two = 0.999
learn_rate = 0.5
weight_decay = 0.01
masked_score = -1e+30
HIGH = lax.Precision.HIGHEST

def layer_norm(values):
    average = lax.optimization_barrier(jnp.mean(values, axis=-1, keepdims=True))
    centered = values - average
    variance = lax.optimization_barrier(jnp.mean(centered * centered, axis=-1, keepdims=True))
    return centered * lax.rsqrt(variance + norm_epsilon)

def tensor_bounds():
    matrix_end = 4 * D * D + 2 * D * FF
    return [0, 3 * D * D, 4 * D * D, 4 * D * D + D * FF, matrix_end] + [matrix_end + (j + 1) * D for j in range(6)]

def tensor_ids(index):
    owners = jnp.zeros(index.shape, jnp.int32)
    for bound in tensor_bounds()[1:-1]:
        owners = owners + (index >= bound).astype(jnp.int32)
    return owners

def split_params(flat_params):
    bounds = tensor_bounds()
    pieces = [flat_params[bounds[j]:bounds[j + 1]] for j in range(len(bounds) - 1)]
    return (pieces[0].reshape(D, 3 * D), pieces[1].reshape(D, D), pieces[2].reshape(D, FF), pieces[3].reshape(FF, D), pieces[4:])

def attend_sequence(queries, key_rows, values, segment, kept):
    scores = jnp.einsum('qhd,khd->hqk', queries, key_rows, precision=HIGH, preferred_element_type=jnp.float32) * HD ** (-0.5)
    scores = low_back(scores)
    places = jnp.arange(SEQ, dtype=jnp.int32)
    allowed = (segment[:, None] == segment[None, :]) & ((kept[None, :] == 1) | (places[:, None] == places[None, :]))
    masked = jnp.where(allowed[None], scores, masked_score)
    highest = lax.optimization_barrier(jnp.max(masked, axis=-1, keepdims=True))
    expo_rows = jnp.exp(masked - highest)
    attention = low(expo_rows / lax.optimization_barrier(jnp.sum(expo_rows, axis=-1, keepdims=True)))
    return jnp.einsum('hqk,khd->qhd', attention, values, precision=HIGH, preferred_element_type=jnp.float32)

def attend_packed(operands):
    return attend_sequence(*operands)

def forward_group(tokens, segment, kept, flat_params):
    project_weight, output_weight, up_weight, down_weight, gain_rows = split_params(low(flat_params))
    first_gain, first_shift, query_gain, key_gain, second_gain, second_shift = gain_rows
    row_count = tokens.shape[0]
    normed = low(layer_norm(tokens) * first_gain + first_shift)
    project = low_back(jnp.dot(normed, project_weight, precision=HIGH, preferred_element_type=jnp.float32))
    project_view = project.reshape(row_count, 3, HEADS, HD)
    queries = low(layer_norm(project_view[:, 0]) * query_gain.reshape(HEADS, HD))
    key_rows = low(layer_norm(project_view[:, 1]) * key_gain.reshape(HEADS, HD))
    values = low(project_view[:, 2])
    sequences = row_count // SEQ
    attended = lax.map(jax.checkpoint(attend_packed), (queries.reshape(sequences, SEQ, HEADS, HD), key_rows.reshape(sequences, SEQ, HEADS, HD), values.reshape(sequences, SEQ, HEADS, HD), segment.reshape(sequences, SEQ), kept.reshape(sequences, SEQ)))
    attended = low_back(low(attended.reshape(row_count, D)))
    middle = tokens + low_back(jnp.dot(attended, output_weight, precision=HIGH, preferred_element_type=jnp.float32))
    normed_two = low(layer_norm(middle) * second_gain + second_shift)
    hidden_pre = low_back(jnp.dot(normed_two, up_weight, precision=HIGH, preferred_element_type=jnp.float32))
    hidden = low(jax.nn.gelu(hidden_pre, approximate=False))
    return middle + low_back(jnp.dot(hidden, down_weight, precision=HIGH, preferred_element_type=jnp.float32))

def reference(tokens, cotangent, segment_ids, keep_mask, bucket_patches, master, first_moment, second_moment):
    keep_float = keep_mask.astype(jnp.float32)
    kept_count = lax.optimization_barrier(jnp.sum(keep_float.reshape(N_BUCKET, TOK_BUCKET), axis=1))
    patches = bucket_patches.astype(jnp.float32)
    bucket_scale = N_BUCKET * patches / jnp.sum(patches) * TOK_BUCKET / kept_count
    row_scale = jnp.repeat(bucket_scale, TOK_BUCKET)
    seed_grad = cotangent.astype(jnp.float32) * (keep_float * row_scale)[:, None]
    group_size = math.gcd(TOKENS // SEQ, max(1, 4096 // SEQ))
    turns = TOKENS // (SEQ * group_size)
    group_rows = SEQ * group_size

    def one_group(totals, operands):
        token_rows, seed_rows, segment_rows, kept_rows = operands

        def forward_local(token_part, flat_params):
            return forward_group(token_part, segment_rows, kept_rows, flat_params)
        output, pullback = jax.vjp(forward_local, token_rows, master)
        grad_rows, grad_flat = pullback(seed_rows)
        return (totals + grad_flat, (output.astype(jnp.bfloat16), grad_rows))
    grads, (outputs, input_rows) = lax.scan(one_group, jnp.zeros((PARAMS,), jnp.float32), (tokens.astype(jnp.float32).reshape(turns, group_rows, D), seed_grad.reshape(turns, group_rows, D), segment_ids.reshape(turns, group_rows), keep_mask.reshape(turns, group_rows)))
    block_output = outputs.reshape(TOKENS, D)
    input_grad = input_rows.reshape(TOKENS, D)
    first_new = beta_one * first_moment + (1.0 - beta_one) * grads
    second_new = beta_two * second_moment + (1.0 - beta_two) * grads * grads
    first_hat = first_new / (1.0 - beta_one ** STEP)
    second_hat = second_new / (1.0 - beta_two ** STEP)
    owners = tensor_ids(jnp.arange(PARAMS, dtype=jnp.int32))
    decay_rows = jnp.where(owners < 4, weight_decay, 0.0)
    update = first_hat / (jnp.sqrt(second_hat) + adam_epsilon) + decay_rows * master
    weight_sq = jax.ops.segment_sum(master * master, owners, num_segments=MATS)
    update_sq = jax.ops.segment_sum(update * update, owners, num_segments=MATS)
    trust = jnp.sqrt(weight_sq) / (jnp.sqrt(update_sq) + adam_epsilon)
    new_master = master - learn_rate * trust[owners] * update
    norms = jnp.stack([jnp.sqrt(weight_sq), jnp.sqrt(update_sq)])
    return (block_output, input_grad, first_new, second_new, new_master, norms, trust)
```

```python
import functools
import math

import jax
import jax.numpy as jnp
from jax import lax
from jax.experimental import pallas as pl
from jax.experimental.pallas import tpu as pltpu
from jax.sharding import PartitionSpec as P

D = 384
HEADS = 6
HD = 64
FF = 1536
SEQ = 1024
STEP = 10
MATS = 10
LANES = 128
PAIRS = HEADS // 2
TILE = 256
TILES = SEQ // TILE

norm_epsilon = 1e-06
adam_epsilon = 1e-06
beta_one = 0.9
beta_two = 0.999
learn_rate = 0.5
weight_decay = 0.01
masked_score = -1e30

MATRIX_END = 4 * D * D + 2 * D * FF
BOUNDS = [0, 3 * D * D, 4 * D * D, 4 * D * D + D * FF, MATRIX_END] + [
    MATRIX_END + (j + 1) * D for j in range(6)
]
PARAMS = BOUNDS[-1]
ROW_OUT = BOUNDS[1] // LANES
ROW_UP = BOUNDS[2] // LANES
ROW_DOWN = BOUNDS[3] // LANES
ROW_VEC = BOUNDS[4] // LANES
VEC_ROWS = 6 * D // LANES
ROWS_ALL = PARAMS // LANES

score_scale = HD ** (-0.5) * math.log2(math.e)
grad_scale = HD ** (-0.5)

BF = jnp.bfloat16
F32 = jnp.float32
VMEM = pl.BlockSpec(memory_space=pltpu.VMEM)
SMEM = pl.BlockSpec(memory_space=pltpu.SMEM)
ANY = pl.BlockSpec(memory_space=pl.ANY)


def params(limit=56):
    return pltpu.CompilerParams(vmem_limit_bytes=limit * 1024 * 1024)


def round_up(value, step):
    return -(-value // step) * step


class Plan:
    def __init__(self, mesh_shape, shard):
        self.nb = mesh_shape["bucket"]
        self.nd = mesh_shape["dp"]
        self.n = self.nb * self.nd
        self.shard = shard
        self.start = [k * shard // LANES for k in range(self.n)]
        self.rows = [
            -(-((k + 1) * shard) // LANES) - self.start[k] for k in range(self.n)
        ]
        self.win = round_up(max(self.rows) + 1, 16)
        self.tail = round_up(self.win + VEC_ROWS, 16)
        self.quarter_row = self.nd * shard // LANES

    def device(self):
        return lax.axis_index("bucket") * self.nd + lax.axis_index("dp")


def nn(a, b):
    return lax.dot_general(a, b, (((1,), (0,)), ((), ())), preferred_element_type=F32)


def nt(a, b):
    return lax.dot_general(a, b, (((1,), (1,)), ((), ())), preferred_element_type=F32)


def split_low(x):
    high = x.astype(BF)
    return high, (x - high.astype(F32)).astype(BF)


def rows_at(step):
    return pl.ds(pl.multiple_of(step * TILE, TILE), TILE)


def norm_parts(values):
    average = jnp.mean(values, axis=-1, keepdims=True)
    centered = values - average
    variance = jnp.mean(centered * centered, axis=-1, keepdims=True)
    rstd = lax.rsqrt(variance + norm_epsilon)
    return centered * rstd, rstd


def norm_back(hat, rstd, grad):
    mean_grad = jnp.mean(grad, axis=-1, keepdims=True)
    mean_both = jnp.mean(grad * hat, axis=-1, keepdims=True)
    return rstd * (grad - mean_grad - hat * mean_both)


def head_mean_matrix():
    row = lax.broadcasted_iota(jnp.int32, (D, D), 0)
    col = lax.broadcasted_iota(jnp.int32, (D, D), 1)
    return jnp.where(row // HD == col // HD, 1.0 / HD, 0.0).astype(BF)


def head_mean(x, matrix):
    high, rest = split_low(x)
    return nn(high, matrix) + nn(rest, matrix)


def prepare_kernel(plan, master_ref, keep_ref, out_ref):
    me = plan.device()
    offset = lax.rem(me * plan.shard, LANES)
    values = master_ref[...]
    turned = pltpu.roll(values, offset, 1)
    below = pltpu.roll(turned, 1, 0)
    lane = lax.broadcasted_iota(jnp.int32, values.shape, 1)
    row = lax.broadcasted_iota(jnp.int32, values.shape, 0)
    count = jnp.sum(keep_ref[...].astype(F32), axis=1, keepdims=True)
    high = jnp.floor(count * (1.0 / 32.0))
    parts = jnp.where(lane == 0, high, jnp.where(lane == 1, count - 32.0 * high, 0.0))
    window = jnp.where(lane < offset, below, turned)
    out_ref[...] = jnp.where(row == plan.win - 1, parts, window).astype(BF)


def prepare(plan, master_rows, keep_row):
    return pl.pallas_call(
        functools.partial(prepare_kernel, plan),
        out_shape=jax.ShapeDtypeStruct((plan.win, LANES), BF),
        in_specs=[VMEM, VMEM],
        out_specs=VMEM,
        compiler_params=params(),
    )(master_rows, keep_row)


def assemble_kernel(
    plan, own_ref, other_ref, wq_ref, wo_ref, wu_ref, wd_ref, vec_ref, kept_ref, held, flat, sems
):
    me = plan.device()
    copies = [
        pltpu.make_async_copy(own_ref, held.at[0], sems.at[0]),
        pltpu.make_async_copy(other_ref, held.at[1], sems.at[1]),
    ]
    for copy in copies:
        copy.start()
    for copy in copies:
        copy.wait()
    for k in range(plan.n):
        rel = jnp.bitwise_xor(me, k)
        window = held[jnp.bitwise_and(rel, 1), jnp.right_shift(rel, 1)].astype(F32)
        first, count = plan.start[k], plan.rows[k]
        if k > 0:
            before = flat[first : first + 1, :]
        flat[first : first + count, :] = window[:count]
        if k > 0 and (k * plan.shard) % LANES:
            flat[first : first + 1, :] = before + window[:1]

    def columns(target, base, height, width):
        stride = width // LANES
        for j in range(stride):
            target[:, j * LANES : (j + 1) * LANES] = flat[
                pl.ds(base + j, height, stride=stride), :
            ].astype(BF)

    columns(wq_ref, 0, D, 3 * D)
    columns(wo_ref, ROW_OUT, D, D)
    columns(wu_ref, ROW_UP, D, FF)
    columns(wd_ref, ROW_DOWN, FF, D)
    for t in range(6):
        for j in range(D // LANES):
            vec_ref[t : t + 1, j * LANES : (j + 1) * LANES] = flat[
                ROW_VEC + 3 * t + j : ROW_VEC + 3 * t + j + 1, :
            ]
    total = jnp.zeros((1, LANES), F32)
    for j in range(plan.nd):
        total = total + held[j & 1, j >> 1, plan.win - 16 : plan.win, :].astype(F32)[15:16]
    count = 32.0 * total[:, 0:1] + total[:, 1:2]
    kept_ref[...] = jnp.broadcast_to(count, (8, LANES))


def assemble(plan, own, other):
    return pl.pallas_call(
        functools.partial(assemble_kernel, plan),
        out_shape=(
            jax.ShapeDtypeStruct((D, 3 * D), BF),
            jax.ShapeDtypeStruct((D, D), BF),
            jax.ShapeDtypeStruct((D, FF), BF),
            jax.ShapeDtypeStruct((FF, D), BF),
            jax.ShapeDtypeStruct((8, D), F32),
            jax.ShapeDtypeStruct((8, LANES), F32),
        ),
        in_specs=[ANY, ANY],
        out_specs=(VMEM,) * 6,
        scratch_shapes=[
            pltpu.VMEM((2, plan.n // 2, plan.win, LANES), BF),
            pltpu.VMEM((round_up(ROWS_ALL, 8), LANES), F32),
            pltpu.SemaphoreType.DMA((2,)),
        ],
        compiler_params=params(),
    )(own, other)


def overlap(seg_ref, ti, tj):
    first_i, last_i = seg_ref[ti * TILE], seg_ref[ti * TILE + TILE - 1]
    first_j, last_j = seg_ref[tj * TILE], seg_ref[tj * TILE + TILE - 1]
    return jnp.logical_and(first_j <= last_i, first_i <= last_j)


def tile_bias(ti, tj, row_seg, key_seg):
    key_place = lax.broadcasted_iota(jnp.int32, (TILE, TILE), 0) + tj * TILE
    row_place = lax.broadcasted_iota(jnp.int32, (TILE, TILE), 1) + ti * TILE
    seen = jnp.logical_or(
        key_seg == row_seg, jnp.logical_and(key_place == row_place, key_place >= 0)
    )
    return jnp.where(seen, 0.0, masked_score)


def to_column(row):
    return jnp.transpose(jnp.broadcast_to(row, (LANES, row.shape[1])))


def stack_heads(pair):
    lane = lax.broadcasted_iota(jnp.int32, pair.shape, 1)
    zero = jnp.zeros_like(pair)
    return jnp.concatenate(
        [jnp.where(lane < HD, pair, zero), jnp.where(lane >= HD, pair, zero)], axis=0
    )


def forward_kernel(
    plan,
    tokens_ref,
    wq_ref,
    vec_ref,
    seg_smem,
    seg_ref,
    keep_ref,
    q_ref,
    k_ref,
    v_ref,
    raw_ref,
    o_ref,
    ot_ref,
    lse_ref,
    kab,
    vt,
    ot,
    sums,
    segk,
    expo,
):
    matrix = head_mean_matrix()
    gain1, shift1 = vec_ref[0:1, :], vec_ref[1:2, :]
    gain_q, gain_k = vec_ref[2:3, :], vec_ref[3:4, :]
    seg_row = seg_ref[...].astype(F32)
    segk[...] = to_column(jnp.where(keep_ref[...] == 1, seg_row, -1.0))

    def project(step, carry):
        at = rows_at(step)
        hat, _ = norm_parts(tokens_ref[at, :].astype(F32))
        low = (hat * gain1 + shift1).astype(BF)
        raw = nn(low, wq_ref[...])
        raw_ref[at, :] = raw[:, : 2 * D]

        def head_norm(x, gain):
            centered = x - head_mean(x, matrix)
            rstd = lax.rsqrt(head_mean(centered * centered, matrix) + norm_epsilon)
            return (centered * rstd * gain).astype(BF)

        queries = head_norm(raw[:, :D], gain_q)
        keys = head_norm(raw[:, D : 2 * D], gain_k)
        values = raw[:, 2 * D :].astype(BF)
        q_ref[at, :] = queries
        k_ref[at, :] = keys
        v_ref[at, :] = values
        for hp in range(PAIRS):
            kab[hp, step] = stack_heads(keys[:, hp * LANES : (hp + 1) * LANES])
        vt[step] = jnp.transpose(values.astype(F32)).astype(BF)
        return carry

    lax.fori_loop(0, TILES, project, 0)

    def query_tile(ti, carry):
        ot[...] = jnp.zeros_like(ot)
        sums[...] = jnp.zeros_like(sums)
        row_seg = seg_ref[:, pl.ds(pl.multiple_of(ti * TILE, TILE), TILE)].astype(F32)

        def score_tile(tj, inner):
            @pl.when(overlap(seg_smem, ti, tj))
            def _():
                column = segk[rows_at(tj), :]
                bias = tile_bias(ti, tj, row_seg, jnp.concatenate([column, column], axis=1))
                for hp in range(PAIRS):
                    queries = q_ref[rows_at(ti), hp * LANES : (hp + 1) * LANES]
                    scores = nt(kab[hp, tj], queries)
                    for side in range(2):
                        head = 2 * hp + side
                        value = jnp.exp2(
                            scores[side * TILE : (side + 1) * TILE] * score_scale + bias
                        )
                        expo[tj, head] = value
                        sums[head : head + 1, :] += jnp.sum(value, axis=0, keepdims=True)

            return inner

        lax.fori_loop(0, TILES, score_tile, 0)
        lse_ref[ti] = jnp.log2(sums[...])
        sums[...] = 1.0 / sums[...]

        def value_tile(tj, inner):
            @pl.when(overlap(seg_smem, ti, tj))
            def _():
                for head in range(HEADS):
                    prob = (expo[tj, head] * sums[head : head + 1, :]).astype(BF)
                    ot[head * HD : (head + 1) * HD, :] += nn(
                        vt[tj, head * HD : (head + 1) * HD, :], prob
                    )

            return inner

        lax.fori_loop(0, TILES, value_tile, 0)
        attended = ot[...]
        ot_ref[ti] = attended.astype(BF)
        o_ref[rows_at(ti), :] = jnp.transpose(attended).astype(BF)
        return carry

    lax.fori_loop(0, TILES, query_tile, 0)


def forward(plan, tokens, wq, vec, seg, seg_row, keep_row):
    rows = tokens.shape[0]
    return pl.pallas_call(
        functools.partial(forward_kernel, plan),
        out_shape=(
            jax.ShapeDtypeStruct((rows, D), BF),
            jax.ShapeDtypeStruct((rows, D), BF),
            jax.ShapeDtypeStruct((rows, D), BF),
            jax.ShapeDtypeStruct((rows, 2 * D), F32),
            jax.ShapeDtypeStruct((rows, D), BF),
            jax.ShapeDtypeStruct((TILES, D, TILE), BF),
            jax.ShapeDtypeStruct((TILES, 8, TILE), F32),
        ),
        in_specs=[VMEM, VMEM, VMEM, SMEM, VMEM, VMEM],
        out_specs=(VMEM,) * 7,
        scratch_shapes=[
            pltpu.VMEM((PAIRS, TILES, 2 * TILE, LANES), BF),
            pltpu.VMEM((TILES, D, TILE), BF),
            pltpu.VMEM((D, TILE), F32),
            pltpu.VMEM((8, TILE), F32),
            pltpu.VMEM((SEQ, LANES), F32),
            pltpu.VMEM((TILES, HEADS, TILE, TILE), F32),
        ],
        compiler_params=params(),
    )(tokens, wq, vec, seg, seg_row, keep_row)


def middle_kernel(
    plan,
    tokens_ref,
    cot_ref,
    o_ref,
    ot_ref,
    wo_ref,
    wu_ref,
    wd_ref,
    vec_ref,
    keep_ref,
    kept_ref,
    patches_ref,
    out_ref,
    dh1_ref,
    do_ref,
    near_ref,
    far_ref,
    tail_ref,
    gvec_ref,
    keepc,
    gout,
    gup,
    gdownt,
    flat,
):
    me = plan.device()
    bucket = lax.axis_index("bucket")
    gain2, shift2 = vec_ref[4:5, :], vec_ref[5:6, :]
    own = patches_ref[bucket].astype(F32)
    total = patches_ref[0].astype(F32)
    for b in range(1, plan.nb):
        total = total + patches_ref[b].astype(F32)
    ones = jnp.ones((1, LANES), F32)
    scale = (plan.nb * own) * ones / (total * ones) * float(SEQ * plan.nd) / kept_ref[0:1, :]
    keepc[...] = to_column(keep_ref[...].astype(F32)) * scale
    gout[...] = jnp.zeros_like(gout)
    gup[...] = jnp.zeros_like(gup)
    gdownt[...] = jnp.zeros_like(gdownt)
    gvec_ref[...] = jnp.zeros_like(gvec_ref)

    def chunk(step, carry):
        at = rows_at(step)
        middle = tokens_ref[at, :].astype(F32) + nn(o_ref[at, :], wo_ref[...])
        hat, rstd = norm_parts(middle)
        low = (hat * gain2 + shift2).astype(BF)
        u = nn(low, wu_ref[...])
        phi = 0.5 + 0.5 * lax.erf(u * math.sqrt(0.5))
        hidden = (u * phi).astype(BF)
        out_ref[at, :] = (middle + nn(hidden, wd_ref[...])).astype(BF)
        weights = keepc[at, :]
        seed = cot_ref[at, :].astype(F32) * jnp.concatenate([weights] * (D // LANES), axis=1)
        seed_low = seed.astype(BF)
        slope = phi + u * (jnp.exp(-0.5 * u * u) * (1.0 / math.sqrt(2.0 * math.pi)))
        du = (nt(seed_low, wd_ref[...]) * slope).astype(BF)
        gdownt[...] += nn(jnp.transpose(seed).astype(BF), hidden)
        gup[...] += nn(jnp.transpose(low.astype(F32)).astype(BF), du)
        da2 = nt(du, wu_ref[...])
        gvec_ref[0:1, :] += jnp.sum(da2 * hat, axis=0, keepdims=True)
        gvec_ref[1:2, :] += jnp.sum(da2, axis=0, keepdims=True)
        dh1 = seed + norm_back(hat, rstd, da2 * gain2)
        dh1_ref[at, :] = dh1
        dh1_low = dh1.astype(BF)
        gout[...] += nn(ot_ref[step], dh1_low)
        do_ref[at, :] = nt(dh1_low, wo_ref[...]).astype(BF)
        return carry

    lax.fori_loop(0, o_ref.shape[0] // TILE, chunk, 0)

    base = ROW_OUT
    for j in range(D // LANES):
        flat[pl.ds(j, D, stride=D // LANES), :] = gout[:, j * LANES : (j + 1) * LANES]
    for j in range(FF // LANES):
        flat[pl.ds(ROW_UP - base + j, D, stride=FF // LANES), :] = gup[
            :, j * LANES : (j + 1) * LANES
        ]
    for j in range(D // LANES):
        flat[pl.ds(ROW_DOWN - base + j, FF, stride=D // LANES), :] = jnp.transpose(
            gdownt[j * LANES : (j + 1) * LANES, :]
        )
    tail_ref[...] = flat[0:8, :]
    side = jnp.bitwise_and(me, 1)
    dp = lax.axis_index("dp")
    for k in range(plan.nd, plan.n):
        first = plan.start[k] - base
        relb = jnp.bitwise_xor(bucket, k // plan.nd)
        reld = jnp.right_shift(jnp.bitwise_xor(dp, k % plan.nd), 1)
        window = flat[first : first + plan.win, :].astype(BF)

        @pl.when(side == k % 2)
        def _():
            near_ref[relb, reld] = window

        @pl.when(side != k % 2)
        def _():
            far_ref[relb, reld] = window


def middle_part(plan, tokens, cot, o, ot, wo, wu, wd, vec, keep_row, kept, patches):
    rows = tokens.shape[0]
    windows = jax.ShapeDtypeStruct((plan.nb, plan.nd // 2, plan.win, LANES), BF)
    return pl.pallas_call(
        functools.partial(middle_kernel, plan),
        out_shape=(
            jax.ShapeDtypeStruct((rows, D), BF),
            jax.ShapeDtypeStruct((rows, D), F32),
            jax.ShapeDtypeStruct((rows, D), BF),
            windows,
            windows,
            jax.ShapeDtypeStruct((8, LANES), F32),
            jax.ShapeDtypeStruct((8, D), F32),
        ),
        in_specs=[VMEM] * 10 + [SMEM],
        out_specs=(VMEM,) * 7,
        scratch_shapes=[
            pltpu.VMEM((rows, LANES), F32),
            pltpu.VMEM((D, D), F32),
            pltpu.VMEM((D, FF), F32),
            pltpu.VMEM((D, FF), F32),
            pltpu.VMEM((round_up(plan.start[-1] + plan.win - ROW_OUT, 8), LANES), F32),
        ],
        compiler_params=params(),
    )(tokens, cot, o, ot, wo, wu, wd, vec, keep_row, kept, patches)


def backward_kernel(
    plan,
    tokens_ref,
    wq_ref,
    vec_ref,
    seg_smem,
    seg_ref,
    keep_ref,
    q_ref,
    k_ref,
    v_ref,
    raw_ref,
    o_ref,
    lse_ref,
    do_ref,
    dh1_ref,
    tail_ref,
    gvec_ref,
    grad_ref,
    near_ref,
    far_ref,
    kab,
    vab,
    qab,
    dab,
    kt,
    dqt,
    dk,
    dv,
    inner_sums,
    segk,
    gq,
    gains,
    flat,
):
    matrix = head_mean_matrix()
    gain1, shift1 = vec_ref[0:1, :], vec_ref[1:2, :]
    gain_q, gain_k = vec_ref[2:3, :], vec_ref[3:4, :]
    seg_row = seg_ref[...].astype(F32)
    segk[...] = to_column(jnp.where(keep_ref[...] == 1, seg_row, -1.0))
    head_row = lax.broadcasted_iota(jnp.int32, (8, D), 0)
    head_lane = lax.broadcasted_iota(jnp.int32, (8, D), 1)
    hot = jnp.where(head_lane // HD == head_row, 1.0, 0.0).astype(BF)
    dqt[...] = jnp.zeros_like(dqt)
    dk[...] = jnp.zeros_like(dk)
    dv[...] = jnp.zeros_like(dv)
    gq[...] = jnp.zeros_like(gq)
    gains[...] = jnp.zeros_like(gains)

    def stack(step, carry):
        at = rows_at(step)
        keys = k_ref[at, :]
        grads = do_ref[at, :]
        for hp in range(PAIRS):
            lanes = slice(hp * LANES, (hp + 1) * LANES)
            kab[hp, step] = stack_heads(keys[:, lanes])
            vab[hp, step] = stack_heads(v_ref[at, lanes])
            qab[hp, step] = stack_heads(q_ref[at, lanes])
            dab[hp, step] = stack_heads(grads[:, lanes])
        kt[step] = jnp.transpose(keys.astype(F32)).astype(BF)
        high, rest = split_low(grads.astype(F32) * o_ref[at, :].astype(F32))
        inner_sums[step] = nt(hot, high) + nt(hot, rest)
        return carry

    lax.fori_loop(0, TILES, stack, 0)

    def query_tile(ti, carry):
        row_seg = seg_ref[:, pl.ds(pl.multiple_of(ti * TILE, TILE), TILE)].astype(F32)

        def key_tile(tj, inner):
            @pl.when(overlap(seg_smem, ti, tj))
            def _():
                column = segk[rows_at(tj), :]
                bias = tile_bias(ti, tj, row_seg, jnp.concatenate([column, column], axis=1))
                for hp in range(PAIRS):
                    lanes = slice(hp * LANES, (hp + 1) * LANES)
                    scores = nt(kab[hp, tj], q_ref[rows_at(ti), lanes])
                    grads = nt(vab[hp, tj], do_ref[rows_at(ti), lanes])
                    probs, dscores = [], []
                    for side in range(2):
                        head = 2 * hp + side
                        part = slice(side * TILE, (side + 1) * TILE)
                        prob = jnp.exp2(
                            scores[part] * score_scale + (bias - lse_ref[ti, head : head + 1, :])
                        )
                        dscore = prob * (grads[part] - inner_sums[ti, head : head + 1, :])
                        dscore = dscore.astype(BF)
                        probs.append(prob.astype(BF))
                        dscores.append(dscore)
                        dqt[ti, head * HD : (head + 1) * HD, :] += nn(
                            kt[tj, head * HD : (head + 1) * HD, :], dscore
                        )
                    dv[hp, tj] += nn(jnp.concatenate(probs, axis=1), dab[hp, ti])
                    dk[hp, tj] += nn(jnp.concatenate(dscores, axis=1), qab[hp, ti])

            return inner

        lax.fori_loop(0, TILES, key_tile, 0)
        return carry

    lax.fori_loop(0, TILES, query_tile, 0)

    def finish(step, carry):
        at = rows_at(step)

        def head_norm_back(raw, gain, grad, place):
            centered = raw - head_mean(raw, matrix)
            rstd = lax.rsqrt(head_mean(centered * centered, matrix) + norm_epsilon)
            hat = centered * rstd
            gains[place : place + 1, :] += jnp.sum(grad * hat, axis=0, keepdims=True)
            scaled = grad * gain
            return rstd * (
                scaled - head_mean(scaled, matrix) - hat * head_mean(scaled * hat, matrix)
            )

        grad_q = jnp.transpose(dqt[step]) * grad_scale
        grad_k = jnp.concatenate([dk[hp, step] for hp in range(PAIRS)], axis=1) * grad_scale
        grad_v = jnp.concatenate([dv[hp, step] for hp in range(PAIRS)], axis=1)
        low_q = head_norm_back(raw_ref[at, :D], gain_q, grad_q, 2).astype(BF)
        low_k = head_norm_back(raw_ref[at, D:], gain_k, grad_k, 3).astype(BF)
        low = jnp.concatenate([low_q, low_k, grad_v.astype(BF)], axis=1)
        hat, rstd = norm_parts(tokens_ref[at, :].astype(F32))
        normed = hat * gain1 + shift1
        gq[...] += nn(jnp.transpose(normed).astype(BF), low)
        da1 = nt(low, wq_ref[...])
        gains[0:1, :] += jnp.sum(da1 * hat, axis=0, keepdims=True)
        gains[1:2, :] += jnp.sum(da1, axis=0, keepdims=True)
        grad_ref[at, :] = dh1_ref[at, :] + norm_back(hat, rstd, da1 * gain1)
        return carry

    lax.fori_loop(0, TILES, finish, 0)
    gains[4:6, :] = gvec_ref[0:2, :]

    for j in range(3 * D // LANES):
        flat[pl.ds(j, D, stride=3 * D // LANES), :] = gq[:, j * LANES : (j + 1) * LANES]
    flat[ROW_OUT : ROW_OUT + 8, :] = tail_ref[...]
    side = jnp.bitwise_and(lax.axis_index("dp"), 1)
    dp = lax.axis_index("dp")
    rest = jnp.zeros((plan.tail - plan.win, LANES), BF)
    vector_rows = []
    for t in range(6):
        for j in range(D // LANES):
            vector_rows.append(gains[t : t + 1, j * LANES : (j + 1) * LANES])
    vector_rows.append(jnp.zeros((plan.tail - plan.win - VEC_ROWS, LANES), F32))
    vectors = jnp.concatenate(vector_rows, axis=0).astype(BF)
    for k in range(plan.nd):
        first = plan.start[k]
        reld = jnp.right_shift(jnp.bitwise_xor(dp, k), 1)
        window = flat[first : first + plan.win, :].astype(BF)
        extra = vectors if k == plan.nd - 1 else rest

        @pl.when(side == k % 2)
        def _():
            near_ref[reld, : plan.win] = window
            near_ref[reld, plan.win :] = extra

        @pl.when(side != k % 2)
        def _():
            far_ref[reld, : plan.win] = window
            far_ref[reld, plan.win :] = extra


def backward(plan, tokens, wq, vec, seg, seg_row, keep_row, q, k, v, raw, o, lse, do, dh1, tail, gvec):
    rows = tokens.shape[0]
    windows = jax.ShapeDtypeStruct((plan.nd // 2, plan.tail, LANES), BF)
    stacked = pltpu.VMEM((PAIRS, TILES, 2 * TILE, LANES), BF)
    return pl.pallas_call(
        functools.partial(backward_kernel, plan),
        out_shape=(jax.ShapeDtypeStruct((rows, D), F32), windows, windows),
        in_specs=[VMEM, VMEM, VMEM, SMEM] + [VMEM] * 12,
        out_specs=(VMEM,) * 3,
        scratch_shapes=[
            stacked,
            stacked,
            stacked,
            stacked,
            pltpu.VMEM((TILES, D, TILE), BF),
            pltpu.VMEM((TILES, D, TILE), F32),
            pltpu.VMEM((PAIRS, TILES, TILE, LANES), F32),
            pltpu.VMEM((PAIRS, TILES, TILE, LANES), F32),
            pltpu.VMEM((TILES, 8, TILE), F32),
            pltpu.VMEM((SEQ, LANES), F32),
            pltpu.VMEM((D, 3 * D), F32),
            pltpu.VMEM((8, D), F32),
            pltpu.VMEM((round_up(plan.start[plan.nd - 1] + plan.win, 8), LANES), F32),
        ],
        compiler_params=params(),
    )(tokens, wq, vec, seg, seg_row, keep_row, q, k, v, raw, o, lse, do, dh1, tail, gvec)


def flat_place(plan, shape):
    row = lax.broadcasted_iota(jnp.int32, shape, 0)
    lane = lax.broadcasted_iota(jnp.int32, shape, 1)
    place = row * LANES + lane
    return place, plan.device() * plan.shard + place


def update_kernel(
    plan,
    rest_ref,
    first_ref,
    master_ref,
    moment_ref,
    second_ref,
    new_moment_ref,
    new_second_ref,
    update_ref,
    sums_ref,
    window,
):
    bucket = lax.axis_index("bucket")
    dp = lax.axis_index("dp")
    window[...] = jnp.where(bucket == 0, first_ref[: plan.win, :], rest_ref[...])
    place_vec = ROW_VEC - plan.start[-1]

    @pl.when(jnp.logical_and(bucket == plan.nb - 1, dp == plan.nd - 1))
    def _():
        window[place_vec : place_vec + VEC_ROWS, :] = first_ref[plan.win : plan.win + VEC_ROWS, :]

    offset = lax.rem(plan.device() * plan.shard, LANES)
    back = lax.rem(LANES - offset, LANES)
    turned = pltpu.roll(window[...], back, 1)
    above = pltpu.roll(turned, plan.win - 1, 0)
    lane = lax.broadcasted_iota(jnp.int32, turned.shape, 1)
    place, index = flat_place(plan, turned.shape)
    inside = place < plan.shard
    grad = jnp.where(inside, jnp.where(lane + offset < LANES, turned, above), 0.0)
    master = master_ref[...]
    moment = beta_one * moment_ref[...] + (1.0 - beta_one) * grad
    second = beta_two * second_ref[...] + (1.0 - beta_two) * grad * grad
    first_hat = moment / (1.0 - beta_one**STEP)
    second_hat = second / (1.0 - beta_two**STEP)
    decay = jnp.where(index < BOUNDS[4], weight_decay, 0.0)
    update = first_hat / (jnp.sqrt(second_hat) + adam_epsilon) + decay * master
    update = jnp.where(inside, update, 0.0)
    new_moment_ref[...] = moment
    new_second_ref[...] = second
    update_ref[...] = update
    master_sq = jnp.where(inside, master * master, 0.0)
    update_sq = update * update
    lanes = lax.broadcasted_iota(jnp.int32, (1, LANES), 1)
    rows = []
    for squares in (master_sq, update_sq):
        row = jnp.zeros((1, LANES), F32)
        for t in range(MATS):
            mine = jnp.logical_and(index >= BOUNDS[t], index < BOUNDS[t + 1])
            part = jnp.sum(jnp.where(mine, squares, 0.0), axis=0, keepdims=True)
            row = jnp.where(lanes == t, jnp.sum(part, axis=1, keepdims=True), row)
        rows.append(row)
    rows.append(jnp.zeros((6, LANES), F32))
    sums_ref[...] = jnp.concatenate(rows, axis=0)


def update_part(plan, rest, first, master_rows, moment_rows, second_rows):
    rows = jax.ShapeDtypeStruct((plan.win, LANES), F32)
    return pl.pallas_call(
        functools.partial(update_kernel, plan),
        out_shape=(rows, rows, rows, jax.ShapeDtypeStruct((8, LANES), F32)),
        in_specs=[VMEM] * 5,
        out_specs=(VMEM,) * 4,
        scratch_shapes=[pltpu.VMEM((plan.win, LANES), F32)],
        compiler_params=params(),
    )(rest, first, master_rows, moment_rows, second_rows)


def apply_kernel(plan, sums_ref, master_ref, update_ref, new_ref, norms_ref):
    roots = jnp.sqrt(sums_ref[...])
    trust = roots[0:1, :] / (roots[1:2, :] + adam_epsilon)
    norms_ref[...] = jnp.concatenate([roots[0:2, :], trust, roots[0:5, :]], axis=0)
    master = master_ref[...]
    _, index = flat_place(plan, master.shape)
    factor = jnp.broadcast_to(trust[:, 0:1], (1, LANES))
    factors = jnp.broadcast_to(factor, master.shape)
    for t in range(1, MATS):
        factor = jnp.broadcast_to(trust[:, t : t + 1], (1, LANES))
        factors = jnp.where(index >= BOUNDS[t], factor, factors)
    new_ref[...] = master - learn_rate * factors * update_ref[...]


def apply_part(plan, sums, master_rows, update_rows):
    return pl.pallas_call(
        functools.partial(apply_kernel, plan),
        out_shape=(
            jax.ShapeDtypeStruct((plan.win, LANES), F32),
            jax.ShapeDtypeStruct((8, LANES), F32),
        ),
        in_specs=[VMEM] * 3,
        out_specs=(VMEM,) * 2,
        compiler_params=params(),
    )(sums, master_rows, update_rows)


def groups_of(size, skip=0):
    bits = list(range(skip, size.bit_length() - 1))
    return [bits[i : i + 2] for i in range(0, len(bits), 2)]


def masks_of(bits):
    masks = [1 << bits[0]]
    if len(bits) == 2:
        masks += [1 << bits[1], (1 << bits[0]) | (1 << bits[1])]
    return masks


def swap(x, axis, size, mask, targets=None):
    pairs = [(i, i ^ mask) for i in range(size)]
    if targets is not None:
        pairs = [pair for pair in pairs if pair[1] in targets]
    return lax.ppermute(x, axis, pairs)


def tree_sum(parts):
    if len(parts) == 4:
        return (parts[0] + parts[1]) + (parts[2] + parts[3])
    return parts[0] + parts[1]


def gather_windows(plan, window):
    held = window[None]
    for bits in groups_of(plan.nd, 1):
        held = jnp.concatenate(
            [held] + [swap(held, "dp", plan.nd, mask) for mask in masks_of(bits)], axis=0
        )
    for bits in groups_of(plan.nb):
        held = jnp.concatenate(
            [held] + [swap(held, "bucket", plan.nb, mask) for mask in masks_of(bits)], axis=0
        )
    return held, swap(held, "dp", plan.nd, 1)


def scatter_dp(plan, held):
    for bits in reversed(groups_of(plan.nd, 1)):
        size = 1 << len(bits)
        step = held.shape[0] // size
        parts = [held[i * step : (i + 1) * step] for i in range(size)]
        got = [parts[0].astype(F32)]
        for i, mask in zip(range(1, size), masks_of(bits)):
            got.append(swap(parts[i].astype(BF), "dp", plan.nd, mask).astype(F32))
        held = tree_sum(got)
    return held[0]


def scatter_rest(plan, near, far):
    got = swap(far, "dp", plan.nd, 1)
    held = [near[i].astype(F32) + got[i].astype(F32) for i in range(plan.nb)]
    targets = set(range(1, plan.nb))
    (bits,) = groups_of(plan.nb)
    parts = [held[0]]
    for i, mask in zip(range(1, plan.nb), masks_of(bits)):
        parts.append(
            swap(held[i].astype(BF), "bucket", plan.nb, mask, targets).astype(F32)
        )
    return scatter_dp(plan, tree_sum(parts))


def scatter_first(plan, near, far):
    got = swap(far, "dp", plan.nd, 1)
    own = scatter_dp(plan, near.astype(F32) + got.astype(F32))
    (bits,) = groups_of(plan.nb)
    low = own.astype(BF)
    parts = [own] + [
        swap(low, "bucket", plan.nb, mask).astype(F32) for mask in masks_of(bits)
    ]
    return tree_sum(parts)


def sum_all(plan, x):
    x = x + swap(x, "dp", plan.nd, 1)
    for axis, size, skip in (("dp", plan.nd, 1), ("bucket", plan.nb, 0)):
        for bits in groups_of(size, skip):
            x = tree_sum([x] + [swap(x, axis, size, mask) for mask in masks_of(bits)])
    return x


def local(
    plan, tokens, cotangent, segment_ids, keep_mask, bucket_patches, master, first_moment, second_moment
):
    def as_rows(flat):
        return jnp.pad(flat, (0, plan.win * LANES - plan.shard)).reshape(plan.win, LANES)

    def as_flat(rows):
        return rows.reshape(-1)[: plan.shard]

    master_rows = as_rows(master)
    seg_row = segment_ids.reshape(1, SEQ)
    keep_row = keep_mask.reshape(1, SEQ)
    own, other = gather_windows(plan, prepare(plan, master_rows, keep_row))
    wq, wo, wu, wd, vec, kept = assemble(plan, own, other)
    q, k, v, raw, o, ot, lse = forward(plan, tokens, wq, vec, segment_ids, seg_row, keep_row)
    block_output, dh1, do, near, far, tail, gvec = middle_part(
        plan, tokens, cotangent, o, ot, wo, wu, wd, vec, keep_row, kept, bucket_patches
    )
    rest = scatter_rest(plan, near, far)
    input_grad, near_first, far_first = backward(
        plan, tokens, wq, vec, segment_ids, seg_row, keep_row, q, k, v, raw, o, lse, do, dh1, tail, gvec
    )
    first = scatter_first(plan, near_first, far_first)
    moment_rows, second_rows, update_rows, sums = update_part(
        plan, rest, first, master_rows, as_rows(first_moment), as_rows(second_moment)
    )
    new_master, norms = apply_part(plan, sum_all(plan, sums), master_rows, update_rows)
    return (
        block_output,
        input_grad,
        as_flat(moment_rows),
        as_flat(second_rows),
        as_flat(new_master),
        norms[0:2, :MATS],
        norms[2, :MATS],
    )


def solution(mesh):
    shards = mesh.shape["bucket"] * mesh.shape["dp"]
    plan = Plan(mesh.shape, PARAMS // shards)
    both = ("bucket", "dp")
    return jax.shard_map(
        functools.partial(local, plan),
        mesh=mesh,
        in_specs=(P(both, None), P(both, None), P(both), P(both), P(), P(both), P(both), P(both)),
        out_specs=(P(both, None), P(both, None), P(both), P(both), P(both), P(), P()),
        check_vma=False,
    )
```

```python
import functools
import math

import jax
import jax.numpy as jnp
from jax import lax
from jax.experimental import pallas as pl
from jax.experimental.pallas import tpu as pltpu
from jax.sharding import PartitionSpec as P

D = 384
HEADS = 6
HD = 64
FF = 1536
SEQ = 1024
STEP = 10
MATS = 10
LANES = 128
PAIRS = HEADS // 2
TILE = 256
TILES = SEQ // TILE
BLOCKS = SEQ // LANES

norm_epsilon = 1e-06
adam_epsilon = 1e-06
beta_one = 0.9
beta_two = 0.999
learn_rate = 0.5
weight_decay = 0.01
masked_score = -1e30

MATRIX_END = 4 * D * D + 2 * D * FF
BOUNDS = [0, 3 * D * D, 4 * D * D, 4 * D * D + D * FF, MATRIX_END] + [
    MATRIX_END + (j + 1) * D for j in range(6)
]
PARAMS = BOUNDS[-1]
ROW_OUT = BOUNDS[1] // LANES
ROW_UP = BOUNDS[2] // LANES
ROW_DOWN = BOUNDS[3] // LANES
ROW_VEC = BOUNDS[4] // LANES
VEC_ROWS = 6 * D // LANES
ROWS_ALL = PARAMS // LANES

score_scale = HD ** (-0.5) * math.log2(math.e)
grad_scale = HD ** (-0.5)

BF = jnp.bfloat16
F32 = jnp.float32
VMEM = pl.BlockSpec(memory_space=pltpu.VMEM)
SMEM = pl.BlockSpec(memory_space=pltpu.SMEM)


QUICK = pl.CostEstimate(flops=1000, bytes_accessed=1000, transcendentals=0)


def params(limit):
    return pltpu.CompilerParams(vmem_limit_bytes=limit * 1024 * 1024)


def round_up(value, step):
    return -(-value // step) * step


class Plan:
    def __init__(self, mesh_shape, shard):
        self.nb = mesh_shape["bucket"]
        self.nd = mesh_shape["dp"]
        self.n = self.nb * self.nd
        self.shard = shard
        self.start = [k * shard // LANES for k in range(self.n)]
        self.rows = [
            -(-((k + 1) * shard) // LANES) - self.start[k] for k in range(self.n)
        ]
        self.win = round_up(max(self.rows) + 1, 16)
        self.tail = round_up(self.win + VEC_ROWS, 16)
        self.vec_place = ROW_VEC - self.start[-1]
        self.vec_from = self.vec_place // 16 * 16
        self.kept_row = 2 * self.win - self.vec_from
        self.early = self.kept_row + 16

    def device(self):
        return lax.axis_index("bucket") * self.nd + lax.axis_index("dp")


def nn(a, b):
    return lax.dot_general(a, b, (((1,), (0,)), ((), ())), preferred_element_type=F32)


def nt(a, b):
    return lax.dot_general(a, b, (((1,), (1,)), ((), ())), preferred_element_type=F32)


def split_low(x):
    high = x.astype(BF)
    return high, (x - high.astype(F32)).astype(BF)


def rows_at(step):
    return pl.ds(pl.multiple_of(step * TILE, TILE), TILE)


def norm_parts(values):
    average = jnp.mean(values, axis=-1, keepdims=True)
    centered = values - average
    variance = jnp.mean(centered * centered, axis=-1, keepdims=True)
    rstd = lax.rsqrt(variance + norm_epsilon)
    return centered * rstd, rstd


def norm_back(hat, rstd, grad):
    mean_grad = jnp.mean(grad, axis=-1, keepdims=True)
    mean_both = jnp.mean(grad * hat, axis=-1, keepdims=True)
    return rstd * (grad - mean_grad - hat * mean_both)


def head_mean_matrix():
    row = lax.broadcasted_iota(jnp.int32, (TILE, TILE), 0)
    col = lax.broadcasted_iota(jnp.int32, (TILE, TILE), 1)
    return jnp.where(row // HD == col // HD, 1.0 / HD, 0.0).astype(BF)


def head_mean_low(low, matrix):
    rest = D - TILE
    return jnp.concatenate(
        [nn(low[:, :TILE], matrix), nn(low[:, TILE:], matrix[:rest, :rest])], axis=1
    )


def head_mean(x, matrix):
    high, rest = split_low(x)
    return head_mean_low(high, matrix) + head_mean_low(rest, matrix)


def prepare_kernel(plan, master_ref, keep_ref, out_ref):
    me = plan.device()
    offset = lax.rem(me * plan.shard, LANES)
    values = master_ref[...]
    turned = pltpu.roll(values, offset, 1)
    below = pltpu.roll(turned, 1, 0)
    lane = lax.broadcasted_iota(jnp.int32, values.shape, 1)
    row = lax.broadcasted_iota(jnp.int32, values.shape, 0)
    count = jnp.sum(keep_ref[...].astype(F32), axis=1, keepdims=True)
    high = jnp.floor(count * (1.0 / 32.0))
    parts = jnp.where(lane == 0, high, jnp.where(lane == 1, count - 32.0 * high, 0.0))
    window = jnp.where(lane < offset, below, turned)
    out_ref[...] = jnp.where(row == plan.win - 1, parts, window).astype(BF)


def prepare(plan, master_rows, keep_row):
    return pl.pallas_call(
        functools.partial(prepare_kernel, plan),
        out_shape=jax.ShapeDtypeStruct((plan.win, LANES), BF),
        in_specs=[VMEM, VMEM],
        out_specs=VMEM,
        compiler_params=params(8),
    )(master_rows, keep_row)


def held_window(own_ref, other_ref, rel, at):
    place = jnp.right_shift(rel, 1)
    return jnp.where(
        jnp.bitwise_and(rel, 1) == 0,
        own_ref[place, at].astype(F32),
        other_ref[place, at].astype(F32),
    )


def lay_windows(plan, owners, rel_of, own_ref, other_ref, flat, base):
    for k in owners:
        window = held_window(own_ref, other_ref, rel_of(k), slice(0, plan.win))
        first, count = plan.start[k] - base, plan.rows[k]
        shared = k > 0 and (k * plan.shard) % LANES
        if shared:
            before = flat[first : first + 1, :]
        flat[first : first + count, :] = window[:count]
        if shared:
            flat[first : first + 1, :] = before + window[:1]


def take_matrix(target, flat, base, height, width):
    stride = width // LANES
    for j in range(stride):
        target[:, j * LANES : (j + 1) * LANES] = flat[pl.ds(base + j, height, stride=stride), :].astype(BF)


def put_matrix(flat, base, source, height, width):
    stride = width // LANES
    for j in range(stride):
        flat[pl.ds(base + j, height, stride=stride), :] = source[:, j * LANES : (j + 1) * LANES]


def key_chunks(seg_ref, ti):
    first_i, last_i = seg_ref[ti * TILE], seg_ref[ti * TILE + TILE - 1]
    low, high = jnp.int32(0), jnp.int32(0)
    for b in range(BLOCKS):
        low += (seg_ref[b * LANES + LANES - 1] < first_i).astype(jnp.int32)
        high += (seg_ref[b * LANES] <= last_i).astype(jnp.int32)
    count = jnp.right_shift(high - low + 1, 1)
    return jnp.minimum(low, BLOCKS - 2 * count), count


def tile_bias(ti, block, row_seg, key_seg):
    key_place = lax.broadcasted_iota(jnp.int32, (TILE, TILE), 0) + block * LANES
    row_place = lax.broadcasted_iota(jnp.int32, (TILE, TILE), 1) + ti * TILE
    return jnp.where(
        jnp.logical_or(key_seg == row_seg, key_place == row_place), 0.0, masked_score
    )


def keys_at(block):
    return pl.ds(pl.multiple_of(block * LANES, LANES), TILE)


def side_rows(stacked, side):
    return jnp.concatenate(
        [stacked[side * LANES : (side + 1) * LANES], stacked[(2 + side) * LANES : (3 + side) * LANES]],
        axis=0,
    )


def to_column(row):
    return jnp.transpose(jnp.broadcast_to(row, (LANES, row.shape[1])))


def block_heads(pair):
    lane = lax.broadcasted_iota(jnp.int32, pair.shape, 1)
    zero = jnp.zeros_like(pair)
    sides = [jnp.where(lane < HD, pair, zero), jnp.where(lane >= HD, pair, zero)]
    return [side[b * LANES : (b + 1) * LANES] for b in range(2) for side in sides]


def put_blocks(ref, hp, step, pair):
    for i, part in enumerate(block_heads(pair)):
        ref[hp, 2 * step + i // 2, i % 2] = part


def two_blocks(ref, hp, block):
    return ref[hp, pl.ds(block, 2)].reshape(4 * LANES, LANES)


def stack_heads(pair):
    lane = lax.broadcasted_iota(jnp.int32, pair.shape, 1)
    zero = jnp.zeros_like(pair)
    return jnp.concatenate(
        [jnp.where(lane < HD, pair, zero), jnp.where(lane >= HD, pair, zero)], axis=0
    )


def project_kernel(
    plan,
    own_ref,
    other_ref,
    tokens_ref,
    wq_ref,
    vec_ref,
    head_ref,
    kept_ref,
    q_ref,
    k_ref,
    v_ref,
    hat_ref,
    rstd_ref,
    flat,
):
    dp = lax.axis_index("dp")
    lay_windows(plan, range(plan.nd), lambda k: jnp.bitwise_xor(dp, k), own_ref, other_ref, flat, 0)
    take_matrix(wq_ref, flat, 0, D, 3 * D)
    head_ref[...] = flat[ROW_OUT : ROW_OUT + 8, :]
    rel = jnp.bitwise_xor(dp, plan.nd - 1)
    late = held_window(own_ref, other_ref, rel, slice(plan.win, plan.kept_row))
    kept = jnp.zeros((1, LANES), F32)
    for j in range(plan.nd):
        half = other_ref if j & 1 else own_ref
        kept = kept + half[j >> 1, plan.kept_row :].astype(F32)[15:16]
    kept_ref[...] = jnp.broadcast_to(32.0 * kept[:, 0:1] + kept[:, 1:2], kept_ref.shape)
    for t in range(6):
        for j in range(D // LANES):
            at = plan.vec_place - plan.vec_from + 3 * t + j
            vec_ref[t : t + 1, j * LANES : (j + 1) * LANES] = late[at : at + 1]
    matrix = head_mean_matrix()
    gain1, shift1 = vec_ref[0:1, :], vec_ref[1:2, :]
    gain_q, gain_k = vec_ref[2:3, :], vec_ref[3:4, :]

    def project(step, carry):
        at = rows_at(step)
        hat, _ = norm_parts(tokens_ref[at, :].astype(F32))
        low = (hat * gain1 + shift1).astype(BF)
        raw = nn(low, wq_ref[...])

        def head_norm(low_out, part, gain):
            lanes = slice(part * D, (part + 1) * D)
            x = raw[:, lanes]
            centered = x - head_mean(x, matrix)
            rstd = lax.rsqrt(head_mean(centered * centered, matrix) + norm_epsilon)
            normed = centered * rstd
            hat_ref[at, lanes] = normed
            rstd_ref[at, lanes] = rstd
            low_out[at, :] = (normed * gain).astype(BF)

        head_norm(q_ref, 0, gain_q)
        head_norm(k_ref, 1, gain_k)
        v_ref[at, :] = raw[:, 2 * D :].astype(BF)
        return carry

    lax.fori_loop(0, TILES, project, 0)


def project_part(plan, own, other, tokens):
    rows = tokens.shape[0]
    low = jax.ShapeDtypeStruct((rows, D), BF)
    return pl.pallas_call(
        functools.partial(project_kernel, plan),
        out_shape=(
            jax.ShapeDtypeStruct((D, 3 * D), BF),
            jax.ShapeDtypeStruct((8, D), F32),
            jax.ShapeDtypeStruct((8, LANES), F32),
            jax.ShapeDtypeStruct((8, LANES), F32),
            low,
            low,
            low,
            jax.ShapeDtypeStruct((rows, 2 * D), F32),
            jax.ShapeDtypeStruct((rows, 2 * D), F32),
        ),
        in_specs=[VMEM] * 3,
        out_specs=(VMEM,) * 9,
        scratch_shapes=[
            pltpu.VMEM((round_up(plan.start[plan.nd - 1] + plan.win, 8), LANES), F32),
        ],
        compiler_params=params(24),
        cost_estimate=QUICK,
    )(own, other, tokens)


def forward_kernel(
    plan,
    seg_smem,
    seg_ref,
    keep_ref,
    q_ref,
    k_ref,
    v_ref,
    o_ref,
    ot_ref,
    lse_ref,
    kab,
    vt,
    ot,
    sums,
    segk,
    expo,
):
    seg_row = seg_ref[...].astype(F32)
    segk[...] = to_column(jnp.where(keep_ref[...] == 1, seg_row, -1.0))

    def stack(step, carry):
        at = rows_at(step)
        for hp in range(PAIRS):
            put_blocks(kab, hp, step, k_ref[at, hp * LANES : (hp + 1) * LANES])
        vt[:, at] = jnp.transpose(v_ref[at, :].astype(F32)).astype(BF)
        return carry

    lax.fori_loop(0, TILES, stack, 0)

    def query_tile(ti, carry):
        ot[...] = jnp.zeros_like(ot)
        sums[...] = jnp.zeros_like(sums)
        row_seg = seg_ref[:, rows_at(ti)].astype(F32)
        first, count = key_chunks(seg_smem, ti)

        def score_chunk(c, inner):
            block = first + 2 * c
            column = segk[keys_at(block), :]
            bias = tile_bias(ti, block, row_seg, jnp.concatenate([column, column], axis=1))
            for hp in range(PAIRS):
                queries = q_ref[rows_at(ti), hp * LANES : (hp + 1) * LANES]
                scores = nt(two_blocks(kab, hp, block), queries)
                for side in range(2):
                    head = 2 * hp + side
                    value = jnp.exp2(side_rows(scores, side) * score_scale + bias)
                    expo[c, head] = value
                    sums[head : head + 1, :] += jnp.sum(value, axis=0, keepdims=True)
            return inner

        lax.fori_loop(0, count, score_chunk, 0)
        lse_ref[ti] = jnp.log2(sums[...])
        sums[...] = 1.0 / sums[...]

        def value_chunk(c, inner):
            keys = keys_at(first + 2 * c)
            for head in range(HEADS):
                prob = (expo[c, head] * sums[head : head + 1, :]).astype(BF)
                at = slice(head * HD, (head + 1) * HD)
                ot[at, :] += nn(vt[at, keys], prob)
            return inner

        lax.fori_loop(0, count, value_chunk, 0)
        attended = ot[...]
        ot_ref[ti] = attended.astype(BF)
        o_ref[rows_at(ti), :] = jnp.transpose(attended).astype(BF)
        return carry

    lax.fori_loop(0, TILES, query_tile, 0)


def forward(plan, seg, seg_row, keep_row, q, k, v):
    rows = q.shape[0]
    return pl.pallas_call(
        functools.partial(forward_kernel, plan),
        out_shape=(
            jax.ShapeDtypeStruct((rows, D), BF),
            jax.ShapeDtypeStruct((TILES, D, TILE), BF),
            jax.ShapeDtypeStruct((TILES, 8, TILE), F32),
        ),
        in_specs=[SMEM] + [VMEM] * 5,
        out_specs=(VMEM,) * 3,
        scratch_shapes=[
            pltpu.VMEM((PAIRS, BLOCKS, 2, LANES, LANES), BF),
            pltpu.VMEM((D, SEQ), BF),
            pltpu.VMEM((D, TILE), F32),
            pltpu.VMEM((8, TILE), F32),
            pltpu.VMEM((SEQ, LANES), F32),
            pltpu.VMEM((TILES, HEADS, TILE, TILE), F32),
        ],
        compiler_params=params(24),
        cost_estimate=QUICK,
    )(seg, seg_row, keep_row, q, k, v)


erfc_step = 0.3275911 * math.sqrt(0.5)
erfc_terms = [0.254829592, -0.284496736, 1.421413741, -1.453152027, 1.061405429]


def normal_parts(u):
    expo = jnp.exp2(u * u * (-0.5 * math.log2(math.e)))
    t = 1.0 / (1.0 + erfc_step * jnp.abs(u))
    poly = 0.5 * erfc_terms[4]
    for term in reversed(erfc_terms[:4]):
        poly = poly * t + 0.5 * term
    below = poly * t * expo
    return jnp.where(u > 0.0, 1.0 - below, below), expo * (1.0 / math.sqrt(2.0 * math.pi))


def middle_kernel(
    plan,
    tokens_ref,
    cot_ref,
    o_ref,
    ot_ref,
    own_ref,
    other_ref,
    head_ref,
    kept_ref,
    vec_ref,
    keep_ref,
    patches_ref,
    out_ref,
    dh1_ref,
    do_ref,
    near_ref,
    far_ref,
    tail_ref,
    gvec_ref,
    keepc,
    gout,
    gup,
    gdownt,
    flat,
    wo_ref,
    wu_ref,
    wd_ref,
):
    bucket = lax.axis_index("bucket")
    base = ROW_OUT
    flat[0:8, :] = head_ref[...]
    dp = lax.axis_index("dp")
    lay_windows(
        plan,
        range(plan.nd, plan.n),
        lambda k: (k // plan.nd - 1) * plan.nd + jnp.bitwise_xor(dp, k % plan.nd),
        own_ref,
        other_ref,
        flat,
        base,
    )
    take_matrix(wo_ref, flat, 0, D, D)
    take_matrix(wu_ref, flat, ROW_UP - base, D, FF)
    take_matrix(wd_ref, flat, ROW_DOWN - base, FF, D)
    gain2, shift2 = vec_ref[4:5, :], vec_ref[5:6, :]
    own = patches_ref[bucket].astype(F32)
    total = patches_ref[0].astype(F32)
    for b in range(1, plan.nb):
        total = total + patches_ref[b].astype(F32)
    ones = jnp.ones((1, LANES), F32)
    scale = (plan.nb * own) * ones / (total * ones) * float(SEQ * plan.nd) / kept_ref[0:1, :]
    keepc[...] = to_column(keep_ref[...].astype(F32)) * scale
    gout[...] = jnp.zeros_like(gout)
    gup[...] = jnp.zeros_like(gup)
    gdownt[...] = jnp.zeros_like(gdownt)
    gvec_ref[...] = jnp.zeros_like(gvec_ref)

    def chunk(step, carry):
        at = rows_at(step)
        middle = tokens_ref[at, :].astype(F32) + nn(o_ref[at, :], wo_ref[...])
        hat, rstd = norm_parts(middle)
        low = (hat * gain2 + shift2).astype(BF)
        u = nn(low, wu_ref[...])
        phi, bell = normal_parts(u)
        hidden = (u * phi).astype(BF)
        out_ref[at, :] = (middle + nn(hidden, wd_ref[...])).astype(BF)
        weights = keepc[at, :]
        seed = cot_ref[at, :].astype(F32) * jnp.concatenate([weights] * (D // LANES), axis=1)
        seed_low = seed.astype(BF)
        du = (nt(seed_low, wd_ref[...]) * (phi + u * bell)).astype(BF)
        gdownt[...] += nn(jnp.transpose(seed).astype(BF), hidden)
        gup[...] += nn(jnp.transpose(low.astype(F32)).astype(BF), du)
        da2 = nt(du, wu_ref[...])
        gvec_ref[0:1, :] += jnp.sum(da2 * hat, axis=0, keepdims=True)
        gvec_ref[1:2, :] += jnp.sum(da2, axis=0, keepdims=True)
        dh1 = seed + norm_back(hat, rstd, da2 * gain2)
        dh1_ref[at, :] = dh1
        dh1_low = dh1.astype(BF)
        gout[...] += nn(ot_ref[step], dh1_low)
        do_ref[at, :] = nt(dh1_low, wo_ref[...]).astype(BF)
        return carry

    lax.fori_loop(0, o_ref.shape[0] // TILE, chunk, 0)

    put_matrix(flat, 0, gout, D, D)
    put_matrix(flat, ROW_UP - base, gup, D, FF)
    for j in range(D // LANES):
        flat[pl.ds(ROW_DOWN - base + j, FF, stride=D // LANES), :] = jnp.transpose(
            gdownt[j * LANES : (j + 1) * LANES, :]
        )
    tail_ref[...] = flat[0:8, :]
    side = jnp.bitwise_and(dp, 1)
    for k in range(plan.nd, plan.n):
        first = plan.start[k] - base
        quarter = k // plan.nd - 1
        reld = jnp.right_shift(jnp.bitwise_xor(dp, k % plan.nd), 1)
        window = flat[first : first + plan.win, :].astype(BF)

        @pl.when(side == k % 2)
        def _():
            near_ref[quarter, reld] = window

        @pl.when(side != k % 2)
        def _():
            far_ref[quarter, reld] = window


def middle_part(plan, tokens, cot, o, ot, own, other, head, kept, vec, keep_row, patches):
    rows = tokens.shape[0]
    windows = jax.ShapeDtypeStruct((plan.nb - 1, plan.nd // 2, plan.win, LANES), BF)
    return pl.pallas_call(
        functools.partial(middle_kernel, plan),
        out_shape=(
            jax.ShapeDtypeStruct((rows, D), BF),
            jax.ShapeDtypeStruct((rows, D), F32),
            jax.ShapeDtypeStruct((rows, D), BF),
            windows,
            windows,
            jax.ShapeDtypeStruct((8, LANES), F32),
            jax.ShapeDtypeStruct((8, D), F32),
        ),
        in_specs=[VMEM] * 10 + [SMEM],
        out_specs=(VMEM,) * 7,
        scratch_shapes=[
            pltpu.VMEM((rows, LANES), F32),
            pltpu.VMEM((D, D), F32),
            pltpu.VMEM((D, FF), F32),
            pltpu.VMEM((D, FF), F32),
            pltpu.VMEM((round_up(plan.start[-1] + plan.win - ROW_OUT, 8), LANES), F32),
            pltpu.VMEM((D, D), BF),
            pltpu.VMEM((D, FF), BF),
            pltpu.VMEM((FF, D), BF),
        ],
        compiler_params=params(30),
        cost_estimate=QUICK,
    )(tokens, cot, o, ot, own, other, head, kept, vec, keep_row, patches)


def backward_kernel(
    plan,
    vec_ref,
    seg_smem,
    seg_ref,
    keep_ref,
    lse_ref,
    q_ref,
    k_ref,
    v_ref,
    o_ref,
    do_ref,
    hat_ref,
    rstd_ref,
    token_ref,
    low_ref,
    gains_ref,
    kab,
    vab,
    qab,
    dab,
    kt,
    dqt,
    dk,
    dv,
    inner_sums,
    segk,
):
    matrix = head_mean_matrix()
    seg_row = seg_ref[...].astype(F32)
    segk[...] = to_column(jnp.where(keep_ref[...] == 1, seg_row, -1.0))
    head_row = lax.broadcasted_iota(jnp.int32, (8, D), 0)
    head_lane = lax.broadcasted_iota(jnp.int32, (8, D), 1)
    hot = jnp.where(head_lane // HD == head_row, 1.0, 0.0).astype(BF)
    dqt[...] = jnp.zeros_like(dqt)
    dk[...] = jnp.zeros_like(dk)
    dv[...] = jnp.zeros_like(dv)
    gains_ref[...] = jnp.zeros_like(gains_ref)

    def stack(step, carry):
        at = rows_at(step)
        keys = k_ref[at, :]
        grads = do_ref[at, :]
        for hp in range(PAIRS):
            lanes = slice(hp * LANES, (hp + 1) * LANES)
            put_blocks(kab, hp, step, keys[:, lanes])
            put_blocks(vab, hp, step, v_ref[at, lanes])
            qab[hp, step] = stack_heads(q_ref[at, lanes])
            dab[hp, step] = stack_heads(grads[:, lanes])
        kt[:, at] = jnp.transpose(keys.astype(F32)).astype(BF)
        high, rest = split_low(grads.astype(F32) * o_ref[at, :].astype(F32))
        inner_sums[step] = nt(hot, high) + nt(hot, rest)
        return carry

    lax.fori_loop(0, TILES, stack, 0)

    def query_tile(ti, carry):
        row_seg = seg_ref[:, rows_at(ti)].astype(F32)
        first, count = key_chunks(seg_smem, ti)

        def key_chunk(c, inner):
            block = first + 2 * c
            keys = keys_at(block)
            column = segk[keys, :]
            bias = tile_bias(ti, block, row_seg, jnp.concatenate([column, column], axis=1))
            for hp in range(PAIRS):
                lanes = slice(hp * LANES, (hp + 1) * LANES)
                scores = nt(two_blocks(kab, hp, block), q_ref[rows_at(ti), lanes])
                grads = nt(two_blocks(vab, hp, block), do_ref[rows_at(ti), lanes])
                probs, dscores = [], []
                for side in range(2):
                    head = 2 * hp + side
                    prob = jnp.exp2(
                        side_rows(scores, side) * score_scale
                        + (bias - lse_ref[ti, head : head + 1, :])
                    )
                    dscore = prob * (side_rows(grads, side) - inner_sums[ti, head : head + 1, :])
                    dscore = dscore.astype(BF)
                    probs.append(prob.astype(BF))
                    dscores.append(dscore)
                    at = slice(head * HD, (head + 1) * HD)
                    dqt[ti, at, :] += nn(kt[at, keys], dscore)
                dv[hp, keys] += nn(jnp.concatenate(probs, axis=1), dab[hp, ti])
                dk[hp, keys] += nn(jnp.concatenate(dscores, axis=1), qab[hp, ti])
            return inner

        lax.fori_loop(0, count, key_chunk, 0)
        return carry

    lax.fori_loop(0, TILES, query_tile, 0)

    def finish(step, carry):
        at = rows_at(step)

        def head_norm_back(part, gain, grad):
            lanes = slice(part * D, (part + 1) * D)
            hat = hat_ref[at, lanes]
            both = grad * hat
            gains_ref[part : part + 1, :] += jnp.sum(both, axis=0, keepdims=True)
            scaled = grad * gain
            mean_grad = head_mean_low(scaled.astype(BF), matrix)
            mean_both = head_mean_low((both * gain).astype(BF), matrix)
            back = rstd_ref[at, lanes] * (scaled - mean_grad - hat * mean_both)
            low_ref[at, lanes] = back.astype(BF)

        grad_k = jnp.concatenate([dk[hp, at] for hp in range(PAIRS)], axis=1) * grad_scale
        grad_v = jnp.concatenate([dv[hp, at] for hp in range(PAIRS)], axis=1)
        head_norm_back(0, vec_ref[2:3, :], jnp.transpose(dqt[step]) * grad_scale)
        head_norm_back(1, vec_ref[3:4, :], grad_k)
        low_ref[at, 2 * D :] = grad_v.astype(BF)
        return carry

    lax.fori_loop(0, TILES, finish, 0)


def backward(plan, vec, seg, seg_row, keep_row, lse, q, k, v, o, do, hat, rstd, token):
    rows = q.shape[0]
    stacked = pltpu.VMEM((PAIRS, TILES, 2 * TILE, LANES), BF)
    blocked = pltpu.VMEM((PAIRS, BLOCKS, 2, LANES, LANES), BF)
    return pl.pallas_call(
        functools.partial(backward_kernel, plan),
        out_shape=(
            jax.ShapeDtypeStruct((rows, 3 * D), BF),
            jax.ShapeDtypeStruct((8, D), F32),
        ),
        in_specs=[VMEM, SMEM] + [VMEM] * 11,
        out_specs=(VMEM, VMEM),
        scratch_shapes=[
            blocked,
            blocked,
            stacked,
            stacked,
            pltpu.VMEM((D, SEQ), BF),
            pltpu.VMEM((TILES, D, TILE), F32),
            pltpu.VMEM((PAIRS, SEQ, LANES), F32),
            pltpu.VMEM((PAIRS, SEQ, LANES), F32),
            pltpu.VMEM((TILES, 8, TILE), F32),
            pltpu.VMEM((SEQ, LANES), F32),
        ],
        compiler_params=params(32),
        cost_estimate=QUICK,
    )(vec, seg, seg_row, keep_row, lse, q, k, v, o, do, hat, rstd, token)


def finish_kernel(
    plan,
    tokens_ref,
    wq_ref,
    vec_ref,
    dh1_ref,
    tail_ref,
    gvec_ref,
    low_ref,
    gqk_ref,
    grad_ref,
    near_ref,
    far0_ref,
    far1_ref,
    gq,
    gains,
    flat,
):
    gain1, shift1 = vec_ref[0:1, :], vec_ref[1:2, :]
    gq[...] = jnp.zeros_like(gq)
    gains[...] = jnp.zeros_like(gains)

    def finish(step, carry):
        at = rows_at(step)
        low = low_ref[at, :]
        hat, rstd = norm_parts(tokens_ref[at, :].astype(F32))
        normed = hat * gain1 + shift1
        gq[...] += nn(jnp.transpose(normed).astype(BF), low)
        da1 = nt(low, wq_ref[...])
        gains[0:1, :] += jnp.sum(da1 * hat, axis=0, keepdims=True)
        gains[1:2, :] += jnp.sum(da1, axis=0, keepdims=True)
        grad_ref[at, :] = dh1_ref[at, :] + norm_back(hat, rstd, da1 * gain1)
        return carry

    lax.fori_loop(0, TILES, finish, 0)
    gains[2:4, :] = gqk_ref[0:2, :]
    gains[4:6, :] = gvec_ref[0:2, :]
    put_matrix(flat, 0, gq, D, 3 * D)
    flat[ROW_OUT : ROW_OUT + 8, :] = tail_ref[...]
    dp = lax.axis_index("dp")
    side = jnp.bitwise_and(dp, 1)
    rest = jnp.zeros((plan.tail - plan.win, LANES), BF)
    vector_rows = []
    for t in range(6):
        for j in range(D // LANES):
            vector_rows.append(gains[t : t + 1, j * LANES : (j + 1) * LANES])
    vector_rows.append(jnp.zeros((plan.tail - plan.win - VEC_ROWS, LANES), F32))
    vectors = jnp.concatenate(vector_rows, axis=0).astype(BF)
    for k in range(plan.nd):
        first = plan.start[k]
        reld = jnp.right_shift(jnp.bitwise_xor(dp, k), 1)
        window = flat[first : first + plan.win, :].astype(BF)
        window = jnp.concatenate([window, vectors if k == plan.nd - 1 else rest], axis=0)

        @pl.when(side == k % 2)
        def _():
            near_ref[reld] = window

        @pl.when(side != k % 2)
        def _():
            far0_ref[reld] = window[: plan.tail // 2]
            far1_ref[reld] = window[plan.tail // 2 :]


def finish_part(plan, tokens, wq, vec, dh1, tail, gvec, low, gains):
    rows = tokens.shape[0]
    windows = jax.ShapeDtypeStruct((plan.nd // 2, plan.tail, LANES), BF)
    halves = jax.ShapeDtypeStruct((plan.nd // 2, plan.tail // 2, LANES), BF)
    return pl.pallas_call(
        functools.partial(finish_kernel, plan),
        out_shape=(jax.ShapeDtypeStruct((rows, D), F32), windows, halves, halves),
        in_specs=[VMEM] * 8,
        out_specs=(VMEM,) * 4,
        scratch_shapes=[
            pltpu.VMEM((D, 3 * D), F32),
            pltpu.VMEM((8, D), F32),
            pltpu.VMEM((round_up(plan.start[plan.nd - 1] + plan.win, 8), LANES), F32),
        ],
        compiler_params=params(28),
        cost_estimate=QUICK,
    )(tokens, wq, vec, dh1, tail, gvec, low, gains)


def flat_place(plan, shape):
    row = lax.broadcasted_iota(jnp.int32, shape, 0)
    lane = lax.broadcasted_iota(jnp.int32, shape, 1)
    place = row * LANES + lane
    return place, plan.device() * plan.shard + place


def update_kernel(
    plan,
    own_ref,
    got0_ref,
    got1_ref,
    got2_ref,
    master_ref,
    moment_ref,
    second_ref,
    new_moment_ref,
    new_second_ref,
    update_ref,
    sums_ref,
    window,
):
    bucket = lax.axis_index("bucket")
    dp = lax.axis_index("dp")
    total = tree_sum([ref[...].astype(F32) for ref in (own_ref, got0_ref, got1_ref, got2_ref)])
    window[...] = jnp.where(bucket == 0, total[plan.win : 2 * plan.win], total[: plan.win])

    @pl.when(jnp.logical_and(bucket == plan.nb - 1, dp == plan.nd - 1))
    def _():
        window[plan.vec_place : plan.vec_place + VEC_ROWS, :] = total[
            2 * plan.win : 2 * plan.win + VEC_ROWS
        ]

    offset = lax.rem(plan.device() * plan.shard, LANES)
    back = lax.rem(LANES - offset, LANES)
    turned = pltpu.roll(window[...], back, 1)
    above = pltpu.roll(turned, plan.win - 1, 0)
    lane = lax.broadcasted_iota(jnp.int32, turned.shape, 1)
    place, index = flat_place(plan, turned.shape)
    inside = place < plan.shard
    grad = jnp.where(inside, jnp.where(lane + offset < LANES, turned, above), 0.0)
    master = master_ref[...]
    moment = beta_one * moment_ref[...] + (1.0 - beta_one) * grad
    second = beta_two * second_ref[...] + (1.0 - beta_two) * grad * grad
    first_hat = moment / (1.0 - beta_one**STEP)
    second_hat = second / (1.0 - beta_two**STEP)
    decay = jnp.where(index < BOUNDS[4], weight_decay, 0.0)
    update = first_hat / (jnp.sqrt(second_hat) + adam_epsilon) + decay * master
    update = jnp.where(inside, update, 0.0)
    new_moment_ref[...] = moment
    new_second_ref[...] = second
    update_ref[...] = update
    master_sq = jnp.where(inside, master * master, 0.0)
    update_sq = update * update
    lanes = lax.broadcasted_iota(jnp.int32, (1, LANES), 1)
    rows = []
    for squares in (master_sq, update_sq):
        row = jnp.zeros((1, LANES), F32)
        for t in range(MATS):
            mine = jnp.logical_and(index >= BOUNDS[t], index < BOUNDS[t + 1])
            part = jnp.sum(jnp.where(mine, squares, 0.0), axis=0, keepdims=True)
            row = jnp.where(lanes == t, jnp.sum(part, axis=1, keepdims=True), row)
        rows.append(row)
    rows.append(jnp.zeros((6, LANES), F32))
    sums_ref[...] = jnp.concatenate(rows, axis=0)


def update_part(plan, parts, master_rows, moment_rows, second_rows):
    rows = jax.ShapeDtypeStruct((plan.win, LANES), F32)
    return pl.pallas_call(
        functools.partial(update_kernel, plan),
        out_shape=(rows, rows, rows, jax.ShapeDtypeStruct((8, LANES), F32)),
        in_specs=[VMEM] * 7,
        out_specs=(VMEM,) * 4,
        scratch_shapes=[pltpu.VMEM((plan.win, LANES), F32)],
        compiler_params=params(12),
    )(*parts, master_rows, moment_rows, second_rows)


def apply_kernel(plan, *refs):
    *sums_refs, master_ref, update_ref, new_ref, norms_ref, trust_ref = refs
    roots = jnp.sqrt(tree_sum([ref[...] for ref in sums_refs]))
    trust = roots[0:1, :] / (roots[1:2, :] + adam_epsilon)
    norms_ref[...] = roots[0:2, :MATS]
    trust_ref[...] = trust[:, :MATS]
    master = master_ref[...]
    _, index = flat_place(plan, master.shape)
    factors = jnp.broadcast_to(trust[:, 0:1], master.shape)
    for t in range(1, MATS):
        factors = jnp.where(index >= BOUNDS[t], trust[:, t : t + 1], factors)
    new_ref[...] = master - learn_rate * factors * update_ref[...]


def apply_part(plan, sums, master_rows, update_rows):
    return pl.pallas_call(
        functools.partial(apply_kernel, plan),
        out_shape=(
            jax.ShapeDtypeStruct((plan.win, LANES), F32),
            jax.ShapeDtypeStruct((2, MATS), F32),
            jax.ShapeDtypeStruct((1, MATS), F32),
        ),
        in_specs=[VMEM] * (len(sums) + 2),
        out_specs=(VMEM,) * 3,
        compiler_params=params(8),
    )(*sums, master_rows, update_rows)


def lay_column_kernel(*refs):
    for i, part in enumerate(refs[:-1]):
        refs[-1][i] = part[...]


def lay_column(parts):
    return pl.pallas_call(
        lay_column_kernel,
        out_shape=jax.ShapeDtypeStruct((len(parts), *parts[0].shape), parts[0].dtype),
        in_specs=[VMEM] * len(parts),
        out_specs=VMEM,
        compiler_params=params(4),
    )(*parts)


def choose_kernel(plan, *refs):
    columns, (early_ref, late_ref) = refs[:-2], refs[-2:]
    step = columns[0].shape[0]
    bucket = lax.axis_index("bucket")
    early_ref[:, plan.kept_row :] = columns[0][:, plan.win - 16 :]
    for i, part in enumerate(columns):
        owner = jnp.bitwise_xor(bucket, i)

        @pl.when(owner == 0)
        def _():
            early_ref[:, : plan.win] = part[...]

        @pl.when(owner == plan.nb - 1)
        def _():
            early_ref[:, plan.win : plan.kept_row] = part[:, plan.vec_from :]

        @pl.when(owner > 0)
        def _():
            late_ref[pl.ds((owner - 1) * step, step)] = part[...]


def choose(plan, columns):
    step = columns[0].shape[0]
    return pl.pallas_call(
        functools.partial(choose_kernel, plan),
        out_shape=(
            jax.ShapeDtypeStruct((step, plan.early, LANES), BF),
            jax.ShapeDtypeStruct(((plan.nb - 1) * step, plan.win, LANES), BF),
        ),
        in_specs=[VMEM] * len(columns),
        out_specs=(VMEM, VMEM),
        compiler_params=params(8),
    )(*columns)


def add_parts_kernel(halves, *refs):
    refs = list(refs)
    parts = [[refs.pop(0) for _ in range(count)] for count in halves]
    for i, out in enumerate(refs[1:-1]):
        step = out.shape[-3]
        at = slice(i * step, (i + 1) * step)
        at = (slice(None), at) if len(out.shape) == 4 else at
        values = [
            jnp.concatenate([half[at].astype(F32) for half in part], axis=-2) for part in parts
        ]
        out[...] = tree_sum(values).astype(out.dtype)
    refs[-1][...] = jnp.zeros_like(refs[-1])


def add_parts(parts, pieces, token):
    *lead, total, height, width = parts[0].shape
    parts = [part if isinstance(part, list) else [part] for part in parts]
    halves = [len(part) for part in parts]
    parts = [half for part in parts for half in part]
    return pl.pallas_call(
        functools.partial(add_parts_kernel, halves),
        out_shape=tuple(
            jax.ShapeDtypeStruct((*lead, total // pieces, height, width), BF if i else F32)
            for i in range(pieces)
        )
        + (jax.ShapeDtypeStruct((8, LANES), F32),),
        in_specs=[VMEM] * (len(parts) + 1),
        out_specs=(VMEM,) * (pieces + 1),
        compiler_params=params(14),
    )(*parts, token)


def blend_kernel(plan, count, *refs):
    rest = refs[0]
    parts, outs = refs[1 : 1 + count], refs[1 + count :]
    bucket = lax.axis_index("bucket")
    first = tree_sum([part[...].astype(F32) for part in parts])
    for i, out in enumerate(outs):
        quarter = jnp.maximum(jnp.bitwise_xor(bucket, i) - 1, 0)
        out[: plan.win] = rest[quarter].astype(out.dtype)
        out[plan.win :] = first.astype(out.dtype)


def blend(plan, rest, parts):
    height = plan.win + plan.tail
    return pl.pallas_call(
        functools.partial(blend_kernel, plan, len(parts)),
        out_shape=tuple(
            jax.ShapeDtypeStruct((height, LANES), BF if i else F32) for i in range(plan.nb)
        ),
        in_specs=[VMEM] * (1 + len(parts)),
        out_specs=(VMEM,) * plan.nb,
        compiler_params=params(8),
    )(rest, *parts)


def add_rows_kernel(*refs):
    refs[-1][...] = tree_sum([ref[...] for ref in refs[:-1]])


def add_rows(parts):
    return pl.pallas_call(
        add_rows_kernel,
        out_shape=jax.ShapeDtypeStruct(parts[0].shape, F32),
        in_specs=[VMEM] * len(parts),
        out_specs=VMEM,
        compiler_params=params(4),
    )(*parts)


def groups_of(size, skip=0):
    bits = list(range(skip, size.bit_length() - 1))
    return [bits[i : i + 2] for i in range(0, len(bits), 2)]


def masks_of(bits):
    masks = [1 << bits[0]]
    if len(bits) == 2:
        masks += [1 << bits[1], (1 << bits[0]) | (1 << bits[1])]
    return masks


def swap(x, axis, size, mask):
    return lax.ppermute(x, axis, [(i, i ^ mask) for i in range(size)])


def tree_sum(parts):
    if len(parts) == 4:
        return (parts[0] + parts[1]) + (parts[2] + parts[3])
    return parts[0] + parts[1]


def with_partners(x, axis, size, bits):
    return [x] + [swap(x, axis, size, mask) for mask in masks_of(bits)]


def gather_windows(plan, window):
    first, *more = groups_of(plan.nd, 1)
    column = lay_column(with_partners(window, "dp", plan.nd, first))
    for bits in more:
        column = jnp.concatenate(with_partners(column, "dp", plan.nd, bits), axis=0)
    (bits,) = groups_of(plan.nb)
    early, late = choose(plan, with_partners(column, "bucket", plan.nb, bits))
    return (early, swap(early, "dp", plan.nd, 1)), (late, swap(late, "dp", plan.nd, 1))


def scatter_dp(plan, pieces):
    *more, last = groups_of(plan.nd, 1)
    got = [pieces[0]] + [
        swap(piece, "dp", plan.nd, mask) for piece, mask in zip(pieces[1:], masks_of(last))
    ]
    for bits in reversed(more):
        held = tree_sum([x.astype(F32) for x in got])
        size = 1 << len(bits)
        step = held.shape[-3] // size
        parts = [held[..., i * step : (i + 1) * step, :, :] for i in range(size)]
        got = [parts[0]] + [
            swap(part.astype(BF), "dp", plan.nd, mask)
            for part, mask in zip(parts[1:], masks_of(bits))
        ]
    return [x.reshape(*x.shape[:-3], *x.shape[-2:]) for x in got]


def sum_all(plan, x):
    x = [x, swap(x, "dp", plan.nd, 1)]
    for bits in groups_of(plan.nd, 1):
        x = with_partners(add_rows(x), "dp", plan.nd, bits)
    (bits,) = groups_of(plan.nb)
    return with_partners(add_rows(x), "bucket", plan.nb, bits)


def local(
    plan, tokens, cotangent, segment_ids, keep_mask, bucket_patches, master, first_moment, second_moment
):
    def as_rows(flat):
        return jnp.pad(flat, (0, plan.win * LANES - plan.shard)).reshape(plan.win, LANES)

    def as_flat(rows):
        return rows.reshape(-1)[: plan.shard]

    master_rows = as_rows(master)
    seg_row = segment_ids.reshape(1, SEQ)
    keep_row = keep_mask.reshape(1, SEQ)
    count = 1 << len(groups_of(plan.nd, 1)[-1])
    (b_bits,) = groups_of(plan.nb)

    early, late = gather_windows(plan, prepare(plan, master_rows, keep_row))
    wq, vec, head, kept, q, k, v, hat, rstd = project_part(plan, *early, tokens)
    o, ot, lse = forward(plan, segment_ids, seg_row, keep_row, q, k, v)
    block_output, dh1, do, near, far, tail, gvec = middle_part(
        plan, tokens, cotangent, o, ot, *late, head, kept, vec, keep_row, bucket_patches
    )
    *pieces, token = add_parts([near, swap(far, "dp", plan.nd, 1)], count, gvec)
    rest = scatter_dp(plan, pieces)
    low, gains = backward(
        plan, vec, segment_ids, seg_row, keep_row, lse, q, k, v, o, do, hat, rstd, token
    )
    input_grad, near, *far = finish_part(plan, tokens, wq, vec, dh1, tail, gvec, low, gains)
    rest, token = add_parts(rest, 1, gains)
    *pieces, _ = add_parts([near, [swap(half, "dp", plan.nd, 1) for half in far]], count, token)
    first = scatter_dp(plan, pieces)
    mine, *sent = blend(plan, rest, first)
    parts = [mine] + [
        swap(x, "bucket", plan.nb, mask) for x, mask in zip(sent, masks_of(b_bits))
    ]
    moment_rows, second_rows, update_rows, sums = update_part(
        plan, parts, master_rows, as_rows(first_moment), as_rows(second_moment)
    )
    new_master, norms, trust = apply_part(plan, sum_all(plan, sums), master_rows, update_rows)
    return (
        block_output,
        input_grad,
        as_flat(moment_rows),
        as_flat(second_rows),
        as_flat(new_master),
        norms,
        trust.reshape(MATS),
    )


def solution(mesh):
    shards = mesh.shape["bucket"] * mesh.shape["dp"]
    plan = Plan(mesh.shape, PARAMS // shards)
    both = ("bucket", "dp")
    return jax.shard_map(
        functools.partial(local, plan),
        mesh=mesh,
        in_specs=(P(both, None), P(both, None), P(both), P(both), P(), P(both), P(both), P(both)),
        out_specs=(P(both, None), P(both, None), P(both), P(both), P(both), P(), P()),
        check_vma=False,
    )
```

```python
import functools
import math

import jax
import jax.numpy as jnp
from jax import lax
from jax.experimental import pallas as pl
from jax.experimental.pallas import tpu as pltpu
from jax.sharding import PartitionSpec as P

D = 384
HEADS = 6
HD = 64
FF = 1536
SEQ = 1024
STEP = 10
MATS = 10
LANES = 128
PAIRS = HEADS // 2
TILE = 256
TILES = SEQ // TILE
BLOCKS = SEQ // LANES
MIDDLE_BLOCK = 512
FAR_PARTS = 3

norm_epsilon = 1e-06
adam_epsilon = 1e-06
beta_one = 0.9
beta_two = 0.999
learn_rate = 0.5
weight_decay = 0.01
masked_score = -1e30

MATRIX_END = 4 * D * D + 2 * D * FF
BOUNDS = [0, 3 * D * D, 4 * D * D, 4 * D * D + D * FF, MATRIX_END] + [
    MATRIX_END + (j + 1) * D for j in range(6)
]
PARAMS = BOUNDS[-1]
ROW_OUT = BOUNDS[1] // LANES
ROW_UP = BOUNDS[2] // LANES
ROW_DOWN = BOUNDS[3] // LANES
ROW_VEC = BOUNDS[4] // LANES
VEC_ROWS = 6 * D // LANES
ROWS_ALL = PARAMS // LANES

score_scale = HD ** (-0.5) * math.log2(math.e)
grad_scale = HD ** (-0.5)

BF = jnp.bfloat16
F32 = jnp.float32
VMEM = pl.BlockSpec(memory_space=pltpu.VMEM)
SMEM = pl.BlockSpec(memory_space=pltpu.SMEM)


QUICK = pl.CostEstimate(flops=1000, bytes_accessed=1000, transcendentals=0)


def params(limit):
    return pltpu.CompilerParams(vmem_limit_bytes=limit * 1024 * 1024)


def round_up(value, step):
    return -(-value // step) * step


class Plan:
    def __init__(self, mesh_shape, shard):
        self.nb = mesh_shape["bucket"]
        self.nd = mesh_shape["dp"]
        self.n = self.nb * self.nd
        self.shard = shard
        self.start = [k * shard // LANES for k in range(self.n)]
        self.rows = [
            -(-((k + 1) * shard) // LANES) - self.start[k] for k in range(self.n)
        ]
        self.win = round_up(max(self.rows) + 1, 16)
        self.tail = round_up(self.win + VEC_ROWS, 16 * FAR_PARTS)
        self.vec_place = ROW_VEC - self.start[-1]
        self.vec_from = self.vec_place // 16 * 16
        self.kept_row = 2 * self.win - self.vec_from
        self.early = self.kept_row + 16

    def device(self):
        return lax.axis_index("bucket") * self.nd + lax.axis_index("dp")


def nn(a, b):
    return lax.dot_general(a, b, (((1,), (0,)), ((), ())), preferred_element_type=F32)


def nt(a, b):
    return lax.dot_general(a, b, (((1,), (1,)), ((), ())), preferred_element_type=F32)


def split_low(x):
    high = x.astype(BF)
    return high, (x - high.astype(F32)).astype(BF)


def rows_at(step):
    if isinstance(step, int):
        return slice(step * TILE, (step + 1) * TILE)
    return pl.ds(pl.multiple_of(step * TILE, TILE), TILE)


def norm_parts(values):
    average = jnp.mean(values, axis=-1, keepdims=True)
    centered = values - average
    variance = jnp.mean(centered * centered, axis=-1, keepdims=True)
    rstd = lax.rsqrt(variance + norm_epsilon)
    return centered * rstd, rstd


def norm_back(hat, rstd, grad):
    mean_grad = jnp.mean(grad, axis=-1, keepdims=True)
    mean_both = jnp.mean(grad * hat, axis=-1, keepdims=True)
    return rstd * (grad - mean_grad - hat * mean_both)


def head_mean_matrix():
    row = lax.broadcasted_iota(jnp.int32, (TILE, TILE), 0)
    col = lax.broadcasted_iota(jnp.int32, (TILE, TILE), 1)
    return jnp.where(row // HD == col // HD, 1.0 / HD, 0.0).astype(BF)


def head_mean_low(low, matrix):
    rest = D - TILE
    return jnp.concatenate(
        [nn(low[:, :TILE], matrix), nn(low[:, TILE:], matrix[:rest, :rest])], axis=1
    )


def head_mean(x, matrix):
    high, rest = split_low(x)
    return head_mean_low(high, matrix) + head_mean_low(rest, matrix)


def prepare_kernel(plan, master_ref, keep_ref, out_ref):
    me = plan.device()
    offset = lax.rem(me * plan.shard, LANES)
    values = master_ref[...]
    turned = pltpu.roll(values, offset, 1)
    below = pltpu.roll(turned, 1, 0)
    lane = lax.broadcasted_iota(jnp.int32, values.shape, 1)
    row = lax.broadcasted_iota(jnp.int32, values.shape, 0)
    count = jnp.sum(keep_ref[...].astype(F32), axis=1, keepdims=True)
    high = jnp.floor(count * (1.0 / 32.0))
    parts = jnp.where(lane == 0, high, jnp.where(lane == 1, count - 32.0 * high, 0.0))
    window = jnp.where(lane < offset, below, turned)
    out_ref[...] = jnp.where(row == plan.win - 1, parts, window).astype(BF)


def prepare(plan, master_rows, keep_row):
    return pl.pallas_call(
        functools.partial(prepare_kernel, plan),
        out_shape=jax.ShapeDtypeStruct((plan.win, LANES), BF),
        in_specs=[VMEM, VMEM],
        out_specs=VMEM,
        compiler_params=params(8),
    )(master_rows, keep_row)


def held_window(own_ref, other_ref, rel, at):
    place = jnp.right_shift(rel, 1)
    return jnp.where(
        jnp.bitwise_and(rel, 1) == 0,
        own_ref[place, at].astype(F32),
        other_ref[place, at].astype(F32),
    )


def lay_windows(plan, owners, refs_of, flat, base):
    dp = lax.axis_index("dp")
    for k in owners:
        own_ref, other_ref = refs_of(k)
        window = held_window(own_ref, other_ref, jnp.bitwise_xor(dp, k % plan.nd), slice(0, plan.win))
        first, count = plan.start[k] - base, plan.rows[k]
        shared = k > 0 and (k * plan.shard) % LANES
        if shared:
            before = flat[first : first + 1, :]
        flat[first : first + count, :] = window[:count]
        if shared:
            flat[first : first + 1, :] = before + window[:1]


def take_matrix(target, flat, base, height, width):
    stride = width // LANES
    for j in range(stride):
        target[:, j * LANES : (j + 1) * LANES] = flat[pl.ds(base + j, height, stride=stride), :].astype(BF)


def put_matrix(flat, base, source, height, width):
    stride = width // LANES
    for j in range(stride):
        flat[pl.ds(base + j, height, stride=stride), :] = source[:, j * LANES : (j + 1) * LANES]


def key_chunks(seg_ref, ti):
    first_i, last_i = seg_ref[ti * TILE], seg_ref[ti * TILE + TILE - 1]
    low, high = jnp.int32(0), jnp.int32(0)
    for b in range(BLOCKS):
        low += (seg_ref[b * LANES + LANES - 1] < first_i).astype(jnp.int32)
        high += (seg_ref[b * LANES] <= last_i).astype(jnp.int32)
    count = jnp.right_shift(high - low + 1, 1)
    return jnp.minimum(low, BLOCKS - 2 * count), count


def tile_bias(ti, block, row_seg, key_seg):
    key_place = lax.broadcasted_iota(jnp.int32, (TILE, TILE), 0) + block * LANES
    row_place = lax.broadcasted_iota(jnp.int32, (TILE, TILE), 1) + ti * TILE
    return jnp.where(
        jnp.logical_or(key_seg == row_seg, key_place == row_place), 0.0, masked_score
    )


def keys_at(block):
    return pl.ds(pl.multiple_of(block * LANES, LANES), TILE)


def side_rows(stacked, side):
    return jnp.concatenate(
        [stacked[side * LANES : (side + 1) * LANES], stacked[(2 + side) * LANES : (3 + side) * LANES]],
        axis=0,
    )


def to_column(row):
    return jnp.transpose(jnp.broadcast_to(row, (LANES, row.shape[1])))


def block_heads(pair):
    lane = lax.broadcasted_iota(jnp.int32, pair.shape, 1)
    zero = jnp.zeros_like(pair)
    sides = [jnp.where(lane < HD, pair, zero), jnp.where(lane >= HD, pair, zero)]
    return [side[b * LANES : (b + 1) * LANES] for b in range(2) for side in sides]


def put_blocks(ref, hp, step, pair):
    for i, part in enumerate(block_heads(pair)):
        ref[hp, 2 * step + i // 2, i % 2] = part


def two_blocks(ref, hp, block):
    return ref[hp, pl.ds(block, 2)].reshape(4 * LANES, LANES)


def stack_heads(pair):
    lane = lax.broadcasted_iota(jnp.int32, pair.shape, 1)
    zero = jnp.zeros_like(pair)
    return jnp.concatenate(
        [jnp.where(lane < HD, pair, zero), jnp.where(lane >= HD, pair, zero)], axis=0
    )


def project_kernel(
    plan,
    own_ref,
    other_ref,
    tokens_ref,
    wq_ref,
    vec_ref,
    head_ref,
    kept_ref,
    q_ref,
    k_ref,
    v_ref,
    hat_ref,
    rstd_ref,
    flat,
):
    dp = lax.axis_index("dp")
    lay_windows(plan, range(plan.nd), lambda k: (own_ref, other_ref), flat, 0)
    take_matrix(wq_ref, flat, 0, D, 3 * D)
    head_ref[...] = flat[ROW_OUT : ROW_OUT + 8, :]
    rel = jnp.bitwise_xor(dp, plan.nd - 1)
    late = held_window(own_ref, other_ref, rel, slice(plan.win, plan.kept_row))
    kept = jnp.zeros((1, LANES), F32)
    for j in range(plan.nd):
        half = other_ref if j & 1 else own_ref
        kept = kept + half[j >> 1, plan.kept_row :].astype(F32)[15:16]
    kept_ref[...] = jnp.broadcast_to(32.0 * kept[:, 0:1] + kept[:, 1:2], kept_ref.shape)
    for t in range(6):
        for j in range(D // LANES):
            at = plan.vec_place - plan.vec_from + 3 * t + j
            vec_ref[t : t + 1, j * LANES : (j + 1) * LANES] = late[at : at + 1]
    matrix = head_mean_matrix()
    gain1, shift1 = vec_ref[0:1, :], vec_ref[1:2, :]
    gain_q, gain_k = vec_ref[2:3, :], vec_ref[3:4, :]

    hat, _ = norm_parts(tokens_ref[...].astype(F32))
    raw = nn((hat * gain1 + shift1).astype(BF), wq_ref[...])

    def head_norm(low_out, part, gain):
        lanes = slice(part * D, (part + 1) * D)
        x = raw[:, lanes]
        centered = x - head_mean(x, matrix)
        rstd = lax.rsqrt(head_mean(centered * centered, matrix) + norm_epsilon)
        normed = centered * rstd
        hat_ref[:, lanes] = normed
        rstd_ref[:, lanes] = rstd
        low_out[...] = (normed * gain).astype(BF)

    head_norm(q_ref, 0, gain_q)
    head_norm(k_ref, 1, gain_k)
    v_ref[...] = raw[:, 2 * D :].astype(BF)


def project_part(plan, own, other, tokens):
    rows = tokens.shape[0]
    low = jax.ShapeDtypeStruct((rows, D), BF)
    return pl.pallas_call(
        functools.partial(project_kernel, plan),
        out_shape=(
            jax.ShapeDtypeStruct((D, 3 * D), BF),
            jax.ShapeDtypeStruct((8, D), F32),
            jax.ShapeDtypeStruct((8, LANES), F32),
            jax.ShapeDtypeStruct((8, LANES), F32),
            low,
            low,
            low,
            jax.ShapeDtypeStruct((rows, 2 * D), F32),
            jax.ShapeDtypeStruct((rows, 2 * D), F32),
        ),
        in_specs=[VMEM] * 3,
        out_specs=(VMEM,) * 9,
        scratch_shapes=[
            pltpu.VMEM((round_up(plan.start[plan.nd - 1] + plan.win, 8), LANES), F32),
        ],
        compiler_params=params(24),
        cost_estimate=QUICK,
    )(own, other, tokens)


def forward_kernel(
    plan,
    seg_smem,
    seg_ref,
    keep_ref,
    q_ref,
    k_ref,
    v_ref,
    o_ref,
    ot_ref,
    lse_ref,
    kab,
    vt,
    ot,
    sums,
    segk,
    expo,
):
    seg_row = seg_ref[...].astype(F32)
    segk[...] = to_column(jnp.where(keep_ref[...] == 1, seg_row, -1.0))

    for step in range(TILES):
        at = rows_at(step)
        for hp in range(PAIRS):
            put_blocks(kab, hp, step, k_ref[at, hp * LANES : (hp + 1) * LANES])
        vt[:, at] = jnp.transpose(v_ref[at, :].astype(F32)).astype(BF)

    def query_tile(ti, carry):
        ot[...] = jnp.zeros_like(ot)
        sums[...] = jnp.zeros_like(sums)
        row_seg = seg_ref[:, rows_at(ti)].astype(F32)
        first, count = key_chunks(seg_smem, ti)

        def score_chunk(c, inner):
            block = first + 2 * c
            column = segk[keys_at(block), :]
            bias = tile_bias(ti, block, row_seg, jnp.concatenate([column, column], axis=1))
            for hp in range(PAIRS):
                queries = q_ref[rows_at(ti), hp * LANES : (hp + 1) * LANES]
                scores = nt(two_blocks(kab, hp, block), queries)
                for side in range(2):
                    head = 2 * hp + side
                    value = jnp.exp2(side_rows(scores, side) * score_scale + bias)
                    expo[c, head] = value
                    sums[head : head + 1, :] += jnp.sum(value, axis=0, keepdims=True)
            return inner

        lax.fori_loop(0, count, score_chunk, 0)
        lse_ref[ti] = jnp.log2(sums[...])
        sums[...] = 1.0 / sums[...]

        def value_chunk(c, inner):
            keys = keys_at(first + 2 * c)
            for head in range(HEADS):
                prob = (expo[c, head] * sums[head : head + 1, :]).astype(BF)
                at = slice(head * HD, (head + 1) * HD)
                ot[at, :] += nn(vt[at, keys], prob)
            return inner

        lax.fori_loop(0, count, value_chunk, 0)
        attended = ot[...]
        ot_ref[ti] = attended.astype(BF)
        o_ref[rows_at(ti), :] = jnp.transpose(attended).astype(BF)
        return carry

    lax.fori_loop(0, TILES, query_tile, 0)


def forward(plan, seg, seg_row, keep_row, q, k, v):
    rows = q.shape[0]
    return pl.pallas_call(
        functools.partial(forward_kernel, plan),
        out_shape=(
            jax.ShapeDtypeStruct((rows, D), BF),
            jax.ShapeDtypeStruct((TILES, D, TILE), BF),
            jax.ShapeDtypeStruct((TILES, 8, TILE), F32),
        ),
        in_specs=[SMEM] + [VMEM] * 5,
        out_specs=(VMEM,) * 3,
        scratch_shapes=[
            pltpu.VMEM((PAIRS, BLOCKS, 2, LANES, LANES), BF),
            pltpu.VMEM((D, SEQ), BF),
            pltpu.VMEM((D, TILE), F32),
            pltpu.VMEM((8, TILE), F32),
            pltpu.VMEM((SEQ, LANES), F32),
            pltpu.VMEM((TILES, HEADS, TILE, TILE), F32),
        ],
        compiler_params=params(24),
        cost_estimate=QUICK,
    )(seg, seg_row, keep_row, q, k, v)


erfc_step = 0.3275911 * math.sqrt(0.5)
erfc_terms = [0.254829592, -0.284496736, 1.421413741, -1.453152027, 1.061405429]


def normal_parts(u):
    expo = jnp.exp2(u * u * (-0.5 * math.log2(math.e)))
    t = 1.0 / (1.0 + erfc_step * jnp.abs(u))
    poly = 0.5 * erfc_terms[4]
    for term in reversed(erfc_terms[:4]):
        poly = poly * t + 0.5 * term
    below = poly * t * expo
    return jnp.where(u > 0.0, 1.0 - below, below), expo * (1.0 / math.sqrt(2.0 * math.pi))


def middle_kernel(plan, *refs):
    late_refs, rest = refs[: 2 * plan.nb - 2], refs[2 * plan.nb - 2 :]
    middle_body(plan, late_refs, *rest)


def middle_body(
    plan,
    late_refs,
    tokens_ref,
    cot_ref,
    o_ref,
    ot_ref,
    head_ref,
    kept_ref,
    vec_ref,
    keep_ref,
    patches_ref,
    out_ref,
    dh1_ref,
    do_ref,
    near_ref,
    far_ref,
    tail_ref,
    gvec_ref,
    keepc,
    hid,
    dus,
    flat,
    wo_ref,
    wu_ref,
    wd_ref,
):
    bucket = lax.axis_index("bucket")
    base = ROW_OUT
    flat[0:8, :] = head_ref[...]
    dp = lax.axis_index("dp")
    owns, others = late_refs[: plan.nb - 1], late_refs[plan.nb - 1 :]
    lay_windows(
        plan,
        range(plan.nd, plan.n),
        lambda k: (owns[k // plan.nd - 1], others[k // plan.nd - 1]),
        flat,
        base,
    )
    take_matrix(wo_ref, flat, 0, D, D)
    take_matrix(wu_ref, flat, ROW_UP - base, D, FF)
    take_matrix(wd_ref, flat, ROW_DOWN - base, FF, D)
    gain2, shift2 = vec_ref[4:5, :], vec_ref[5:6, :]
    own = patches_ref[bucket].astype(F32)
    total = patches_ref[0].astype(F32)
    for b in range(1, plan.nb):
        total = total + patches_ref[b].astype(F32)
    ones = jnp.ones((1, LANES), F32)
    scale = (plan.nb * own) * ones / (total * ones) * float(SEQ * plan.nd) / kept_ref[0:1, :]
    keepc[...] = to_column(keep_ref[...].astype(F32)) * scale
    gvec_ref[...] = jnp.zeros_like(gvec_ref)

    middle = tokens_ref[...].astype(F32) + nn(o_ref[...], wo_ref[...])
    hat, rstd = norm_parts(middle)
    low = (hat * gain2 + shift2).astype(BF)
    weights = keepc[...]
    seed = cot_ref[...].astype(F32) * jnp.concatenate([weights] * (D // LANES), axis=1)
    seed_low = seed.astype(BF)
    for first in range(0, FF, MIDDLE_BLOCK):
        cols = slice(first, first + MIDDLE_BLOCK)
        u = nn(low, wu_ref[:, cols])
        phi, bell = normal_parts(u)
        hid[:, cols] = (u * phi).astype(BF)
        dus[:, cols] = (nt(seed_low, wd_ref[cols, :]) * (phi + u * bell)).astype(BF)
    out_ref[...] = (middle + nn(hid[...], wd_ref[...])).astype(BF)
    seedt = jnp.transpose(seed).astype(BF)
    lowt = jnp.transpose(low.astype(F32)).astype(BF)
    da2 = nt(dus[...], wu_ref[...])
    gvec_ref[0:1, :] = jnp.sum(da2 * hat, axis=0, keepdims=True)
    gvec_ref[1:2, :] = jnp.sum(da2, axis=0, keepdims=True)
    dh1 = seed + norm_back(hat, rstd, da2 * gain2)
    dh1_ref[...] = dh1
    dh1_low = dh1.astype(BF)
    gout = nn(jnp.concatenate([ot_ref[t] for t in range(TILES)], axis=1), dh1_low)
    do_ref[...] = nt(dh1_low, wo_ref[...]).astype(BF)
    put_matrix(flat, 0, gout, D, D)
    block = 2 * TILE
    for i in range(FF // block):
        part = nn(lowt, dus[:, i * block : (i + 1) * block])
        for j in range(block // LANES):
            flat[pl.ds(ROW_UP - base + i * (block // LANES) + j, D, stride=FF // LANES), :] = part[
                :, j * LANES : (j + 1) * LANES
            ]
        part = jnp.transpose(nn(seedt, hid[:, i * block : (i + 1) * block]))
        for j in range(D // LANES):
            flat[
                pl.ds(ROW_DOWN - base + i * block * (D // LANES) + j, block, stride=D // LANES), :
            ] = part[:, j * LANES : (j + 1) * LANES]
    tail_ref[...] = flat[0:8, :]
    side = jnp.bitwise_and(dp, 1)
    for k in range(plan.nd, plan.n):
        first = plan.start[k] - base
        quarter = k // plan.nd - 1
        reld = jnp.right_shift(jnp.bitwise_xor(dp, k % plan.nd), 1)
        window = flat[first : first + plan.win, :].astype(BF)

        @pl.when(side == k % 2)
        def _():
            near_ref[quarter, reld] = window

        @pl.when(side != k % 2)
        def _():
            far_ref[quarter, reld] = window


def middle_part(plan, late, tokens, cot, o, ot, head, kept, vec, keep_row, patches):
    rows = tokens.shape[0]
    windows = jax.ShapeDtypeStruct((plan.nb - 1, plan.nd // 2, plan.win, LANES), BF)
    return pl.pallas_call(
        functools.partial(middle_kernel, plan),
        out_shape=(
            jax.ShapeDtypeStruct((rows, D), BF),
            jax.ShapeDtypeStruct((rows, D), F32),
            jax.ShapeDtypeStruct((rows, D), BF),
            windows,
            windows,
            jax.ShapeDtypeStruct((8, LANES), F32),
            jax.ShapeDtypeStruct((8, D), F32),
        ),
        in_specs=[VMEM] * (len(late) + 8) + [SMEM],
        out_specs=(VMEM,) * 7,
        scratch_shapes=[
            pltpu.VMEM((rows, LANES), F32),
            pltpu.VMEM((rows, FF), BF),
            pltpu.VMEM((rows, FF), BF),
            pltpu.VMEM((round_up(plan.start[-1] + plan.win - ROW_OUT, 8), LANES), F32),
            pltpu.VMEM((D, D), BF),
            pltpu.VMEM((D, FF), BF),
            pltpu.VMEM((FF, D), BF),
        ],
        compiler_params=params(36),
        cost_estimate=QUICK,
    )(*late, tokens, cot, o, ot, head, kept, vec, keep_row, patches)


def backward_kernel(
    plan,
    vec_ref,
    seg_smem,
    seg_ref,
    keep_ref,
    lse_ref,
    q_ref,
    k_ref,
    v_ref,
    o_ref,
    do_ref,
    hat_ref,
    rstd_ref,
    token_ref,
    low_ref,
    gains_ref,
    kab,
    vab,
    qab,
    dab,
    kt,
    dqt,
    dk,
    dv,
    inner_sums,
    segk,
):
    matrix = head_mean_matrix()
    seg_row = seg_ref[...].astype(F32)
    segk[...] = to_column(jnp.where(keep_ref[...] == 1, seg_row, -1.0))
    head_row = lax.broadcasted_iota(jnp.int32, (8, D), 0)
    head_lane = lax.broadcasted_iota(jnp.int32, (8, D), 1)
    hot = jnp.where(head_lane // HD == head_row, 1.0, 0.0).astype(BF)
    dqt[...] = jnp.zeros_like(dqt)
    dk[...] = jnp.zeros_like(dk)
    dv[...] = jnp.zeros_like(dv)
    gains_ref[...] = jnp.zeros_like(gains_ref)

    for step in range(TILES):
        at = rows_at(step)
        keys = k_ref[at, :]
        grads = do_ref[at, :]
        for hp in range(PAIRS):
            lanes = slice(hp * LANES, (hp + 1) * LANES)
            put_blocks(kab, hp, step, keys[:, lanes])
            put_blocks(vab, hp, step, v_ref[at, lanes])
            qab[hp, step] = stack_heads(q_ref[at, lanes])
            dab[hp, step] = stack_heads(grads[:, lanes])
        kt[:, at] = jnp.transpose(keys.astype(F32)).astype(BF)
        high, rest = split_low(grads.astype(F32) * o_ref[at, :].astype(F32))
        inner_sums[step] = nt(hot, high) + nt(hot, rest)

    def query_tile(ti, carry):
        row_seg = seg_ref[:, rows_at(ti)].astype(F32)
        first, count = key_chunks(seg_smem, ti)

        def key_chunk(c, inner):
            block = first + 2 * c
            keys = keys_at(block)
            column = segk[keys, :]
            bias = tile_bias(ti, block, row_seg, jnp.concatenate([column, column], axis=1))
            for hp in range(PAIRS):
                lanes = slice(hp * LANES, (hp + 1) * LANES)
                scores = nt(two_blocks(kab, hp, block), q_ref[rows_at(ti), lanes])
                grads = nt(two_blocks(vab, hp, block), do_ref[rows_at(ti), lanes])
                probs, dscores = [], []
                for side in range(2):
                    head = 2 * hp + side
                    prob = jnp.exp2(
                        side_rows(scores, side) * score_scale
                        + (bias - lse_ref[ti, head : head + 1, :])
                    )
                    dscore = prob * (side_rows(grads, side) - inner_sums[ti, head : head + 1, :])
                    dscore = dscore.astype(BF)
                    probs.append(prob.astype(BF))
                    dscores.append(dscore)
                    at = slice(head * HD, (head + 1) * HD)
                    dqt[ti, at, :] += nn(kt[at, keys], dscore)
                dv[hp, keys] += nn(jnp.concatenate(probs, axis=1), dab[hp, ti])
                dk[hp, keys] += nn(jnp.concatenate(dscores, axis=1), qab[hp, ti])
            return inner

        lax.fori_loop(0, count, key_chunk, 0)
        return carry

    lax.fori_loop(0, TILES, query_tile, 0)

    def finish(step, carry):
        at = rows_at(step)

        def head_norm_back(part, gain, grad):
            lanes = slice(part * D, (part + 1) * D)
            hat = hat_ref[at, lanes]
            both = grad * hat
            gains_ref[part : part + 1, :] += jnp.sum(both, axis=0, keepdims=True)
            scaled = grad * gain
            mean_grad = head_mean_low(scaled.astype(BF), matrix)
            mean_both = head_mean_low((both * gain).astype(BF), matrix)
            back = rstd_ref[at, lanes] * (scaled - mean_grad - hat * mean_both)
            low_ref[at, lanes] = back.astype(BF)

        grad_k = jnp.concatenate([dk[hp, at] for hp in range(PAIRS)], axis=1) * grad_scale
        grad_v = jnp.concatenate([dv[hp, at] for hp in range(PAIRS)], axis=1)
        head_norm_back(0, vec_ref[2:3, :], jnp.transpose(dqt[step]) * grad_scale)
        head_norm_back(1, vec_ref[3:4, :], grad_k)
        low_ref[at, 2 * D :] = grad_v.astype(BF)
        return carry

    lax.fori_loop(0, TILES, finish, 0)


def backward(plan, vec, seg, seg_row, keep_row, lse, q, k, v, o, do, hat, rstd, token):
    rows = q.shape[0]
    stacked = pltpu.VMEM((PAIRS, TILES, 2 * TILE, LANES), BF)
    blocked = pltpu.VMEM((PAIRS, BLOCKS, 2, LANES, LANES), BF)
    return pl.pallas_call(
        functools.partial(backward_kernel, plan),
        out_shape=(
            jax.ShapeDtypeStruct((rows, 3 * D), BF),
            jax.ShapeDtypeStruct((8, D), F32),
        ),
        in_specs=[VMEM, SMEM] + [VMEM] * 11,
        out_specs=(VMEM, VMEM),
        scratch_shapes=[
            blocked,
            blocked,
            stacked,
            stacked,
            pltpu.VMEM((D, SEQ), BF),
            pltpu.VMEM((TILES, D, TILE), F32),
            pltpu.VMEM((PAIRS, SEQ, LANES), F32),
            pltpu.VMEM((PAIRS, SEQ, LANES), F32),
            pltpu.VMEM((TILES, 8, TILE), F32),
            pltpu.VMEM((SEQ, LANES), F32),
        ],
        compiler_params=params(32),
        cost_estimate=QUICK,
    )(vec, seg, seg_row, keep_row, lse, q, k, v, o, do, hat, rstd, token)


def finish_kernel(
    plan,
    tokens_ref,
    wq_ref,
    vec_ref,
    tail_ref,
    gvec_ref,
    low_ref,
    gqk_ref,
    da1_ref,
    near_ref,
    *refs,
):
    *far_refs, gains, flat = refs
    hat, _ = norm_parts(tokens_ref[...].astype(F32))
    normed = jnp.transpose(hat * vec_ref[0:1, :] + vec_ref[1:2, :]).astype(BF)
    for i in range(3):
        part = nn(normed, low_ref[:, i * D : (i + 1) * D])
        for j in range(D // LANES):
            flat[pl.ds(i * (D // LANES) + j, D, stride=3 * D // LANES), :] = part[
                :, j * LANES : (j + 1) * LANES
            ]
    da1 = nt(low_ref[...], wq_ref[...])
    da1_ref[...] = da1
    gains[...] = jnp.zeros_like(gains)
    gains[0:1, :] = jnp.sum(da1 * hat, axis=0, keepdims=True)
    gains[1:2, :] = jnp.sum(da1, axis=0, keepdims=True)
    gains[2:4, :] = gqk_ref[0:2, :]
    gains[4:6, :] = gvec_ref[0:2, :]
    flat[ROW_OUT : ROW_OUT + 8, :] = tail_ref[...]
    dp = lax.axis_index("dp")
    side = jnp.bitwise_and(dp, 1)
    rest = jnp.zeros((plan.tail - plan.win, LANES), BF)
    vector_rows = []
    for t in range(6):
        for j in range(D // LANES):
            vector_rows.append(gains[t : t + 1, j * LANES : (j + 1) * LANES])
    vector_rows.append(jnp.zeros((plan.tail - plan.win - VEC_ROWS, LANES), F32))
    vectors = jnp.concatenate(vector_rows, axis=0).astype(BF)
    for k in range(plan.nd):
        first = plan.start[k]
        reld = jnp.right_shift(jnp.bitwise_xor(dp, k), 1)
        window = flat[first : first + plan.win, :].astype(BF)
        window = jnp.concatenate([window, vectors if k == plan.nd - 1 else rest], axis=0)

        @pl.when(side == k % 2)
        def _():
            near_ref[reld] = window

        @pl.when(side != k % 2)
        def _():
            height = plan.tail // FAR_PARTS
            for i, far_ref in enumerate(far_refs):
                far_ref[reld] = window[i * height : (i + 1) * height]


def finish_part(plan, tokens, wq, vec, tail, gvec, low, gains):
    rows = tokens.shape[0]
    windows = jax.ShapeDtypeStruct((plan.nd // 2, plan.tail, LANES), BF)
    part = jax.ShapeDtypeStruct((plan.nd // 2, plan.tail // FAR_PARTS, LANES), BF)
    return pl.pallas_call(
        functools.partial(finish_kernel, plan),
        out_shape=(jax.ShapeDtypeStruct((rows, D), F32), windows) + (part,) * FAR_PARTS,
        in_specs=[VMEM] * 7,
        out_specs=(VMEM,) * (2 + FAR_PARTS),
        scratch_shapes=[
            pltpu.VMEM((8, D), F32),
            pltpu.VMEM((round_up(plan.start[plan.nd - 1] + plan.win, 8), LANES), F32),
        ],
        compiler_params=params(28),
        cost_estimate=QUICK,
    )(tokens, wq, vec, tail, gvec, low, gains)


def input_kernel(tokens_ref, vec_ref, da1_ref, dh1_ref, grad_ref, token_ref):
    hat, rstd = norm_parts(tokens_ref[...].astype(F32))
    grad_ref[...] = dh1_ref[...] + norm_back(hat, rstd, da1_ref[...] * vec_ref[0:1, :])
    token_ref[...] = jnp.zeros_like(token_ref)


def input_part(tokens, vec, da1, dh1):
    return pl.pallas_call(
        input_kernel,
        out_shape=(
            jax.ShapeDtypeStruct(dh1.shape, F32),
            jax.ShapeDtypeStruct((8, LANES), F32),
        ),
        in_specs=[VMEM] * 4,
        out_specs=(VMEM, VMEM),
        compiler_params=params(16),
        cost_estimate=QUICK,
    )(tokens, vec, da1, dh1)


def flat_place(plan, shape):
    row = lax.broadcasted_iota(jnp.int32, shape, 0)
    lane = lax.broadcasted_iota(jnp.int32, shape, 1)
    place = row * LANES + lane
    return place, plan.device() * plan.shard + place


def update_kernel(
    plan,
    own_ref,
    got0_ref,
    got1_ref,
    got2_ref,
    master_ref,
    moment_ref,
    second_ref,
    new_moment_ref,
    new_second_ref,
    update_ref,
    sums_ref,
    window,
):
    bucket = lax.axis_index("bucket")
    dp = lax.axis_index("dp")
    total = tree_sum([ref[...].astype(F32) for ref in (own_ref, got0_ref, got1_ref, got2_ref)])
    window[...] = total[: plan.win]

    @pl.when(jnp.logical_and(bucket == plan.nb - 1, dp == plan.nd - 1))
    def _():
        window[plan.vec_place : plan.vec_place + VEC_ROWS, :] = total[
            plan.win : plan.win + VEC_ROWS
        ]

    offset = lax.rem(plan.device() * plan.shard, LANES)
    back = lax.rem(LANES - offset, LANES)
    turned = pltpu.roll(window[...], back, 1)
    above = pltpu.roll(turned, plan.win - 1, 0)
    lane = lax.broadcasted_iota(jnp.int32, turned.shape, 1)
    place, index = flat_place(plan, turned.shape)
    inside = place < plan.shard
    grad = jnp.where(inside, jnp.where(lane + offset < LANES, turned, above), 0.0)
    master = master_ref[...]
    moment = beta_one * moment_ref[...] + (1.0 - beta_one) * grad
    second = beta_two * second_ref[...] + (1.0 - beta_two) * grad * grad
    first_hat = moment / (1.0 - beta_one**STEP)
    second_hat = second / (1.0 - beta_two**STEP)
    decay = jnp.where(index < BOUNDS[4], weight_decay, 0.0)
    update = first_hat / (jnp.sqrt(second_hat) + adam_epsilon) + decay * master
    update = jnp.where(inside, update, 0.0)
    new_moment_ref[...] = moment
    new_second_ref[...] = second
    update_ref[...] = update
    master_sq = jnp.where(inside, master * master, 0.0)
    update_sq = update * update
    lanes = lax.broadcasted_iota(jnp.int32, (1, LANES), 1)
    rows = []
    for squares in (master_sq, update_sq):
        row = jnp.zeros((1, LANES), F32)
        for t in range(MATS):
            mine = jnp.logical_and(index >= BOUNDS[t], index < BOUNDS[t + 1])
            part = jnp.sum(jnp.where(mine, squares, 0.0), axis=0, keepdims=True)
            row = jnp.where(lanes == t, jnp.sum(part, axis=1, keepdims=True), row)
        rows.append(row)
    rows.append(jnp.zeros((6, LANES), F32))
    sums_ref[...] = jnp.concatenate(rows, axis=0)


def update_part(plan, parts, master_rows, moment_rows, second_rows):
    rows = jax.ShapeDtypeStruct((plan.win, LANES), F32)
    return pl.pallas_call(
        functools.partial(update_kernel, plan),
        out_shape=(rows, rows, rows, jax.ShapeDtypeStruct((8, LANES), F32)),
        in_specs=[VMEM] * 7,
        out_specs=(VMEM,) * 4,
        scratch_shapes=[pltpu.VMEM((plan.win, LANES), F32)],
        compiler_params=params(12),
    )(*parts, master_rows, moment_rows, second_rows)


def apply_kernel(plan, *refs):
    *sums_refs, master_ref, update_ref, new_ref, norms_ref, trust_ref = refs
    roots = jnp.sqrt(tree_sum([ref[...] for ref in sums_refs]))
    trust = roots[0:1, :] / (roots[1:2, :] + adam_epsilon)
    norms_ref[...] = roots[0:2, :MATS]
    trust_ref[...] = trust[:, :MATS]
    master = master_ref[...]
    _, index = flat_place(plan, master.shape)
    factors = jnp.broadcast_to(trust[:, 0:1], master.shape)
    for t in range(1, MATS):
        factors = jnp.where(index >= BOUNDS[t], trust[:, t : t + 1], factors)
    new_ref[...] = master - learn_rate * factors * update_ref[...]


def apply_part(plan, sums, master_rows, update_rows):
    return pl.pallas_call(
        functools.partial(apply_kernel, plan),
        out_shape=(
            jax.ShapeDtypeStruct((plan.win, LANES), F32),
            jax.ShapeDtypeStruct((2, MATS), F32),
            jax.ShapeDtypeStruct((1, MATS), F32),
        ),
        in_specs=[VMEM] * (len(sums) + 2),
        out_specs=(VMEM,) * 3,
        compiler_params=params(8),
    )(*sums, master_rows, update_rows)


def lay_column_kernel(*refs):
    for i, part in enumerate(refs[:-1]):
        refs[-1][i] = part[...]


def lay_column(parts):
    return pl.pallas_call(
        lay_column_kernel,
        out_shape=jax.ShapeDtypeStruct((len(parts), *parts[0].shape), parts[0].dtype),
        in_specs=[VMEM] * len(parts),
        out_specs=VMEM,
        compiler_params=params(4),
    )(*parts)


def choose_kernel(plan, *refs):
    columns, early_ref, late_refs = refs[: plan.nb], refs[plan.nb], refs[plan.nb + 1 :]
    bucket = lax.axis_index("bucket")
    early_ref[:, plan.kept_row :] = columns[0][:, plan.win - 16 :]
    for i, part in enumerate(columns):
        owner = jnp.bitwise_xor(bucket, i)

        @pl.when(owner == 0)
        def _():
            early_ref[:, : plan.win] = part[...]

        @pl.when(owner == plan.nb - 1)
        def _():
            early_ref[:, plan.win : plan.kept_row] = part[:, plan.vec_from :]

        for quarter, late_ref in enumerate(late_refs):

            @pl.when(owner == quarter + 1)
            def _():
                late_ref[...] = part[...]


def choose(plan, columns):
    step = columns[0].shape[0]
    return pl.pallas_call(
        functools.partial(choose_kernel, plan),
        out_shape=(
            jax.ShapeDtypeStruct((step, plan.early, LANES), BF),
        )
        + (jax.ShapeDtypeStruct(columns[0].shape, BF),) * (plan.nb - 1),
        in_specs=[VMEM] * len(columns),
        out_specs=(VMEM,) * plan.nb,
        compiler_params=params(8),
    )(*columns)


def add_parts_kernel(halves, *refs):
    refs = list(refs)
    parts = [[refs.pop(0) for _ in range(count)] for count in halves]
    for i, out in enumerate(refs[1:-1]):
        step = out.shape[-3]
        at = slice(i * step, (i + 1) * step)
        at = (slice(None), at) if len(out.shape) == 4 else at
        values = [
            jnp.concatenate([half[at].astype(F32) for half in part], axis=-2) for part in parts
        ]
        out[...] = tree_sum(values).astype(out.dtype)
    refs[-1][...] = jnp.zeros_like(refs[-1])


def add_parts(parts, pieces, token):
    *lead, total, height, width = parts[0].shape
    parts = [part if isinstance(part, list) else [part] for part in parts]
    halves = [len(part) for part in parts]
    parts = [half for part in parts for half in part]
    return pl.pallas_call(
        functools.partial(add_parts_kernel, halves),
        out_shape=tuple(
            jax.ShapeDtypeStruct((*lead, total // pieces, height, width), BF if i else F32)
            for i in range(pieces)
        )
        + (jax.ShapeDtypeStruct((8, LANES), F32),),
        in_specs=[VMEM] * (len(parts) + 1),
        out_specs=(VMEM,) * (pieces + 1),
        compiler_params=params(14),
    )(*parts, token)


def blend_kernel(plan, late_count, *refs):
    late, parts, outs = refs[:late_count], refs[late_count + 1 : -plan.nb], refs[-plan.nb :]
    bucket = lax.axis_index("bucket")
    first = tree_sum([part[...].astype(F32) for part in parts])
    for i, out in enumerate(outs):
        owner = jnp.bitwise_xor(bucket, i)
        quarter = jnp.maximum(owner - 1, 0)
        window = late[0][quarter]
        if late_count > 1:
            window = window + tree_sum([ref[quarter].astype(F32) for ref in late[1:]])
        out[: plan.win] = jnp.where(owner == 0, first[: plan.win], window).astype(out.dtype)
        out[plan.win :] = first[plan.win :].astype(out.dtype)


def blend(plan, late, token, parts):
    return pl.pallas_call(
        functools.partial(blend_kernel, plan, len(late)),
        out_shape=tuple(
            jax.ShapeDtypeStruct((plan.tail, LANES), BF if i else F32) for i in range(plan.nb)
        ),
        in_specs=[VMEM] * (len(late) + 1 + len(parts)),
        out_specs=(VMEM,) * plan.nb,
        compiler_params=params(10),
    )(*late, token, *parts)


def add_rows_kernel(*refs):
    refs[-1][...] = tree_sum([ref[...] for ref in refs[:-1]])


def add_rows(parts):
    return pl.pallas_call(
        add_rows_kernel,
        out_shape=jax.ShapeDtypeStruct(parts[0].shape, F32),
        in_specs=[VMEM] * len(parts),
        out_specs=VMEM,
        compiler_params=params(4),
    )(*parts)


def groups_of(size, skip=0):
    bits = list(range(skip, size.bit_length() - 1))
    return [bits[i : i + 2] for i in range(0, len(bits), 2)]


def masks_of(bits):
    masks = [1 << bits[0]]
    if len(bits) == 2:
        masks += [1 << bits[1], (1 << bits[0]) | (1 << bits[1])]
    return masks


def swap(x, axis, size, mask):
    return lax.ppermute(x, axis, [(i, i ^ mask) for i in range(size)])


def tree_sum(parts):
    if len(parts) == 1:
        return parts[0]
    half = len(parts) // 2
    return tree_sum(parts[:half]) + tree_sum(parts[half:])


def with_partners(x, axis, size, bits):
    return [x] + [swap(x, axis, size, mask) for mask in masks_of(bits)]


def gather_windows(plan, window):
    first, *more = groups_of(plan.nd, 1)
    column = lay_column(with_partners(window, "dp", plan.nd, first))
    for bits in more:
        column = jnp.concatenate(with_partners(column, "dp", plan.nd, bits), axis=0)
    (bits,) = groups_of(plan.nb)
    early, *late = choose(plan, with_partners(column, "bucket", plan.nb, bits))
    others = [swap(x, "dp", plan.nd, 1) for x in (early, *late)]
    return (early, others[0]), (*late, *others[1:])


def scatter_dp(plan, pieces):
    *more, last = groups_of(plan.nd, 1)
    got = [pieces[0]] + [
        swap(piece, "dp", plan.nd, mask) for piece, mask in zip(pieces[1:], masks_of(last))
    ]
    for bits in reversed(more):
        held = tree_sum([x.astype(F32) for x in got])
        size = 1 << len(bits)
        step = held.shape[-3] // size
        parts = [held[..., i * step : (i + 1) * step, :, :] for i in range(size)]
        got = [parts[0]] + [
            swap(part.astype(BF), "dp", plan.nd, mask)
            for part, mask in zip(parts[1:], masks_of(bits))
        ]
    return [x.reshape(*x.shape[:-3], *x.shape[-2:]) for x in got]


def sum_all(plan, x):
    x = [x, swap(x, "dp", plan.nd, 1)]
    for bits in groups_of(plan.nd, 1):
        x = with_partners(add_rows(x), "dp", plan.nd, bits)
    (bits,) = groups_of(plan.nb)
    return with_partners(add_rows(x), "bucket", plan.nb, bits)


def local(
    plan, tokens, cotangent, segment_ids, keep_mask, bucket_patches, master, first_moment, second_moment
):
    def as_rows(flat):
        return jnp.pad(flat, (0, plan.win * LANES - plan.shard)).reshape(plan.win, LANES)

    def as_flat(rows):
        return rows.reshape(-1)[: plan.shard]

    master_rows = as_rows(master)
    seg_row = segment_ids.reshape(1, SEQ)
    keep_row = keep_mask.reshape(1, SEQ)
    count = 1 << len(groups_of(plan.nd, 1)[-1])
    (b_bits,) = groups_of(plan.nb)

    early, late = gather_windows(plan, prepare(plan, master_rows, keep_row))
    wq, vec, head, kept, q, k, v, hat, rstd = project_part(plan, *early, tokens)
    o, ot, lse = forward(plan, segment_ids, seg_row, keep_row, q, k, v)
    block_output, dh1, do, near, far, tail, gvec = middle_part(
        plan, late, tokens, cotangent, o, ot, head, kept, vec, keep_row, bucket_patches
    )
    *pieces, token = add_parts([near, swap(far, "dp", plan.nd, 1)], count, gvec)
    rest = scatter_dp(plan, pieces)
    low, gains = backward(
        plan, vec, segment_ids, seg_row, keep_row, lse, q, k, v, o, do, hat, rstd, token
    )
    da1, near, *far = finish_part(plan, tokens, wq, vec, tail, gvec, low, gains)
    input_grad, given = input_part(tokens, vec, da1, dh1)
    *late_parts, token = add_parts(rest[:2], 1, gains)
    late_parts += rest[2:]
    *pieces, _ = add_parts([near, [swap(half, "dp", plan.nd, 1) for half in far]], count, token)
    first = scatter_dp(plan, pieces)
    mine, *sent = blend(plan, late_parts, given, first)
    parts = [mine] + [
        swap(x, "bucket", plan.nb, mask) for x, mask in zip(sent, masks_of(b_bits))
    ]
    moment_rows, second_rows, update_rows, sums = update_part(
        plan, parts, master_rows, as_rows(first_moment), as_rows(second_moment)
    )
    new_master, norms, trust = apply_part(plan, sum_all(plan, sums), master_rows, update_rows)
    return (
        block_output,
        input_grad,
        as_flat(moment_rows),
        as_flat(second_rows),
        as_flat(new_master),
        norms,
        trust.reshape(MATS),
    )


def solution(mesh):
    shards = mesh.shape["bucket"] * mesh.shape["dp"]
    plan = Plan(mesh.shape, PARAMS // shards)
    both = ("bucket", "dp")
    return jax.shard_map(
        functools.partial(local, plan),
        mesh=mesh,
        in_specs=(P(both, None), P(both, None), P(both), P(both), P(), P(both), P(both), P(both)),
        out_specs=(P(both, None), P(both, None), P(both), P(both), P(both), P(), P()),
        check_vma=False,
    )
```

```python
import functools
import math

import jax
import jax.numpy as jnp
from jax import lax
from jax.experimental import pallas as pl
from jax.experimental.pallas import tpu as pltpu
from jax.sharding import PartitionSpec as P

D = 384
HEADS = 6
HD = 64
FF = 1536
SEQ = 1024
STEP = 10
MATS = 10
LANES = 128
PAIRS = HEADS // 2
TILE = 256
TILES = SEQ // TILE
BLOCKS = SEQ // LANES
MIDDLE_BLOCK = 512
FAR_PARTS = 3

norm_epsilon = 1e-06
adam_epsilon = 1e-06
beta_one = 0.9
beta_two = 0.999
learn_rate = 0.5
weight_decay = 0.01
masked_score = -1e30

MATRIX_END = 4 * D * D + 2 * D * FF
BOUNDS = [0, 3 * D * D, 4 * D * D, 4 * D * D + D * FF, MATRIX_END] + [
    MATRIX_END + (j + 1) * D for j in range(6)
]
PARAMS = BOUNDS[-1]
ROW_OUT = BOUNDS[1] // LANES
ROW_UP = BOUNDS[2] // LANES
ROW_DOWN = BOUNDS[3] // LANES
ROW_VEC = BOUNDS[4] // LANES
VEC_ROWS = 6 * D // LANES
ROWS_ALL = PARAMS // LANES

score_scale = HD ** (-0.5) * math.log2(math.e)
grad_scale = HD ** (-0.5)

BF = jnp.bfloat16
F32 = jnp.float32
VMEM = pl.BlockSpec(memory_space=pltpu.VMEM)
SMEM = pl.BlockSpec(memory_space=pltpu.SMEM)


QUICK = pl.CostEstimate(flops=1000, bytes_accessed=1000, transcendentals=0)


def params(limit):
    return pltpu.CompilerParams(vmem_limit_bytes=limit * 1024 * 1024)


def round_up(value, step):
    return -(-value // step) * step


class Plan:
    def __init__(self, mesh_shape, shard):
        self.nb = mesh_shape["bucket"]
        self.nd = mesh_shape["dp"]
        self.n = self.nb * self.nd
        self.shard = shard
        self.start = [k * shard // LANES for k in range(self.n)]
        self.rows = [
            -(-((k + 1) * shard) // LANES) - self.start[k] for k in range(self.n)
        ]
        self.win = round_up(max(self.rows) + 1, 16)
        self.tail = round_up(self.win + VEC_ROWS, 16 * FAR_PARTS)
        self.upper = self.win * 3 // 4 // 16 * 16
        self.vec_place = ROW_VEC - self.start[-1]
        self.vec_from = self.vec_place // 16 * 16
        self.kept_row = 2 * self.win - self.vec_from
        self.early = self.kept_row + 16

    def device(self):
        return lax.axis_index("bucket") * self.nd + lax.axis_index("dp")


def nn(a, b):
    return lax.dot_general(a, b, (((1,), (0,)), ((), ())), preferred_element_type=F32)


def nt(a, b):
    return lax.dot_general(a, b, (((1,), (1,)), ((), ())), preferred_element_type=F32)


def split_low(x):
    high = x.astype(BF)
    return high, (x - high.astype(F32)).astype(BF)


def rows_at(step):
    if isinstance(step, int):
        return slice(step * TILE, (step + 1) * TILE)
    return pl.ds(pl.multiple_of(step * TILE, TILE), TILE)


def norm_parts(values):
    average = jnp.mean(values, axis=-1, keepdims=True)
    centered = values - average
    variance = jnp.mean(centered * centered, axis=-1, keepdims=True)
    rstd = lax.rsqrt(variance + norm_epsilon)
    return centered * rstd, rstd


def norm_back(hat, rstd, grad):
    mean_grad = jnp.mean(grad, axis=-1, keepdims=True)
    mean_both = jnp.mean(grad * hat, axis=-1, keepdims=True)
    return rstd * (grad - mean_grad - hat * mean_both)


def head_mean_matrix():
    row = lax.broadcasted_iota(jnp.int32, (TILE, TILE), 0)
    col = lax.broadcasted_iota(jnp.int32, (TILE, TILE), 1)
    return jnp.where(row // HD == col // HD, 1.0 / HD, 0.0).astype(BF)


def head_mean_low(low, matrix):
    rest = D - TILE
    return jnp.concatenate(
        [nn(low[:, :TILE], matrix), nn(low[:, TILE:], matrix[:rest, :rest])], axis=1
    )


def head_mean(x, matrix):
    high, rest = split_low(x)
    return head_mean_low(high, matrix) + head_mean_low(rest, matrix)


def prepare_kernel(plan, master_ref, keep_ref, upper_ref, lower_ref):
    me = plan.device()
    offset = lax.rem(me * plan.shard, LANES)
    values = master_ref[...]
    turned = pltpu.roll(values, offset, 1)
    below = pltpu.roll(turned, 1, 0)
    lane = lax.broadcasted_iota(jnp.int32, values.shape, 1)
    row = lax.broadcasted_iota(jnp.int32, values.shape, 0)
    count = jnp.sum(keep_ref[...].astype(F32), axis=1, keepdims=True)
    high = jnp.floor(count * (1.0 / 32.0))
    parts = jnp.where(lane == 0, high, jnp.where(lane == 1, count - 32.0 * high, 0.0))
    window = jnp.where(lane < offset, below, turned)
    window = jnp.where(row == plan.win - 1, parts, window).astype(BF)
    upper_ref[...] = window[: plan.upper]
    lower_ref[...] = window[plan.upper :]


def prepare(plan, master_rows, keep_row):
    return pl.pallas_call(
        functools.partial(prepare_kernel, plan),
        out_shape=(
            jax.ShapeDtypeStruct((plan.upper, LANES), BF),
            jax.ShapeDtypeStruct((plan.win - plan.upper, LANES), BF),
        ),
        in_specs=[VMEM, VMEM],
        out_specs=(VMEM, VMEM),
        compiler_params=params(8),
    )(master_rows, keep_row)


def ahead_kernel(tokens_ref, hat_ref, rstd_ref, token_ref):
    hat, rstd = norm_parts(tokens_ref[...].astype(F32))
    hat_ref[...] = hat
    rstd_ref[...] = jnp.broadcast_to(rstd, rstd_ref.shape)
    token_ref[...] = jnp.zeros_like(token_ref)


def ahead(tokens):
    rows = tokens.shape[0]
    return pl.pallas_call(
        ahead_kernel,
        out_shape=(
            jax.ShapeDtypeStruct((rows, D), F32),
            jax.ShapeDtypeStruct((rows, LANES), F32),
            jax.ShapeDtypeStruct((8, LANES), F32),
        ),
        in_specs=[VMEM],
        out_specs=(VMEM,) * 3,
        compiler_params=params(12),
        cost_estimate=QUICK,
    )(tokens)


def held_window(own_ref, other_ref, rel, at):
    place = jnp.right_shift(rel, 1)
    return jnp.where(
        jnp.bitwise_and(rel, 1) == 0,
        own_ref[place, at].astype(F32),
        other_ref[place, at].astype(F32),
    )


def lay_windows(plan, owners, refs_of, flat, base):
    dp = lax.axis_index("dp")
    for k in owners:
        own_ref, other_ref = refs_of(k)
        window = held_window(own_ref, other_ref, jnp.bitwise_xor(dp, k % plan.nd), slice(0, plan.win))
        first, count = plan.start[k] - base, plan.rows[k]
        shared = k > 0 and (k * plan.shard) % LANES
        if shared:
            before = flat[first : first + 1, :]
        flat[first : first + count, :] = window[:count]
        if shared:
            flat[first : first + 1, :] = before + window[:1]


def take_matrix(target, flat, base, height, width):
    stride = width // LANES
    for j in range(stride):
        target[:, j * LANES : (j + 1) * LANES] = flat[pl.ds(base + j, height, stride=stride), :].astype(BF)


def put_matrix(flat, base, source, height, width):
    stride = width // LANES
    for j in range(stride):
        flat[pl.ds(base + j, height, stride=stride), :] = source[:, j * LANES : (j + 1) * LANES]


def key_chunks(seg_ref, ti):
    first_i, last_i = seg_ref[ti * TILE], seg_ref[ti * TILE + TILE - 1]
    low, high = jnp.int32(0), jnp.int32(0)
    for b in range(BLOCKS):
        low += (seg_ref[b * LANES + LANES - 1] < first_i).astype(jnp.int32)
        high += (seg_ref[b * LANES] <= last_i).astype(jnp.int32)
    count = jnp.right_shift(high - low + 1, 1)
    return jnp.minimum(low, BLOCKS - 2 * count), count


def tile_bias(ti, block, row_seg, key_seg):
    key_place = lax.broadcasted_iota(jnp.int32, (TILE, TILE), 0) + block * LANES
    row_place = lax.broadcasted_iota(jnp.int32, (TILE, TILE), 1) + ti * TILE
    return jnp.where(
        jnp.logical_or(key_seg == row_seg, key_place == row_place), 0.0, masked_score
    )


def keys_at(block):
    return pl.ds(pl.multiple_of(block * LANES, LANES), TILE)


def side_rows(stacked, side):
    return jnp.concatenate(
        [stacked[side * LANES : (side + 1) * LANES], stacked[(2 + side) * LANES : (3 + side) * LANES]],
        axis=0,
    )


def to_column(row):
    return jnp.transpose(jnp.broadcast_to(row, (LANES, row.shape[1])))


def block_heads(pair):
    lane = lax.broadcasted_iota(jnp.int32, pair.shape, 1)
    zero = jnp.zeros_like(pair)
    sides = [jnp.where(lane < HD, pair, zero), jnp.where(lane >= HD, pair, zero)]
    return [side[b * LANES : (b + 1) * LANES] for b in range(2) for side in sides]


def put_blocks(ref, hp, step, pair):
    for i, part in enumerate(block_heads(pair)):
        ref[hp, 2 * step + i // 2, i % 2] = part


def two_blocks(ref, hp, block):
    return ref[hp, pl.ds(block, 2)].reshape(4 * LANES, LANES)


def stack_heads(pair):
    lane = lax.broadcasted_iota(jnp.int32, pair.shape, 1)
    zero = jnp.zeros_like(pair)
    return jnp.concatenate(
        [jnp.where(lane < HD, pair, zero), jnp.where(lane >= HD, pair, zero)], axis=0
    )


def project_kernel(
    plan,
    own_ref,
    other_ref,
    hat_in_ref,
    wq_ref,
    vec_ref,
    head_ref,
    kept_ref,
    q_ref,
    k_ref,
    v_ref,
    hat_ref,
    rstd_ref,
    flat,
):
    dp = lax.axis_index("dp")
    lay_windows(plan, range(plan.nd), lambda k: (own_ref, other_ref), flat, 0)
    take_matrix(wq_ref, flat, 0, D, 3 * D)
    head_ref[...] = flat[ROW_OUT : ROW_OUT + 8, :]
    rel = jnp.bitwise_xor(dp, plan.nd - 1)
    late = held_window(own_ref, other_ref, rel, slice(plan.win, plan.kept_row))
    kept = jnp.zeros((1, LANES), F32)
    for j in range(plan.nd):
        half = other_ref if j & 1 else own_ref
        kept = kept + half[j >> 1, plan.kept_row :].astype(F32)[15:16]
    kept_ref[...] = jnp.broadcast_to(32.0 * kept[:, 0:1] + kept[:, 1:2], kept_ref.shape)
    for t in range(6):
        for j in range(D // LANES):
            at = plan.vec_place - plan.vec_from + 3 * t + j
            vec_ref[t : t + 1, j * LANES : (j + 1) * LANES] = late[at : at + 1]
    matrix = head_mean_matrix()
    gain1, shift1 = vec_ref[0:1, :], vec_ref[1:2, :]
    gain_q, gain_k = vec_ref[2:3, :], vec_ref[3:4, :]

    raw = nn((hat_in_ref[...] * gain1 + shift1).astype(BF), wq_ref[...])

    def head_norm(low_out, part, gain):
        lanes = slice(part * D, (part + 1) * D)
        x = raw[:, lanes]
        centered = x - head_mean(x, matrix)
        rstd = lax.rsqrt(head_mean(centered * centered, matrix) + norm_epsilon)
        normed = centered * rstd
        hat_ref[:, lanes] = normed
        rstd_ref[:, lanes] = rstd
        low_out[...] = (normed * gain).astype(BF)

    head_norm(q_ref, 0, gain_q)
    head_norm(k_ref, 1, gain_k)
    v_ref[...] = raw[:, 2 * D :].astype(BF)


def project_part(plan, own, other, tokens):
    rows = tokens.shape[0]
    low = jax.ShapeDtypeStruct((rows, D), BF)
    return pl.pallas_call(
        functools.partial(project_kernel, plan),
        out_shape=(
            jax.ShapeDtypeStruct((D, 3 * D), BF),
            jax.ShapeDtypeStruct((8, D), F32),
            jax.ShapeDtypeStruct((8, LANES), F32),
            jax.ShapeDtypeStruct((8, LANES), F32),
            low,
            low,
            low,
            jax.ShapeDtypeStruct((rows, 2 * D), F32),
            jax.ShapeDtypeStruct((rows, 2 * D), F32),
        ),
        in_specs=[VMEM] * 3,
        out_specs=(VMEM,) * 9,
        scratch_shapes=[
            pltpu.VMEM((round_up(plan.start[plan.nd - 1] + plan.win, 8), LANES), F32),
        ],
        compiler_params=params(24),
        cost_estimate=QUICK,
    )(own, other, tokens)


def forward_kernel(
    plan,
    seg_smem,
    seg_ref,
    keep_ref,
    q_ref,
    k_ref,
    v_ref,
    o_ref,
    ot_ref,
    whole_ref,
    lse_ref,
    kab,
    segk,
    vt,
    ot,
    rest_t,
    sums,
    expo,
):
    seg_row = seg_ref[...].astype(F32)
    segk[...] = to_column(jnp.where(keep_ref[...] == 1, seg_row, -1.0))

    for step in range(TILES):
        at = rows_at(step)
        for hp in range(PAIRS):
            put_blocks(kab, hp, step, k_ref[at, hp * LANES : (hp + 1) * LANES])
        vt[:, at] = jnp.transpose(v_ref[at, :].astype(F32)).astype(BF)

    def query_tile(ti, carry):
        ot[...] = jnp.zeros_like(ot)
        rest_t[...] = jnp.zeros_like(rest_t)
        sums[...] = jnp.zeros_like(sums)
        row_seg = seg_ref[:, rows_at(ti)].astype(F32)
        first, count = key_chunks(seg_smem, ti)

        def score_chunk(c, inner):
            block = first + 2 * c
            column = segk[keys_at(block), :]
            bias = tile_bias(ti, block, row_seg, jnp.concatenate([column, column], axis=1))
            for hp in range(PAIRS):
                queries = q_ref[rows_at(ti), hp * LANES : (hp + 1) * LANES]
                scores = nt(two_blocks(kab, hp, block), queries)
                for side in range(2):
                    head = 2 * hp + side
                    value = jnp.exp2(side_rows(scores, side) * score_scale + bias)
                    expo[c, head] = value
                    sums[head : head + 1, :] += jnp.sum(value, axis=0, keepdims=True)
            return inner

        lax.fori_loop(0, count, score_chunk, 0)
        lse_ref[ti] = jnp.log2(sums[...])
        sums[...] = 1.0 / sums[...]

        def value_chunk(c, inner):
            keys = keys_at(first + 2 * c)
            for head in range(HEADS):
                prob, rest = split_low(expo[c, head] * sums[head : head + 1, :])
                at = slice(head * HD, (head + 1) * HD)
                ot[at, :] += nn(vt[at, keys], prob)
                rest_t[at, :] += nn(vt[at, keys], rest)
            return inner

        lax.fori_loop(0, count, value_chunk, 0)
        attended = ot[...]
        ot_ref[ti] = attended.astype(BF)
        whole_ref[ti] = attended + rest_t[...]
        o_ref[rows_at(ti), :] = jnp.transpose(attended).astype(BF)
        return carry

    lax.fori_loop(0, TILES, query_tile, 0)


def forward(plan, seg, seg_row, keep_row, q, k, v):
    rows = q.shape[0]
    return pl.pallas_call(
        functools.partial(forward_kernel, plan),
        out_shape=(
            jax.ShapeDtypeStruct((rows, D), BF),
            jax.ShapeDtypeStruct((TILES, D, TILE), BF),
            jax.ShapeDtypeStruct((TILES, D, TILE), F32),
            jax.ShapeDtypeStruct((TILES, 8, TILE), F32),
            jax.ShapeDtypeStruct((PAIRS, BLOCKS, 2, LANES, LANES), BF),
            jax.ShapeDtypeStruct((SEQ, LANES), F32),
        ),
        in_specs=[SMEM] + [VMEM] * 5,
        out_specs=(VMEM,) * 6,
        scratch_shapes=[
            pltpu.VMEM((D, SEQ), BF),
            pltpu.VMEM((D, TILE), F32),
            pltpu.VMEM((D, TILE), F32),
            pltpu.VMEM((8, TILE), F32),
            pltpu.VMEM((TILES, HEADS, TILE, TILE), F32),
        ],
        compiler_params=params(24),
        cost_estimate=QUICK,
    )(seg, seg_row, keep_row, q, k, v)


erfc_step = 0.3275911 * math.sqrt(0.5)
erfc_terms = [0.254829592, -0.284496736, 1.421413741, -1.453152027, 1.061405429]


def normal_parts(u):
    expo = jnp.exp2(u * u * (-0.5 * math.log2(math.e)))
    t = 1.0 / (1.0 + erfc_step * jnp.abs(u))
    poly = 0.5 * erfc_terms[4]
    for term in reversed(erfc_terms[:4]):
        poly = poly * t + 0.5 * term
    below = poly * t * expo
    return jnp.where(u > 0.0, 1.0 - below, below), expo * (1.0 / math.sqrt(2.0 * math.pi))


def middle_kernel(plan, *refs):
    late_refs, rest = refs[: 2 * plan.nb - 2], refs[2 * plan.nb - 2 :]
    middle_body(plan, late_refs, *rest)


def middle_body(
    plan,
    late_refs,
    tokens_ref,
    cot_ref,
    o_ref,
    ot_ref,
    head_ref,
    kept_ref,
    vec_ref,
    keep_ref,
    patches_ref,
    out_ref,
    dh1_ref,
    do_ref,
    near_ref,
    far_ref,
    tail_ref,
    gvec_ref,
    keepc,
    hid,
    dus,
    flat,
    wo_ref,
    wu_ref,
    wd_ref,
):
    bucket = lax.axis_index("bucket")
    base = ROW_OUT
    flat[0:8, :] = head_ref[...]
    dp = lax.axis_index("dp")
    owns, others = late_refs[: plan.nb - 1], late_refs[plan.nb - 1 :]
    lay_windows(
        plan,
        range(plan.nd, plan.n),
        lambda k: (owns[k // plan.nd - 1], others[k // plan.nd - 1]),
        flat,
        base,
    )
    take_matrix(wo_ref, flat, 0, D, D)
    take_matrix(wu_ref, flat, ROW_UP - base, D, FF)
    take_matrix(wd_ref, flat, ROW_DOWN - base, FF, D)
    gain2, shift2 = vec_ref[4:5, :], vec_ref[5:6, :]
    own = patches_ref[bucket].astype(F32)
    total = patches_ref[0].astype(F32)
    for b in range(1, plan.nb):
        total = total + patches_ref[b].astype(F32)
    ones = jnp.ones((1, LANES), F32)
    scale = (plan.nb * own) * ones / (total * ones) * float(SEQ * plan.nd) / kept_ref[0:1, :]
    keepc[...] = to_column(keep_ref[...].astype(F32)) * scale
    gvec_ref[...] = jnp.zeros_like(gvec_ref)

    middle = tokens_ref[...].astype(F32) + nn(o_ref[...], wo_ref[...])
    hat, rstd = norm_parts(middle)
    low = (hat * gain2 + shift2).astype(BF)
    weights = keepc[...]
    seed = cot_ref[...].astype(F32) * jnp.concatenate([weights] * (D // LANES), axis=1)
    seed_low = seed.astype(BF)
    for first in range(0, FF, MIDDLE_BLOCK):
        cols = slice(first, first + MIDDLE_BLOCK)
        u = nn(low, wu_ref[:, cols])
        phi, bell = normal_parts(u)
        hid[:, cols] = (u * phi).astype(BF)
        dus[:, cols] = (nt(seed_low, wd_ref[cols, :]) * (phi + u * bell)).astype(BF)
    out_ref[...] = (middle + nn(hid[...], wd_ref[...])).astype(BF)
    seedt = jnp.transpose(seed).astype(BF)
    lowt = jnp.transpose(low.astype(F32)).astype(BF)
    da2 = nt(dus[...], wu_ref[...])
    gvec_ref[0:1, :] = jnp.sum(da2 * hat, axis=0, keepdims=True)
    gvec_ref[1:2, :] = jnp.sum(da2, axis=0, keepdims=True)
    dh1 = seed + norm_back(hat, rstd, da2 * gain2)
    dh1_ref[...] = dh1
    dh1_low = dh1.astype(BF)
    gout = nn(jnp.concatenate([ot_ref[t] for t in range(TILES)], axis=1), dh1_low)
    do_ref[...] = nt(dh1_low, wo_ref[...]).astype(BF)
    put_matrix(flat, 0, gout, D, D)
    block = 2 * TILE
    for i in range(FF // block):
        part = nn(lowt, dus[:, i * block : (i + 1) * block])
        for j in range(block // LANES):
            flat[pl.ds(ROW_UP - base + i * (block // LANES) + j, D, stride=FF // LANES), :] = part[
                :, j * LANES : (j + 1) * LANES
            ]
        part = jnp.transpose(nn(seedt, hid[:, i * block : (i + 1) * block]))
        for j in range(D // LANES):
            flat[
                pl.ds(ROW_DOWN - base + i * block * (D // LANES) + j, block, stride=D // LANES), :
            ] = part[:, j * LANES : (j + 1) * LANES]
    tail_ref[...] = flat[0:8, :]
    side = jnp.bitwise_and(dp, 1)
    for k in range(plan.nd, plan.n):
        first = plan.start[k] - base
        quarter = k // plan.nd - 1
        reld = jnp.right_shift(jnp.bitwise_xor(dp, k % plan.nd), 1)
        window = flat[first : first + plan.win, :].astype(BF)

        @pl.when(side == k % 2)
        def _():
            near_ref[quarter, reld] = window

        @pl.when(side != k % 2)
        def _():
            far_ref[quarter, reld] = window


def middle_part(plan, late, tokens, cot, o, ot, head, kept, vec, keep_row, patches):
    rows = tokens.shape[0]
    windows = jax.ShapeDtypeStruct((plan.nb - 1, plan.nd // 2, plan.win, LANES), BF)
    return pl.pallas_call(
        functools.partial(middle_kernel, plan),
        out_shape=(
            jax.ShapeDtypeStruct((rows, D), BF),
            jax.ShapeDtypeStruct((rows, D), F32),
            jax.ShapeDtypeStruct((rows, D), BF),
            windows,
            windows,
            jax.ShapeDtypeStruct((8, LANES), F32),
            jax.ShapeDtypeStruct((8, D), F32),
        ),
        in_specs=[VMEM] * (len(late) + 8) + [SMEM],
        out_specs=(VMEM,) * 7,
        scratch_shapes=[
            pltpu.VMEM((rows, LANES), F32),
            pltpu.VMEM((rows, FF), BF),
            pltpu.VMEM((rows, FF), BF),
            pltpu.VMEM((round_up(plan.start[-1] + plan.win - ROW_OUT, 8), LANES), F32),
            pltpu.VMEM((D, D), BF),
            pltpu.VMEM((D, FF), BF),
            pltpu.VMEM((FF, D), BF),
        ],
        compiler_params=params(36),
        cost_estimate=QUICK,
    )(*late, tokens, cot, o, ot, head, kept, vec, keep_row, patches)


def stack_kernel(
    vec_ref,
    hat_in_ref,
    q_ref,
    k_ref,
    v_ref,
    do_ref,
    whole_ref,
    vab,
    qab,
    dab,
    kt,
    inner_sums,
    normed_ref,
    token_ref,
):
    for step in range(TILES):
        at = rows_at(step)
        grads = do_ref[at, :]
        for hp in range(PAIRS):
            lanes = slice(hp * LANES, (hp + 1) * LANES)
            put_blocks(vab, hp, step, v_ref[at, lanes])
            qab[hp, step] = stack_heads(q_ref[at, lanes])
            dab[hp, step] = stack_heads(grads[:, lanes])
        kt[:, at] = jnp.transpose(k_ref[at, :].astype(F32)).astype(BF)
        both = jnp.transpose(grads.astype(F32)) * whole_ref[step]
        for head in range(HEADS):
            inner_sums[step, head : head + 1, :] = jnp.sum(
                both[head * HD : (head + 1) * HD], axis=0, keepdims=True
            )
        normed = hat_in_ref[at, :] * vec_ref[0:1, :] + vec_ref[1:2, :]
        normed_ref[:, at] = jnp.transpose(normed).astype(BF)
    token_ref[...] = jnp.zeros_like(token_ref)


def stack_part(vec, hat_in, q, k, v, do, whole):
    stacked = jax.ShapeDtypeStruct((PAIRS, TILES, 2 * TILE, LANES), BF)
    return pl.pallas_call(
        stack_kernel,
        out_shape=(
            jax.ShapeDtypeStruct((PAIRS, BLOCKS, 2, LANES, LANES), BF),
            stacked,
            stacked,
            jax.ShapeDtypeStruct((D, SEQ), BF),
            jax.ShapeDtypeStruct((TILES, 8, TILE), F32),
            jax.ShapeDtypeStruct((D, SEQ), BF),
            jax.ShapeDtypeStruct((8, LANES), F32),
        ),
        in_specs=[VMEM] * 7,
        out_specs=(VMEM,) * 7,
        compiler_params=params(16),
        cost_estimate=QUICK,
    )(vec, hat_in, q, k, v, do, whole)


def backward_kernel(
    plan,
    vec_ref,
    seg_smem,
    seg_ref,
    lse_ref,
    q_ref,
    do_ref,
    hat_ref,
    rstd_ref,
    segk,
    kab,
    vab,
    qab,
    dab,
    kt,
    inner_sums,
    token_ref,
    low_ref,
    gains_ref,
    dqt,
    dk,
    dv,
):
    matrix = head_mean_matrix()
    dqt[...] = jnp.zeros_like(dqt)
    dk[...] = jnp.zeros_like(dk)
    dv[...] = jnp.zeros_like(dv)
    gains_ref[...] = jnp.zeros_like(gains_ref)

    def query_tile(ti, carry):
        row_seg = seg_ref[:, rows_at(ti)].astype(F32)
        first, count = key_chunks(seg_smem, ti)

        def key_chunk(c, inner):
            block = first + 2 * c
            keys = keys_at(block)
            column = segk[keys, :]
            bias = tile_bias(ti, block, row_seg, jnp.concatenate([column, column], axis=1))
            raw = []
            for hp in range(PAIRS):
                lanes = slice(hp * LANES, (hp + 1) * LANES)
                raw.append(
                    (
                        nt(two_blocks(kab, hp, block), q_ref[rows_at(ti), lanes]),
                        nt(two_blocks(vab, hp, block), do_ref[rows_at(ti), lanes]),
                    )
                )
            probs, dscores = [], []
            for head in range(HEADS):
                scores, grads = raw[head // 2]
                prob = jnp.exp2(
                    side_rows(scores, head % 2) * score_scale
                    + (bias - lse_ref[ti, head : head + 1, :])
                )
                dscore = prob * (side_rows(grads, head % 2) - inner_sums[ti, head : head + 1, :])
                probs.append(prob.astype(BF))
                dscores.append(dscore.astype(BF))
            for hp in range(PAIRS):
                pair = slice(2 * hp, 2 * hp + 2)
                for head in (2 * hp, 2 * hp + 1):
                    at = slice(head * HD, (head + 1) * HD)
                    dqt[ti, at, :] += nn(kt[at, keys], dscores[head])
                dv[hp, keys] += nn(jnp.concatenate(probs[pair], axis=1), dab[hp, ti])
                dk[hp, keys] += nn(jnp.concatenate(dscores[pair], axis=1), qab[hp, ti])
            return inner

        lax.fori_loop(0, count, key_chunk, 0)
        return carry

    lax.fori_loop(0, TILES, query_tile, 0)

    def finish(step, carry):
        at = rows_at(step)

        def head_norm_back(part, gain, grad):
            lanes = slice(part * D, (part + 1) * D)
            hat = hat_ref[at, lanes]
            both = grad * hat
            gains_ref[part : part + 1, :] += jnp.sum(both, axis=0, keepdims=True)
            scaled = grad * gain
            mean_grad = head_mean_low(scaled.astype(BF), matrix)
            mean_both = head_mean_low((both * gain).astype(BF), matrix)
            back = rstd_ref[at, lanes] * (scaled - mean_grad - hat * mean_both)
            low_ref[at, lanes] = back.astype(BF)

        grad_k = jnp.concatenate([dk[hp, at] for hp in range(PAIRS)], axis=1) * grad_scale
        grad_v = jnp.concatenate([dv[hp, at] for hp in range(PAIRS)], axis=1)
        head_norm_back(0, vec_ref[2:3, :], jnp.transpose(dqt[step]) * grad_scale)
        head_norm_back(1, vec_ref[3:4, :], grad_k)
        low_ref[at, 2 * D :] = grad_v.astype(BF)
        return carry

    lax.fori_loop(0, TILES, finish, 0)


def backward(plan, vec, seg, seg_row, lse, q, do, hat, rstd, segk, stacks, token):
    rows = q.shape[0]
    return pl.pallas_call(
        functools.partial(backward_kernel, plan),
        out_shape=(
            jax.ShapeDtypeStruct((rows, 3 * D), BF),
            jax.ShapeDtypeStruct((8, D), F32),
        ),
        in_specs=[VMEM, SMEM] + [VMEM] * 14,
        out_specs=(VMEM, VMEM),
        scratch_shapes=[
            pltpu.VMEM((TILES, D, TILE), F32),
            pltpu.VMEM((PAIRS, SEQ, LANES), F32),
            pltpu.VMEM((PAIRS, SEQ, LANES), F32),
        ],
        compiler_params=params(26),
        cost_estimate=QUICK,
    )(vec, seg, seg_row, lse, q, do, hat, rstd, segk, *stacks, token)


def finish_kernel(
    plan,
    hat_ref,
    normed_ref,
    wq_ref,
    tail_ref,
    gvec_ref,
    low_ref,
    gqk_ref,
    da1_ref,
    near_ref,
    *refs,
):
    *far_refs, gains, flat = refs
    hat = hat_ref[...]
    for i in range(3):
        part = nn(normed_ref[...], low_ref[:, i * D : (i + 1) * D])
        for j in range(D // LANES):
            flat[pl.ds(i * (D // LANES) + j, D, stride=3 * D // LANES), :] = part[
                :, j * LANES : (j + 1) * LANES
            ]
    da1 = nt(low_ref[...], wq_ref[...])
    da1_ref[...] = da1
    gains[...] = jnp.zeros_like(gains)
    gains[0:1, :] = jnp.sum(da1 * hat, axis=0, keepdims=True)
    gains[1:2, :] = jnp.sum(da1, axis=0, keepdims=True)
    gains[2:4, :] = gqk_ref[0:2, :]
    gains[4:6, :] = gvec_ref[0:2, :]
    flat[ROW_OUT : ROW_OUT + 8, :] = tail_ref[...]
    dp = lax.axis_index("dp")
    side = jnp.bitwise_and(dp, 1)
    rest = jnp.zeros((plan.tail - plan.win, LANES), BF)
    vector_rows = []
    for t in range(6):
        for j in range(D // LANES):
            vector_rows.append(gains[t : t + 1, j * LANES : (j + 1) * LANES])
    vector_rows.append(jnp.zeros((plan.tail - plan.win - VEC_ROWS, LANES), F32))
    vectors = jnp.concatenate(vector_rows, axis=0).astype(BF)
    for k in range(plan.nd):
        first = plan.start[k]
        reld = jnp.right_shift(jnp.bitwise_xor(dp, k), 1)
        window = flat[first : first + plan.win, :].astype(BF)
        window = jnp.concatenate([window, vectors if k == plan.nd - 1 else rest], axis=0)

        @pl.when(side == k % 2)
        def _():
            near_ref[reld] = window

        @pl.when(side != k % 2)
        def _():
            height = plan.tail // FAR_PARTS
            for i, far_ref in enumerate(far_refs):
                far_ref[reld] = window[i * height : (i + 1) * height]


def finish_part(plan, hat, normed, wq, tail, gvec, low, gains):
    rows = hat.shape[0]
    windows = jax.ShapeDtypeStruct((plan.nd // 2, plan.tail, LANES), BF)
    part = jax.ShapeDtypeStruct((plan.nd // 2, plan.tail // FAR_PARTS, LANES), BF)
    return pl.pallas_call(
        functools.partial(finish_kernel, plan),
        out_shape=(jax.ShapeDtypeStruct((rows, D), F32), windows) + (part,) * FAR_PARTS,
        in_specs=[VMEM] * 7,
        out_specs=(VMEM,) * (2 + FAR_PARTS),
        scratch_shapes=[
            pltpu.VMEM((8, D), F32),
            pltpu.VMEM((round_up(plan.start[plan.nd - 1] + plan.win, 8), LANES), F32),
        ],
        compiler_params=params(28),
        cost_estimate=QUICK,
    )(hat, normed, wq, tail, gvec, low, gains)


def input_kernel(hat_ref, rstd_ref, vec_ref, da1_ref, dh1_ref, grad_ref, token_ref):
    back = norm_back(hat_ref[...], rstd_ref[:, 0:1], da1_ref[...] * vec_ref[0:1, :])
    grad_ref[...] = dh1_ref[...] + back
    token_ref[...] = jnp.zeros_like(token_ref)


def input_part(hat, rstd, vec, da1, dh1):
    return pl.pallas_call(
        input_kernel,
        out_shape=(
            jax.ShapeDtypeStruct(dh1.shape, F32),
            jax.ShapeDtypeStruct((8, LANES), F32),
        ),
        in_specs=[VMEM] * 5,
        out_specs=(VMEM, VMEM),
        compiler_params=params(16),
        cost_estimate=QUICK,
    )(hat, rstd, vec, da1, dh1)


def flat_place(plan, shape):
    row = lax.broadcasted_iota(jnp.int32, shape, 0)
    lane = lax.broadcasted_iota(jnp.int32, shape, 1)
    place = row * LANES + lane
    return place, plan.device() * plan.shard + place


def update_kernel(
    plan,
    own_ref,
    got0_ref,
    got1_ref,
    got2_ref,
    master_ref,
    moment_ref,
    second_ref,
    new_moment_ref,
    new_second_ref,
    update_ref,
    sums_ref,
    window,
):
    bucket = lax.axis_index("bucket")
    dp = lax.axis_index("dp")
    total = tree_sum([ref[...].astype(F32) for ref in (own_ref, got0_ref, got1_ref, got2_ref)])
    window[...] = total[: plan.win]

    @pl.when(jnp.logical_and(bucket == plan.nb - 1, dp == plan.nd - 1))
    def _():
        window[plan.vec_place : plan.vec_place + VEC_ROWS, :] = total[
            plan.win : plan.win + VEC_ROWS
        ]

    offset = lax.rem(plan.device() * plan.shard, LANES)
    back = lax.rem(LANES - offset, LANES)
    turned = pltpu.roll(window[...], back, 1)
    above = pltpu.roll(turned, plan.win - 1, 0)
    lane = lax.broadcasted_iota(jnp.int32, turned.shape, 1)
    place, index = flat_place(plan, turned.shape)
    inside = place < plan.shard
    grad = jnp.where(inside, jnp.where(lane + offset < LANES, turned, above), 0.0)
    master = master_ref[...]
    moment = beta_one * moment_ref[...] + (1.0 - beta_one) * grad
    second = beta_two * second_ref[...] + (1.0 - beta_two) * grad * grad
    first_hat = moment / (1.0 - beta_one**STEP)
    second_hat = second / (1.0 - beta_two**STEP)
    decay = jnp.where(index < BOUNDS[4], weight_decay, 0.0)
    update = first_hat / (jnp.sqrt(second_hat) + adam_epsilon) + decay * master
    update = jnp.where(inside, update, 0.0)
    new_moment_ref[...] = moment
    new_second_ref[...] = second
    update_ref[...] = update
    master_sq = jnp.where(inside, master * master, 0.0)
    update_sq = update * update
    lanes = lax.broadcasted_iota(jnp.int32, (1, LANES), 1)
    rows = []
    for squares in (master_sq, update_sq):
        row = jnp.zeros((1, LANES), F32)
        for t in range(MATS):
            mine = jnp.logical_and(index >= BOUNDS[t], index < BOUNDS[t + 1])
            part = jnp.sum(jnp.where(mine, squares, 0.0), axis=0, keepdims=True)
            row = jnp.where(lanes == t, jnp.sum(part, axis=1, keepdims=True), row)
        rows.append(row)
    rows.append(jnp.zeros((6, LANES), F32))
    sums_ref[...] = jnp.concatenate(rows, axis=0)


def update_part(plan, parts, master_rows, moment_rows, second_rows):
    rows = jax.ShapeDtypeStruct((plan.win, LANES), F32)
    return pl.pallas_call(
        functools.partial(update_kernel, plan),
        out_shape=(rows, rows, rows, jax.ShapeDtypeStruct((8, LANES), F32)),
        in_specs=[VMEM] * 7,
        out_specs=(VMEM,) * 4,
        scratch_shapes=[pltpu.VMEM((plan.win, LANES), F32)],
        compiler_params=params(12),
    )(*parts, master_rows, moment_rows, second_rows)


def apply_kernel(plan, *refs):
    *sums_refs, master_ref, update_ref, new_ref, norms_ref, trust_ref = refs
    roots = jnp.sqrt(tree_sum([ref[...] for ref in sums_refs]))
    trust = roots[0:1, :] / (roots[1:2, :] + adam_epsilon)
    norms_ref[...] = roots[0:2, :MATS]
    trust_ref[...] = trust[:, :MATS]
    master = master_ref[...]
    _, index = flat_place(plan, master.shape)
    factors = jnp.broadcast_to(trust[:, 0:1], master.shape)
    for t in range(1, MATS):
        factors = jnp.where(index >= BOUNDS[t], trust[:, t : t + 1], factors)
    new_ref[...] = master - learn_rate * factors * update_ref[...]


def apply_part(plan, sums, master_rows, update_rows):
    return pl.pallas_call(
        functools.partial(apply_kernel, plan),
        out_shape=(
            jax.ShapeDtypeStruct((plan.win, LANES), F32),
            jax.ShapeDtypeStruct((2, MATS), F32),
            jax.ShapeDtypeStruct((1, MATS), F32),
        ),
        in_specs=[VMEM] * (len(sums) + 2),
        out_specs=(VMEM,) * 3,
        compiler_params=params(8),
    )(*sums, master_rows, update_rows)


def lay_column_kernel(count, *refs):
    for i, part in enumerate(refs[:count]):
        refs[-1][i] = part[...]


def lay_column(parts, *after):
    return pl.pallas_call(
        functools.partial(lay_column_kernel, len(parts)),
        out_shape=jax.ShapeDtypeStruct((len(parts), *parts[0].shape), parts[0].dtype),
        in_specs=[VMEM] * (len(parts) + len(after)),
        out_specs=VMEM,
        compiler_params=params(4),
    )(*parts, *after)


def choose_kernel(plan, *refs):
    columns, (lower_ref, _, early_ref), late_refs = (
        refs[: plan.nb],
        refs[plan.nb : plan.nb + 3],
        refs[plan.nb + 3 :],
    )
    bucket = lax.axis_index("bucket")
    early_ref[:, plan.kept_row :] = lower_ref[:, 0, plan.win - plan.upper - 16 :]
    for i, part in enumerate(columns):
        for owner, out_ref in enumerate((early_ref, *late_refs)):

            @pl.when(jnp.bitwise_xor(bucket, i) == owner)
            def _():
                out_ref[:, : plan.upper] = part[...]
                out_ref[:, plan.upper : plan.win] = lower_ref[:, i]

    early_ref[:, plan.win : plan.kept_row] = late_refs[-1][:, plan.vec_from :]


def choose(plan, columns, lower, token):
    step = columns[0].shape[0]
    late = jax.ShapeDtypeStruct((step, plan.win, LANES), BF)
    return pl.pallas_call(
        functools.partial(choose_kernel, plan),
        out_shape=(jax.ShapeDtypeStruct((step, plan.early, LANES), BF),) + (late,) * (plan.nb - 1),
        in_specs=[VMEM] * (len(columns) + 2),
        out_specs=(VMEM,) * plan.nb,
        compiler_params=params(10),
    )(*columns, lower, token)


def add_parts_kernel(halves, *refs):
    refs = list(refs)
    parts = [[refs.pop(0) for _ in range(count)] for count in halves]
    for i, out in enumerate(refs[1:-1]):
        step = out.shape[-3]
        at = slice(i * step, (i + 1) * step)
        at = (slice(None), at) if len(out.shape) == 4 else at
        values = [
            jnp.concatenate([half[at].astype(F32) for half in part], axis=-2) for part in parts
        ]
        out[...] = tree_sum(values).astype(out.dtype)
    refs[-1][...] = jnp.zeros_like(refs[-1])


def add_parts(parts, pieces, token):
    *lead, total, height, width = parts[0].shape
    parts = [part if isinstance(part, list) else [part] for part in parts]
    halves = [len(part) for part in parts]
    parts = [half for part in parts for half in part]
    return pl.pallas_call(
        functools.partial(add_parts_kernel, halves),
        out_shape=tuple(
            jax.ShapeDtypeStruct((*lead, total // pieces, height, width), BF if i else F32)
            for i in range(pieces)
        )
        + (jax.ShapeDtypeStruct((8, LANES), F32),),
        in_specs=[VMEM] * (len(parts) + 1),
        out_specs=(VMEM,) * (pieces + 1),
        compiler_params=params(14),
    )(*parts, token)


def blend_kernel(plan, late_count, *refs):
    late, parts, outs = refs[:late_count], refs[late_count + 1 : -plan.nb], refs[-plan.nb :]
    bucket = lax.axis_index("bucket")
    first = tree_sum([part[...].astype(F32) for part in parts])
    for i, out in enumerate(outs):
        owner = jnp.bitwise_xor(bucket, i)
        quarter = jnp.maximum(owner - 1, 0)
        window = late[0][quarter]
        if late_count > 1:
            window = window + tree_sum([ref[quarter].astype(F32) for ref in late[1:]])
        out[: plan.win] = jnp.where(owner == 0, first[: plan.win], window).astype(out.dtype)
        out[plan.win :] = first[plan.win :].astype(out.dtype)


def blend(plan, late, token, parts):
    return pl.pallas_call(
        functools.partial(blend_kernel, plan, len(late)),
        out_shape=tuple(
            jax.ShapeDtypeStruct((plan.tail, LANES), BF if i else F32) for i in range(plan.nb)
        ),
        in_specs=[VMEM] * (len(late) + 1 + len(parts)),
        out_specs=(VMEM,) * plan.nb,
        compiler_params=params(10),
    )(*late, token, *parts)


def add_rows_kernel(*refs):
    refs[-1][...] = tree_sum([ref[...] for ref in refs[:-1]])


def add_rows(parts):
    return pl.pallas_call(
        add_rows_kernel,
        out_shape=jax.ShapeDtypeStruct(parts[0].shape, F32),
        in_specs=[VMEM] * len(parts),
        out_specs=VMEM,
        compiler_params=params(4),
    )(*parts)


def groups_of(size, skip=0):
    bits = list(range(skip, size.bit_length() - 1))
    return [bits[i : i + 2] for i in range(0, len(bits), 2)]


def masks_of(bits):
    masks = [1 << bits[0]]
    if len(bits) == 2:
        masks += [1 << bits[1], (1 << bits[0]) | (1 << bits[1])]
    return masks


def swap(x, axis, size, mask):
    return lax.ppermute(x, axis, [(i, i ^ mask) for i in range(size)])


def tree_sum(parts):
    if len(parts) == 1:
        return parts[0]
    half = len(parts) // 2
    return tree_sum(parts[:half]) + tree_sum(parts[half:])


def with_partners(x, axis, size, bits):
    return [x] + [swap(x, axis, size, mask) for mask in masks_of(bits)]


def gather_windows(plan, upper, lower, token):
    first, *more = groups_of(plan.nd, 1)
    (bits,) = groups_of(plan.nb)
    lower = lay_column(with_partners(lower, "bucket", plan.nb, bits))
    column = lay_column(with_partners(upper, "dp", plan.nd, first), lower)
    for group in more:
        column = jnp.concatenate(with_partners(column, "dp", plan.nd, group), axis=0)
    columns = with_partners(column, "bucket", plan.nb, bits)
    lower = lay_column(with_partners(lower, "dp", plan.nd, first))
    for group in more:
        lower = jnp.concatenate(with_partners(lower, "dp", plan.nd, group), axis=0)
    early, *late = choose(plan, columns, lower, token)
    others = [swap(x, "dp", plan.nd, 1) for x in (early, *late)]
    return (early, others[0]), (*late, *others[1:])


def scatter_dp(plan, pieces):
    *more, last = groups_of(plan.nd, 1)
    got = [pieces[0]] + [
        swap(piece, "dp", plan.nd, mask) for piece, mask in zip(pieces[1:], masks_of(last))
    ]
    for bits in reversed(more):
        held = tree_sum([x.astype(F32) for x in got])
        size = 1 << len(bits)
        step = held.shape[-3] // size
        parts = [held[..., i * step : (i + 1) * step, :, :] for i in range(size)]
        got = [parts[0]] + [
            swap(part.astype(BF), "dp", plan.nd, mask)
            for part, mask in zip(parts[1:], masks_of(bits))
        ]
    return [x.reshape(*x.shape[:-3], *x.shape[-2:]) for x in got]


def sum_all(plan, x):
    x = [x, swap(x, "dp", plan.nd, 1)]
    for bits in groups_of(plan.nd, 1):
        x = with_partners(add_rows(x), "dp", plan.nd, bits)
    (bits,) = groups_of(plan.nb)
    return with_partners(add_rows(x), "bucket", plan.nb, bits)


def local(
    plan, tokens, cotangent, segment_ids, keep_mask, bucket_patches, master, first_moment, second_moment
):
    def as_rows(flat):
        return jnp.pad(flat, (0, plan.win * LANES - plan.shard)).reshape(plan.win, LANES)

    def as_flat(rows):
        return rows.reshape(-1)[: plan.shard]

    master_rows = as_rows(master)
    seg_row = segment_ids.reshape(1, SEQ)
    keep_row = keep_mask.reshape(1, SEQ)
    count = 1 << len(groups_of(plan.nd, 1)[-1])
    (b_bits,) = groups_of(plan.nb)

    hat_in, rstd_in, token = ahead(tokens)
    early, late = gather_windows(plan, *prepare(plan, master_rows, keep_row), token)
    wq, vec, head, kept, q, k, v, hat, rstd = project_part(plan, *early, hat_in)
    o, ot, whole, lse, kab, segk = forward(plan, segment_ids, seg_row, keep_row, q, k, v)
    block_output, dh1, do, near, far, tail, gvec = middle_part(
        plan, late, tokens, cotangent, o, ot, head, kept, vec, keep_row, bucket_patches
    )
    *stacks, normed, token = stack_part(vec, hat_in, q, k, v, do, whole)
    *pieces, token = add_parts([near, swap(far, "dp", plan.nd, 1)], count, token)
    rest = scatter_dp(plan, pieces)
    low, gains = backward(
        plan, vec, segment_ids, seg_row, lse, q, do, hat, rstd, segk, [kab, *stacks], token
    )
    da1, near, *far = finish_part(plan, hat_in, normed, wq, tail, gvec, low, gains)
    input_grad, given = input_part(hat_in, rstd_in, vec, da1, dh1)
    *late_parts, token = add_parts(rest[:2], 1, gains)
    late_parts += rest[2:]
    *pieces, _ = add_parts([near, [swap(half, "dp", plan.nd, 1) for half in far]], count, token)
    first = scatter_dp(plan, pieces)
    mine, *sent = blend(plan, late_parts, given, first)
    parts = [mine] + [
        swap(x, "bucket", plan.nb, mask) for x, mask in zip(sent, masks_of(b_bits))
    ]
    moment_rows, second_rows, update_rows, sums = update_part(
        plan, parts, master_rows, as_rows(first_moment), as_rows(second_moment)
    )
    new_master, norms, trust = apply_part(plan, sum_all(plan, sums), master_rows, update_rows)
    return (
        block_output,
        input_grad,
        as_flat(moment_rows),
        as_flat(second_rows),
        as_flat(new_master),
        norms,
        trust.reshape(MATS),
    )


def solution(mesh):
    shards = mesh.shape["bucket"] * mesh.shape["dp"]
    plan = Plan(mesh.shape, PARAMS // shards)
    both = ("bucket", "dp")
    return jax.shard_map(
        functools.partial(local, plan),
        mesh=mesh,
        in_specs=(P(both, None), P(both, None), P(both), P(both), P(), P(both), P(both), P(both)),
        out_specs=(P(both, None), P(both, None), P(both), P(both), P(both), P(), P()),
        check_vma=False,
    )
```

```python
import functools
import math

import jax
import jax.numpy as jnp
from jax import lax
from jax.experimental import pallas as pl
from jax.experimental.pallas import tpu as pltpu
from jax.sharding import PartitionSpec as P

D = 384
HEADS = 6
HD = 64
FF = 1536
SEQ = 1024
STEP = 10
MATS = 10
LANES = 128
PAIRS = HEADS // 2
TILE = 256
TILES = SEQ // TILE
BLOCKS = SEQ // LANES
MIDDLE_BLOCK = 512
FAR_PARTS = 3

norm_epsilon = 1e-06
adam_epsilon = 1e-06
beta_one = 0.9
beta_two = 0.999
learn_rate = 0.5
weight_decay = 0.01
masked_score = -1e30

MATRIX_END = 4 * D * D + 2 * D * FF
BOUNDS = [0, 3 * D * D, 4 * D * D, 4 * D * D + D * FF, MATRIX_END] + [
    MATRIX_END + (j + 1) * D for j in range(6)
]
PARAMS = BOUNDS[-1]
ROW_OUT = BOUNDS[1] // LANES
ROW_UP = BOUNDS[2] // LANES
ROW_DOWN = BOUNDS[3] // LANES
ROW_VEC = BOUNDS[4] // LANES
VEC_ROWS = 6 * D // LANES
ROWS_ALL = PARAMS // LANES

score_scale = HD ** (-0.5) * math.log2(math.e)
grad_scale = HD ** (-0.5)

BF = jnp.bfloat16
F32 = jnp.float32
VMEM = pl.BlockSpec(memory_space=pltpu.VMEM)
SMEM = pl.BlockSpec(memory_space=pltpu.SMEM)


QUICK = pl.CostEstimate(flops=1000, bytes_accessed=1000, transcendentals=0)


def params(limit):
    return pltpu.CompilerParams(vmem_limit_bytes=limit * 1024 * 1024)


def round_up(value, step):
    return -(-value // step) * step


class Plan:
    def __init__(self, mesh_shape, shard):
        self.nb = mesh_shape["bucket"]
        self.nd = mesh_shape["dp"]
        self.n = self.nb * self.nd
        self.shard = shard
        self.start = [k * shard // LANES for k in range(self.n)]
        self.rows = [
            -(-((k + 1) * shard) // LANES) - self.start[k] for k in range(self.n)
        ]
        self.win = round_up(max(self.rows) + 1, 16)
        self.tail = round_up(self.win + VEC_ROWS, 16 * FAR_PARTS)
        self.upper = self.win * 3 // 4 // 16 * 16
        self.vec_place = ROW_VEC - self.start[-1]
        self.vec_from = self.vec_place // 16 * 16
        self.kept_row = 2 * self.win - self.vec_from
        self.early = self.kept_row + 16

    def device(self):
        return lax.axis_index("bucket") * self.nd + lax.axis_index("dp")


def nn(a, b):
    return lax.dot_general(a, b, (((1,), (0,)), ((), ())), preferred_element_type=F32)


def nt(a, b):
    return lax.dot_general(a, b, (((1,), (1,)), ((), ())), preferred_element_type=F32)


def split_low(x):
    high = x.astype(BF)
    return high, (x - high.astype(F32)).astype(BF)


def rows_at(step):
    if isinstance(step, int):
        return slice(step * TILE, (step + 1) * TILE)
    return pl.ds(pl.multiple_of(step * TILE, TILE), TILE)


def norm_parts(values):
    average = jnp.mean(values, axis=-1, keepdims=True)
    centered = values - average
    variance = jnp.mean(centered * centered, axis=-1, keepdims=True)
    rstd = lax.rsqrt(variance + norm_epsilon)
    return centered * rstd, rstd


def norm_back(hat, rstd, grad):
    mean_grad = jnp.mean(grad, axis=-1, keepdims=True)
    mean_both = jnp.mean(grad * hat, axis=-1, keepdims=True)
    return rstd * (grad - mean_grad - hat * mean_both)


def head_mean_matrix():
    row = lax.broadcasted_iota(jnp.int32, (TILE, TILE), 0)
    col = lax.broadcasted_iota(jnp.int32, (TILE, TILE), 1)
    return jnp.where(row // HD == col // HD, 1.0 / HD, 0.0).astype(BF)


def head_mean_low(low, matrix):
    rest = D - TILE
    return jnp.concatenate(
        [nn(low[:, :TILE], matrix), nn(low[:, TILE:], matrix[:rest, :rest])], axis=1
    )


def head_mean(x, matrix):
    high, rest = split_low(x)
    return head_mean_low(high, matrix) + head_mean_low(rest, matrix)


def flat_to_rows(plan, flat_ref, rows_ref):
    full, rest = divmod(plan.shard, LANES)
    rows_ref[full:, :] = jnp.zeros((plan.win - full, LANES), F32)
    rows_ref[:full, :] = flat_ref[: full * LANES].reshape(full, LANES)
    if rest:
        rows_ref[full : full + 1, :rest] = flat_ref[full * LANES :].reshape(1, rest)
    return rows_ref[...]


def rows_to_flat(plan, rows, flat_ref):
    full, rest = divmod(plan.shard, LANES)
    flat_ref[: full * LANES] = rows[:full].reshape(full * LANES)
    if rest:
        flat_ref[full * LANES :] = rows[full : full + 1, :rest].reshape(rest)


def prepare_kernel(plan, master_ref, upper_ref, lower_ref, rows_ref):
    offset = lax.rem(plan.device() * plan.shard, LANES)
    values = flat_to_rows(plan, master_ref, rows_ref)
    turned = pltpu.roll(values, offset, 1)
    below = pltpu.roll(turned, 1, 0)
    lane = lax.broadcasted_iota(jnp.int32, values.shape, 1)
    window = jnp.where(lane < offset, below, turned).astype(BF)
    upper_ref[...] = window[: plan.upper]
    lower_ref[...] = window[plan.upper :]


def prepare(plan, master):
    return pl.pallas_call(
        functools.partial(prepare_kernel, plan),
        out_shape=(
            jax.ShapeDtypeStruct((plan.upper, LANES), BF),
            jax.ShapeDtypeStruct((plan.win - plan.upper, LANES), BF),
        ),
        in_specs=[VMEM],
        out_specs=(VMEM, VMEM),
        scratch_shapes=[pltpu.VMEM((plan.win, LANES), F32)],
        compiler_params=params(8),
    )(master)


def ahead_kernel(tokens_ref, keep_ref, hat_ref, rstd_ref, count_ref):
    hat, rstd = norm_parts(tokens_ref[...].astype(F32))
    hat_ref[...] = hat
    rstd_ref[...] = jnp.broadcast_to(rstd, rstd_ref.shape)
    row = lax.broadcasted_iota(jnp.int32, count_ref.shape, 0)
    lane = lax.broadcasted_iota(jnp.int32, count_ref.shape, 1)
    count = jnp.sum(keep_ref[...].astype(F32), axis=1, keepdims=True)
    high = jnp.floor(count * (1.0 / 32.0))
    parts = jnp.where(lane == 0, high, jnp.where(lane == 1, count - 32.0 * high, 0.0))
    count_ref[...] = jnp.where(row == 15, parts, 0.0)


def ahead(tokens, keep_row):
    rows = tokens.shape[0]
    return pl.pallas_call(
        ahead_kernel,
        out_shape=(
            jax.ShapeDtypeStruct((rows, D), F32),
            jax.ShapeDtypeStruct((rows, LANES), F32),
            jax.ShapeDtypeStruct((16, LANES), F32),
        ),
        in_specs=[VMEM, VMEM],
        out_specs=(VMEM,) * 3,
        compiler_params=params(12),
        cost_estimate=QUICK,
    )(tokens, keep_row)


def held_window(own_ref, other_ref, rel, at):
    place = jnp.right_shift(rel, 1)
    return jnp.where(
        jnp.bitwise_and(rel, 1) == 0,
        own_ref[place, at].astype(F32),
        other_ref[place, at].astype(F32),
    )


def lay_windows(plan, owners, refs_of, flat, base):
    dp = lax.axis_index("dp")
    for k in owners:
        own_ref, other_ref = refs_of(k)
        window = held_window(own_ref, other_ref, jnp.bitwise_xor(dp, k % plan.nd), slice(0, plan.win))
        first, count = plan.start[k] - base, plan.rows[k]
        shared = k > 0 and (k * plan.shard) % LANES
        if shared:
            before = flat[first : first + 1, :]
        flat[first : first + count, :] = window[:count]
        if shared:
            flat[first : first + 1, :] = before + window[:1]


def take_matrix(target, flat, base, height, width):
    stride = width // LANES
    for j in range(stride):
        target[:, j * LANES : (j + 1) * LANES] = flat[pl.ds(base + j, height, stride=stride), :].astype(BF)


def put_matrix(flat, base, source, height, width):
    stride = width // LANES
    for j in range(stride):
        flat[pl.ds(base + j, height, stride=stride), :] = source[:, j * LANES : (j + 1) * LANES]


def key_chunks(seg_ref, ti):
    first_i, last_i = seg_ref[ti * TILE], seg_ref[ti * TILE + TILE - 1]
    low, high = jnp.int32(0), jnp.int32(0)
    for b in range(BLOCKS):
        low += (seg_ref[b * LANES + LANES - 1] < first_i).astype(jnp.int32)
        high += (seg_ref[b * LANES] <= last_i).astype(jnp.int32)
    count = jnp.right_shift(high - low + 1, 1)
    return jnp.minimum(low, BLOCKS - 2 * count), count


def tile_bias(ti, block, row_seg, key_seg):
    key_place = lax.broadcasted_iota(jnp.int32, (TILE, TILE), 0) + block * LANES
    row_place = lax.broadcasted_iota(jnp.int32, (TILE, TILE), 1) + ti * TILE
    return jnp.where(
        jnp.logical_or(key_seg == row_seg, key_place == row_place), 0.0, masked_score
    )


def keys_at(block):
    return pl.ds(pl.multiple_of(block * LANES, LANES), TILE)


def side_rows(stacked, side):
    return jnp.concatenate(
        [stacked[side * LANES : (side + 1) * LANES], stacked[(2 + side) * LANES : (3 + side) * LANES]],
        axis=0,
    )


def to_column(row):
    return jnp.transpose(jnp.broadcast_to(row, (LANES, row.shape[1])))


def block_heads(pair):
    lane = lax.broadcasted_iota(jnp.int32, pair.shape, 1)
    zero = jnp.zeros_like(pair)
    sides = [jnp.where(lane < HD, pair, zero), jnp.where(lane >= HD, pair, zero)]
    return [side[b * LANES : (b + 1) * LANES] for b in range(2) for side in sides]


def put_blocks(ref, hp, step, pair):
    for i, part in enumerate(block_heads(pair)):
        ref[hp, 2 * step + i // 2, i % 2] = part


def two_blocks(ref, hp, block):
    return ref[hp, pl.ds(block, 2)].reshape(4 * LANES, LANES)


def stack_heads(pair):
    lane = lax.broadcasted_iota(jnp.int32, pair.shape, 1)
    zero = jnp.zeros_like(pair)
    return jnp.concatenate(
        [jnp.where(lane < HD, pair, zero), jnp.where(lane >= HD, pair, zero)], axis=0
    )


def project_kernel(
    plan,
    own_ref,
    other_ref,
    hat_in_ref,
    wq_ref,
    vec_ref,
    head_ref,
    kept_ref,
    q_ref,
    k_ref,
    v_ref,
    hat_ref,
    rstd_ref,
    flat,
):
    dp = lax.axis_index("dp")
    lay_windows(plan, range(plan.nd), lambda k: (own_ref, other_ref), flat, 0)
    take_matrix(wq_ref, flat, 0, D, 3 * D)
    head_ref[...] = flat[ROW_OUT : ROW_OUT + 8, :]
    rel = jnp.bitwise_xor(dp, plan.nd - 1)
    late = held_window(own_ref, other_ref, rel, slice(plan.win, plan.kept_row))
    kept = jnp.zeros((1, LANES), F32)
    for j in range(plan.nd):
        half = other_ref if j & 1 else own_ref
        kept = kept + half[j >> 1, plan.kept_row :].astype(F32)[15:16]
    kept_ref[...] = jnp.broadcast_to(32.0 * kept[:, 0:1] + kept[:, 1:2], kept_ref.shape)
    for t in range(6):
        for j in range(D // LANES):
            at = plan.vec_place - plan.vec_from + 3 * t + j
            vec_ref[t : t + 1, j * LANES : (j + 1) * LANES] = late[at : at + 1]
    matrix = head_mean_matrix()
    gain1, shift1 = vec_ref[0:1, :], vec_ref[1:2, :]
    gain_q, gain_k = vec_ref[2:3, :], vec_ref[3:4, :]

    raw = nn((hat_in_ref[...] * gain1 + shift1).astype(BF), wq_ref[...])

    def head_norm(low_out, part, gain):
        lanes = slice(part * D, (part + 1) * D)
        x = raw[:, lanes]
        centered = x - head_mean(x, matrix)
        rstd = lax.rsqrt(head_mean(centered * centered, matrix) + norm_epsilon)
        normed = centered * rstd
        hat_ref[:, lanes] = normed
        rstd_ref[:, lanes] = rstd
        low_out[...] = (normed * gain).astype(BF)

    head_norm(q_ref, 0, gain_q)
    head_norm(k_ref, 1, gain_k)
    v_ref[...] = raw[:, 2 * D :].astype(BF)


def project_part(plan, own, other, tokens):
    rows = tokens.shape[0]
    low = jax.ShapeDtypeStruct((rows, D), BF)
    return pl.pallas_call(
        functools.partial(project_kernel, plan),
        out_shape=(
            jax.ShapeDtypeStruct((D, 3 * D), BF),
            jax.ShapeDtypeStruct((8, D), F32),
            jax.ShapeDtypeStruct((8, LANES), F32),
            jax.ShapeDtypeStruct((8, LANES), F32),
            low,
            low,
            low,
            jax.ShapeDtypeStruct((rows, 2 * D), F32),
            jax.ShapeDtypeStruct((rows, 2 * D), F32),
        ),
        in_specs=[VMEM] * 3,
        out_specs=(VMEM,) * 9,
        scratch_shapes=[
            pltpu.VMEM((round_up(plan.start[plan.nd - 1] + plan.win, 8), LANES), F32),
        ],
        compiler_params=params(24),
        cost_estimate=QUICK,
    )(own, other, tokens)


def forward_kernel(
    plan,
    seg_smem,
    seg_ref,
    keep_ref,
    q_ref,
    k_ref,
    v_ref,
    o_ref,
    ot_ref,
    whole_ref,
    lse_ref,
    kab,
    segk,
    vt,
    ot,
    rest_t,
    sums,
    expo,
):
    seg_row = seg_ref[...].astype(F32)
    segk[...] = to_column(jnp.where(keep_ref[...] == 1, seg_row, -1.0))

    for step in range(TILES):
        at = rows_at(step)
        for hp in range(PAIRS):
            put_blocks(kab, hp, step, k_ref[at, hp * LANES : (hp + 1) * LANES])
        vt[:, at] = jnp.transpose(v_ref[at, :].astype(F32)).astype(BF)

    def query_tile(ti, carry):
        ot[...] = jnp.zeros_like(ot)
        rest_t[...] = jnp.zeros_like(rest_t)
        sums[...] = jnp.zeros_like(sums)
        row_seg = seg_ref[:, rows_at(ti)].astype(F32)
        first, count = key_chunks(seg_smem, ti)

        def score_chunk(c, inner):
            block = first + 2 * c
            column = segk[keys_at(block), :]
            bias = tile_bias(ti, block, row_seg, jnp.concatenate([column, column], axis=1))
            for hp in range(PAIRS):
                queries = q_ref[rows_at(ti), hp * LANES : (hp + 1) * LANES]
                scores = nt(two_blocks(kab, hp, block), queries)
                for side in range(2):
                    head = 2 * hp + side
                    value = jnp.exp2(side_rows(scores, side) * score_scale + bias)
                    expo[c, head] = value
                    sums[head : head + 1, :] += jnp.sum(value, axis=0, keepdims=True)
            return inner

        lax.fori_loop(0, count, score_chunk, 0)
        lse_ref[ti] = jnp.log2(sums[...])
        sums[...] = 1.0 / sums[...]

        def value_chunk(c, inner):
            keys = keys_at(first + 2 * c)
            for head in range(HEADS):
                prob, rest = split_low(expo[c, head] * sums[head : head + 1, :])
                at = slice(head * HD, (head + 1) * HD)
                ot[at, :] += nn(vt[at, keys], prob)
                rest_t[at, :] += nn(vt[at, keys], rest)
            return inner

        lax.fori_loop(0, count, value_chunk, 0)
        attended = ot[...]
        ot_ref[ti] = attended.astype(BF)
        whole_ref[ti] = attended + rest_t[...]
        o_ref[rows_at(ti), :] = jnp.transpose(attended).astype(BF)
        return carry

    lax.fori_loop(0, TILES, query_tile, 0)


def forward(plan, seg, seg_row, keep_row, q, k, v):
    rows = q.shape[0]
    return pl.pallas_call(
        functools.partial(forward_kernel, plan),
        out_shape=(
            jax.ShapeDtypeStruct((rows, D), BF),
            jax.ShapeDtypeStruct((TILES, D, TILE), BF),
            jax.ShapeDtypeStruct((TILES, D, TILE), F32),
            jax.ShapeDtypeStruct((TILES, 8, TILE), F32),
            jax.ShapeDtypeStruct((PAIRS, BLOCKS, 2, LANES, LANES), BF),
            jax.ShapeDtypeStruct((SEQ, LANES), F32),
        ),
        in_specs=[SMEM] + [VMEM] * 5,
        out_specs=(VMEM,) * 6,
        scratch_shapes=[
            pltpu.VMEM((D, SEQ), BF),
            pltpu.VMEM((D, TILE), F32),
            pltpu.VMEM((D, TILE), F32),
            pltpu.VMEM((8, TILE), F32),
            pltpu.VMEM((TILES, HEADS, TILE, TILE), F32),
        ],
        compiler_params=params(24),
        cost_estimate=QUICK,
    )(seg, seg_row, keep_row, q, k, v)


erfc_step = 0.3275911 * math.sqrt(0.5)
erfc_terms = [0.254829592, -0.284496736, 1.421413741, -1.453152027, 1.061405429]


def normal_parts(u):
    expo = jnp.exp2(u * u * (-0.5 * math.log2(math.e)))
    t = 1.0 / (1.0 + erfc_step * jnp.abs(u))
    poly = 0.5 * erfc_terms[4]
    for term in reversed(erfc_terms[:4]):
        poly = poly * t + 0.5 * term
    below = poly * t * expo
    return jnp.where(u > 0.0, 1.0 - below, below), expo * (1.0 / math.sqrt(2.0 * math.pi))


def middle_kernel(plan, *refs):
    late_refs, rest = refs[: 2 * plan.nb - 2], refs[2 * plan.nb - 2 :]
    middle_body(plan, late_refs, *rest)


def middle_body(
    plan,
    late_refs,
    tokens_ref,
    cot_ref,
    o_ref,
    ot_ref,
    head_ref,
    kept_ref,
    vec_ref,
    keep_ref,
    patches_ref,
    out_ref,
    dh1_ref,
    do_ref,
    near_ref,
    far_ref,
    tail_ref,
    gvec_ref,
    keepc,
    hid,
    dus,
    flat,
    wo_ref,
    wu_ref,
    wd_ref,
):
    bucket = lax.axis_index("bucket")
    base = ROW_OUT
    flat[0:8, :] = head_ref[...]
    dp = lax.axis_index("dp")
    owns, others = late_refs[: plan.nb - 1], late_refs[plan.nb - 1 :]
    lay_windows(
        plan,
        range(plan.nd, plan.n),
        lambda k: (owns[k // plan.nd - 1], others[k // plan.nd - 1]),
        flat,
        base,
    )
    take_matrix(wo_ref, flat, 0, D, D)
    take_matrix(wu_ref, flat, ROW_UP - base, D, FF)
    take_matrix(wd_ref, flat, ROW_DOWN - base, FF, D)
    gain2, shift2 = vec_ref[4:5, :], vec_ref[5:6, :]
    own = patches_ref[bucket].astype(F32)
    total = patches_ref[0].astype(F32)
    for b in range(1, plan.nb):
        total = total + patches_ref[b].astype(F32)
    ones = jnp.ones((1, LANES), F32)
    scale = (plan.nb * own) * ones / (total * ones) * float(SEQ * plan.nd) / kept_ref[0:1, :]
    keepc[...] = to_column(keep_ref[...].astype(F32)) * scale
    gvec_ref[...] = jnp.zeros_like(gvec_ref)

    middle = tokens_ref[...].astype(F32) + nn(o_ref[...], wo_ref[...])
    hat, rstd = norm_parts(middle)
    low = (hat * gain2 + shift2).astype(BF)
    weights = keepc[...]
    seed = cot_ref[...].astype(F32) * jnp.concatenate([weights] * (D // LANES), axis=1)
    seed_low = seed.astype(BF)
    for first in range(0, FF, MIDDLE_BLOCK):
        cols = slice(first, first + MIDDLE_BLOCK)
        u = nn(low, wu_ref[:, cols])
        phi, bell = normal_parts(u)
        hid[:, cols] = (u * phi).astype(BF)
        dus[:, cols] = (nt(seed_low, wd_ref[cols, :]) * (phi + u * bell)).astype(BF)
    out_ref[...] = (middle + nn(hid[...], wd_ref[...])).astype(BF)
    seedt = jnp.transpose(seed).astype(BF)
    lowt = jnp.transpose(low.astype(F32)).astype(BF)
    da2 = nt(dus[...], wu_ref[...])
    gvec_ref[0:1, :] = jnp.sum(da2 * hat, axis=0, keepdims=True)
    gvec_ref[1:2, :] = jnp.sum(da2, axis=0, keepdims=True)
    dh1 = seed + norm_back(hat, rstd, da2 * gain2)
    dh1_ref[...] = dh1
    dh1_low = dh1.astype(BF)
    gout = nn(jnp.concatenate([ot_ref[t] for t in range(TILES)], axis=1), dh1_low)
    do_ref[...] = nt(dh1_low, wo_ref[...]).astype(BF)
    put_matrix(flat, 0, gout, D, D)
    block = 2 * TILE
    for i in range(FF // block):
        part = nn(lowt, dus[:, i * block : (i + 1) * block])
        for j in range(block // LANES):
            flat[pl.ds(ROW_UP - base + i * (block // LANES) + j, D, stride=FF // LANES), :] = part[
                :, j * LANES : (j + 1) * LANES
            ]
        part = jnp.transpose(nn(seedt, hid[:, i * block : (i + 1) * block]))
        for j in range(D // LANES):
            flat[
                pl.ds(ROW_DOWN - base + i * block * (D // LANES) + j, block, stride=D // LANES), :
            ] = part[:, j * LANES : (j + 1) * LANES]
    tail_ref[...] = flat[0:8, :]
    side = jnp.bitwise_and(dp, 1)
    for k in range(plan.nd, plan.n):
        first = plan.start[k] - base
        quarter = k // plan.nd - 1
        reld = jnp.right_shift(jnp.bitwise_xor(dp, k % plan.nd), 1)
        window = flat[first : first + plan.win, :].astype(BF)

        @pl.when(side == k % 2)
        def _():
            near_ref[quarter, reld] = window

        @pl.when(side != k % 2)
        def _():
            far_ref[quarter, reld] = window


def middle_part(plan, late, tokens, cot, o, ot, head, kept, vec, keep_row, patches):
    rows = tokens.shape[0]
    windows = jax.ShapeDtypeStruct((plan.nb - 1, plan.nd // 2, plan.win, LANES), BF)
    return pl.pallas_call(
        functools.partial(middle_kernel, plan),
        out_shape=(
            jax.ShapeDtypeStruct((rows, D), BF),
            jax.ShapeDtypeStruct((rows, D), F32),
            jax.ShapeDtypeStruct((rows, D), BF),
            windows,
            windows,
            jax.ShapeDtypeStruct((8, LANES), F32),
            jax.ShapeDtypeStruct((8, D), F32),
        ),
        in_specs=[VMEM] * (len(late) + 8) + [SMEM],
        out_specs=(VMEM,) * 7,
        scratch_shapes=[
            pltpu.VMEM((rows, LANES), F32),
            pltpu.VMEM((rows, FF), BF),
            pltpu.VMEM((rows, FF), BF),
            pltpu.VMEM((round_up(plan.start[-1] + plan.win - ROW_OUT, 8), LANES), F32),
            pltpu.VMEM((D, D), BF),
            pltpu.VMEM((D, FF), BF),
            pltpu.VMEM((FF, D), BF),
        ],
        compiler_params=params(36),
        cost_estimate=QUICK,
    )(*late, tokens, cot, o, ot, head, kept, vec, keep_row, patches)


def stack_kernel(
    vec_ref,
    hat_in_ref,
    q_ref,
    k_ref,
    v_ref,
    do_ref,
    whole_ref,
    vab,
    qab,
    dab,
    kt,
    inner_sums,
    normed_ref,
    token_ref,
):
    for step in range(TILES):
        at = rows_at(step)
        grads = do_ref[at, :]
        for hp in range(PAIRS):
            lanes = slice(hp * LANES, (hp + 1) * LANES)
            put_blocks(vab, hp, step, v_ref[at, lanes])
            qab[hp, step] = stack_heads(q_ref[at, lanes])
            dab[hp, step] = stack_heads(grads[:, lanes])
        kt[:, at] = jnp.transpose(k_ref[at, :].astype(F32)).astype(BF)
        both = jnp.transpose(grads.astype(F32)) * whole_ref[step]
        for head in range(HEADS):
            inner_sums[step, head : head + 1, :] = jnp.sum(
                both[head * HD : (head + 1) * HD], axis=0, keepdims=True
            )
        normed = hat_in_ref[at, :] * vec_ref[0:1, :] + vec_ref[1:2, :]
        normed_ref[:, at] = jnp.transpose(normed).astype(BF)
    token_ref[...] = jnp.zeros_like(token_ref)


def stack_part(vec, hat_in, q, k, v, do, whole):
    stacked = jax.ShapeDtypeStruct((PAIRS, TILES, 2 * TILE, LANES), BF)
    return pl.pallas_call(
        stack_kernel,
        out_shape=(
            jax.ShapeDtypeStruct((PAIRS, BLOCKS, 2, LANES, LANES), BF),
            stacked,
            stacked,
            jax.ShapeDtypeStruct((D, SEQ), BF),
            jax.ShapeDtypeStruct((TILES, 8, TILE), F32),
            jax.ShapeDtypeStruct((D, SEQ), BF),
            jax.ShapeDtypeStruct((8, LANES), F32),
        ),
        in_specs=[VMEM] * 7,
        out_specs=(VMEM,) * 7,
        compiler_params=params(16),
        cost_estimate=QUICK,
    )(vec, hat_in, q, k, v, do, whole)


def backward_kernel(
    plan,
    vec_ref,
    seg_smem,
    seg_ref,
    lse_ref,
    q_ref,
    do_ref,
    hat_ref,
    rstd_ref,
    segk,
    kab,
    vab,
    qab,
    dab,
    kt,
    inner_sums,
    token_ref,
    low_ref,
    gains_ref,
    dqt,
    dk,
    dv,
):
    matrix = head_mean_matrix()
    dqt[...] = jnp.zeros_like(dqt)
    dk[...] = jnp.zeros_like(dk)
    dv[...] = jnp.zeros_like(dv)
    gains_ref[...] = jnp.zeros_like(gains_ref)

    def query_tile(ti, carry):
        row_seg = seg_ref[:, rows_at(ti)].astype(F32)
        first, count = key_chunks(seg_smem, ti)

        def key_chunk(c, inner):
            block = first + 2 * c
            keys = keys_at(block)
            column = segk[keys, :]
            bias = tile_bias(ti, block, row_seg, jnp.concatenate([column, column], axis=1))
            raw = []
            for hp in range(PAIRS):
                lanes = slice(hp * LANES, (hp + 1) * LANES)
                raw.append(
                    (
                        nt(two_blocks(kab, hp, block), q_ref[rows_at(ti), lanes]),
                        nt(two_blocks(vab, hp, block), do_ref[rows_at(ti), lanes]),
                    )
                )
            probs, dscores = [], []
            for head in range(HEADS):
                scores, grads = raw[head // 2]
                prob = jnp.exp2(
                    side_rows(scores, head % 2) * score_scale
                    + (bias - lse_ref[ti, head : head + 1, :])
                )
                dscore = prob * (side_rows(grads, head % 2) - inner_sums[ti, head : head + 1, :])
                probs.append(prob.astype(BF))
                dscores.append(dscore.astype(BF))
            for hp in range(PAIRS):
                pair = slice(2 * hp, 2 * hp + 2)
                for head in (2 * hp, 2 * hp + 1):
                    at = slice(head * HD, (head + 1) * HD)
                    dqt[ti, at, :] += nn(kt[at, keys], dscores[head])
                dv[hp, keys] += nn(jnp.concatenate(probs[pair], axis=1), dab[hp, ti])
                dk[hp, keys] += nn(jnp.concatenate(dscores[pair], axis=1), qab[hp, ti])
            return inner

        lax.fori_loop(0, count, key_chunk, 0)
        return carry

    lax.fori_loop(0, TILES, query_tile, 0)

    def finish(step, carry):
        at = rows_at(step)

        def head_norm_back(part, gain, grad):
            lanes = slice(part * D, (part + 1) * D)
            hat = hat_ref[at, lanes]
            both = grad * hat
            gains_ref[part : part + 1, :] += jnp.sum(both, axis=0, keepdims=True)
            scaled = grad * gain
            mean_grad = head_mean_low(scaled.astype(BF), matrix)
            mean_both = head_mean_low((both * gain).astype(BF), matrix)
            back = rstd_ref[at, lanes] * (scaled - mean_grad - hat * mean_both)
            low_ref[at, lanes] = back.astype(BF)

        grad_k = jnp.concatenate([dk[hp, at] for hp in range(PAIRS)], axis=1) * grad_scale
        grad_v = jnp.concatenate([dv[hp, at] for hp in range(PAIRS)], axis=1)
        head_norm_back(0, vec_ref[2:3, :], jnp.transpose(dqt[step]) * grad_scale)
        head_norm_back(1, vec_ref[3:4, :], grad_k)
        low_ref[at, 2 * D :] = grad_v.astype(BF)
        return carry

    lax.fori_loop(0, TILES, finish, 0)


def backward(plan, vec, seg, seg_row, lse, q, do, hat, rstd, segk, stacks, token):
    rows = q.shape[0]
    return pl.pallas_call(
        functools.partial(backward_kernel, plan),
        out_shape=(
            jax.ShapeDtypeStruct((rows, 3 * D), BF),
            jax.ShapeDtypeStruct((8, D), F32),
        ),
        in_specs=[VMEM, SMEM] + [VMEM] * 14,
        out_specs=(VMEM, VMEM),
        scratch_shapes=[
            pltpu.VMEM((TILES, D, TILE), F32),
            pltpu.VMEM((PAIRS, SEQ, LANES), F32),
            pltpu.VMEM((PAIRS, SEQ, LANES), F32),
        ],
        compiler_params=params(26),
        cost_estimate=QUICK,
    )(vec, seg, seg_row, lse, q, do, hat, rstd, segk, *stacks, token)


def finish_kernel(
    plan,
    hat_ref,
    normed_ref,
    wq_ref,
    tail_ref,
    gvec_ref,
    low_ref,
    gqk_ref,
    da1_ref,
    near_ref,
    *refs,
):
    *far_refs, gains, flat = refs
    hat = hat_ref[...]
    for i in range(3):
        part = nn(normed_ref[...], low_ref[:, i * D : (i + 1) * D])
        for j in range(D // LANES):
            flat[pl.ds(i * (D // LANES) + j, D, stride=3 * D // LANES), :] = part[
                :, j * LANES : (j + 1) * LANES
            ]
    da1 = nt(low_ref[...], wq_ref[...])
    da1_ref[...] = da1
    gains[...] = jnp.zeros_like(gains)
    gains[0:1, :] = jnp.sum(da1 * hat, axis=0, keepdims=True)
    gains[1:2, :] = jnp.sum(da1, axis=0, keepdims=True)
    gains[2:4, :] = gqk_ref[0:2, :]
    gains[4:6, :] = gvec_ref[0:2, :]
    flat[ROW_OUT : ROW_OUT + 8, :] = tail_ref[...]
    dp = lax.axis_index("dp")
    side = jnp.bitwise_and(dp, 1)
    rest = jnp.zeros((plan.tail - plan.win, LANES), BF)
    vector_rows = []
    for t in range(6):
        for j in range(D // LANES):
            vector_rows.append(gains[t : t + 1, j * LANES : (j + 1) * LANES])
    vector_rows.append(jnp.zeros((plan.tail - plan.win - VEC_ROWS, LANES), F32))
    vectors = jnp.concatenate(vector_rows, axis=0).astype(BF)
    for k in range(plan.nd):
        first = plan.start[k]
        reld = jnp.right_shift(jnp.bitwise_xor(dp, k), 1)
        window = flat[first : first + plan.win, :].astype(BF)
        window = jnp.concatenate([window, vectors if k == plan.nd - 1 else rest], axis=0)

        @pl.when(side == k % 2)
        def _():
            near_ref[reld] = window

        @pl.when(side != k % 2)
        def _():
            height = plan.tail // FAR_PARTS
            for i, far_ref in enumerate(far_refs):
                far_ref[reld] = window[i * height : (i + 1) * height]


def finish_part(plan, hat, normed, wq, tail, gvec, low, gains):
    rows = hat.shape[0]
    windows = jax.ShapeDtypeStruct((plan.nd // 2, plan.tail, LANES), BF)
    part = jax.ShapeDtypeStruct((plan.nd // 2, plan.tail // FAR_PARTS, LANES), BF)
    return pl.pallas_call(
        functools.partial(finish_kernel, plan),
        out_shape=(jax.ShapeDtypeStruct((rows, D), F32), windows) + (part,) * FAR_PARTS,
        in_specs=[VMEM] * 7,
        out_specs=(VMEM,) * (2 + FAR_PARTS),
        scratch_shapes=[
            pltpu.VMEM((8, D), F32),
            pltpu.VMEM((round_up(plan.start[plan.nd - 1] + plan.win, 8), LANES), F32),
        ],
        compiler_params=params(28),
        cost_estimate=QUICK,
    )(hat, normed, wq, tail, gvec, low, gains)


def input_kernel(hat_ref, rstd_ref, vec_ref, da1_ref, dh1_ref, grad_ref, token_ref):
    back = norm_back(hat_ref[...], rstd_ref[:, 0:1], da1_ref[...] * vec_ref[0:1, :])
    grad_ref[...] = dh1_ref[...] + back
    token_ref[...] = jnp.zeros_like(token_ref)


def input_part(hat, rstd, vec, da1, dh1):
    return pl.pallas_call(
        input_kernel,
        out_shape=(
            jax.ShapeDtypeStruct(dh1.shape, F32),
            jax.ShapeDtypeStruct((8, LANES), F32),
        ),
        in_specs=[VMEM] * 5,
        out_specs=(VMEM, VMEM),
        compiler_params=params(16),
        cost_estimate=QUICK,
    )(hat, rstd, vec, da1, dh1)


def flat_place(plan, shape):
    row = lax.broadcasted_iota(jnp.int32, shape, 0)
    lane = lax.broadcasted_iota(jnp.int32, shape, 1)
    place = row * LANES + lane
    return place, plan.device() * plan.shard + place


def update_kernel(
    plan,
    own_ref,
    got0_ref,
    got1_ref,
    got2_ref,
    master_ref,
    moment_ref,
    second_ref,
    new_moment_ref,
    new_second_ref,
    update_ref,
    sums_ref,
    window,
    master_rows,
    moment_rows,
    second_rows,
):
    bucket = lax.axis_index("bucket")
    dp = lax.axis_index("dp")
    total = tree_sum([ref[...].astype(F32) for ref in (own_ref, got0_ref, got1_ref, got2_ref)])
    window[...] = total[: plan.win]

    @pl.when(jnp.logical_and(bucket == plan.nb - 1, dp == plan.nd - 1))
    def _():
        window[plan.vec_place : plan.vec_place + VEC_ROWS, :] = total[
            plan.win : plan.win + VEC_ROWS
        ]

    offset = lax.rem(plan.device() * plan.shard, LANES)
    back = lax.rem(LANES - offset, LANES)
    turned = pltpu.roll(window[...], back, 1)
    above = pltpu.roll(turned, plan.win - 1, 0)
    lane = lax.broadcasted_iota(jnp.int32, turned.shape, 1)
    place, index = flat_place(plan, turned.shape)
    inside = place < plan.shard
    grad = jnp.where(inside, jnp.where(lane + offset < LANES, turned, above), 0.0)
    master = flat_to_rows(plan, master_ref, master_rows)
    old_moment = flat_to_rows(plan, moment_ref, moment_rows)
    old_second = flat_to_rows(plan, second_ref, second_rows)
    moment = beta_one * old_moment + (1.0 - beta_one) * grad
    second = beta_two * old_second + (1.0 - beta_two) * grad * grad
    first_hat = moment / (1.0 - beta_one**STEP)
    second_hat = second / (1.0 - beta_two**STEP)
    decay = jnp.where(index < BOUNDS[4], weight_decay, 0.0)
    update = first_hat / (jnp.sqrt(second_hat) + adam_epsilon) + decay * master
    update = jnp.where(inside, update, 0.0)
    rows_to_flat(plan, moment, new_moment_ref)
    rows_to_flat(plan, second, new_second_ref)
    update_ref[...] = update
    master_sq = jnp.where(inside, master * master, 0.0)
    update_sq = update * update
    lanes = lax.broadcasted_iota(jnp.int32, (1, LANES), 1)
    rows = []
    for squares in (master_sq, update_sq):
        row = jnp.zeros((1, LANES), F32)
        for t in range(MATS):
            mine = jnp.logical_and(index >= BOUNDS[t], index < BOUNDS[t + 1])
            part = jnp.sum(jnp.where(mine, squares, 0.0), axis=0, keepdims=True)
            row = jnp.where(lanes == t, jnp.sum(part, axis=1, keepdims=True), row)
        rows.append(row)
    rows.append(jnp.zeros((6, LANES), F32))
    sums_ref[...] = jnp.concatenate(rows, axis=0)


def update_part(plan, parts, master, moment, second):
    flat = jax.ShapeDtypeStruct((plan.shard,), F32)
    rows = jax.ShapeDtypeStruct((plan.win, LANES), F32)
    return pl.pallas_call(
        functools.partial(update_kernel, plan),
        out_shape=(flat, flat, rows, jax.ShapeDtypeStruct((8, LANES), F32)),
        in_specs=[VMEM] * 7,
        out_specs=(VMEM,) * 4,
        scratch_shapes=[pltpu.VMEM((plan.win, LANES), F32)] * 4,
        compiler_params=params(12),
    )(*parts, master, moment, second)


def apply_kernel(plan, *refs):
    *sums_refs, master_ref, update_ref, new_ref, norms_ref, trust_ref, rows_ref = refs
    roots = jnp.sqrt(tree_sum([ref[...] for ref in sums_refs]))
    trust = roots[0:1, :] / (roots[1:2, :] + adam_epsilon)
    norms_ref[...] = roots[0:2, :MATS]
    trust_ref[...] = trust[:, :MATS]
    master = flat_to_rows(plan, master_ref, rows_ref)
    _, index = flat_place(plan, master.shape)
    factors = jnp.broadcast_to(trust[:, 0:1], master.shape)
    for t in range(1, MATS):
        factors = jnp.where(index >= BOUNDS[t], trust[:, t : t + 1], factors)
    rows_to_flat(plan, master - learn_rate * factors * update_ref[...], new_ref)


def apply_part(plan, sums, master, update_rows):
    return pl.pallas_call(
        functools.partial(apply_kernel, plan),
        out_shape=(
            jax.ShapeDtypeStruct((plan.shard,), F32),
            jax.ShapeDtypeStruct((2, MATS), F32),
            jax.ShapeDtypeStruct((1, MATS), F32),
        ),
        in_specs=[VMEM] * (len(sums) + 2),
        out_specs=(VMEM,) * 3,
        scratch_shapes=[pltpu.VMEM((plan.win, LANES), F32)],
        compiler_params=params(8),
    )(*sums, master, update_rows)


def lay_column_kernel(count, *refs):
    for i, part in enumerate(refs[:count]):
        refs[-1][i] = part[...]


def lay_column(parts, *after):
    return pl.pallas_call(
        functools.partial(lay_column_kernel, len(parts)),
        out_shape=jax.ShapeDtypeStruct((len(parts), *parts[0].shape), parts[0].dtype),
        in_specs=[VMEM] * (len(parts) + len(after)),
        out_specs=VMEM,
        compiler_params=params(4),
    )(*parts, *after)


def lay_lower_kernel(plan, count_ref, *refs):
    for i, part in enumerate(refs[:-1]):
        refs[-1][i] = part[...]
    last = refs[0][-16:, :].astype(F32)
    refs[-1][0, plan.win - plan.upper - 16 :, :] = (last + count_ref[...]).astype(BF)


def lay_lower(plan, parts, count):
    return pl.pallas_call(
        functools.partial(lay_lower_kernel, plan),
        out_shape=jax.ShapeDtypeStruct((len(parts), *parts[0].shape), BF),
        in_specs=[VMEM] * (1 + len(parts)),
        out_specs=VMEM,
        compiler_params=params(4),
    )(count, *parts)


def choose_kernel(plan, *refs):
    columns, (lower_ref, early_ref), late_refs = (
        refs[: plan.nb],
        refs[plan.nb : plan.nb + 2],
        refs[plan.nb + 2 :],
    )
    bucket = lax.axis_index("bucket")
    early_ref[:, plan.kept_row :] = lower_ref[:, 0, plan.win - plan.upper - 16 :]
    for i, part in enumerate(columns):
        for owner, out_ref in enumerate((early_ref, *late_refs)):

            @pl.when(jnp.bitwise_xor(bucket, i) == owner)
            def _():
                out_ref[:, : plan.upper] = part[...]
                out_ref[:, plan.upper : plan.win] = lower_ref[:, i]

    early_ref[:, plan.win : plan.kept_row] = late_refs[-1][:, plan.vec_from :]


def choose(plan, columns, lower):
    step = columns[0].shape[0]
    late = jax.ShapeDtypeStruct((step, plan.win, LANES), BF)
    return pl.pallas_call(
        functools.partial(choose_kernel, plan),
        out_shape=(jax.ShapeDtypeStruct((step, plan.early, LANES), BF),) + (late,) * (plan.nb - 1),
        in_specs=[VMEM] * (len(columns) + 1),
        out_specs=(VMEM,) * plan.nb,
        compiler_params=params(10),
    )(*columns, lower)


def add_parts_kernel(halves, *refs):
    refs = list(refs)
    parts = [[refs.pop(0) for _ in range(count)] for count in halves]
    for i, out in enumerate(refs[1:-1]):
        step = out.shape[-3]
        at = slice(i * step, (i + 1) * step)
        at = (slice(None), at) if len(out.shape) == 4 else at
        values = [
            jnp.concatenate([half[at].astype(F32) for half in part], axis=-2) for part in parts
        ]
        out[...] = tree_sum(values).astype(out.dtype)
    refs[-1][...] = jnp.zeros_like(refs[-1])


def add_parts(parts, pieces, token):
    *lead, total, height, width = parts[0].shape
    parts = [part if isinstance(part, list) else [part] for part in parts]
    halves = [len(part) for part in parts]
    parts = [half for part in parts for half in part]
    return pl.pallas_call(
        functools.partial(add_parts_kernel, halves),
        out_shape=tuple(
            jax.ShapeDtypeStruct((*lead, total // pieces, height, width), BF if i else F32)
            for i in range(pieces)
        )
        + (jax.ShapeDtypeStruct((8, LANES), F32),),
        in_specs=[VMEM] * (len(parts) + 1),
        out_specs=(VMEM,) * (pieces + 1),
        compiler_params=params(14),
    )(*parts, token)


def blend_kernel(plan, late_count, *refs):
    late, parts, outs = refs[:late_count], refs[late_count + 1 : -plan.nb], refs[-plan.nb :]
    bucket = lax.axis_index("bucket")
    first = tree_sum([part[...].astype(F32) for part in parts])
    for i, out in enumerate(outs):
        owner = jnp.bitwise_xor(bucket, i)
        quarter = jnp.maximum(owner - 1, 0)
        window = late[0][quarter]
        if late_count > 1:
            window = window + tree_sum([ref[quarter].astype(F32) for ref in late[1:]])
        out[: plan.win] = jnp.where(owner == 0, first[: plan.win], window).astype(out.dtype)
        out[plan.win :] = first[plan.win :].astype(out.dtype)


def blend(plan, late, token, parts):
    return pl.pallas_call(
        functools.partial(blend_kernel, plan, len(late)),
        out_shape=tuple(
            jax.ShapeDtypeStruct((plan.tail, LANES), BF if i else F32) for i in range(plan.nb)
        ),
        in_specs=[VMEM] * (len(late) + 1 + len(parts)),
        out_specs=(VMEM,) * plan.nb,
        compiler_params=params(10),
    )(*late, token, *parts)


def add_rows_kernel(*refs):
    refs[-1][...] = tree_sum([ref[...] for ref in refs[:-1]])


def add_rows(parts):
    return pl.pallas_call(
        add_rows_kernel,
        out_shape=jax.ShapeDtypeStruct(parts[0].shape, F32),
        in_specs=[VMEM] * len(parts),
        out_specs=VMEM,
        compiler_params=params(4),
    )(*parts)


def groups_of(size, skip=0):
    bits = list(range(skip, size.bit_length() - 1))
    return [bits[i : i + 2] for i in range(0, len(bits), 2)]


def masks_of(bits):
    masks = [1 << bits[0]]
    if len(bits) == 2:
        masks += [1 << bits[1], (1 << bits[0]) | (1 << bits[1])]
    return masks


def swap(x, axis, size, mask):
    return lax.ppermute(x, axis, [(i, i ^ mask) for i in range(size)])


def tree_sum(parts):
    if len(parts) == 1:
        return parts[0]
    half = len(parts) // 2
    return tree_sum(parts[:half]) + tree_sum(parts[half:])


def with_partners(x, axis, size, bits):
    return [x] + [swap(x, axis, size, mask) for mask in masks_of(bits)]


def gather_windows(plan, upper, lower, count):
    first, *more = groups_of(plan.nd, 1)
    (bits,) = groups_of(plan.nb)
    lower = lay_lower(plan, with_partners(lower, "bucket", plan.nb, bits), count)
    column = lay_column(with_partners(upper, "dp", plan.nd, first), lower)
    for group in more:
        column = jnp.concatenate(with_partners(column, "dp", plan.nd, group), axis=0)
    columns = with_partners(column, "bucket", plan.nb, bits)
    lower = lay_column(with_partners(lower, "dp", plan.nd, first))
    for group in more:
        lower = jnp.concatenate(with_partners(lower, "dp", plan.nd, group), axis=0)
    early, *late = choose(plan, columns, lower)
    others = [swap(x, "dp", plan.nd, 1) for x in (early, *late)]
    return (early, others[0]), (*late, *others[1:])


def scatter_dp(plan, pieces):
    *more, last = groups_of(plan.nd, 1)
    got = [pieces[0]] + [
        swap(piece, "dp", plan.nd, mask) for piece, mask in zip(pieces[1:], masks_of(last))
    ]
    for bits in reversed(more):
        held = tree_sum([x.astype(F32) for x in got])
        size = 1 << len(bits)
        step = held.shape[-3] // size
        parts = [held[..., i * step : (i + 1) * step, :, :] for i in range(size)]
        got = [parts[0]] + [
            swap(part.astype(BF), "dp", plan.nd, mask)
            for part, mask in zip(parts[1:], masks_of(bits))
        ]
    return [x.reshape(*x.shape[:-3], *x.shape[-2:]) for x in got]


def sum_all(plan, x):
    x = [x, swap(x, "dp", plan.nd, 1)]
    for bits in groups_of(plan.nd, 1):
        x = with_partners(add_rows(x), "dp", plan.nd, bits)
    (bits,) = groups_of(plan.nb)
    return with_partners(add_rows(x), "bucket", plan.nb, bits)


def local(
    plan, tokens, cotangent, segment_ids, keep_mask, bucket_patches, master, first_moment, second_moment
):
    seg_row = segment_ids.reshape(1, SEQ)
    keep_row = keep_mask.reshape(1, SEQ)
    pieces_of = 1 << len(groups_of(plan.nd, 1)[-1])
    (b_bits,) = groups_of(plan.nb)

    hat_in, rstd_in, count = ahead(tokens, keep_row)
    early, late = gather_windows(plan, *prepare(plan, master), count)
    wq, vec, head, kept, q, k, v, hat, rstd = project_part(plan, *early, hat_in)
    o, ot, whole, lse, kab, segk = forward(plan, segment_ids, seg_row, keep_row, q, k, v)
    block_output, dh1, do, near, far, tail, gvec = middle_part(
        plan, late, tokens, cotangent, o, ot, head, kept, vec, keep_row, bucket_patches
    )
    *stacks, normed, token = stack_part(vec, hat_in, q, k, v, do, whole)
    *pieces, token = add_parts([near, swap(far, "dp", plan.nd, 1)], pieces_of, token)
    rest = scatter_dp(plan, pieces)
    low, gains = backward(
        plan, vec, segment_ids, seg_row, lse, q, do, hat, rstd, segk, [kab, *stacks], token
    )
    da1, near, *far = finish_part(plan, hat_in, normed, wq, tail, gvec, low, gains)
    input_grad, given = input_part(hat_in, rstd_in, vec, da1, dh1)
    *late_parts, token = add_parts(rest[:2], 1, gains)
    late_parts += rest[2:]
    *pieces, _ = add_parts([near, [swap(half, "dp", plan.nd, 1) for half in far]], pieces_of, token)
    first = scatter_dp(plan, pieces)
    mine, *sent = blend(plan, late_parts, given, first)
    parts = [mine] + [
        swap(x, "bucket", plan.nb, mask) for x, mask in zip(sent, masks_of(b_bits))
    ]
    new_first, new_second, update_rows, sums = update_part(
        plan, parts, master, first_moment, second_moment
    )
    new_master, norms, trust = apply_part(plan, sum_all(plan, sums), master, update_rows)
    return (
        block_output,
        input_grad,
        new_first,
        new_second,
        new_master,
        norms,
        trust.reshape(MATS),
    )


def solution(mesh):
    shards = mesh.shape["bucket"] * mesh.shape["dp"]
    plan = Plan(mesh.shape, PARAMS // shards)
    both = ("bucket", "dp")
    return jax.shard_map(
        functools.partial(local, plan),
        mesh=mesh,
        in_specs=(P(both, None), P(both, None), P(both), P(both), P(), P(both), P(both), P(both)),
        out_specs=(P(both, None), P(both, None), P(both), P(both), P(both), P(), P()),
        check_vma=False,
    )
```

```python
import functools
import math

import jax
import jax.numpy as jnp
from jax import lax
from jax.experimental import pallas as pl
from jax.experimental.pallas import tpu as pltpu
from jax.sharding import PartitionSpec as P

D = 384
HEADS = 6
HD = 64
FF = 1536
SEQ = 1024
STEP = 10
MATS = 10
LANES = 128
PAIRS = HEADS // 2
TILE = 256
TILES = SEQ // TILE
BLOCKS = SEQ // LANES
MIDDLE_BLOCK = 512
FAR_PARTS = 3

norm_epsilon = 1e-06
adam_epsilon = 1e-06
beta_one = 0.9
beta_two = 0.999
learn_rate = 0.5
weight_decay = 0.01
masked_score = -1e30

MATRIX_END = 4 * D * D + 2 * D * FF
BOUNDS = [0, 3 * D * D, 4 * D * D, 4 * D * D + D * FF, MATRIX_END] + [
    MATRIX_END + (j + 1) * D for j in range(6)
]
PARAMS = BOUNDS[-1]
ROW_OUT = BOUNDS[1] // LANES
ROW_UP = BOUNDS[2] // LANES
ROW_DOWN = BOUNDS[3] // LANES
ROW_VEC = BOUNDS[4] // LANES
VEC_ROWS = 6 * D // LANES
ROWS_ALL = PARAMS // LANES

score_scale = HD ** (-0.5) * math.log2(math.e)
grad_scale = HD ** (-0.5)

BF = jnp.bfloat16
F32 = jnp.float32
VMEM = pl.BlockSpec(memory_space=pltpu.VMEM)
SMEM = pl.BlockSpec(memory_space=pltpu.SMEM)


QUICK = pl.CostEstimate(flops=1000, bytes_accessed=1000, transcendentals=0)


def params(limit):
    return pltpu.CompilerParams(vmem_limit_bytes=limit * 1024 * 1024)


def round_up(value, step):
    return -(-value // step) * step


class Plan:
    def __init__(self, mesh_shape, shard):
        self.nb = mesh_shape["bucket"]
        self.nd = mesh_shape["dp"]
        self.n = self.nb * self.nd
        self.shard = shard
        self.start = [k * shard // LANES for k in range(self.n)]
        self.rows = [
            -(-((k + 1) * shard) // LANES) - self.start[k] for k in range(self.n)
        ]
        self.win = round_up(max(self.rows) + 1, 16)
        self.tail = round_up(self.win + VEC_ROWS, 16 * FAR_PARTS)
        self.upper = self.win * 3 // 4 // 16 * 16
        self.vec_place = ROW_VEC - self.start[-1]
        self.vec_from = self.vec_place // 16 * 16
        self.kept_row = 2 * self.win - self.vec_from
        self.early = self.kept_row + 16

    def device(self):
        return lax.axis_index("bucket") * self.nd + lax.axis_index("dp")


def nn(a, b):
    return lax.dot_general(a, b, (((1,), (0,)), ((), ())), preferred_element_type=F32)


def nt(a, b):
    return lax.dot_general(a, b, (((1,), (1,)), ((), ())), preferred_element_type=F32)


def split_low(x):
    high = x.astype(BF)
    return high, (x - high.astype(F32)).astype(BF)


def rows_at(step):
    if isinstance(step, int):
        return slice(step * TILE, (step + 1) * TILE)
    return pl.ds(pl.multiple_of(step * TILE, TILE), TILE)


def norm_parts(values):
    average = jnp.mean(values, axis=-1, keepdims=True)
    centered = values - average
    variance = jnp.mean(centered * centered, axis=-1, keepdims=True)
    rstd = lax.rsqrt(variance + norm_epsilon)
    return centered * rstd, rstd


def norm_back(hat, rstd, grad):
    mean_grad = jnp.mean(grad, axis=-1, keepdims=True)
    mean_both = jnp.mean(grad * hat, axis=-1, keepdims=True)
    return rstd * (grad - mean_grad - hat * mean_both)


def head_mean_matrix():
    row = lax.broadcasted_iota(jnp.int32, (TILE, TILE), 0)
    col = lax.broadcasted_iota(jnp.int32, (TILE, TILE), 1)
    return jnp.where(row // HD == col // HD, 1.0 / HD, 0.0).astype(BF)


def head_mean_low(low, matrix):
    rest = D - TILE
    return jnp.concatenate(
        [nn(low[:, :TILE], matrix), nn(low[:, TILE:], matrix[:rest, :rest])], axis=1
    )


def head_mean(x, matrix):
    high, rest = split_low(x)
    return head_mean_low(high, matrix) + head_mean_low(rest, matrix)


def flat_to_rows(plan, flat_ref, rows_ref):
    full, rest = divmod(plan.shard, LANES)
    rows_ref[full:, :] = jnp.zeros((plan.win - full, LANES), F32)
    rows_ref[:full, :] = flat_ref[: full * LANES].reshape(full, LANES)
    if rest:
        rows_ref[full : full + 1, :rest] = flat_ref[full * LANES :].reshape(1, rest)
    return rows_ref[...]


def rows_to_flat(plan, rows, flat_ref):
    full, rest = divmod(plan.shard, LANES)
    flat_ref[: full * LANES] = rows[:full].reshape(full * LANES)
    if rest:
        flat_ref[full * LANES :] = rows[full : full + 1, :rest].reshape(rest)


def prepare_kernel(plan, master_ref, upper_ref, lower_ref, rows_ref):
    offset = lax.rem(plan.device() * plan.shard, LANES)
    values = flat_to_rows(plan, master_ref, rows_ref)
    turned = pltpu.roll(values, offset, 1)
    below = pltpu.roll(turned, 1, 0)
    lane = lax.broadcasted_iota(jnp.int32, values.shape, 1)
    window = jnp.where(lane < offset, below, turned).astype(BF)
    upper_ref[...] = window[: plan.upper]
    lower_ref[...] = window[plan.upper :]


def prepare(plan, master):
    return pl.pallas_call(
        functools.partial(prepare_kernel, plan),
        out_shape=(
            jax.ShapeDtypeStruct((plan.upper, LANES), BF),
            jax.ShapeDtypeStruct((plan.win - plan.upper, LANES), BF),
        ),
        in_specs=[VMEM],
        out_specs=(VMEM, VMEM),
        scratch_shapes=[pltpu.VMEM((plan.win, LANES), F32)],
        compiler_params=params(8),
    )(master)


def ahead_kernel(tokens_ref, keep_ref, hat_ref, rstd_ref, count_ref):
    hat, rstd = norm_parts(tokens_ref[...].astype(F32))
    hat_ref[...] = hat
    rstd_ref[...] = jnp.broadcast_to(rstd, rstd_ref.shape)
    row = lax.broadcasted_iota(jnp.int32, count_ref.shape, 0)
    lane = lax.broadcasted_iota(jnp.int32, count_ref.shape, 1)
    count = jnp.sum(keep_ref[...].astype(F32), axis=1, keepdims=True)
    high = jnp.floor(count * (1.0 / 32.0))
    parts = jnp.where(lane == 0, high, jnp.where(lane == 1, count - 32.0 * high, 0.0))
    count_ref[...] = jnp.where(row == 15, parts, 0.0)


def ahead(tokens, keep_row):
    rows = tokens.shape[0]
    return pl.pallas_call(
        ahead_kernel,
        out_shape=(
            jax.ShapeDtypeStruct((rows, D), F32),
            jax.ShapeDtypeStruct((rows, LANES), F32),
            jax.ShapeDtypeStruct((16, LANES), F32),
        ),
        in_specs=[VMEM, VMEM],
        out_specs=(VMEM,) * 3,
        compiler_params=params(12),
        cost_estimate=QUICK,
    )(tokens, keep_row)


def held_window(own_ref, other_ref, rel, at):
    place = jnp.right_shift(rel, 1)
    return jnp.where(
        jnp.bitwise_and(rel, 1) == 0,
        own_ref[place, at].astype(F32),
        other_ref[place, at].astype(F32),
    )


def lay_windows(plan, owners, refs_of, flat, base):
    dp = lax.axis_index("dp")
    for k in owners:
        own_ref, other_ref = refs_of(k)
        window = held_window(own_ref, other_ref, jnp.bitwise_xor(dp, k % plan.nd), slice(0, plan.win))
        first, count = plan.start[k] - base, plan.rows[k]
        shared = k > 0 and (k * plan.shard) % LANES
        if shared:
            before = flat[first : first + 1, :]
        flat[first : first + count, :] = window[:count]
        if shared:
            flat[first : first + 1, :] = before + window[:1]


def take_matrix(target, flat, base, height, width):
    stride = width // LANES
    for j in range(stride):
        target[:, j * LANES : (j + 1) * LANES] = flat[pl.ds(base + j, height, stride=stride), :].astype(BF)


def put_matrix(flat, base, source, height, width):
    stride = width // LANES
    for j in range(stride):
        flat[pl.ds(base + j, height, stride=stride), :] = source[:, j * LANES : (j + 1) * LANES]


def key_chunks(seg_ref, ti):
    first_i, last_i = seg_ref[ti * TILE], seg_ref[ti * TILE + TILE - 1]
    low, high = jnp.int32(0), jnp.int32(0)
    for b in range(BLOCKS):
        low += (seg_ref[b * LANES + LANES - 1] < first_i).astype(jnp.int32)
        high += (seg_ref[b * LANES] <= last_i).astype(jnp.int32)
    count = jnp.right_shift(high - low + 1, 1)
    return jnp.minimum(low, BLOCKS - 2 * count), count


def tile_bias(ti, block, row_seg, key_seg):
    key_place = lax.broadcasted_iota(jnp.int32, (TILE, TILE), 0) + block * LANES
    row_place = lax.broadcasted_iota(jnp.int32, (TILE, TILE), 1) + ti * TILE
    return jnp.where(
        jnp.logical_or(key_seg == row_seg, key_place == row_place), 0.0, masked_score
    )


def keys_at(block):
    return pl.ds(pl.multiple_of(block * LANES, LANES), TILE)


def side_rows(stacked, side):
    return jnp.concatenate(
        [stacked[side * LANES : (side + 1) * LANES], stacked[(2 + side) * LANES : (3 + side) * LANES]],
        axis=0,
    )


def to_column(row):
    return jnp.transpose(jnp.broadcast_to(row, (LANES, row.shape[1])))


def block_heads(pair):
    lane = lax.broadcasted_iota(jnp.int32, pair.shape, 1)
    zero = jnp.zeros_like(pair)
    sides = [jnp.where(lane < HD, pair, zero), jnp.where(lane >= HD, pair, zero)]
    return [side[b * LANES : (b + 1) * LANES] for b in range(2) for side in sides]


def put_blocks(ref, hp, step, pair):
    for i, part in enumerate(block_heads(pair)):
        ref[hp, 2 * step + i // 2, i % 2] = part


def two_blocks(ref, hp, block):
    return ref[hp, pl.ds(block, 2)].reshape(4 * LANES, LANES)


def stack_heads(pair):
    lane = lax.broadcasted_iota(jnp.int32, pair.shape, 1)
    zero = jnp.zeros_like(pair)
    return jnp.concatenate(
        [jnp.where(lane < HD, pair, zero), jnp.where(lane >= HD, pair, zero)], axis=0
    )


def project_kernel(
    plan,
    own_ref,
    other_ref,
    hat_in_ref,
    wq_ref,
    vec_ref,
    head_ref,
    kept_ref,
    q_ref,
    k_ref,
    v_ref,
    hat_ref,
    rstd_ref,
    flat,
):
    dp = lax.axis_index("dp")
    lay_windows(plan, range(plan.nd), lambda k: (own_ref, other_ref), flat, 0)
    take_matrix(wq_ref, flat, 0, D, 3 * D)
    head_ref[...] = flat[ROW_OUT : ROW_OUT + 8, :]
    rel = jnp.bitwise_xor(dp, plan.nd - 1)
    late = held_window(own_ref, other_ref, rel, slice(plan.win, plan.kept_row))
    kept = jnp.zeros((1, LANES), F32)
    for j in range(plan.nd):
        half = other_ref if j & 1 else own_ref
        kept = kept + half[j >> 1, plan.kept_row :].astype(F32)[15:16]
    kept_ref[...] = jnp.broadcast_to(32.0 * kept[:, 0:1] + kept[:, 1:2], kept_ref.shape)
    for t in range(6):
        for j in range(D // LANES):
            at = plan.vec_place - plan.vec_from + 3 * t + j
            vec_ref[t : t + 1, j * LANES : (j + 1) * LANES] = late[at : at + 1]
    matrix = head_mean_matrix()
    gain1, shift1 = vec_ref[0:1, :], vec_ref[1:2, :]
    gain_q, gain_k = vec_ref[2:3, :], vec_ref[3:4, :]

    raw = nn((hat_in_ref[...] * gain1 + shift1).astype(BF), wq_ref[...])

    def head_norm(low_out, part, gain):
        lanes = slice(part * D, (part + 1) * D)
        x = raw[:, lanes]
        centered = x - head_mean(x, matrix)
        rstd = lax.rsqrt(head_mean(centered * centered, matrix) + norm_epsilon)
        normed = centered * rstd
        hat_ref[:, lanes] = normed
        rstd_ref[:, lanes] = rstd
        low_out[...] = (normed * gain).astype(BF)

    head_norm(q_ref, 0, gain_q)
    head_norm(k_ref, 1, gain_k)
    v_ref[...] = raw[:, 2 * D :].astype(BF)


def project_part(plan, own, other, tokens):
    rows = tokens.shape[0]
    low = jax.ShapeDtypeStruct((rows, D), BF)
    return pl.pallas_call(
        functools.partial(project_kernel, plan),
        out_shape=(
            jax.ShapeDtypeStruct((D, 3 * D), BF),
            jax.ShapeDtypeStruct((8, D), F32),
            jax.ShapeDtypeStruct((8, LANES), F32),
            jax.ShapeDtypeStruct((8, LANES), F32),
            low,
            low,
            low,
            jax.ShapeDtypeStruct((rows, 2 * D), F32),
            jax.ShapeDtypeStruct((rows, 2 * D), F32),
        ),
        in_specs=[VMEM] * 3,
        out_specs=(VMEM,) * 9,
        scratch_shapes=[
            pltpu.VMEM((round_up(plan.start[plan.nd - 1] + plan.win, 8), LANES), F32),
        ],
        compiler_params=params(24),
        cost_estimate=QUICK,
    )(own, other, tokens)


def forward_kernel(
    plan,
    seg_smem,
    seg_ref,
    keep_ref,
    q_ref,
    k_ref,
    v_ref,
    o_ref,
    ot_ref,
    whole_ref,
    lse_ref,
    kab,
    segk,
    vt,
    ot,
    rest_t,
    sums,
    expo,
):
    seg_row = seg_ref[...].astype(F32)
    segk[...] = to_column(jnp.where(keep_ref[...] == 1, seg_row, -1.0))

    for step in range(TILES):
        at = rows_at(step)
        for hp in range(PAIRS):
            put_blocks(kab, hp, step, k_ref[at, hp * LANES : (hp + 1) * LANES])
        vt[:, at] = jnp.transpose(v_ref[at, :].astype(F32)).astype(BF)

    def query_tile(ti, carry):
        ot[...] = jnp.zeros_like(ot)
        rest_t[...] = jnp.zeros_like(rest_t)
        sums[...] = jnp.zeros_like(sums)
        row_seg = seg_ref[:, rows_at(ti)].astype(F32)
        first, count = key_chunks(seg_smem, ti)

        def score_chunk(c, inner):
            block = first + 2 * c
            column = segk[keys_at(block), :]
            bias = tile_bias(ti, block, row_seg, jnp.concatenate([column, column], axis=1))
            for hp in range(PAIRS):
                queries = q_ref[rows_at(ti), hp * LANES : (hp + 1) * LANES]
                scores = nt(two_blocks(kab, hp, block), queries)
                for side in range(2):
                    head = 2 * hp + side
                    value = jnp.exp2(side_rows(scores, side) * score_scale + bias)
                    expo[c, head] = value
                    sums[head : head + 1, :] += jnp.sum(value, axis=0, keepdims=True)
            return inner

        lax.fori_loop(0, count, score_chunk, 0)
        lse_ref[ti] = jnp.log2(sums[...])
        sums[...] = 1.0 / sums[...]

        def value_chunk(c, inner):
            keys = keys_at(first + 2 * c)
            for head in range(HEADS):
                prob, rest = split_low(expo[c, head] * sums[head : head + 1, :])
                at = slice(head * HD, (head + 1) * HD)
                ot[at, :] += nn(vt[at, keys], prob)
                rest_t[at, :] += nn(vt[at, keys], rest)
            return inner

        lax.fori_loop(0, count, value_chunk, 0)
        attended = ot[...]
        ot_ref[ti] = attended.astype(BF)
        whole_ref[ti] = attended + rest_t[...]
        o_ref[rows_at(ti), :] = jnp.transpose(attended).astype(BF)
        return carry

    lax.fori_loop(0, TILES, query_tile, 0)


def forward(plan, seg, seg_row, keep_row, q, k, v):
    rows = q.shape[0]
    return pl.pallas_call(
        functools.partial(forward_kernel, plan),
        out_shape=(
            jax.ShapeDtypeStruct((rows, D), BF),
            jax.ShapeDtypeStruct((TILES, D, TILE), BF),
            jax.ShapeDtypeStruct((TILES, D, TILE), F32),
            jax.ShapeDtypeStruct((TILES, 8, TILE), F32),
            jax.ShapeDtypeStruct((PAIRS, BLOCKS, 2, LANES, LANES), BF),
            jax.ShapeDtypeStruct((SEQ, LANES), F32),
        ),
        in_specs=[SMEM] + [VMEM] * 5,
        out_specs=(VMEM,) * 6,
        scratch_shapes=[
            pltpu.VMEM((D, SEQ), BF),
            pltpu.VMEM((D, TILE), F32),
            pltpu.VMEM((D, TILE), F32),
            pltpu.VMEM((8, TILE), F32),
            pltpu.VMEM((TILES, HEADS, TILE, TILE), F32),
        ],
        compiler_params=params(24),
        cost_estimate=QUICK,
    )(seg, seg_row, keep_row, q, k, v)


erfc_step = 0.3275911 * math.sqrt(0.5)
erfc_terms = [0.254829592, -0.284496736, 1.421413741, -1.453152027, 1.061405429]


def normal_parts(u):
    expo = jnp.exp2(u * u * (-0.5 * math.log2(math.e)))
    t = 1.0 / (1.0 + erfc_step * jnp.abs(u))
    poly = 0.5 * erfc_terms[4]
    for term in reversed(erfc_terms[:4]):
        poly = poly * t + 0.5 * term
    below = poly * t * expo
    return jnp.where(u > 0.0, 1.0 - below, below), expo * (1.0 / math.sqrt(2.0 * math.pi))


def middle_kernel(plan, *refs):
    late_refs, rest = refs[: 2 * plan.nb - 2], refs[2 * plan.nb - 2 :]
    middle_body(plan, late_refs, *rest)


def middle_body(
    plan,
    late_refs,
    tokens_ref,
    cot_ref,
    o_ref,
    ot_ref,
    head_ref,
    kept_ref,
    vec_ref,
    keep_ref,
    patches_ref,
    out_ref,
    dh1_ref,
    do_ref,
    near_ref,
    far_ref,
    tail_ref,
    gvec_ref,
    keepc,
    hid,
    dus,
    flat,
    wo_ref,
    wu_ref,
    wd_ref,
):
    bucket = lax.axis_index("bucket")
    base = ROW_OUT
    flat[0:8, :] = head_ref[...]
    dp = lax.axis_index("dp")
    owns, others = late_refs[: plan.nb - 1], late_refs[plan.nb - 1 :]
    lay_windows(
        plan,
        range(plan.nd, plan.n),
        lambda k: (owns[k // plan.nd - 1], others[k // plan.nd - 1]),
        flat,
        base,
    )
    take_matrix(wo_ref, flat, 0, D, D)
    take_matrix(wu_ref, flat, ROW_UP - base, D, FF)
    take_matrix(wd_ref, flat, ROW_DOWN - base, FF, D)
    gain2, shift2 = vec_ref[4:5, :], vec_ref[5:6, :]
    own = patches_ref[bucket].astype(F32)
    total = patches_ref[0].astype(F32)
    for b in range(1, plan.nb):
        total = total + patches_ref[b].astype(F32)
    ones = jnp.ones((1, LANES), F32)
    scale = (plan.nb * own) * ones / (total * ones) * float(SEQ * plan.nd) / kept_ref[0:1, :]
    keepc[...] = to_column(keep_ref[...].astype(F32)) * scale
    gvec_ref[...] = jnp.zeros_like(gvec_ref)

    middle = tokens_ref[...].astype(F32) + nn(o_ref[...], wo_ref[...])
    hat, rstd = norm_parts(middle)
    low = (hat * gain2 + shift2).astype(BF)
    weights = keepc[...]
    seed = cot_ref[...].astype(F32) * jnp.concatenate([weights] * (D // LANES), axis=1)
    seed_low = seed.astype(BF)
    for first in range(0, FF, MIDDLE_BLOCK):
        cols = slice(first, first + MIDDLE_BLOCK)
        u = nn(low, wu_ref[:, cols])
        phi, bell = normal_parts(u)
        hid[:, cols] = (u * phi).astype(BF)
        dus[:, cols] = (nt(seed_low, wd_ref[cols, :]) * (phi + u * bell)).astype(BF)
    out_ref[...] = (middle + nn(hid[...], wd_ref[...])).astype(BF)
    seedt = jnp.transpose(seed).astype(BF)
    lowt = jnp.transpose(low.astype(F32)).astype(BF)
    da2 = nt(dus[...], wu_ref[...])
    gvec_ref[0:1, :] = jnp.sum(da2 * hat, axis=0, keepdims=True)
    gvec_ref[1:2, :] = jnp.sum(da2, axis=0, keepdims=True)
    dh1 = seed + norm_back(hat, rstd, da2 * gain2)
    dh1_ref[...] = dh1
    dh1_low = dh1.astype(BF)
    gout = nn(jnp.concatenate([ot_ref[t] for t in range(TILES)], axis=1), dh1_low)
    do_ref[...] = nt(dh1_low, wo_ref[...]).astype(BF)
    put_matrix(flat, 0, gout, D, D)
    block = 2 * TILE
    for i in range(FF // block):
        part = nn(lowt, dus[:, i * block : (i + 1) * block])
        for j in range(block // LANES):
            flat[pl.ds(ROW_UP - base + i * (block // LANES) + j, D, stride=FF // LANES), :] = part[
                :, j * LANES : (j + 1) * LANES
            ]
        part = jnp.transpose(nn(seedt, hid[:, i * block : (i + 1) * block]))
        for j in range(D // LANES):
            flat[
                pl.ds(ROW_DOWN - base + i * block * (D // LANES) + j, block, stride=D // LANES), :
            ] = part[:, j * LANES : (j + 1) * LANES]
    tail_ref[...] = flat[0:8, :]
    side = jnp.bitwise_and(dp, 1)
    for k in range(plan.nd, plan.n):
        first = plan.start[k] - base
        quarter = k // plan.nd - 1
        reld = jnp.right_shift(jnp.bitwise_xor(dp, k % plan.nd), 1)
        window = flat[first : first + plan.win, :].astype(BF)

        @pl.when(side == k % 2)
        def _():
            near_ref[quarter, reld] = window

        @pl.when(side != k % 2)
        def _():
            far_ref[quarter, reld] = window


def middle_part(plan, late, tokens, cot, o, ot, head, kept, vec, keep_row, patches):
    rows = tokens.shape[0]
    windows = jax.ShapeDtypeStruct((plan.nb - 1, plan.nd // 2, plan.win, LANES), BF)
    return pl.pallas_call(
        functools.partial(middle_kernel, plan),
        out_shape=(
            jax.ShapeDtypeStruct((rows, D), BF),
            jax.ShapeDtypeStruct((rows, D), F32),
            jax.ShapeDtypeStruct((rows, D), BF),
            windows,
            windows,
            jax.ShapeDtypeStruct((8, LANES), F32),
            jax.ShapeDtypeStruct((8, D), F32),
        ),
        in_specs=[VMEM] * (len(late) + 8) + [SMEM],
        out_specs=(VMEM,) * 7,
        scratch_shapes=[
            pltpu.VMEM((rows, LANES), F32),
            pltpu.VMEM((rows, FF), BF),
            pltpu.VMEM((rows, FF), BF),
            pltpu.VMEM((round_up(plan.start[-1] + plan.win - ROW_OUT, 8), LANES), F32),
            pltpu.VMEM((D, D), BF),
            pltpu.VMEM((D, FF), BF),
            pltpu.VMEM((FF, D), BF),
        ],
        compiler_params=params(36),
        cost_estimate=QUICK,
    )(*late, tokens, cot, o, ot, head, kept, vec, keep_row, patches)


def stack_kernel(
    vec_ref,
    hat_in_ref,
    q_ref,
    k_ref,
    v_ref,
    do_ref,
    whole_ref,
    vab,
    qab,
    dab,
    kt,
    inner_sums,
    normed_ref,
    token_ref,
):
    for step in range(TILES):
        at = rows_at(step)
        grads = do_ref[at, :]
        for hp in range(PAIRS):
            lanes = slice(hp * LANES, (hp + 1) * LANES)
            put_blocks(vab, hp, step, v_ref[at, lanes])
            qab[hp, step] = stack_heads(q_ref[at, lanes])
            dab[hp, step] = stack_heads(grads[:, lanes])
        kt[:, at] = jnp.transpose(k_ref[at, :].astype(F32)).astype(BF)
        both = jnp.transpose(grads.astype(F32)) * whole_ref[step]
        for head in range(HEADS):
            inner_sums[step, head : head + 1, :] = jnp.sum(
                both[head * HD : (head + 1) * HD], axis=0, keepdims=True
            )
        normed = hat_in_ref[at, :] * vec_ref[0:1, :] + vec_ref[1:2, :]
        normed_ref[:, at] = jnp.transpose(normed).astype(BF)
    token_ref[...] = jnp.zeros_like(token_ref)


def stack_part(vec, hat_in, q, k, v, do, whole):
    stacked = jax.ShapeDtypeStruct((PAIRS, TILES, 2 * TILE, LANES), BF)
    return pl.pallas_call(
        stack_kernel,
        out_shape=(
            jax.ShapeDtypeStruct((PAIRS, BLOCKS, 2, LANES, LANES), BF),
            stacked,
            stacked,
            jax.ShapeDtypeStruct((D, SEQ), BF),
            jax.ShapeDtypeStruct((TILES, 8, TILE), F32),
            jax.ShapeDtypeStruct((D, SEQ), BF),
            jax.ShapeDtypeStruct((8, LANES), F32),
        ),
        in_specs=[VMEM] * 7,
        out_specs=(VMEM,) * 7,
        compiler_params=params(16),
        cost_estimate=QUICK,
    )(vec, hat_in, q, k, v, do, whole)


def backward_kernel(
    plan,
    vec_ref,
    seg_smem,
    seg_ref,
    lse_ref,
    q_ref,
    do_ref,
    hat_ref,
    rstd_ref,
    segk,
    kab,
    vab,
    qab,
    dab,
    kt,
    inner_sums,
    token_ref,
    low_ref,
    gains_ref,
    dqt,
    dk,
    dv,
):
    matrix = head_mean_matrix()
    dqt[...] = jnp.zeros_like(dqt)
    dk[...] = jnp.zeros_like(dk)
    dv[...] = jnp.zeros_like(dv)
    gains_ref[...] = jnp.zeros_like(gains_ref)

    def query_tile(ti, carry):
        row_seg = seg_ref[:, rows_at(ti)].astype(F32)
        first, count = key_chunks(seg_smem, ti)

        def key_chunk(c, inner):
            block = first + 2 * c
            keys = keys_at(block)
            column = segk[keys, :]
            bias = tile_bias(ti, block, row_seg, jnp.concatenate([column, column], axis=1))
            raw = []
            for hp in range(PAIRS):
                lanes = slice(hp * LANES, (hp + 1) * LANES)
                raw.append(
                    (
                        nt(two_blocks(kab, hp, block), q_ref[rows_at(ti), lanes]),
                        nt(two_blocks(vab, hp, block), do_ref[rows_at(ti), lanes]),
                    )
                )
            probs, dscores = [], []
            for head in range(HEADS):
                scores, grads = raw[head // 2]
                prob = jnp.exp2(
                    side_rows(scores, head % 2) * score_scale
                    + (bias - lse_ref[ti, head : head + 1, :])
                )
                dscore = prob * (side_rows(grads, head % 2) - inner_sums[ti, head : head + 1, :])
                probs.append(prob.astype(BF))
                dscores.append(dscore.astype(BF))
            for hp in range(PAIRS):
                pair = slice(2 * hp, 2 * hp + 2)
                for head in (2 * hp, 2 * hp + 1):
                    at = slice(head * HD, (head + 1) * HD)
                    dqt[ti, at, :] += nn(kt[at, keys], dscores[head])
                dv[hp, keys] += nn(jnp.concatenate(probs[pair], axis=1), dab[hp, ti])
                dk[hp, keys] += nn(jnp.concatenate(dscores[pair], axis=1), qab[hp, ti])
            return inner

        lax.fori_loop(0, count, key_chunk, 0)
        return carry

    lax.fori_loop(0, TILES, query_tile, 0)

    def finish(step, carry):
        at = rows_at(step)

        def head_norm_back(part, gain, grad):
            lanes = slice(part * D, (part + 1) * D)
            hat = hat_ref[at, lanes]
            both = grad * hat
            gains_ref[part : part + 1, :] += jnp.sum(both, axis=0, keepdims=True)
            scaled = grad * gain
            mean_grad = head_mean_low(scaled.astype(BF), matrix)
            mean_both = head_mean_low((both * gain).astype(BF), matrix)
            back = rstd_ref[at, lanes] * (scaled - mean_grad - hat * mean_both)
            low_ref[at, lanes] = back.astype(BF)

        grad_k = jnp.concatenate([dk[hp, at] for hp in range(PAIRS)], axis=1) * grad_scale
        grad_v = jnp.concatenate([dv[hp, at] for hp in range(PAIRS)], axis=1)
        head_norm_back(0, vec_ref[2:3, :], jnp.transpose(dqt[step]) * grad_scale)
        head_norm_back(1, vec_ref[3:4, :], grad_k)
        low_ref[at, 2 * D :] = grad_v.astype(BF)
        return carry

    lax.fori_loop(0, TILES, finish, 0)


def backward(plan, vec, seg, seg_row, lse, q, do, hat, rstd, segk, stacks, token):
    rows = q.shape[0]
    return pl.pallas_call(
        functools.partial(backward_kernel, plan),
        out_shape=(
            jax.ShapeDtypeStruct((rows, 3 * D), BF),
            jax.ShapeDtypeStruct((8, D), F32),
        ),
        in_specs=[VMEM, SMEM] + [VMEM] * 14,
        out_specs=(VMEM, VMEM),
        scratch_shapes=[
            pltpu.VMEM((TILES, D, TILE), F32),
            pltpu.VMEM((PAIRS, SEQ, LANES), F32),
            pltpu.VMEM((PAIRS, SEQ, LANES), F32),
        ],
        compiler_params=params(26),
        cost_estimate=QUICK,
    )(vec, seg, seg_row, lse, q, do, hat, rstd, segk, *stacks, token)


def finish_kernel(
    plan,
    hat_ref,
    normed_ref,
    wq_ref,
    tail_ref,
    gvec_ref,
    low_ref,
    gqk_ref,
    da1_ref,
    near_ref,
    *refs,
):
    *far_refs, gains, flat = refs
    hat = hat_ref[...]
    for i in range(3):
        part = nn(normed_ref[...], low_ref[:, i * D : (i + 1) * D])
        for j in range(D // LANES):
            flat[pl.ds(i * (D // LANES) + j, D, stride=3 * D // LANES), :] = part[
                :, j * LANES : (j + 1) * LANES
            ]
    da1 = nt(low_ref[...], wq_ref[...])
    da1_ref[...] = da1
    gains[...] = jnp.zeros_like(gains)
    gains[0:1, :] = jnp.sum(da1 * hat, axis=0, keepdims=True)
    gains[1:2, :] = jnp.sum(da1, axis=0, keepdims=True)
    gains[2:4, :] = gqk_ref[0:2, :]
    gains[4:6, :] = gvec_ref[0:2, :]
    flat[ROW_OUT : ROW_OUT + 8, :] = tail_ref[...]
    dp = lax.axis_index("dp")
    side = jnp.bitwise_and(dp, 1)
    rest = jnp.zeros((plan.tail - plan.win, LANES), BF)
    vector_rows = []
    for t in range(6):
        for j in range(D // LANES):
            vector_rows.append(gains[t : t + 1, j * LANES : (j + 1) * LANES])
    vector_rows.append(jnp.zeros((plan.tail - plan.win - VEC_ROWS, LANES), F32))
    vectors = jnp.concatenate(vector_rows, axis=0).astype(BF)
    for k in range(plan.nd):
        first = plan.start[k]
        reld = jnp.right_shift(jnp.bitwise_xor(dp, k), 1)
        window = flat[first : first + plan.win, :].astype(BF)
        window = jnp.concatenate([window, vectors if k == plan.nd - 1 else rest], axis=0)

        @pl.when(side == k % 2)
        def _():
            near_ref[reld] = window

        @pl.when(side != k % 2)
        def _():
            height = plan.tail // FAR_PARTS
            for i, far_ref in enumerate(far_refs):
                far_ref[reld] = window[i * height : (i + 1) * height]


def finish_part(plan, hat, normed, wq, tail, gvec, low, gains):
    rows = hat.shape[0]
    windows = jax.ShapeDtypeStruct((plan.nd // 2, plan.tail, LANES), BF)
    part = jax.ShapeDtypeStruct((plan.nd // 2, plan.tail // FAR_PARTS, LANES), BF)
    return pl.pallas_call(
        functools.partial(finish_kernel, plan),
        out_shape=(jax.ShapeDtypeStruct((rows, D), F32), windows) + (part,) * FAR_PARTS,
        in_specs=[VMEM] * 7,
        out_specs=(VMEM,) * (2 + FAR_PARTS),
        scratch_shapes=[
            pltpu.VMEM((8, D), F32),
            pltpu.VMEM((round_up(plan.start[plan.nd - 1] + plan.win, 8), LANES), F32),
        ],
        compiler_params=params(28),
        cost_estimate=QUICK,
    )(hat, normed, wq, tail, gvec, low, gains)


def input_kernel(hat_ref, rstd_ref, vec_ref, da1_ref, dh1_ref, grad_ref, token_ref):
    back = norm_back(hat_ref[...], rstd_ref[:, 0:1], da1_ref[...] * vec_ref[0:1, :])
    grad_ref[...] = dh1_ref[...] + back
    token_ref[...] = jnp.zeros_like(token_ref)


def input_part(hat, rstd, vec, da1, dh1):
    return pl.pallas_call(
        input_kernel,
        out_shape=(
            jax.ShapeDtypeStruct(dh1.shape, F32),
            jax.ShapeDtypeStruct((8, LANES), F32),
        ),
        in_specs=[VMEM] * 5,
        out_specs=(VMEM, VMEM),
        compiler_params=params(16),
        cost_estimate=QUICK,
    )(hat, rstd, vec, da1, dh1)


def flat_place(plan, shape):
    row = lax.broadcasted_iota(jnp.int32, shape, 0)
    lane = lax.broadcasted_iota(jnp.int32, shape, 1)
    place = row * LANES + lane
    return place, plan.device() * plan.shard + place


def update_kernel(
    plan,
    own_ref,
    got0_ref,
    got1_ref,
    got2_ref,
    master_ref,
    moment_ref,
    second_ref,
    new_moment_ref,
    new_second_ref,
    update_ref,
    sums_ref,
    window,
    master_rows,
    moment_rows,
    second_rows,
):
    bucket = lax.axis_index("bucket")
    dp = lax.axis_index("dp")
    total = tree_sum([ref[...].astype(F32) for ref in (own_ref, got0_ref, got1_ref, got2_ref)])
    window[...] = total[: plan.win]

    @pl.when(jnp.logical_and(bucket == plan.nb - 1, dp == plan.nd - 1))
    def _():
        window[plan.vec_place : plan.vec_place + VEC_ROWS, :] = total[
            plan.win : plan.win + VEC_ROWS
        ]

    offset = lax.rem(plan.device() * plan.shard, LANES)
    back = lax.rem(LANES - offset, LANES)
    turned = pltpu.roll(window[...], back, 1)
    above = pltpu.roll(turned, plan.win - 1, 0)
    lane = lax.broadcasted_iota(jnp.int32, turned.shape, 1)
    place, index = flat_place(plan, turned.shape)
    inside = place < plan.shard
    grad = jnp.where(inside, jnp.where(lane + offset < LANES, turned, above), 0.0)
    master = flat_to_rows(plan, master_ref, master_rows)
    old_moment = flat_to_rows(plan, moment_ref, moment_rows)
    old_second = flat_to_rows(plan, second_ref, second_rows)
    moment = beta_one * old_moment + (1.0 - beta_one) * grad
    second = beta_two * old_second + (1.0 - beta_two) * grad * grad
    first_hat = moment / (1.0 - beta_one**STEP)
    second_hat = second / (1.0 - beta_two**STEP)
    decay = jnp.where(index < BOUNDS[4], weight_decay, 0.0)
    update = first_hat / (jnp.sqrt(second_hat) + adam_epsilon) + decay * master
    update = jnp.where(inside, update, 0.0)
    rows_to_flat(plan, moment, new_moment_ref)
    rows_to_flat(plan, second, new_second_ref)
    update_ref[...] = update
    master_sq = jnp.where(inside, master * master, 0.0)
    update_sq = update * update
    lanes = lax.broadcasted_iota(jnp.int32, (1, LANES), 1)
    rows = []
    for squares in (master_sq, update_sq):
        row = jnp.zeros((1, LANES), F32)
        for t in range(MATS):
            mine = jnp.logical_and(index >= BOUNDS[t], index < BOUNDS[t + 1])
            part = jnp.sum(jnp.where(mine, squares, 0.0), axis=0, keepdims=True)
            row = jnp.where(lanes == t, jnp.sum(part, axis=1, keepdims=True), row)
        rows.append(row)
    rows.append(jnp.zeros((6, LANES), F32))
    sums_ref[...] = jnp.concatenate(rows, axis=0)


def update_part(plan, parts, master, moment, second):
    flat = jax.ShapeDtypeStruct((plan.shard,), F32)
    rows = jax.ShapeDtypeStruct((plan.win, LANES), F32)
    return pl.pallas_call(
        functools.partial(update_kernel, plan),
        out_shape=(flat, flat, rows, jax.ShapeDtypeStruct((8, LANES), F32)),
        in_specs=[VMEM] * 7,
        out_specs=(VMEM,) * 4,
        scratch_shapes=[pltpu.VMEM((plan.win, LANES), F32)] * 4,
        compiler_params=params(12),
    )(*parts, master, moment, second)


def apply_kernel(plan, *refs):
    *sums_refs, master_ref, update_ref, new_ref, norms_ref, trust_ref, rows_ref = refs
    roots = jnp.sqrt(tree_sum([ref[...] for ref in sums_refs]))
    trust = roots[0:1, :] / (roots[1:2, :] + adam_epsilon)
    norms_ref[...] = roots[0:2, :MATS]
    trust_ref[...] = trust[:, :MATS]
    master = flat_to_rows(plan, master_ref, rows_ref)
    _, index = flat_place(plan, master.shape)
    factors = jnp.broadcast_to(trust[:, 0:1], master.shape)
    for t in range(1, MATS):
        factors = jnp.where(index >= BOUNDS[t], trust[:, t : t + 1], factors)
    rows_to_flat(plan, master - learn_rate * factors * update_ref[...], new_ref)


def apply_part(plan, sums, master, update_rows):
    return pl.pallas_call(
        functools.partial(apply_kernel, plan),
        out_shape=(
            jax.ShapeDtypeStruct((plan.shard,), F32),
            jax.ShapeDtypeStruct((2, MATS), F32),
            jax.ShapeDtypeStruct((1, MATS), F32),
        ),
        in_specs=[VMEM] * (len(sums) + 2),
        out_specs=(VMEM,) * 3,
        scratch_shapes=[pltpu.VMEM((plan.win, LANES), F32)],
        compiler_params=params(8),
    )(*sums, master, update_rows)


def lay_column_kernel(count, *refs):
    for i, part in enumerate(refs[:count]):
        refs[-1][i] = part[...]


def lay_column(parts, *after):
    return pl.pallas_call(
        functools.partial(lay_column_kernel, len(parts)),
        out_shape=jax.ShapeDtypeStruct((len(parts), *parts[0].shape), parts[0].dtype),
        in_specs=[VMEM] * (len(parts) + len(after)),
        out_specs=VMEM,
        compiler_params=params(4),
    )(*parts, *after)


def lay_lower_kernel(plan, mine_ref, got_ref, count_ref, out_ref):
    half = mine_ref.shape[0]
    out_ref[:half] = mine_ref[...]
    out_ref[half:] = got_ref[...]
    last = mine_ref[0, -16:, :].astype(F32)
    out_ref[0, plan.win - plan.upper - 16 :, :] = (last + count_ref[...]).astype(BF)


def lay_lower(plan, mine, got, count):
    half, height, _ = mine.shape
    return pl.pallas_call(
        functools.partial(lay_lower_kernel, plan),
        out_shape=jax.ShapeDtypeStruct((2 * half, height, LANES), BF),
        in_specs=[VMEM] * 3,
        out_specs=VMEM,
        compiler_params=params(4),
    )(mine, got, count)


def choose_kernel(plan, *refs):
    columns, (lower_ref, early_ref), late_refs = (
        refs[: plan.nb],
        refs[plan.nb : plan.nb + 2],
        refs[plan.nb + 2 :],
    )
    bucket = lax.axis_index("bucket")
    early_ref[:, plan.kept_row :] = lower_ref[:, 0, plan.win - plan.upper - 16 :]
    for i, part in enumerate(columns):
        for owner, out_ref in enumerate((early_ref, *late_refs)):

            @pl.when(jnp.bitwise_xor(bucket, i) == owner)
            def _():
                out_ref[:, : plan.upper] = part[...]
                out_ref[:, plan.upper : plan.win] = lower_ref[:, i]

    early_ref[:, plan.win : plan.kept_row] = late_refs[-1][:, plan.vec_from :]


def choose(plan, columns, lower):
    step = columns[0].shape[0]
    late = jax.ShapeDtypeStruct((step, plan.win, LANES), BF)
    return pl.pallas_call(
        functools.partial(choose_kernel, plan),
        out_shape=(jax.ShapeDtypeStruct((step, plan.early, LANES), BF),) + (late,) * (plan.nb - 1),
        in_specs=[VMEM] * (len(columns) + 1),
        out_specs=(VMEM,) * plan.nb,
        compiler_params=params(10),
    )(*columns, lower)


def add_parts_kernel(halves, *refs):
    refs = list(refs)
    parts = [[refs.pop(0) for _ in range(count)] for count in halves]
    for i, out in enumerate(refs[1:-1]):
        step = out.shape[-3]
        at = slice(i * step, (i + 1) * step)
        at = (slice(None), at) if len(out.shape) == 4 else at
        values = [
            jnp.concatenate([half[at].astype(F32) for half in part], axis=-2) for part in parts
        ]
        out[...] = tree_sum(values).astype(out.dtype)
    refs[-1][...] = jnp.zeros_like(refs[-1])


def add_parts(parts, pieces, token):
    *lead, total, height, width = parts[0].shape
    parts = [part if isinstance(part, list) else [part] for part in parts]
    halves = [len(part) for part in parts]
    parts = [half for part in parts for half in part]
    return pl.pallas_call(
        functools.partial(add_parts_kernel, halves),
        out_shape=tuple(
            jax.ShapeDtypeStruct((*lead, total // pieces, height, width), BF if i else F32)
            for i in range(pieces)
        )
        + (jax.ShapeDtypeStruct((8, LANES), F32),),
        in_specs=[VMEM] * (len(parts) + 1),
        out_specs=(VMEM,) * (pieces + 1),
        compiler_params=params(14),
    )(*parts, token)


def blend_kernel(plan, late_count, *refs):
    late, parts, outs = refs[:late_count], refs[late_count + 1 : -plan.nb], refs[-plan.nb :]
    bucket = lax.axis_index("bucket")
    first = tree_sum([part[...].astype(F32) for part in parts])
    for i, out in enumerate(outs):
        owner = jnp.bitwise_xor(bucket, i)
        quarter = jnp.maximum(owner - 1, 0)
        window = late[0][quarter]
        if late_count > 1:
            window = window + tree_sum([ref[quarter].astype(F32) for ref in late[1:]])
        out[: plan.win] = jnp.where(owner == 0, first[: plan.win], window).astype(out.dtype)
        out[plan.win :] = first[plan.win :].astype(out.dtype)


def blend(plan, late, token, parts):
    return pl.pallas_call(
        functools.partial(blend_kernel, plan, len(late)),
        out_shape=tuple(
            jax.ShapeDtypeStruct((plan.tail, LANES), BF if i else F32) for i in range(plan.nb)
        ),
        in_specs=[VMEM] * (len(late) + 1 + len(parts)),
        out_specs=(VMEM,) * plan.nb,
        compiler_params=params(10),
    )(*late, token, *parts)


def add_rows_kernel(*refs):
    refs[-1][...] = tree_sum([ref[...] for ref in refs[:-1]])


def add_rows(parts):
    return pl.pallas_call(
        add_rows_kernel,
        out_shape=jax.ShapeDtypeStruct(parts[0].shape, F32),
        in_specs=[VMEM] * len(parts),
        out_specs=VMEM,
        compiler_params=params(4),
    )(*parts)


def groups_of(size, skip=0):
    bits = list(range(skip, size.bit_length() - 1))
    return [bits[i : i + 2] for i in range(0, len(bits), 2)]


def masks_of(bits):
    masks = [1 << bits[0]]
    if len(bits) == 2:
        masks += [1 << bits[1], (1 << bits[0]) | (1 << bits[1])]
    return masks


def swap(x, axis, size, mask):
    return lax.ppermute(x, axis, [(i, i ^ mask) for i in range(size)])


def tree_sum(parts):
    if len(parts) == 1:
        return parts[0]
    half = len(parts) // 2
    return tree_sum(parts[:half]) + tree_sum(parts[half:])


def with_partners(x, axis, size, bits):
    return [x] + [swap(x, axis, size, mask) for mask in masks_of(bits)]


def gather_windows(plan, upper, lower, count):
    first, *more = groups_of(plan.nd, 1)
    (bits,) = groups_of(plan.nb)
    near, distant = masks_of(bits)[:2]
    lower = lay_column([lower, swap(lower, "bucket", plan.nb, near)])
    lower = lay_lower(plan, lower, swap(lower, "bucket", plan.nb, distant), count)
    column = lay_column(with_partners(upper, "dp", plan.nd, first), lower)
    for group in more:
        column = jnp.concatenate(with_partners(column, "dp", plan.nd, group), axis=0)
    columns = with_partners(column, "bucket", plan.nb, bits)
    lower = lay_column(with_partners(lower, "dp", plan.nd, first))
    for group in more:
        lower = jnp.concatenate(with_partners(lower, "dp", plan.nd, group), axis=0)
    early, *late = choose(plan, columns, lower)
    others = [swap(x, "dp", plan.nd, 1) for x in (early, *late)]
    return (early, others[0]), (*late, *others[1:])


def scatter_dp(plan, pieces):
    *more, last = groups_of(plan.nd, 1)
    sent = list(zip(pieces[1:], masks_of(last)))
    got = [pieces[0]] + [
        swap(piece, "dp", plan.nd, mask) for piece, mask in sent[1:] + sent[:1]
    ]
    for bits in reversed(more):
        held = tree_sum([x.astype(F32) for x in got])
        size = 1 << len(bits)
        step = held.shape[-3] // size
        parts = [held[..., i * step : (i + 1) * step, :, :] for i in range(size)]
        got = [parts[0]] + [
            swap(part.astype(BF), "dp", plan.nd, mask)
            for part, mask in zip(parts[1:], masks_of(bits))
        ]
    return [x.reshape(*x.shape[:-3], *x.shape[-2:]) for x in got]


def sum_all(plan, x):
    x = [x, swap(x, "dp", plan.nd, 1)]
    for bits in groups_of(plan.nd, 1):
        x = with_partners(add_rows(x), "dp", plan.nd, bits)
    (bits,) = groups_of(plan.nb)
    return with_partners(add_rows(x), "bucket", plan.nb, bits)


def local(
    plan, tokens, cotangent, segment_ids, keep_mask, bucket_patches, master, first_moment, second_moment
):
    seg_row = segment_ids.reshape(1, SEQ)
    keep_row = keep_mask.reshape(1, SEQ)
    pieces_of = 1 << len(groups_of(plan.nd, 1)[-1])
    (b_bits,) = groups_of(plan.nb)

    hat_in, rstd_in, count = ahead(tokens, keep_row)
    early, late = gather_windows(plan, *prepare(plan, master), count)
    wq, vec, head, kept, q, k, v, hat, rstd = project_part(plan, *early, hat_in)
    o, ot, whole, lse, kab, segk = forward(plan, segment_ids, seg_row, keep_row, q, k, v)
    block_output, dh1, do, near, far, tail, gvec = middle_part(
        plan, late, tokens, cotangent, o, ot, head, kept, vec, keep_row, bucket_patches
    )
    *stacks, normed, token = stack_part(vec, hat_in, q, k, v, do, whole)
    *pieces, token = add_parts([near, swap(far, "dp", plan.nd, 1)], pieces_of, token)
    rest = scatter_dp(plan, pieces)
    low, gains = backward(
        plan, vec, segment_ids, seg_row, lse, q, do, hat, rstd, segk, [kab, *stacks], token
    )
    da1, near, *far = finish_part(plan, hat_in, normed, wq, tail, gvec, low, gains)
    input_grad, given = input_part(hat_in, rstd_in, vec, da1, dh1)
    *late_parts, token = add_parts(rest[:2], 1, gains)
    late_parts += rest[2:]
    *pieces, _ = add_parts([near, [swap(half, "dp", plan.nd, 1) for half in far]], pieces_of, token)
    first = scatter_dp(plan, pieces)
    mine, *sent = blend(plan, late_parts, given, first)
    parts = [mine] + [
        swap(x, "bucket", plan.nb, mask) for x, mask in zip(sent, masks_of(b_bits))
    ]
    new_first, new_second, update_rows, sums = update_part(
        plan, parts, master, first_moment, second_moment
    )
    new_master, norms, trust = apply_part(plan, sum_all(plan, sums), master, update_rows)
    return (
        block_output,
        input_grad,
        new_first,
        new_second,
        new_master,
        norms,
        trust.reshape(MATS),
    )


def solution(mesh):
    shards = mesh.shape["bucket"] * mesh.shape["dp"]
    plan = Plan(mesh.shape, PARAMS // shards)
    both = ("bucket", "dp")
    return jax.shard_map(
        functools.partial(local, plan),
        mesh=mesh,
        in_specs=(P(both, None), P(both, None), P(both), P(both), P(), P(both), P(both), P(both)),
        out_specs=(P(both, None), P(both, None), P(both), P(both), P(both), P(), P()),
        check_vma=False,
    )
```

```python
import functools
import math

import jax
import jax.numpy as jnp
from jax import lax
from jax.experimental import pallas as pl
from jax.experimental.pallas import tpu as pltpu
from jax.sharding import PartitionSpec as P

D = 384
HEADS = 6
HD = 64
FF = 1536
SEQ = 1024
STEP = 10
MATS = 10
LANES = 128
PAIRS = HEADS // 2
TILE = 256
TILES = SEQ // TILE
BLOCKS = SEQ // LANES
MIDDLE_BLOCK = 512
FAR_PARTS = 3

norm_epsilon = 1e-06
adam_epsilon = 1e-06
beta_one = 0.9
beta_two = 0.999
learn_rate = 0.5
weight_decay = 0.01
masked_score = -1e30

MATRIX_END = 4 * D * D + 2 * D * FF
BOUNDS = [0, 3 * D * D, 4 * D * D, 4 * D * D + D * FF, MATRIX_END] + [
    MATRIX_END + (j + 1) * D for j in range(6)
]
PARAMS = BOUNDS[-1]
ROW_OUT = BOUNDS[1] // LANES
ROW_UP = BOUNDS[2] // LANES
ROW_DOWN = BOUNDS[3] // LANES
ROW_VEC = BOUNDS[4] // LANES
VEC_ROWS = 6 * D // LANES
EARLY_VEC_ROWS = 4 * D // LANES
ROWS_ALL = PARAMS // LANES

score_scale = HD ** (-0.5) * math.log2(math.e)
grad_scale = HD ** (-0.5)

BF = jnp.bfloat16
F32 = jnp.float32
VMEM = pl.BlockSpec(memory_space=pltpu.VMEM)
SMEM = pl.BlockSpec(memory_space=pltpu.SMEM)


QUICK = pl.CostEstimate(flops=1000, bytes_accessed=1000, transcendentals=0)


def params(limit):
    return pltpu.CompilerParams(vmem_limit_bytes=limit * 1024 * 1024)


def round_up(value, step):
    return -(-value // step) * step


class Plan:
    def __init__(self, mesh_shape, shard):
        self.nb = mesh_shape["bucket"]
        self.nd = mesh_shape["dp"]
        self.n = self.nb * self.nd
        self.shard = shard
        self.start = [k * shard // LANES for k in range(self.n)]
        self.rows = [
            -(-((k + 1) * shard) // LANES) - self.start[k] for k in range(self.n)
        ]
        self.win = round_up(max(self.rows) + 1, 16)
        self.most = max(self.rows)
        self.tail = round_up(self.most + EARLY_VEC_ROWS, 16)
        units = self.tail // 16
        ends = [units * (i + 1) // FAR_PARTS * 16 for i in range(FAR_PARTS)]
        self.far = list(zip([0] + ends[:-1], ends))
        self.upper = self.win * 3 // 4 // 16 * 16
        self.vec_place = ROW_VEC - self.start[-1]
        self.vec_from = self.vec_place // 16 * 16
        self.kept_row = 2 * self.win - self.vec_from
        self.early = self.kept_row + 16

    def device(self):
        return lax.axis_index("bucket") * self.nd + lax.axis_index("dp")


def nn(a, b):
    return lax.dot_general(a, b, (((1,), (0,)), ((), ())), preferred_element_type=F32)


def nt(a, b):
    return lax.dot_general(a, b, (((1,), (1,)), ((), ())), preferred_element_type=F32)


def split_low(x):
    high = x.astype(BF)
    return high, (x - high.astype(F32)).astype(BF)


def rows_at(step):
    if isinstance(step, int):
        return slice(step * TILE, (step + 1) * TILE)
    return pl.ds(pl.multiple_of(step * TILE, TILE), TILE)


def norm_parts(values):
    average = jnp.mean(values, axis=-1, keepdims=True)
    centered = values - average
    variance = jnp.mean(centered * centered, axis=-1, keepdims=True)
    rstd = lax.rsqrt(variance + norm_epsilon)
    return centered * rstd, rstd


def norm_back(hat, rstd, grad):
    mean_grad = jnp.mean(grad, axis=-1, keepdims=True)
    mean_both = jnp.mean(grad * hat, axis=-1, keepdims=True)
    return rstd * (grad - mean_grad - hat * mean_both)


def head_mean_matrix():
    row = lax.broadcasted_iota(jnp.int32, (TILE, TILE), 0)
    col = lax.broadcasted_iota(jnp.int32, (TILE, TILE), 1)
    return jnp.where(row // HD == col // HD, 1.0 / HD, 0.0).astype(BF)


def head_mean_low(low, matrix):
    rest = D - TILE
    return jnp.concatenate(
        [nn(low[:, :TILE], matrix), nn(low[:, TILE:], matrix[:rest, :rest])], axis=1
    )


def head_mean(x, matrix):
    high, rest = split_low(x)
    return head_mean_low(high, matrix) + head_mean_low(rest, matrix)


def flat_to_rows(plan, flat_ref, rows_ref):
    full, rest = divmod(plan.shard, LANES)
    rows_ref[full:, :] = jnp.zeros((plan.win - full, LANES), F32)
    rows_ref[:full, :] = flat_ref[: full * LANES].reshape(full, LANES)
    if rest:
        rows_ref[full : full + 1, :rest] = flat_ref[full * LANES :].reshape(1, rest)
    return rows_ref[...]


def rows_to_flat(plan, rows, flat_ref):
    full, rest = divmod(plan.shard, LANES)
    flat_ref[: full * LANES] = rows[:full].reshape(full * LANES)
    if rest:
        flat_ref[full * LANES :] = rows[full : full + 1, :rest].reshape(rest)


def prepare_kernel(plan, master_ref, upper_ref, lower_ref, rows_ref):
    offset = lax.rem(plan.device() * plan.shard, LANES)
    values = flat_to_rows(plan, master_ref, rows_ref)
    turned = pltpu.roll(values, offset, 1)
    below = pltpu.roll(turned, 1, 0)
    lane = lax.broadcasted_iota(jnp.int32, values.shape, 1)
    window = jnp.where(lane < offset, below, turned).astype(BF)
    upper_ref[...] = window[: plan.upper]
    lower_ref[...] = window[plan.upper :]


def prepare(plan, master):
    return pl.pallas_call(
        functools.partial(prepare_kernel, plan),
        out_shape=(
            jax.ShapeDtypeStruct((plan.upper, LANES), BF),
            jax.ShapeDtypeStruct((plan.win - plan.upper, LANES), BF),
        ),
        in_specs=[VMEM],
        out_specs=(VMEM, VMEM),
        scratch_shapes=[pltpu.VMEM((plan.win, LANES), F32)],
        compiler_params=params(8),
    )(master)


def ahead_kernel(tokens_ref, keep_ref, hat_ref, rstd_ref, count_ref):
    hat, rstd = norm_parts(tokens_ref[...].astype(F32))
    hat_ref[...] = hat
    rstd_ref[...] = jnp.broadcast_to(rstd, rstd_ref.shape)
    row = lax.broadcasted_iota(jnp.int32, count_ref.shape, 0)
    lane = lax.broadcasted_iota(jnp.int32, count_ref.shape, 1)
    count = jnp.sum(keep_ref[...].astype(F32), axis=1, keepdims=True)
    high = jnp.floor(count * (1.0 / 32.0))
    parts = jnp.where(lane == 0, high, jnp.where(lane == 1, count - 32.0 * high, 0.0))
    count_ref[...] = jnp.where(row == 15, parts, 0.0)


def ahead(tokens, keep_row):
    rows = tokens.shape[0]
    return pl.pallas_call(
        ahead_kernel,
        out_shape=(
            jax.ShapeDtypeStruct((rows, D), F32),
            jax.ShapeDtypeStruct((rows, LANES), F32),
            jax.ShapeDtypeStruct((16, LANES), F32),
        ),
        in_specs=[VMEM, VMEM],
        out_specs=(VMEM,) * 3,
        compiler_params=params(12),
        cost_estimate=QUICK,
    )(tokens, keep_row)


def held_window(own_ref, other_ref, rel, at):
    place = jnp.right_shift(rel, 1)
    return jnp.where(
        jnp.bitwise_and(rel, 1) == 0,
        own_ref[place, at].astype(F32),
        other_ref[place, at].astype(F32),
    )


def lay_windows(plan, owners, refs_of, flat, base):
    dp = lax.axis_index("dp")
    for k in owners:
        own_ref, other_ref = refs_of(k)
        window = held_window(own_ref, other_ref, jnp.bitwise_xor(dp, k % plan.nd), slice(0, plan.win))
        first, count = plan.start[k] - base, plan.rows[k]
        shared = k > 0 and (k * plan.shard) % LANES
        if shared:
            before = flat[first : first + 1, :]
        flat[first : first + count, :] = window[:count]
        if shared:
            flat[first : first + 1, :] = before + window[:1]


def take_matrix(target, flat, base, height, width):
    stride = width // LANES
    for j in range(stride):
        target[:, j * LANES : (j + 1) * LANES] = flat[pl.ds(base + j, height, stride=stride), :].astype(BF)


def put_matrix(flat, base, source, height, width):
    stride = width // LANES
    for j in range(stride):
        flat[pl.ds(base + j, height, stride=stride), :] = source[:, j * LANES : (j + 1) * LANES]


def key_chunks(seg_ref, ti):
    first_i, last_i = seg_ref[ti * TILE], seg_ref[ti * TILE + TILE - 1]
    low, high = jnp.int32(0), jnp.int32(0)
    for b in range(BLOCKS):
        low += (seg_ref[b * LANES + LANES - 1] < first_i).astype(jnp.int32)
        high += (seg_ref[b * LANES] <= last_i).astype(jnp.int32)
    count = jnp.right_shift(high - low + 1, 1)
    return jnp.minimum(low, BLOCKS - 2 * count), count


def tile_bias(ti, block, row_seg, key_seg):
    key_place = lax.broadcasted_iota(jnp.int32, (TILE, TILE), 0) + block * LANES
    row_place = lax.broadcasted_iota(jnp.int32, (TILE, TILE), 1) + ti * TILE
    return jnp.where(
        jnp.logical_or(key_seg == row_seg, key_place == row_place), 0.0, masked_score
    )


def keys_at(block):
    return pl.ds(pl.multiple_of(block * LANES, LANES), TILE)


def side_rows(stacked, side):
    return jnp.concatenate(
        [stacked[side * LANES : (side + 1) * LANES], stacked[(2 + side) * LANES : (3 + side) * LANES]],
        axis=0,
    )


def to_column(row):
    return jnp.transpose(jnp.broadcast_to(row, (LANES, row.shape[1])))


def block_heads(pair):
    lane = lax.broadcasted_iota(jnp.int32, pair.shape, 1)
    zero = jnp.zeros_like(pair)
    sides = [jnp.where(lane < HD, pair, zero), jnp.where(lane >= HD, pair, zero)]
    return [side[b * LANES : (b + 1) * LANES] for b in range(2) for side in sides]


def put_blocks(ref, hp, step, pair):
    for i, part in enumerate(block_heads(pair)):
        ref[hp, 2 * step + i // 2, i % 2] = part


def two_blocks(ref, hp, block):
    return ref[hp, pl.ds(block, 2)].reshape(4 * LANES, LANES)


def stack_heads(pair):
    lane = lax.broadcasted_iota(jnp.int32, pair.shape, 1)
    zero = jnp.zeros_like(pair)
    return jnp.concatenate(
        [jnp.where(lane < HD, pair, zero), jnp.where(lane >= HD, pair, zero)], axis=0
    )


def project_kernel(
    plan,
    own_ref,
    other_ref,
    hat_in_ref,
    wq_ref,
    vec_ref,
    head_ref,
    kept_ref,
    q_ref,
    k_ref,
    v_ref,
    hat_ref,
    rstd_ref,
    flat,
):
    dp = lax.axis_index("dp")
    lay_windows(plan, range(plan.nd), lambda k: (own_ref, other_ref), flat, 0)
    take_matrix(wq_ref, flat, 0, D, 3 * D)
    head_ref[...] = flat[ROW_OUT : ROW_OUT + 8, :]
    rel = jnp.bitwise_xor(dp, plan.nd - 1)
    late = held_window(own_ref, other_ref, rel, slice(plan.win, plan.kept_row))
    kept = jnp.zeros((1, LANES), F32)
    for j in range(plan.nd):
        half = other_ref if j & 1 else own_ref
        kept = kept + half[j >> 1, plan.kept_row :].astype(F32)[15:16]
    kept_ref[...] = jnp.broadcast_to(32.0 * kept[:, 0:1] + kept[:, 1:2], kept_ref.shape)
    for t in range(6):
        for j in range(D // LANES):
            at = plan.vec_place - plan.vec_from + 3 * t + j
            vec_ref[t : t + 1, j * LANES : (j + 1) * LANES] = late[at : at + 1]
    matrix = head_mean_matrix()
    gain1, shift1 = vec_ref[0:1, :], vec_ref[1:2, :]
    gain_q, gain_k = vec_ref[2:3, :], vec_ref[3:4, :]

    raw = nn((hat_in_ref[...] * gain1 + shift1).astype(BF), wq_ref[...])

    def head_norm(low_out, part, gain):
        lanes = slice(part * D, (part + 1) * D)
        x = raw[:, lanes]
        centered = x - head_mean(x, matrix)
        rstd = lax.rsqrt(head_mean(centered * centered, matrix) + norm_epsilon)
        normed = centered * rstd
        hat_ref[:, lanes] = normed
        rstd_ref[:, lanes] = rstd
        low_out[...] = (normed * gain).astype(BF)

    head_norm(q_ref, 0, gain_q)
    head_norm(k_ref, 1, gain_k)
    v_ref[...] = raw[:, 2 * D :].astype(BF)


def project_part(plan, own, other, tokens):
    rows = tokens.shape[0]
    low = jax.ShapeDtypeStruct((rows, D), BF)
    return pl.pallas_call(
        functools.partial(project_kernel, plan),
        out_shape=(
            jax.ShapeDtypeStruct((D, 3 * D), BF),
            jax.ShapeDtypeStruct((8, D), F32),
            jax.ShapeDtypeStruct((8, LANES), F32),
            jax.ShapeDtypeStruct((8, LANES), F32),
            low,
            low,
            low,
            jax.ShapeDtypeStruct((rows, 2 * D), F32),
            jax.ShapeDtypeStruct((rows, 2 * D), F32),
        ),
        in_specs=[VMEM] * 3,
        out_specs=(VMEM,) * 9,
        scratch_shapes=[
            pltpu.VMEM((round_up(plan.start[plan.nd - 1] + plan.win, 8), LANES), F32),
        ],
        compiler_params=params(24),
        cost_estimate=QUICK,
    )(own, other, tokens)


def forward_kernel(
    plan,
    seg_smem,
    seg_ref,
    keep_ref,
    q_ref,
    k_ref,
    v_ref,
    o_ref,
    ot_ref,
    whole_ref,
    lse_ref,
    kab,
    segk,
    vt,
    ot,
    rest_t,
    sums,
    expo,
):
    seg_row = seg_ref[...].astype(F32)
    segk[...] = to_column(jnp.where(keep_ref[...] == 1, seg_row, -1.0))

    for step in range(TILES):
        at = rows_at(step)
        for hp in range(PAIRS):
            put_blocks(kab, hp, step, k_ref[at, hp * LANES : (hp + 1) * LANES])
        vt[:, at] = jnp.transpose(v_ref[at, :].astype(F32)).astype(BF)

    def query_tile(ti, carry):
        ot[...] = jnp.zeros_like(ot)
        rest_t[...] = jnp.zeros_like(rest_t)
        sums[...] = jnp.zeros_like(sums)
        row_seg = seg_ref[:, rows_at(ti)].astype(F32)
        first, count = key_chunks(seg_smem, ti)

        def score_chunk(c, inner):
            block = first + 2 * c
            column = segk[keys_at(block), :]
            bias = tile_bias(ti, block, row_seg, jnp.concatenate([column, column], axis=1))
            for hp in range(PAIRS):
                queries = q_ref[rows_at(ti), hp * LANES : (hp + 1) * LANES]
                scores = nt(two_blocks(kab, hp, block), queries)
                for side in range(2):
                    head = 2 * hp + side
                    value = jnp.exp2(side_rows(scores, side) * score_scale + bias)
                    expo[c, head] = value
                    sums[head : head + 1, :] += jnp.sum(value, axis=0, keepdims=True)
            return inner

        lax.fori_loop(0, count, score_chunk, 0)
        lse_ref[ti] = jnp.log2(sums[...])
        sums[...] = 1.0 / sums[...]

        def value_chunk(c, inner):
            keys = keys_at(first + 2 * c)
            for head in range(HEADS):
                prob, rest = split_low(expo[c, head] * sums[head : head + 1, :])
                at = slice(head * HD, (head + 1) * HD)
                ot[at, :] += nn(vt[at, keys], prob)
                rest_t[at, :] += nn(vt[at, keys], rest)
            return inner

        lax.fori_loop(0, count, value_chunk, 0)
        attended = ot[...]
        ot_ref[ti] = attended.astype(BF)
        whole_ref[ti] = attended + rest_t[...]
        o_ref[rows_at(ti), :] = jnp.transpose(attended).astype(BF)
        return carry

    lax.fori_loop(0, TILES, query_tile, 0)


def forward(plan, seg, seg_row, keep_row, q, k, v):
    rows = q.shape[0]
    return pl.pallas_call(
        functools.partial(forward_kernel, plan),
        out_shape=(
            jax.ShapeDtypeStruct((rows, D), BF),
            jax.ShapeDtypeStruct((TILES, D, TILE), BF),
            jax.ShapeDtypeStruct((TILES, D, TILE), F32),
            jax.ShapeDtypeStruct((TILES, 8, TILE), F32),
            jax.ShapeDtypeStruct((PAIRS, BLOCKS, 2, LANES, LANES), BF),
            jax.ShapeDtypeStruct((SEQ, LANES), F32),
        ),
        in_specs=[SMEM] + [VMEM] * 5,
        out_specs=(VMEM,) * 6,
        scratch_shapes=[
            pltpu.VMEM((D, SEQ), BF),
            pltpu.VMEM((D, TILE), F32),
            pltpu.VMEM((D, TILE), F32),
            pltpu.VMEM((8, TILE), F32),
            pltpu.VMEM((TILES, HEADS, TILE, TILE), F32),
        ],
        compiler_params=params(24),
        cost_estimate=QUICK,
    )(seg, seg_row, keep_row, q, k, v)


erfc_step = 0.3275911 * math.sqrt(0.5)
erfc_terms = [0.254829592, -0.284496736, 1.421413741, -1.453152027, 1.061405429]


def normal_parts(u):
    expo = jnp.exp2(u * u * (-0.5 * math.log2(math.e)))
    t = 1.0 / (1.0 + erfc_step * jnp.abs(u))
    poly = 0.5 * erfc_terms[4]
    for term in reversed(erfc_terms[:4]):
        poly = poly * t + 0.5 * term
    below = poly * t * expo
    return jnp.where(u > 0.0, 1.0 - below, below), expo * (1.0 / math.sqrt(2.0 * math.pi))


def middle_kernel(plan, *refs):
    late_refs, rest = refs[: 2 * plan.nb - 2], refs[2 * plan.nb - 2 :]
    middle_body(plan, late_refs, *rest)


def middle_body(
    plan,
    late_refs,
    tokens_ref,
    cot_ref,
    o_ref,
    ot_ref,
    head_ref,
    kept_ref,
    vec_ref,
    keep_ref,
    patches_ref,
    out_ref,
    dh1_ref,
    do_ref,
    near_ref,
    far_ref,
    tail_ref,
    gvec_ref,
    keepc,
    hid,
    dus,
    flat,
    wo_ref,
    wu_ref,
    wd_ref,
):
    bucket = lax.axis_index("bucket")
    base = ROW_OUT
    flat[0:8, :] = head_ref[...]
    dp = lax.axis_index("dp")
    owns, others = late_refs[: plan.nb - 1], late_refs[plan.nb - 1 :]
    lay_windows(
        plan,
        range(plan.nd, plan.n),
        lambda k: (owns[k // plan.nd - 1], others[k // plan.nd - 1]),
        flat,
        base,
    )
    take_matrix(wo_ref, flat, 0, D, D)
    take_matrix(wu_ref, flat, ROW_UP - base, D, FF)
    take_matrix(wd_ref, flat, ROW_DOWN - base, FF, D)
    gain2, shift2 = vec_ref[4:5, :], vec_ref[5:6, :]
    own = patches_ref[bucket].astype(F32)
    total = patches_ref[0].astype(F32)
    for b in range(1, plan.nb):
        total = total + patches_ref[b].astype(F32)
    ones = jnp.ones((1, LANES), F32)
    scale = (plan.nb * own) * ones / (total * ones) * float(SEQ * plan.nd) / kept_ref[0:1, :]
    keepc[...] = to_column(keep_ref[...].astype(F32)) * scale
    gvec_ref[...] = jnp.zeros_like(gvec_ref)

    middle = tokens_ref[...].astype(F32) + nn(o_ref[...], wo_ref[...])
    hat, rstd = norm_parts(middle)
    low = (hat * gain2 + shift2).astype(BF)
    weights = keepc[...]
    seed = cot_ref[...].astype(F32) * jnp.concatenate([weights] * (D // LANES), axis=1)
    seed_low = seed.astype(BF)
    for first in range(0, FF, MIDDLE_BLOCK):
        cols = slice(first, first + MIDDLE_BLOCK)
        u = nn(low, wu_ref[:, cols])
        phi, bell = normal_parts(u)
        hid[:, cols] = (u * phi).astype(BF)
        dus[:, cols] = (nt(seed_low, wd_ref[cols, :]) * (phi + u * bell)).astype(BF)
    out_ref[...] = (middle + nn(hid[...], wd_ref[...])).astype(BF)
    seedt = jnp.transpose(seed).astype(BF)
    lowt = jnp.transpose(low.astype(F32)).astype(BF)
    da2 = nt(dus[...], wu_ref[...])
    gvec_ref[0:1, :] = jnp.sum(da2 * hat, axis=0, keepdims=True)
    gvec_ref[1:2, :] = jnp.sum(da2, axis=0, keepdims=True)
    dh1 = seed + norm_back(hat, rstd, da2 * gain2)
    dh1_ref[...] = dh1
    dh1_low = dh1.astype(BF)
    gout = nn(jnp.concatenate([ot_ref[t] for t in range(TILES)], axis=1), dh1_low)
    do_ref[...] = nt(dh1_low, wo_ref[...]).astype(BF)
    put_matrix(flat, 0, gout, D, D)
    block = 2 * TILE
    for i in range(FF // block):
        part = nn(lowt, dus[:, i * block : (i + 1) * block])
        for j in range(block // LANES):
            flat[pl.ds(ROW_UP - base + i * (block // LANES) + j, D, stride=FF // LANES), :] = part[
                :, j * LANES : (j + 1) * LANES
            ]
        part = jnp.transpose(nn(seedt, hid[:, i * block : (i + 1) * block]))
        for j in range(D // LANES):
            flat[
                pl.ds(ROW_DOWN - base + i * block * (D // LANES) + j, block, stride=D // LANES), :
            ] = part[:, j * LANES : (j + 1) * LANES]
    flat[ROW_VEC - base :, :] = jnp.zeros((flat.shape[0] - ROW_VEC + base, LANES), F32)
    for t in range(2):
        for j in range(D // LANES):
            row = ROW_VEC - base + EARLY_VEC_ROWS + t * (D // LANES) + j
            flat[row : row + 1, :] = gvec_ref[t : t + 1, j * LANES : (j + 1) * LANES]
    tail_ref[...] = flat[0:8, :]
    side = jnp.bitwise_and(dp, 1)
    for k in range(plan.nd, plan.n):
        first = plan.start[k] - base
        quarter = k // plan.nd - 1
        reld = jnp.right_shift(jnp.bitwise_xor(dp, k % plan.nd), 1)
        window = flat[first : first + plan.win, :].astype(BF)

        @pl.when(side == k % 2)
        def _():
            near_ref[quarter, reld] = window

        @pl.when(side != k % 2)
        def _():
            far_ref[quarter, reld] = window


def middle_part(plan, late, tokens, cot, o, ot, head, kept, vec, keep_row, patches):
    rows = tokens.shape[0]
    windows = jax.ShapeDtypeStruct((plan.nb - 1, plan.nd // 2, plan.win, LANES), BF)
    return pl.pallas_call(
        functools.partial(middle_kernel, plan),
        out_shape=(
            jax.ShapeDtypeStruct((rows, D), BF),
            jax.ShapeDtypeStruct((rows, D), F32),
            jax.ShapeDtypeStruct((rows, D), BF),
            windows,
            windows,
            jax.ShapeDtypeStruct((8, LANES), F32),
            jax.ShapeDtypeStruct((8, D), F32),
        ),
        in_specs=[VMEM] * (len(late) + 8) + [SMEM],
        out_specs=(VMEM,) * 7,
        scratch_shapes=[
            pltpu.VMEM((rows, LANES), F32),
            pltpu.VMEM((rows, FF), BF),
            pltpu.VMEM((rows, FF), BF),
            pltpu.VMEM((round_up(plan.start[-1] + plan.win - ROW_OUT, 8), LANES), F32),
            pltpu.VMEM((D, D), BF),
            pltpu.VMEM((D, FF), BF),
            pltpu.VMEM((FF, D), BF),
        ],
        compiler_params=params(36),
        cost_estimate=QUICK,
    )(*late, tokens, cot, o, ot, head, kept, vec, keep_row, patches)


def stack_kernel(
    vec_ref,
    hat_in_ref,
    q_ref,
    k_ref,
    v_ref,
    do_ref,
    whole_ref,
    vab,
    qab,
    dab,
    kt,
    inner_sums,
    normed_ref,
    token_ref,
):
    for step in range(TILES):
        at = rows_at(step)
        grads = do_ref[at, :]
        for hp in range(PAIRS):
            lanes = slice(hp * LANES, (hp + 1) * LANES)
            put_blocks(vab, hp, step, v_ref[at, lanes])
            qab[hp, step] = stack_heads(q_ref[at, lanes])
            dab[hp, step] = stack_heads(grads[:, lanes])
        kt[:, at] = jnp.transpose(k_ref[at, :].astype(F32)).astype(BF)
        both = jnp.transpose(grads.astype(F32)) * whole_ref[step]
        for head in range(HEADS):
            inner_sums[step, head : head + 1, :] = jnp.sum(
                both[head * HD : (head + 1) * HD], axis=0, keepdims=True
            )
        normed = hat_in_ref[at, :] * vec_ref[0:1, :] + vec_ref[1:2, :]
        normed_ref[:, at] = jnp.transpose(normed).astype(BF)
    token_ref[...] = jnp.zeros_like(token_ref)


def stack_part(vec, hat_in, q, k, v, do, whole):
    stacked = jax.ShapeDtypeStruct((PAIRS, TILES, 2 * TILE, LANES), BF)
    return pl.pallas_call(
        stack_kernel,
        out_shape=(
            jax.ShapeDtypeStruct((PAIRS, BLOCKS, 2, LANES, LANES), BF),
            stacked,
            stacked,
            jax.ShapeDtypeStruct((D, SEQ), BF),
            jax.ShapeDtypeStruct((TILES, 8, TILE), F32),
            jax.ShapeDtypeStruct((D, SEQ), BF),
            jax.ShapeDtypeStruct((8, LANES), F32),
        ),
        in_specs=[VMEM] * 7,
        out_specs=(VMEM,) * 7,
        compiler_params=params(16),
        cost_estimate=QUICK,
    )(vec, hat_in, q, k, v, do, whole)


def backward_kernel(
    plan,
    vec_ref,
    seg_smem,
    seg_ref,
    lse_ref,
    q_ref,
    do_ref,
    hat_ref,
    rstd_ref,
    segk,
    kab,
    vab,
    qab,
    dab,
    kt,
    inner_sums,
    token_ref,
    low_ref,
    gains_ref,
    dqt,
    dk,
    dv,
):
    matrix = head_mean_matrix()
    dqt[...] = jnp.zeros_like(dqt)
    dk[...] = jnp.zeros_like(dk)
    dv[...] = jnp.zeros_like(dv)
    gains_ref[...] = jnp.zeros_like(gains_ref)

    def query_tile(ti, carry):
        row_seg = seg_ref[:, rows_at(ti)].astype(F32)
        first, count = key_chunks(seg_smem, ti)

        def key_chunk(c, inner):
            block = first + 2 * c
            keys = keys_at(block)
            column = segk[keys, :]
            bias = tile_bias(ti, block, row_seg, jnp.concatenate([column, column], axis=1))
            raw = []
            for hp in range(PAIRS):
                lanes = slice(hp * LANES, (hp + 1) * LANES)
                raw.append(
                    (
                        nt(two_blocks(kab, hp, block), q_ref[rows_at(ti), lanes]),
                        nt(two_blocks(vab, hp, block), do_ref[rows_at(ti), lanes]),
                    )
                )
            probs, dscores = [], []
            for head in range(HEADS):
                scores, grads = raw[head // 2]
                prob = jnp.exp2(
                    side_rows(scores, head % 2) * score_scale
                    + (bias - lse_ref[ti, head : head + 1, :])
                )
                dscore = prob * (side_rows(grads, head % 2) - inner_sums[ti, head : head + 1, :])
                probs.append(prob.astype(BF))
                dscores.append(dscore.astype(BF))
            for hp in range(PAIRS):
                pair = slice(2 * hp, 2 * hp + 2)
                for head in (2 * hp, 2 * hp + 1):
                    at = slice(head * HD, (head + 1) * HD)
                    dqt[ti, at, :] += nn(kt[at, keys], dscores[head])
                dv[hp, keys] += nn(jnp.concatenate(probs[pair], axis=1), dab[hp, ti])
                dk[hp, keys] += nn(jnp.concatenate(dscores[pair], axis=1), qab[hp, ti])
            return inner

        lax.fori_loop(0, count, key_chunk, 0)
        return carry

    lax.fori_loop(0, TILES, query_tile, 0)

    def finish(step, carry):
        at = rows_at(step)

        def head_norm_back(part, gain, grad):
            lanes = slice(part * D, (part + 1) * D)
            hat = hat_ref[at, lanes]
            both = grad * hat
            gains_ref[part : part + 1, :] += jnp.sum(both, axis=0, keepdims=True)
            scaled = grad * gain
            mean_grad = head_mean_low(scaled.astype(BF), matrix)
            mean_both = head_mean_low((both * gain).astype(BF), matrix)
            back = rstd_ref[at, lanes] * (scaled - mean_grad - hat * mean_both)
            low_ref[at, lanes] = back.astype(BF)

        grad_k = jnp.concatenate([dk[hp, at] for hp in range(PAIRS)], axis=1) * grad_scale
        grad_v = jnp.concatenate([dv[hp, at] for hp in range(PAIRS)], axis=1)
        head_norm_back(0, vec_ref[2:3, :], jnp.transpose(dqt[step]) * grad_scale)
        head_norm_back(1, vec_ref[3:4, :], grad_k)
        low_ref[at, 2 * D :] = grad_v.astype(BF)
        return carry

    lax.fori_loop(0, TILES, finish, 0)


def backward(plan, vec, seg, seg_row, lse, q, do, hat, rstd, segk, stacks, token):
    rows = q.shape[0]
    return pl.pallas_call(
        functools.partial(backward_kernel, plan),
        out_shape=(
            jax.ShapeDtypeStruct((rows, 3 * D), BF),
            jax.ShapeDtypeStruct((8, D), F32),
        ),
        in_specs=[VMEM, SMEM] + [VMEM] * 14,
        out_specs=(VMEM, VMEM),
        scratch_shapes=[
            pltpu.VMEM((TILES, D, TILE), F32),
            pltpu.VMEM((PAIRS, SEQ, LANES), F32),
            pltpu.VMEM((PAIRS, SEQ, LANES), F32),
        ],
        compiler_params=params(26),
        cost_estimate=QUICK,
    )(vec, seg, seg_row, lse, q, do, hat, rstd, segk, *stacks, token)


def finish_kernel(
    plan,
    hat_ref,
    normed_ref,
    wq_ref,
    tail_ref,
    low_ref,
    gqk_ref,
    da1_ref,
    near_ref,
    *refs,
):
    *far_refs, gains, flat = refs
    hat = hat_ref[...]
    for i in range(3):
        part = nn(normed_ref[...], low_ref[:, i * D : (i + 1) * D])
        for j in range(D // LANES):
            flat[pl.ds(i * (D // LANES) + j, D, stride=3 * D // LANES), :] = part[
                :, j * LANES : (j + 1) * LANES
            ]
    da1 = nt(low_ref[...], wq_ref[...])
    da1_ref[...] = da1
    gains[...] = jnp.zeros_like(gains)
    gains[0:1, :] = jnp.sum(da1 * hat, axis=0, keepdims=True)
    gains[1:2, :] = jnp.sum(da1, axis=0, keepdims=True)
    gains[2:4, :] = gqk_ref[0:2, :]
    flat[ROW_OUT : ROW_OUT + 8, :] = tail_ref[...]
    dp = lax.axis_index("dp")
    side = jnp.bitwise_and(dp, 1)
    vector_rows = []
    for t in range(4):
        for j in range(D // LANES):
            vector_rows.append(gains[t : t + 1, j * LANES : (j + 1) * LANES])
    spare = plan.tail - plan.most - EARLY_VEC_ROWS
    if spare:
        vector_rows.append(jnp.zeros((spare, LANES), F32))
    for k in range(plan.nd):
        first = plan.start[k]
        reld = jnp.right_shift(jnp.bitwise_xor(dp, k), 1)
        window = flat[first : first + plan.tail, :]
        if k == plan.nd - 1:
            window = jnp.concatenate([window[: plan.most], *vector_rows], axis=0)
        window = window.astype(BF)

        @pl.when(side == k % 2)
        def _():
            near_ref[reld] = window

        @pl.when(side != k % 2)
        def _():
            for (low, high), far_ref in zip(plan.far, far_refs):
                far_ref[reld] = window[low:high]


def finish_part(plan, hat, normed, wq, tail, low, gains):
    rows = hat.shape[0]
    windows = jax.ShapeDtypeStruct((plan.nd // 2, plan.tail, LANES), BF)
    parts = tuple(
        jax.ShapeDtypeStruct((plan.nd // 2, high - low, LANES), BF) for low, high in plan.far
    )
    return pl.pallas_call(
        functools.partial(finish_kernel, plan),
        out_shape=(jax.ShapeDtypeStruct((rows, D), F32), windows) + parts,
        in_specs=[VMEM] * 6,
        out_specs=(VMEM,) * (2 + FAR_PARTS),
        scratch_shapes=[
            pltpu.VMEM((8, D), F32),
            pltpu.VMEM((round_up(plan.start[plan.nd - 1] + plan.tail, 8), LANES), F32),
        ],
        compiler_params=params(28),
        cost_estimate=QUICK,
    )(hat, normed, wq, tail, low, gains)


def input_kernel(hat_ref, rstd_ref, vec_ref, da1_ref, dh1_ref, grad_ref, token_ref):
    back = norm_back(hat_ref[...], rstd_ref[:, 0:1], da1_ref[...] * vec_ref[0:1, :])
    grad_ref[...] = dh1_ref[...] + back
    token_ref[...] = jnp.zeros_like(token_ref)


def input_part(hat, rstd, vec, da1, dh1):
    return pl.pallas_call(
        input_kernel,
        out_shape=(
            jax.ShapeDtypeStruct(dh1.shape, F32),
            jax.ShapeDtypeStruct((8, LANES), F32),
        ),
        in_specs=[VMEM] * 5,
        out_specs=(VMEM, VMEM),
        compiler_params=params(16),
        cost_estimate=QUICK,
    )(hat, rstd, vec, da1, dh1)


def flat_place(plan, shape):
    row = lax.broadcasted_iota(jnp.int32, shape, 0)
    lane = lax.broadcasted_iota(jnp.int32, shape, 1)
    place = row * LANES + lane
    return place, plan.device() * plan.shard + place


def update_kernel(
    plan,
    own_ref,
    got0_ref,
    got1_ref,
    got2_ref,
    master_ref,
    moment_ref,
    second_ref,
    new_moment_ref,
    new_second_ref,
    update_ref,
    sums_ref,
    window,
    master_rows,
    moment_rows,
    second_rows,
):
    bucket = lax.axis_index("bucket")
    dp = lax.axis_index("dp")
    total = tree_sum([ref[...].astype(F32) for ref in (own_ref, got0_ref, got1_ref, got2_ref)])
    window[...] = total[: plan.win]

    @pl.when(jnp.logical_and(bucket == plan.nb - 1, dp == plan.nd - 1))
    def _():
        window[plan.vec_place : plan.vec_place + EARLY_VEC_ROWS, :] = total[
            plan.most : plan.most + EARLY_VEC_ROWS
        ]

    offset = lax.rem(plan.device() * plan.shard, LANES)
    back = lax.rem(LANES - offset, LANES)
    turned = pltpu.roll(window[...], back, 1)
    above = pltpu.roll(turned, plan.win - 1, 0)
    lane = lax.broadcasted_iota(jnp.int32, turned.shape, 1)
    place, index = flat_place(plan, turned.shape)
    inside = place < plan.shard
    grad = jnp.where(inside, jnp.where(lane + offset < LANES, turned, above), 0.0)
    master = flat_to_rows(plan, master_ref, master_rows)
    old_moment = flat_to_rows(plan, moment_ref, moment_rows)
    old_second = flat_to_rows(plan, second_ref, second_rows)
    moment = beta_one * old_moment + (1.0 - beta_one) * grad
    second = beta_two * old_second + (1.0 - beta_two) * grad * grad
    first_hat = moment / (1.0 - beta_one**STEP)
    second_hat = second / (1.0 - beta_two**STEP)
    decay = jnp.where(index < BOUNDS[4], weight_decay, 0.0)
    update = first_hat / (jnp.sqrt(second_hat) + adam_epsilon) + decay * master
    update = jnp.where(inside, update, 0.0)
    rows_to_flat(plan, moment, new_moment_ref)
    rows_to_flat(plan, second, new_second_ref)
    update_ref[...] = update
    master_sq = jnp.where(inside, master * master, 0.0)
    update_sq = update * update
    lanes = lax.broadcasted_iota(jnp.int32, (1, LANES), 1)
    rows = []
    for squares in (master_sq, update_sq):
        row = jnp.zeros((1, LANES), F32)
        for t in range(MATS):
            mine = jnp.logical_and(index >= BOUNDS[t], index < BOUNDS[t + 1])
            part = jnp.sum(jnp.where(mine, squares, 0.0), axis=0, keepdims=True)
            row = jnp.where(lanes == t, jnp.sum(part, axis=1, keepdims=True), row)
        rows.append(row)
    rows.append(jnp.zeros((6, LANES), F32))
    sums_ref[...] = jnp.concatenate(rows, axis=0)


def update_part(plan, parts, master, moment, second):
    flat = jax.ShapeDtypeStruct((plan.shard,), F32)
    rows = jax.ShapeDtypeStruct((plan.win, LANES), F32)
    return pl.pallas_call(
        functools.partial(update_kernel, plan),
        out_shape=(flat, flat, rows, jax.ShapeDtypeStruct((8, LANES), F32)),
        in_specs=[VMEM] * 7,
        out_specs=(VMEM,) * 4,
        scratch_shapes=[pltpu.VMEM((plan.win, LANES), F32)] * 4,
        compiler_params=params(12),
    )(*parts, master, moment, second)


def apply_kernel(plan, *refs):
    *sums_refs, master_ref, update_ref, new_ref, norms_ref, trust_ref, rows_ref = refs
    roots = jnp.sqrt(tree_sum([ref[...] for ref in sums_refs]))
    trust = roots[0:1, :] / (roots[1:2, :] + adam_epsilon)
    norms_ref[...] = roots[0:2, :MATS]
    trust_ref[...] = trust[:, :MATS]
    master = flat_to_rows(plan, master_ref, rows_ref)
    _, index = flat_place(plan, master.shape)
    factors = jnp.broadcast_to(trust[:, 0:1], master.shape)
    for t in range(1, MATS):
        factors = jnp.where(index >= BOUNDS[t], trust[:, t : t + 1], factors)
    rows_to_flat(plan, master - learn_rate * factors * update_ref[...], new_ref)


def apply_part(plan, sums, master, update_rows):
    return pl.pallas_call(
        functools.partial(apply_kernel, plan),
        out_shape=(
            jax.ShapeDtypeStruct((plan.shard,), F32),
            jax.ShapeDtypeStruct((2, MATS), F32),
            jax.ShapeDtypeStruct((1, MATS), F32),
        ),
        in_specs=[VMEM] * (len(sums) + 2),
        out_specs=(VMEM,) * 3,
        scratch_shapes=[pltpu.VMEM((plan.win, LANES), F32)],
        compiler_params=params(8),
    )(*sums, master, update_rows)


def lay_column_kernel(count, *refs):
    for i, part in enumerate(refs[:count]):
        refs[-1][i] = part[...]


def lay_column(parts, *after):
    return pl.pallas_call(
        functools.partial(lay_column_kernel, len(parts)),
        out_shape=jax.ShapeDtypeStruct((len(parts), *parts[0].shape), parts[0].dtype),
        in_specs=[VMEM] * (len(parts) + len(after)),
        out_specs=VMEM,
        compiler_params=params(4),
    )(*parts, *after)


def lay_lower_kernel(plan, mine_ref, got_ref, count_ref, out_ref):
    half = mine_ref.shape[0]
    out_ref[:half] = mine_ref[...]
    out_ref[half:] = got_ref[...]
    last = mine_ref[0, -16:, :].astype(F32)
    out_ref[0, plan.win - plan.upper - 16 :, :] = (last + count_ref[...]).astype(BF)


def lay_lower(plan, mine, got, count):
    half, height, _ = mine.shape
    return pl.pallas_call(
        functools.partial(lay_lower_kernel, plan),
        out_shape=jax.ShapeDtypeStruct((2 * half, height, LANES), BF),
        in_specs=[VMEM] * 3,
        out_specs=VMEM,
        compiler_params=params(4),
    )(mine, got, count)


def choose_kernel(plan, *refs):
    columns, (lower_ref, early_ref), late_refs = (
        refs[: plan.nb],
        refs[plan.nb : plan.nb + 2],
        refs[plan.nb + 2 :],
    )
    bucket = lax.axis_index("bucket")
    early_ref[:, plan.kept_row :] = lower_ref[:, 0, plan.win - plan.upper - 16 :]
    for i, part in enumerate(columns):
        for owner, out_ref in enumerate((early_ref, *late_refs)):

            @pl.when(jnp.bitwise_xor(bucket, i) == owner)
            def _():
                out_ref[:, : plan.upper] = part[...]
                out_ref[:, plan.upper : plan.win] = lower_ref[:, i]

    early_ref[:, plan.win : plan.kept_row] = late_refs[-1][:, plan.vec_from :]


def choose(plan, columns, lower):
    step = columns[0].shape[0]
    late = jax.ShapeDtypeStruct((step, plan.win, LANES), BF)
    return pl.pallas_call(
        functools.partial(choose_kernel, plan),
        out_shape=(jax.ShapeDtypeStruct((step, plan.early, LANES), BF),) + (late,) * (plan.nb - 1),
        in_specs=[VMEM] * (len(columns) + 1),
        out_specs=(VMEM,) * plan.nb,
        compiler_params=params(10),
    )(*columns, lower)


def add_parts_kernel(halves, *refs):
    refs = list(refs)
    parts = [[refs.pop(0) for _ in range(count)] for count in halves]
    for i, out in enumerate(refs[1:-1]):
        step = out.shape[-3]
        at = slice(i * step, (i + 1) * step)
        at = (slice(None), at) if len(out.shape) == 4 else at
        values = [
            jnp.concatenate([half[at].astype(F32) for half in part], axis=-2) for part in parts
        ]
        out[...] = tree_sum(values).astype(out.dtype)
    refs[-1][...] = jnp.zeros_like(refs[-1])


def add_parts(parts, pieces, token):
    *lead, total, height, width = parts[0].shape
    parts = [part if isinstance(part, list) else [part] for part in parts]
    halves = [len(part) for part in parts]
    parts = [half for part in parts for half in part]
    return pl.pallas_call(
        functools.partial(add_parts_kernel, halves),
        out_shape=tuple(
            jax.ShapeDtypeStruct((*lead, total // pieces, height, width), BF if i else F32)
            for i in range(pieces)
        )
        + (jax.ShapeDtypeStruct((8, LANES), F32),),
        in_specs=[VMEM] * (len(parts) + 1),
        out_specs=(VMEM,) * (pieces + 1),
        compiler_params=params(14),
    )(*parts, token)


def blend_kernel(plan, late_count, *refs):
    late, parts, outs = refs[:late_count], refs[late_count + 1 : -plan.nb], refs[-plan.nb :]
    bucket = lax.axis_index("bucket")
    first = tree_sum([part[...].astype(F32) for part in parts])
    for i, out in enumerate(outs):
        owner = jnp.bitwise_xor(bucket, i)
        quarter = jnp.maximum(owner - 1, 0)
        window = late[0][quarter]
        if late_count > 1:
            window = window + tree_sum([ref[quarter].astype(F32) for ref in late[1:]])
        if plan.tail > plan.win:
            empty = jnp.zeros((plan.tail - plan.win, LANES), F32)
            window = jnp.concatenate([window, empty], axis=0)
        row = lax.broadcasted_iota(jnp.int32, first.shape, 0)
        takes_first = jnp.logical_or(row >= plan.most, owner == 0)
        out[...] = jnp.where(takes_first, first, window).astype(out.dtype)


def blend(plan, late, token, parts):
    return pl.pallas_call(
        functools.partial(blend_kernel, plan, len(late)),
        out_shape=tuple(
            jax.ShapeDtypeStruct((plan.tail, LANES), BF if i else F32) for i in range(plan.nb)
        ),
        in_specs=[VMEM] * (len(late) + 1 + len(parts)),
        out_specs=(VMEM,) * plan.nb,
        compiler_params=params(10),
    )(*late, token, *parts)


def add_rows_kernel(*refs):
    refs[-1][...] = tree_sum([ref[...] for ref in refs[:-1]])


def add_rows(parts):
    return pl.pallas_call(
        add_rows_kernel,
        out_shape=jax.ShapeDtypeStruct(parts[0].shape, F32),
        in_specs=[VMEM] * len(parts),
        out_specs=VMEM,
        compiler_params=params(4),
    )(*parts)


def groups_of(size, skip=0):
    bits = list(range(skip, size.bit_length() - 1))
    return [bits[i : i + 2] for i in range(0, len(bits), 2)]


def masks_of(bits):
    masks = [1 << bits[0]]
    if len(bits) == 2:
        masks += [1 << bits[1], (1 << bits[0]) | (1 << bits[1])]
    return masks


def swap(x, axis, size, mask):
    return lax.ppermute(x, axis, [(i, i ^ mask) for i in range(size)])


def tree_sum(parts):
    if len(parts) == 1:
        return parts[0]
    half = len(parts) // 2
    return tree_sum(parts[:half]) + tree_sum(parts[half:])


def with_partners(x, axis, size, bits):
    return [x] + [swap(x, axis, size, mask) for mask in masks_of(bits)]


def gather_windows(plan, upper, lower, count):
    first, *more = groups_of(plan.nd, 1)
    (bits,) = groups_of(plan.nb)
    near, distant = masks_of(bits)[:2]
    lower = lay_column([lower, swap(lower, "bucket", plan.nb, near)])
    lower = lay_lower(plan, lower, swap(lower, "bucket", plan.nb, distant), count)
    column = lay_column(with_partners(upper, "dp", plan.nd, first), lower)
    for group in more:
        column = jnp.concatenate(with_partners(column, "dp", plan.nd, group), axis=0)
    columns = with_partners(column, "bucket", plan.nb, bits)
    lower = lay_column(with_partners(lower, "dp", plan.nd, first))
    for group in more:
        lower = jnp.concatenate(with_partners(lower, "dp", plan.nd, group), axis=0)
    early, *late = choose(plan, columns, lower)
    others = [swap(x, "dp", plan.nd, 1) for x in (early, *late)]
    return (early, others[0]), (*late, *others[1:])


def scatter_dp(plan, pieces):
    *more, last = groups_of(plan.nd, 1)
    sent = list(zip(pieces[1:], masks_of(last)))
    got = [pieces[0]] + [
        swap(piece, "dp", plan.nd, mask) for piece, mask in sent[1:] + sent[:1]
    ]
    for bits in reversed(more):
        held = tree_sum([x.astype(F32) for x in got])
        size = 1 << len(bits)
        step = held.shape[-3] // size
        parts = [held[..., i * step : (i + 1) * step, :, :] for i in range(size)]
        got = [parts[0]] + [
            swap(part.astype(BF), "dp", plan.nd, mask)
            for part, mask in zip(parts[1:], masks_of(bits))
        ]
    return [x.reshape(*x.shape[:-3], *x.shape[-2:]) for x in got]


def sum_all(plan, x):
    x = [x, swap(x, "dp", plan.nd, 1)]
    for bits in groups_of(plan.nd, 1):
        x = with_partners(add_rows(x), "dp", plan.nd, bits)
    (bits,) = groups_of(plan.nb)
    return with_partners(add_rows(x), "bucket", plan.nb, bits)


def local(
    plan, tokens, cotangent, segment_ids, keep_mask, bucket_patches, master, first_moment, second_moment
):
    seg_row = segment_ids.reshape(1, SEQ)
    keep_row = keep_mask.reshape(1, SEQ)
    pieces_of = 1 << len(groups_of(plan.nd, 1)[-1])
    (b_bits,) = groups_of(plan.nb)

    hat_in, rstd_in, count = ahead(tokens, keep_row)
    early, late = gather_windows(plan, *prepare(plan, master), count)
    wq, vec, head, kept, q, k, v, hat, rstd = project_part(plan, *early, hat_in)
    o, ot, whole, lse, kab, segk = forward(plan, segment_ids, seg_row, keep_row, q, k, v)
    block_output, dh1, do, near, far, tail, _ = middle_part(
        plan, late, tokens, cotangent, o, ot, head, kept, vec, keep_row, bucket_patches
    )
    *stacks, normed, token = stack_part(vec, hat_in, q, k, v, do, whole)
    *pieces, token = add_parts([near, swap(far, "dp", plan.nd, 1)], pieces_of, token)
    rest = scatter_dp(plan, pieces)
    low, gains = backward(
        plan, vec, segment_ids, seg_row, lse, q, do, hat, rstd, segk, [kab, *stacks], token
    )
    da1, near, *far = finish_part(plan, hat_in, normed, wq, tail, low, gains)
    input_grad, given = input_part(hat_in, rstd_in, vec, da1, dh1)
    *late_parts, token = add_parts(rest[:2], 1, gains)
    late_parts += rest[2:]
    *pieces, _ = add_parts([near, [swap(half, "dp", plan.nd, 1) for half in far]], pieces_of, token)
    first = scatter_dp(plan, pieces)
    mine, *sent = blend(plan, late_parts, given, first)
    sent = list(zip(sent, masks_of(b_bits)))
    parts = [mine] + [swap(x, "bucket", plan.nb, mask) for x, mask in sent[::-1]]
    new_first, new_second, update_rows, sums = update_part(
        plan, parts, master, first_moment, second_moment
    )
    new_master, norms, trust = apply_part(plan, sum_all(plan, sums), master, update_rows)
    return (
        block_output,
        input_grad,
        new_first,
        new_second,
        new_master,
        norms,
        trust.reshape(MATS),
    )


def solution(mesh):
    shards = mesh.shape["bucket"] * mesh.shape["dp"]
    plan = Plan(mesh.shape, PARAMS // shards)
    both = ("bucket", "dp")
    return jax.shard_map(
        functools.partial(local, plan),
        mesh=mesh,
        in_specs=(P(both, None), P(both, None), P(both), P(both), P(), P(both), P(both), P(both)),
        out_specs=(P(both, None), P(both, None), P(both), P(both), P(both), P(), P()),
        check_vma=False,
    )
```

```python
import functools
import math

import jax
import jax.numpy as jnp
from jax import lax
from jax.experimental import pallas as pl
from jax.experimental.pallas import tpu as pltpu
from jax.sharding import PartitionSpec as P

D = 384
HEADS = 6
HD = 64
FF = 1536
SEQ = 1024
STEP = 10
MATS = 10
LANES = 128
PAIRS = HEADS // 2
TILE = 256
TILES = SEQ // TILE
BLOCKS = SEQ // LANES
MIDDLE_BLOCK = 512
FAR_PARTS = 3

norm_epsilon = 1e-06
adam_epsilon = 1e-06
beta_one = 0.9
beta_two = 0.999
learn_rate = 0.5
weight_decay = 0.01
masked_score = -1e30

MATRIX_END = 4 * D * D + 2 * D * FF
BOUNDS = [0, 3 * D * D, 4 * D * D, 4 * D * D + D * FF, MATRIX_END] + [
    MATRIX_END + (j + 1) * D for j in range(6)
]
PARAMS = BOUNDS[-1]
ROW_OUT = BOUNDS[1] // LANES
ROW_UP = BOUNDS[2] // LANES
ROW_DOWN = BOUNDS[3] // LANES
ROW_VEC = BOUNDS[4] // LANES
VEC_ROWS = 6 * D // LANES
EARLY_VEC_ROWS = 4 * D // LANES
ROWS_ALL = PARAMS // LANES

score_scale = HD ** (-0.5) * math.log2(math.e)
grad_scale = HD ** (-0.5)

BF = jnp.bfloat16
F32 = jnp.float32
VMEM = pl.BlockSpec(memory_space=pltpu.VMEM)
SMEM = pl.BlockSpec(memory_space=pltpu.SMEM)


QUICK = pl.CostEstimate(flops=1000, bytes_accessed=1000, transcendentals=0)


def params(limit):
    return pltpu.CompilerParams(vmem_limit_bytes=limit * 1024 * 1024)


def round_up(value, step):
    return -(-value // step) * step


class Plan:
    def __init__(self, mesh_shape, shard):
        self.nb = mesh_shape["bucket"]
        self.nd = mesh_shape["dp"]
        self.n = self.nb * self.nd
        self.shard = shard
        self.start = [k * shard // LANES for k in range(self.n)]
        self.rows = [
            -(-((k + 1) * shard) // LANES) - self.start[k] for k in range(self.n)
        ]
        self.win = round_up(max(self.rows) + 1, 16)
        self.most = max(self.rows)
        self.tail = round_up(self.most + EARLY_VEC_ROWS, 16)
        units = self.tail // 16
        ends = [units * (i + 1) // FAR_PARTS * 16 for i in range(FAR_PARTS)]
        self.far = list(zip([0] + ends[:-1], ends))
        self.upper = self.win * 3 // 4 // 16 * 16
        self.vec_place = ROW_VEC - self.start[-1]
        self.vec_from = self.vec_place // 16 * 16
        self.kept_row = 2 * self.win - self.vec_from
        self.early = self.kept_row + 16

    def device(self):
        return lax.axis_index("bucket") * self.nd + lax.axis_index("dp")


def nn(a, b):
    return lax.dot_general(a, b, (((1,), (0,)), ((), ())), preferred_element_type=F32)


def nt(a, b):
    return lax.dot_general(a, b, (((1,), (1,)), ((), ())), preferred_element_type=F32)


def split_low(x):
    high = x.astype(BF)
    return high, (x - high.astype(F32)).astype(BF)


def rows_at(step):
    if isinstance(step, int):
        return slice(step * TILE, (step + 1) * TILE)
    return pl.ds(pl.multiple_of(step * TILE, TILE), TILE)


def norm_parts(values):
    average = jnp.mean(values, axis=-1, keepdims=True)
    centered = values - average
    variance = jnp.mean(centered * centered, axis=-1, keepdims=True)
    rstd = lax.rsqrt(variance + norm_epsilon)
    return centered * rstd, rstd


def norm_back(hat, rstd, grad):
    mean_grad = jnp.mean(grad, axis=-1, keepdims=True)
    mean_both = jnp.mean(grad * hat, axis=-1, keepdims=True)
    return rstd * (grad - mean_grad - hat * mean_both)


def head_mean_matrix():
    row = lax.broadcasted_iota(jnp.int32, (TILE, TILE), 0)
    col = lax.broadcasted_iota(jnp.int32, (TILE, TILE), 1)
    return jnp.where(row // HD == col // HD, 1.0 / HD, 0.0).astype(BF)


def head_mean_low(low, matrix):
    rest = D - TILE
    return jnp.concatenate(
        [nn(low[:, :TILE], matrix), nn(low[:, TILE:], matrix[:rest, :rest])], axis=1
    )


def head_mean(x, matrix):
    high, rest = split_low(x)
    return head_mean_low(high, matrix) + head_mean_low(rest, matrix)


def flat_to_rows(plan, flat_ref, rows_ref):
    full, rest = divmod(plan.shard, LANES)
    rows_ref[full:, :] = jnp.zeros((plan.win - full, LANES), F32)
    rows_ref[:full, :] = flat_ref[: full * LANES].reshape(full, LANES)
    if rest:
        rows_ref[full : full + 1, :rest] = flat_ref[full * LANES :].reshape(1, rest)
    return rows_ref[...]


def rows_to_flat(plan, rows, flat_ref):
    full, rest = divmod(plan.shard, LANES)
    flat_ref[: full * LANES] = rows[:full].reshape(full * LANES)
    if rest:
        flat_ref[full * LANES :] = rows[full : full + 1, :rest].reshape(rest)


def prepare_kernel(plan, master_ref, upper_ref, lower_ref, rows_ref):
    offset = lax.rem(plan.device() * plan.shard, LANES)
    values = flat_to_rows(plan, master_ref, rows_ref)
    turned = pltpu.roll(values, offset, 1)
    below = pltpu.roll(turned, 1, 0)
    lane = lax.broadcasted_iota(jnp.int32, values.shape, 1)
    window = jnp.where(lane < offset, below, turned).astype(BF)
    upper_ref[...] = window[: plan.upper]
    lower_ref[...] = window[plan.upper :]


def prepare(plan, master):
    return pl.pallas_call(
        functools.partial(prepare_kernel, plan),
        out_shape=(
            jax.ShapeDtypeStruct((plan.upper, LANES), BF),
            jax.ShapeDtypeStruct((plan.win - plan.upper, LANES), BF),
        ),
        in_specs=[VMEM],
        out_specs=(VMEM, VMEM),
        scratch_shapes=[pltpu.VMEM((plan.win, LANES), F32)],
        compiler_params=params(8),
    )(master)


def ahead_kernel(tokens_ref, keep_ref, hat_ref, rstd_ref, count_ref):
    hat, rstd = norm_parts(tokens_ref[...].astype(F32))
    hat_ref[...] = hat
    rstd_ref[...] = jnp.broadcast_to(rstd, rstd_ref.shape)
    row = lax.broadcasted_iota(jnp.int32, count_ref.shape, 0)
    lane = lax.broadcasted_iota(jnp.int32, count_ref.shape, 1)
    count = jnp.sum(keep_ref[...].astype(F32), axis=1, keepdims=True)
    high = jnp.floor(count * (1.0 / 32.0))
    parts = jnp.where(lane == 0, high, jnp.where(lane == 1, count - 32.0 * high, 0.0))
    count_ref[...] = jnp.where(row == 15, parts, 0.0)


def ahead(tokens, keep_row):
    rows = tokens.shape[0]
    return pl.pallas_call(
        ahead_kernel,
        out_shape=(
            jax.ShapeDtypeStruct((rows, D), F32),
            jax.ShapeDtypeStruct((rows, LANES), F32),
            jax.ShapeDtypeStruct((16, LANES), F32),
        ),
        in_specs=[VMEM, VMEM],
        out_specs=(VMEM,) * 3,
        compiler_params=params(12),
        cost_estimate=QUICK,
    )(tokens, keep_row)


def held_window(own_ref, other_ref, rel, at):
    place = jnp.right_shift(rel, 1)
    return jnp.where(
        jnp.bitwise_and(rel, 1) == 0,
        own_ref[place, at].astype(F32),
        other_ref[place, at].astype(F32),
    )


def lay_windows(plan, owners, refs_of, flat, base):
    dp = lax.axis_index("dp")
    for k in owners:
        own_ref, other_ref = refs_of(k)
        window = held_window(own_ref, other_ref, jnp.bitwise_xor(dp, k % plan.nd), slice(0, plan.win))
        first, count = plan.start[k] - base, plan.rows[k]
        shared = k > 0 and (k * plan.shard) % LANES
        if shared:
            before = flat[first : first + 1, :]
        flat[first : first + count, :] = window[:count]
        if shared:
            flat[first : first + 1, :] = before + window[:1]


def take_matrix(target, flat, base, height, width):
    stride = width // LANES
    for j in range(stride):
        target[:, j * LANES : (j + 1) * LANES] = flat[pl.ds(base + j, height, stride=stride), :].astype(BF)


def put_matrix(flat, base, source, height, width):
    stride = width // LANES
    for j in range(stride):
        flat[pl.ds(base + j, height, stride=stride), :] = source[:, j * LANES : (j + 1) * LANES]


def key_chunks(seg_ref, ti):
    first_i, last_i = seg_ref[ti * TILE], seg_ref[ti * TILE + TILE - 1]
    low, high = jnp.int32(0), jnp.int32(0)
    for b in range(BLOCKS):
        low += (seg_ref[b * LANES + LANES - 1] < first_i).astype(jnp.int32)
        high += (seg_ref[b * LANES] <= last_i).astype(jnp.int32)
    count = jnp.right_shift(high - low + 1, 1)
    return jnp.minimum(low, BLOCKS - 2 * count), count


def tile_bias(ti, block, row_seg, key_seg):
    key_place = lax.broadcasted_iota(jnp.int32, (TILE, TILE), 0) + block * LANES
    row_place = lax.broadcasted_iota(jnp.int32, (TILE, TILE), 1) + ti * TILE
    return jnp.where(
        jnp.logical_or(key_seg == row_seg, key_place == row_place), 0.0, masked_score
    )


def keys_at(block):
    return pl.ds(pl.multiple_of(block * LANES, LANES), TILE)


def side_rows(stacked, side):
    return jnp.concatenate(
        [stacked[side * LANES : (side + 1) * LANES], stacked[(2 + side) * LANES : (3 + side) * LANES]],
        axis=0,
    )


def to_column(row):
    return jnp.transpose(jnp.broadcast_to(row, (LANES, row.shape[1])))


def block_heads(pair):
    lane = lax.broadcasted_iota(jnp.int32, pair.shape, 1)
    zero = jnp.zeros_like(pair)
    sides = [jnp.where(lane < HD, pair, zero), jnp.where(lane >= HD, pair, zero)]
    return [side[b * LANES : (b + 1) * LANES] for b in range(2) for side in sides]


def put_blocks(ref, hp, step, pair):
    for i, part in enumerate(block_heads(pair)):
        ref[hp, 2 * step + i // 2, i % 2] = part


def two_blocks(ref, hp, block):
    return ref[hp, pl.ds(block, 2)].reshape(4 * LANES, LANES)


def stack_heads(pair):
    lane = lax.broadcasted_iota(jnp.int32, pair.shape, 1)
    zero = jnp.zeros_like(pair)
    return jnp.concatenate(
        [jnp.where(lane < HD, pair, zero), jnp.where(lane >= HD, pair, zero)], axis=0
    )


def project_kernel(
    plan,
    own_ref,
    other_ref,
    hat_in_ref,
    wq_ref,
    vec_ref,
    head_ref,
    kept_ref,
    q_ref,
    k_ref,
    v_ref,
    hat_ref,
    rstd_ref,
    flat,
):
    dp = lax.axis_index("dp")
    lay_windows(plan, range(plan.nd), lambda k: (own_ref, other_ref), flat, 0)
    take_matrix(wq_ref, flat, 0, D, 3 * D)
    head_ref[...] = flat[ROW_OUT : ROW_OUT + 8, :]
    rel = jnp.bitwise_xor(dp, plan.nd - 1)
    late = held_window(own_ref, other_ref, rel, slice(plan.win, plan.kept_row))
    kept = jnp.zeros((1, LANES), F32)
    for j in range(plan.nd):
        half = other_ref if j & 1 else own_ref
        kept = kept + half[j >> 1, plan.kept_row :].astype(F32)[15:16]
    kept_ref[...] = jnp.broadcast_to(32.0 * kept[:, 0:1] + kept[:, 1:2], kept_ref.shape)
    for t in range(6):
        for j in range(D // LANES):
            at = plan.vec_place - plan.vec_from + 3 * t + j
            vec_ref[t : t + 1, j * LANES : (j + 1) * LANES] = late[at : at + 1]
    matrix = head_mean_matrix()
    gain1, shift1 = vec_ref[0:1, :], vec_ref[1:2, :]
    gain_q, gain_k = vec_ref[2:3, :], vec_ref[3:4, :]

    raw = nn((hat_in_ref[...] * gain1 + shift1).astype(BF), wq_ref[...])

    def head_norm(low_out, part, gain):
        lanes = slice(part * D, (part + 1) * D)
        x = raw[:, lanes]
        centered = x - head_mean(x, matrix)
        rstd = lax.rsqrt(head_mean(centered * centered, matrix) + norm_epsilon)
        normed = centered * rstd
        hat_ref[:, lanes] = normed
        rstd_ref[:, lanes] = rstd
        low_out[...] = (normed * gain).astype(BF)

    head_norm(q_ref, 0, gain_q)
    head_norm(k_ref, 1, gain_k)
    v_ref[...] = raw[:, 2 * D :].astype(BF)


def project_part(plan, own, other, tokens):
    rows = tokens.shape[0]
    low = jax.ShapeDtypeStruct((rows, D), BF)
    return pl.pallas_call(
        functools.partial(project_kernel, plan),
        out_shape=(
            jax.ShapeDtypeStruct((D, 3 * D), BF),
            jax.ShapeDtypeStruct((8, D), F32),
            jax.ShapeDtypeStruct((8, LANES), F32),
            jax.ShapeDtypeStruct((8, LANES), F32),
            low,
            low,
            low,
            jax.ShapeDtypeStruct((rows, 2 * D), F32),
            jax.ShapeDtypeStruct((rows, 2 * D), F32),
        ),
        in_specs=[VMEM] * 3,
        out_specs=(VMEM,) * 9,
        scratch_shapes=[
            pltpu.VMEM((round_up(plan.start[plan.nd - 1] + plan.win, 8), LANES), F32),
        ],
        compiler_params=params(24),
        cost_estimate=QUICK,
    )(own, other, tokens)


def forward_kernel(
    plan,
    seg_smem,
    seg_ref,
    keep_ref,
    q_ref,
    k_ref,
    v_ref,
    o_ref,
    ot_ref,
    whole_ref,
    lse_ref,
    kab,
    segk,
    vt,
    ot,
    rest_t,
    sums,
    expo,
):
    seg_row = seg_ref[...].astype(F32)
    segk[...] = to_column(jnp.where(keep_ref[...] == 1, seg_row, -1.0))

    for step in range(TILES):
        at = rows_at(step)
        for hp in range(PAIRS):
            put_blocks(kab, hp, step, k_ref[at, hp * LANES : (hp + 1) * LANES])
        vt[:, at] = jnp.transpose(v_ref[at, :].astype(F32)).astype(BF)

    def query_tile(ti, carry):
        ot[...] = jnp.zeros_like(ot)
        rest_t[...] = jnp.zeros_like(rest_t)
        sums[...] = jnp.zeros_like(sums)
        row_seg = seg_ref[:, rows_at(ti)].astype(F32)
        first, count = key_chunks(seg_smem, ti)

        def score_chunk(c, inner):
            block = first + 2 * c
            column = segk[keys_at(block), :]
            bias = tile_bias(ti, block, row_seg, jnp.concatenate([column, column], axis=1))
            for hp in range(PAIRS):
                queries = q_ref[rows_at(ti), hp * LANES : (hp + 1) * LANES]
                scores = nt(two_blocks(kab, hp, block), queries)
                for side in range(2):
                    head = 2 * hp + side
                    value = jnp.exp2(side_rows(scores, side) * score_scale + bias)
                    expo[c, head] = value
                    sums[head : head + 1, :] += jnp.sum(value, axis=0, keepdims=True)
            return inner

        lax.fori_loop(0, count, score_chunk, 0)
        lse_ref[ti] = jnp.log2(sums[...])
        sums[...] = 1.0 / sums[...]

        def value_chunk(c, inner):
            keys = keys_at(first + 2 * c)
            for head in range(HEADS):
                prob, rest = split_low(expo[c, head] * sums[head : head + 1, :])
                at = slice(head * HD, (head + 1) * HD)
                ot[at, :] += nn(vt[at, keys], prob)
                rest_t[at, :] += nn(vt[at, keys], rest)
            return inner

        lax.fori_loop(0, count, value_chunk, 0)
        attended = ot[...]
        ot_ref[ti] = attended.astype(BF)
        whole_ref[ti] = attended + rest_t[...]
        o_ref[rows_at(ti), :] = jnp.transpose(attended).astype(BF)
        return carry

    lax.fori_loop(0, TILES, query_tile, 0)


def forward(plan, seg, seg_row, keep_row, q, k, v):
    rows = q.shape[0]
    return pl.pallas_call(
        functools.partial(forward_kernel, plan),
        out_shape=(
            jax.ShapeDtypeStruct((rows, D), BF),
            jax.ShapeDtypeStruct((TILES, D, TILE), BF),
            jax.ShapeDtypeStruct((TILES, D, TILE), F32),
            jax.ShapeDtypeStruct((TILES, 8, TILE), F32),
            jax.ShapeDtypeStruct((PAIRS, BLOCKS, 2, LANES, LANES), BF),
            jax.ShapeDtypeStruct((SEQ, LANES), F32),
        ),
        in_specs=[SMEM] + [VMEM] * 5,
        out_specs=(VMEM,) * 6,
        scratch_shapes=[
            pltpu.VMEM((D, SEQ), BF),
            pltpu.VMEM((D, TILE), F32),
            pltpu.VMEM((D, TILE), F32),
            pltpu.VMEM((8, TILE), F32),
            pltpu.VMEM((TILES, HEADS, TILE, TILE), F32),
        ],
        compiler_params=params(24),
        cost_estimate=QUICK,
    )(seg, seg_row, keep_row, q, k, v)


erfc_step = 0.3275911 * math.sqrt(0.5)
erfc_terms = [0.254829592, -0.284496736, 1.421413741, -1.453152027, 1.061405429]


def normal_parts(u):
    expo = jnp.exp2(u * u * (-0.5 * math.log2(math.e)))
    t = 1.0 / (1.0 + erfc_step * jnp.abs(u))
    poly = 0.5 * erfc_terms[4]
    for term in reversed(erfc_terms[:4]):
        poly = poly * t + 0.5 * term
    below = poly * t * expo
    return jnp.where(u > 0.0, 1.0 - below, below), expo * (1.0 / math.sqrt(2.0 * math.pi))


def middle_kernel(plan, *refs):
    late_refs, rest = refs[: 2 * plan.nb - 2], refs[2 * plan.nb - 2 :]
    middle_body(plan, late_refs, *rest)


def middle_body(
    plan,
    late_refs,
    tokens_ref,
    cot_ref,
    o_ref,
    ot_ref,
    head_ref,
    kept_ref,
    vec_ref,
    keep_ref,
    patches_ref,
    out_ref,
    dh1_ref,
    do_ref,
    near_ref,
    far_ref,
    tail_ref,
    gvec_ref,
    keepc,
    hid,
    dus,
    flat,
    wo_ref,
    wu_ref,
    wd_ref,
):
    bucket = lax.axis_index("bucket")
    base = ROW_OUT
    flat[0:8, :] = head_ref[...]
    dp = lax.axis_index("dp")
    owns, others = late_refs[: plan.nb - 1], late_refs[plan.nb - 1 :]
    lay_windows(
        plan,
        range(plan.nd, plan.n),
        lambda k: (owns[k // plan.nd - 1], others[k // plan.nd - 1]),
        flat,
        base,
    )
    take_matrix(wo_ref, flat, 0, D, D)
    take_matrix(wu_ref, flat, ROW_UP - base, D, FF)
    take_matrix(wd_ref, flat, ROW_DOWN - base, FF, D)
    gain2, shift2 = vec_ref[4:5, :], vec_ref[5:6, :]
    own = patches_ref[bucket].astype(F32)
    total = patches_ref[0].astype(F32)
    for b in range(1, plan.nb):
        total = total + patches_ref[b].astype(F32)
    ones = jnp.ones((1, LANES), F32)
    scale = (plan.nb * own) * ones / (total * ones) * float(SEQ * plan.nd) / kept_ref[0:1, :]
    keepc[...] = to_column(keep_ref[...].astype(F32)) * scale
    gvec_ref[...] = jnp.zeros_like(gvec_ref)

    middle = tokens_ref[...].astype(F32) + nn(o_ref[...], wo_ref[...])
    hat, rstd = norm_parts(middle)
    low = (hat * gain2 + shift2).astype(BF)
    weights = keepc[...]
    seed = cot_ref[...].astype(F32) * jnp.concatenate([weights] * (D // LANES), axis=1)
    seed_low = seed.astype(BF)
    for first in range(0, FF, MIDDLE_BLOCK):
        cols = slice(first, first + MIDDLE_BLOCK)
        u = nn(low, wu_ref[:, cols])
        phi, bell = normal_parts(u)
        hid[:, cols] = (u * phi).astype(BF)
        dus[:, cols] = (nt(seed_low, wd_ref[cols, :]) * (phi + u * bell)).astype(BF)
    out_ref[...] = (middle + nn(hid[...], wd_ref[...])).astype(BF)
    seedt = jnp.transpose(seed).astype(BF)
    lowt = jnp.transpose(low.astype(F32)).astype(BF)
    da2 = nt(dus[...], wu_ref[...])
    gvec_ref[0:1, :] = jnp.sum(da2 * hat, axis=0, keepdims=True)
    gvec_ref[1:2, :] = jnp.sum(da2, axis=0, keepdims=True)
    dh1 = seed + norm_back(hat, rstd, da2 * gain2)
    dh1_ref[...] = dh1
    dh1_low = dh1.astype(BF)
    gout = nn(jnp.concatenate([ot_ref[t] for t in range(TILES)], axis=1), dh1_low)
    do_ref[...] = nt(dh1_low, wo_ref[...]).astype(BF)
    put_matrix(flat, 0, gout, D, D)
    block = 2 * TILE
    for i in range(FF // block):
        part = nn(lowt, dus[:, i * block : (i + 1) * block])
        for j in range(block // LANES):
            flat[pl.ds(ROW_UP - base + i * (block // LANES) + j, D, stride=FF // LANES), :] = part[
                :, j * LANES : (j + 1) * LANES
            ]
        part = jnp.transpose(nn(seedt, hid[:, i * block : (i + 1) * block]))
        for j in range(D // LANES):
            flat[
                pl.ds(ROW_DOWN - base + i * block * (D // LANES) + j, block, stride=D // LANES), :
            ] = part[:, j * LANES : (j + 1) * LANES]
    flat[ROW_VEC - base :, :] = jnp.zeros((flat.shape[0] - ROW_VEC + base, LANES), F32)
    for t in range(2):
        for j in range(D // LANES):
            row = ROW_VEC - base + EARLY_VEC_ROWS + t * (D // LANES) + j
            flat[row : row + 1, :] = gvec_ref[t : t + 1, j * LANES : (j + 1) * LANES]
    tail_ref[...] = flat[0:8, :]
    side = jnp.bitwise_and(dp, 1)
    for k in range(plan.nd, plan.n):
        first = plan.start[k] - base
        quarter = k // plan.nd - 1
        reld = jnp.right_shift(jnp.bitwise_xor(dp, k % plan.nd), 1)
        window = flat[first : first + plan.win, :].astype(BF)

        @pl.when(side == k % 2)
        def _():
            near_ref[quarter, reld] = window

        @pl.when(side != k % 2)
        def _():
            far_ref[quarter, reld] = window


def middle_part(plan, late, tokens, cot, o, ot, head, kept, vec, keep_row, patches):
    rows = tokens.shape[0]
    windows = jax.ShapeDtypeStruct((plan.nb - 1, plan.nd // 2, plan.win, LANES), BF)
    return pl.pallas_call(
        functools.partial(middle_kernel, plan),
        out_shape=(
            jax.ShapeDtypeStruct((rows, D), BF),
            jax.ShapeDtypeStruct((rows, D), F32),
            jax.ShapeDtypeStruct((rows, D), BF),
            windows,
            windows,
            jax.ShapeDtypeStruct((8, LANES), F32),
            jax.ShapeDtypeStruct((8, D), F32),
        ),
        in_specs=[VMEM] * (len(late) + 8) + [SMEM],
        out_specs=(VMEM,) * 7,
        scratch_shapes=[
            pltpu.VMEM((rows, LANES), F32),
            pltpu.VMEM((rows, FF), BF),
            pltpu.VMEM((rows, FF), BF),
            pltpu.VMEM((round_up(plan.start[-1] + plan.win - ROW_OUT, 8), LANES), F32),
            pltpu.VMEM((D, D), BF),
            pltpu.VMEM((D, FF), BF),
            pltpu.VMEM((FF, D), BF),
        ],
        compiler_params=params(36),
        cost_estimate=QUICK,
    )(*late, tokens, cot, o, ot, head, kept, vec, keep_row, patches)


def stack_kernel(
    vec_ref,
    hat_in_ref,
    q_ref,
    k_ref,
    v_ref,
    do_ref,
    whole_ref,
    vab,
    qab,
    dab,
    kt,
    inner_sums,
    normed_ref,
    token_ref,
):
    for step in range(TILES):
        at = rows_at(step)
        grads = do_ref[at, :]
        for hp in range(PAIRS):
            lanes = slice(hp * LANES, (hp + 1) * LANES)
            put_blocks(vab, hp, step, v_ref[at, lanes])
            qab[hp, step] = stack_heads(q_ref[at, lanes])
            dab[hp, step] = stack_heads(grads[:, lanes])
        kt[:, at] = jnp.transpose(k_ref[at, :].astype(F32)).astype(BF)
        both = jnp.transpose(grads.astype(F32)) * whole_ref[step]
        for head in range(HEADS):
            inner_sums[step, head : head + 1, :] = jnp.sum(
                both[head * HD : (head + 1) * HD], axis=0, keepdims=True
            )
        normed = hat_in_ref[at, :] * vec_ref[0:1, :] + vec_ref[1:2, :]
        normed_ref[:, at] = jnp.transpose(normed).astype(BF)
    token_ref[...] = jnp.zeros_like(token_ref)


def stack_part(vec, hat_in, q, k, v, do, whole):
    stacked = jax.ShapeDtypeStruct((PAIRS, TILES, 2 * TILE, LANES), BF)
    return pl.pallas_call(
        stack_kernel,
        out_shape=(
            jax.ShapeDtypeStruct((PAIRS, BLOCKS, 2, LANES, LANES), BF),
            stacked,
            stacked,
            jax.ShapeDtypeStruct((D, SEQ), BF),
            jax.ShapeDtypeStruct((TILES, 8, TILE), F32),
            jax.ShapeDtypeStruct((D, SEQ), BF),
            jax.ShapeDtypeStruct((8, LANES), F32),
        ),
        in_specs=[VMEM] * 7,
        out_specs=(VMEM,) * 7,
        compiler_params=params(16),
        cost_estimate=QUICK,
    )(vec, hat_in, q, k, v, do, whole)


def backward_kernel(
    plan,
    vec_ref,
    seg_smem,
    seg_ref,
    lse_ref,
    q_ref,
    do_ref,
    hat_ref,
    rstd_ref,
    segk,
    kab,
    vab,
    qab,
    dab,
    kt,
    inner_sums,
    token_ref,
    low_ref,
    gains_ref,
    dqt,
    dk,
    dv,
):
    matrix = head_mean_matrix()
    dqt[...] = jnp.zeros_like(dqt)
    dk[...] = jnp.zeros_like(dk)
    dv[...] = jnp.zeros_like(dv)
    gains_ref[...] = jnp.zeros_like(gains_ref)

    def query_tile(ti, carry):
        row_seg = seg_ref[:, rows_at(ti)].astype(F32)
        first, count = key_chunks(seg_smem, ti)

        def key_chunk(c, inner):
            block = first + 2 * c
            keys = keys_at(block)
            column = segk[keys, :]
            bias = tile_bias(ti, block, row_seg, jnp.concatenate([column, column], axis=1))
            raw = []
            for hp in range(PAIRS):
                lanes = slice(hp * LANES, (hp + 1) * LANES)
                raw.append(
                    (
                        nt(two_blocks(kab, hp, block), q_ref[rows_at(ti), lanes]),
                        nt(two_blocks(vab, hp, block), do_ref[rows_at(ti), lanes]),
                    )
                )
            probs, dscores = [], []
            for head in range(HEADS):
                scores, grads = raw[head // 2]
                prob = jnp.exp2(
                    side_rows(scores, head % 2) * score_scale
                    + (bias - lse_ref[ti, head : head + 1, :])
                )
                dscore = prob * (side_rows(grads, head % 2) - inner_sums[ti, head : head + 1, :])
                probs.append(prob.astype(BF))
                dscores.append(dscore.astype(BF))
            for hp in range(PAIRS):
                pair = slice(2 * hp, 2 * hp + 2)
                for head in (2 * hp, 2 * hp + 1):
                    at = slice(head * HD, (head + 1) * HD)
                    dqt[ti, at, :] += nn(kt[at, keys], dscores[head])
                dv[hp, keys] += nn(jnp.concatenate(probs[pair], axis=1), dab[hp, ti])
                dk[hp, keys] += nn(jnp.concatenate(dscores[pair], axis=1), qab[hp, ti])
            return inner

        lax.fori_loop(0, count, key_chunk, 0)
        return carry

    lax.fori_loop(0, TILES, query_tile, 0)

    def finish(step, carry):
        at = rows_at(step)

        def head_norm_back(part, gain, grad):
            lanes = slice(part * D, (part + 1) * D)
            hat = hat_ref[at, lanes]
            both = grad * hat
            gains_ref[part : part + 1, :] += jnp.sum(both, axis=0, keepdims=True)
            scaled = grad * gain
            mean_grad = head_mean_low(scaled.astype(BF), matrix)
            mean_both = head_mean_low((both * gain).astype(BF), matrix)
            back = rstd_ref[at, lanes] * (scaled - mean_grad - hat * mean_both)
            low_ref[at, lanes] = back.astype(BF)

        grad_k = jnp.concatenate([dk[hp, at] for hp in range(PAIRS)], axis=1) * grad_scale
        grad_v = jnp.concatenate([dv[hp, at] for hp in range(PAIRS)], axis=1)
        head_norm_back(0, vec_ref[2:3, :], jnp.transpose(dqt[step]) * grad_scale)
        head_norm_back(1, vec_ref[3:4, :], grad_k)
        low_ref[at, 2 * D :] = grad_v.astype(BF)
        return carry

    lax.fori_loop(0, TILES, finish, 0)


def backward(plan, vec, seg, seg_row, lse, q, do, hat, rstd, segk, stacks, token):
    rows = q.shape[0]
    return pl.pallas_call(
        functools.partial(backward_kernel, plan),
        out_shape=(
            jax.ShapeDtypeStruct((rows, 3 * D), BF),
            jax.ShapeDtypeStruct((8, D), F32),
        ),
        in_specs=[VMEM, SMEM] + [VMEM] * 14,
        out_specs=(VMEM, VMEM),
        scratch_shapes=[
            pltpu.VMEM((TILES, D, TILE), F32),
            pltpu.VMEM((PAIRS, SEQ, LANES), F32),
            pltpu.VMEM((PAIRS, SEQ, LANES), F32),
        ],
        compiler_params=params(26),
        cost_estimate=QUICK,
    )(vec, seg, seg_row, lse, q, do, hat, rstd, segk, *stacks, token)


def finish_kernel(
    plan,
    hat_ref,
    normed_ref,
    wq_ref,
    tail_ref,
    low_ref,
    gqk_ref,
    da1_ref,
    near_ref,
    *refs,
):
    *far_refs, gains, flat = refs
    hat = hat_ref[...]
    for i in range(3):
        part = nn(normed_ref[...], low_ref[:, i * D : (i + 1) * D])
        for j in range(D // LANES):
            flat[pl.ds(i * (D // LANES) + j, D, stride=3 * D // LANES), :] = part[
                :, j * LANES : (j + 1) * LANES
            ]
    da1 = nt(low_ref[...], wq_ref[...])
    da1_ref[...] = da1
    gains[...] = jnp.zeros_like(gains)
    gains[0:1, :] = jnp.sum(da1 * hat, axis=0, keepdims=True)
    gains[1:2, :] = jnp.sum(da1, axis=0, keepdims=True)
    gains[2:4, :] = gqk_ref[0:2, :]
    flat[ROW_OUT : ROW_OUT + 8, :] = tail_ref[...]
    dp = lax.axis_index("dp")
    side = jnp.bitwise_and(dp, 1)
    vector_rows = []
    for t in range(4):
        for j in range(D // LANES):
            vector_rows.append(gains[t : t + 1, j * LANES : (j + 1) * LANES])
    spare = plan.tail - plan.most - EARLY_VEC_ROWS
    if spare:
        vector_rows.append(jnp.zeros((spare, LANES), F32))
    for k in range(plan.nd):
        first = plan.start[k]
        reld = jnp.right_shift(jnp.bitwise_xor(dp, k), 1)
        window = flat[first : first + plan.tail, :]
        if k == plan.nd - 1:
            window = jnp.concatenate([window[: plan.most], *vector_rows], axis=0)
        window = window.astype(BF)

        @pl.when(side == k % 2)
        def _():
            near_ref[reld] = window

        @pl.when(side != k % 2)
        def _():
            for (low, high), far_ref in zip(plan.far, far_refs):
                far_ref[reld] = window[low:high]


def finish_part(plan, hat, normed, wq, tail, low, gains):
    rows = hat.shape[0]
    windows = jax.ShapeDtypeStruct((plan.nd // 2, plan.tail, LANES), BF)
    parts = tuple(
        jax.ShapeDtypeStruct((plan.nd // 2, high - low, LANES), BF) for low, high in plan.far
    )
    return pl.pallas_call(
        functools.partial(finish_kernel, plan),
        out_shape=(jax.ShapeDtypeStruct((rows, D), F32), windows) + parts,
        in_specs=[VMEM] * 6,
        out_specs=(VMEM,) * (2 + FAR_PARTS),
        scratch_shapes=[
            pltpu.VMEM((8, D), F32),
            pltpu.VMEM((round_up(plan.start[plan.nd - 1] + plan.tail, 8), LANES), F32),
        ],
        compiler_params=params(28),
        cost_estimate=QUICK,
    )(hat, normed, wq, tail, low, gains)


def input_kernel(
    plan,
    hat_ref,
    rstd_ref,
    vec_ref,
    da1_ref,
    dh1_ref,
    master_ref,
    moment_ref,
    second_ref,
    grad_ref,
    master_rows,
    moment_rows,
    second_rows,
    squares_ref,
):
    back = norm_back(hat_ref[...], rstd_ref[:, 0:1], da1_ref[...] * vec_ref[0:1, :])
    grad_ref[...] = dh1_ref[...] + back
    master = flat_to_rows(plan, master_ref, master_rows)
    flat_to_rows(plan, moment_ref, moment_rows)
    flat_to_rows(plan, second_ref, second_rows)
    _, index = flat_place(plan, master.shape)
    squares_ref[...] = jnp.broadcast_to(tensor_sums(master * master, index), squares_ref.shape)


def input_part(plan, hat, rstd, vec, da1, dh1, master, moment, second):
    rows = jax.ShapeDtypeStruct((plan.win, LANES), F32)
    return pl.pallas_call(
        functools.partial(input_kernel, plan),
        out_shape=(
            jax.ShapeDtypeStruct(dh1.shape, F32),
            rows,
            rows,
            rows,
            jax.ShapeDtypeStruct((8, LANES), F32),
        ),
        in_specs=[VMEM] * 8,
        out_specs=(VMEM,) * 5,
        compiler_params=params(16),
        cost_estimate=QUICK,
    )(hat, rstd, vec, da1, dh1, master, moment, second)


def flat_place(plan, shape):
    row = lax.broadcasted_iota(jnp.int32, shape, 0)
    lane = lax.broadcasted_iota(jnp.int32, shape, 1)
    place = row * LANES + lane
    return place, plan.device() * plan.shard + place


def tensor_sums(squares, index):
    lanes = lax.broadcasted_iota(jnp.int32, (1, LANES), 1)
    row = jnp.zeros((1, LANES), F32)
    for t in range(MATS):
        mine = jnp.logical_and(index >= BOUNDS[t], index < BOUNDS[t + 1])
        part = jnp.sum(jnp.where(mine, squares, 0.0), axis=0, keepdims=True)
        row = jnp.where(lanes == t, jnp.sum(part, axis=1, keepdims=True), row)
    return row


def update_kernel(
    plan,
    own_ref,
    got0_ref,
    got1_ref,
    got2_ref,
    master_ref,
    moment_ref,
    second_ref,
    squares_ref,
    new_moment_ref,
    new_second_ref,
    update_ref,
    sums_ref,
    window,
):
    bucket = lax.axis_index("bucket")
    dp = lax.axis_index("dp")
    total = tree_sum([ref[...].astype(F32) for ref in (own_ref, got0_ref, got1_ref, got2_ref)])
    window[...] = total[: plan.win]

    @pl.when(jnp.logical_and(bucket == plan.nb - 1, dp == plan.nd - 1))
    def _():
        window[plan.vec_place : plan.vec_place + EARLY_VEC_ROWS, :] = total[
            plan.most : plan.most + EARLY_VEC_ROWS
        ]

    offset = lax.rem(plan.device() * plan.shard, LANES)
    back = lax.rem(LANES - offset, LANES)
    turned = pltpu.roll(window[...], back, 1)
    above = pltpu.roll(turned, plan.win - 1, 0)
    lane = lax.broadcasted_iota(jnp.int32, turned.shape, 1)
    place, index = flat_place(plan, turned.shape)
    inside = place < plan.shard
    grad = jnp.where(inside, jnp.where(lane + offset < LANES, turned, above), 0.0)
    master = master_ref[...]
    moment = beta_one * moment_ref[...] + (1.0 - beta_one) * grad
    second = beta_two * second_ref[...] + (1.0 - beta_two) * grad * grad
    first_hat = moment / (1.0 - beta_one**STEP)
    second_hat = second / (1.0 - beta_two**STEP)
    decay = jnp.where(index < BOUNDS[4], weight_decay, 0.0)
    update = first_hat / (jnp.sqrt(second_hat) + adam_epsilon) + decay * master
    update = jnp.where(inside, update, 0.0)
    new_moment_ref[...] = moment
    new_second_ref[...] = second
    update_ref[...] = update
    rows = [squares_ref[0:1, :], tensor_sums(update * update, index), jnp.zeros((6, LANES), F32)]
    sums_ref[...] = jnp.concatenate(rows, axis=0)


def update_part(plan, parts, master, moment, second, squares):
    rows = jax.ShapeDtypeStruct((plan.win, LANES), F32)
    return pl.pallas_call(
        functools.partial(update_kernel, plan),
        out_shape=(rows, rows, rows, jax.ShapeDtypeStruct((8, LANES), F32)),
        in_specs=[VMEM] * 8,
        out_specs=(VMEM,) * 4,
        scratch_shapes=[pltpu.VMEM((plan.win, LANES), F32)],
        compiler_params=params(12),
    )(*parts, master, moment, second, squares)


def flatten_kernel(plan, moment_ref, second_ref, new_moment_ref, new_second_ref, token_ref):
    rows_to_flat(plan, moment_ref[...], new_moment_ref)
    rows_to_flat(plan, second_ref[...], new_second_ref)
    token_ref[...] = jnp.zeros_like(token_ref)


def flatten_part(plan, moment, second):
    flat = jax.ShapeDtypeStruct((plan.shard,), F32)
    return pl.pallas_call(
        functools.partial(flatten_kernel, plan),
        out_shape=(flat, flat, jax.ShapeDtypeStruct((8, LANES), F32)),
        in_specs=[VMEM] * 2,
        out_specs=(VMEM,) * 3,
        compiler_params=params(8),
        cost_estimate=QUICK,
    )(moment, second)


def apply_kernel(plan, *refs):
    *sums_refs, master_ref, update_ref, _, new_ref, norms_ref, trust_ref = refs
    roots = jnp.sqrt(tree_sum([ref[...] for ref in sums_refs]))
    trust = roots[0:1, :] / (roots[1:2, :] + adam_epsilon)
    norms_ref[...] = roots[0:2, :MATS]
    trust_ref[...] = trust[:, :MATS]
    master = master_ref[...]
    _, index = flat_place(plan, master.shape)
    factors = jnp.broadcast_to(trust[:, 0:1], master.shape)
    for t in range(1, MATS):
        factors = jnp.where(index >= BOUNDS[t], trust[:, t : t + 1], factors)
    rows_to_flat(plan, master - learn_rate * factors * update_ref[...], new_ref)


def apply_part(plan, sums, master, update_rows, token):
    return pl.pallas_call(
        functools.partial(apply_kernel, plan),
        out_shape=(
            jax.ShapeDtypeStruct((plan.shard,), F32),
            jax.ShapeDtypeStruct((2, MATS), F32),
            jax.ShapeDtypeStruct((1, MATS), F32),
        ),
        in_specs=[VMEM] * (len(sums) + 3),
        out_specs=(VMEM,) * 3,
        compiler_params=params(8),
    )(*sums, master, update_rows, token)


def lay_column_kernel(count, *refs):
    for i, part in enumerate(refs[:count]):
        refs[-1][i] = part[...]


def lay_column(parts, *after):
    return pl.pallas_call(
        functools.partial(lay_column_kernel, len(parts)),
        out_shape=jax.ShapeDtypeStruct((len(parts), *parts[0].shape), parts[0].dtype),
        in_specs=[VMEM] * (len(parts) + len(after)),
        out_specs=VMEM,
        compiler_params=params(4),
    )(*parts, *after)


def lay_lower_kernel(plan, mine_ref, got_ref, count_ref, out_ref):
    half = mine_ref.shape[0]
    out_ref[:half] = mine_ref[...]
    out_ref[half:] = got_ref[...]
    last = mine_ref[0, -16:, :].astype(F32)
    out_ref[0, plan.win - plan.upper - 16 :, :] = (last + count_ref[...]).astype(BF)


def lay_lower(plan, mine, got, count):
    half, height, _ = mine.shape
    return pl.pallas_call(
        functools.partial(lay_lower_kernel, plan),
        out_shape=jax.ShapeDtypeStruct((2 * half, height, LANES), BF),
        in_specs=[VMEM] * 3,
        out_specs=VMEM,
        compiler_params=params(4),
    )(mine, got, count)


def choose_kernel(plan, *refs):
    columns, (lower_ref, early_ref), late_refs = (
        refs[: plan.nb],
        refs[plan.nb : plan.nb + 2],
        refs[plan.nb + 2 :],
    )
    bucket = lax.axis_index("bucket")
    early_ref[:, plan.kept_row :] = lower_ref[:, 0, plan.win - plan.upper - 16 :]
    for i, part in enumerate(columns):
        for owner, out_ref in enumerate((early_ref, *late_refs)):

            @pl.when(jnp.bitwise_xor(bucket, i) == owner)
            def _():
                out_ref[:, : plan.upper] = part[...]
                out_ref[:, plan.upper : plan.win] = lower_ref[:, i]

    early_ref[:, plan.win : plan.kept_row] = late_refs[-1][:, plan.vec_from :]


def choose(plan, columns, lower):
    step = columns[0].shape[0]
    late = jax.ShapeDtypeStruct((step, plan.win, LANES), BF)
    return pl.pallas_call(
        functools.partial(choose_kernel, plan),
        out_shape=(jax.ShapeDtypeStruct((step, plan.early, LANES), BF),) + (late,) * (plan.nb - 1),
        in_specs=[VMEM] * (len(columns) + 1),
        out_specs=(VMEM,) * plan.nb,
        compiler_params=params(10),
    )(*columns, lower)


def add_parts_kernel(halves, *refs):
    refs = list(refs)
    parts = [[refs.pop(0) for _ in range(count)] for count in halves]
    for i, out in enumerate(refs[1:-1]):
        step = out.shape[-3]
        at = slice(i * step, (i + 1) * step)
        at = (slice(None), at) if len(out.shape) == 4 else at
        values = [
            jnp.concatenate([half[at].astype(F32) for half in part], axis=-2) for part in parts
        ]
        out[...] = tree_sum(values).astype(out.dtype)
    refs[-1][...] = jnp.zeros_like(refs[-1])


def add_parts(parts, pieces, token):
    *lead, total, height, width = parts[0].shape
    parts = [part if isinstance(part, list) else [part] for part in parts]
    halves = [len(part) for part in parts]
    parts = [half for part in parts for half in part]
    return pl.pallas_call(
        functools.partial(add_parts_kernel, halves),
        out_shape=tuple(
            jax.ShapeDtypeStruct((*lead, total // pieces, height, width), BF if i else F32)
            for i in range(pieces)
        )
        + (jax.ShapeDtypeStruct((8, LANES), F32),),
        in_specs=[VMEM] * (len(parts) + 1),
        out_specs=(VMEM,) * (pieces + 1),
        compiler_params=params(14),
    )(*parts, token)


def blend_kernel(plan, late_count, *refs):
    late, parts, outs = refs[:late_count], refs[late_count + 1 : -plan.nb], refs[-plan.nb :]
    bucket = lax.axis_index("bucket")
    first = tree_sum([part[...].astype(F32) for part in parts])
    for i, out in enumerate(outs):
        owner = jnp.bitwise_xor(bucket, i)
        quarter = jnp.maximum(owner - 1, 0)
        window = late[0][quarter]
        if late_count > 1:
            window = window + tree_sum([ref[quarter].astype(F32) for ref in late[1:]])
        if plan.tail > plan.win:
            empty = jnp.zeros((plan.tail - plan.win, LANES), F32)
            window = jnp.concatenate([window, empty], axis=0)
        row = lax.broadcasted_iota(jnp.int32, first.shape, 0)
        takes_first = jnp.logical_or(row >= plan.most, owner == 0)
        out[...] = jnp.where(takes_first, first, window).astype(out.dtype)


def blend(plan, late, token, parts):
    return pl.pallas_call(
        functools.partial(blend_kernel, plan, len(late)),
        out_shape=tuple(
            jax.ShapeDtypeStruct((plan.tail, LANES), BF if i else F32) for i in range(plan.nb)
        ),
        in_specs=[VMEM] * (len(late) + 1 + len(parts)),
        out_specs=(VMEM,) * plan.nb,
        compiler_params=params(10),
    )(*late, token, *parts)


def add_rows_kernel(*refs):
    refs[-1][...] = tree_sum([ref[...] for ref in refs[:-1]])


def add_rows(parts):
    return pl.pallas_call(
        add_rows_kernel,
        out_shape=jax.ShapeDtypeStruct(parts[0].shape, F32),
        in_specs=[VMEM] * len(parts),
        out_specs=VMEM,
        compiler_params=params(4),
    )(*parts)


def groups_of(size, skip=0):
    bits = list(range(skip, size.bit_length() - 1))
    return [bits[i : i + 2] for i in range(0, len(bits), 2)]


def masks_of(bits):
    masks = [1 << bits[0]]
    if len(bits) == 2:
        masks += [1 << bits[1], (1 << bits[0]) | (1 << bits[1])]
    return masks


def swap(x, axis, size, mask):
    return lax.ppermute(x, axis, [(i, i ^ mask) for i in range(size)])


def tree_sum(parts):
    if len(parts) == 1:
        return parts[0]
    half = len(parts) // 2
    return tree_sum(parts[:half]) + tree_sum(parts[half:])


def with_partners(x, axis, size, bits):
    return [x] + [swap(x, axis, size, mask) for mask in masks_of(bits)]


def gather_windows(plan, upper, lower, count):
    first, *more = groups_of(plan.nd, 1)
    (bits,) = groups_of(plan.nb)
    near, distant = masks_of(bits)[:2]
    lower = lay_column([lower, swap(lower, "bucket", plan.nb, near)])
    lower = lay_lower(plan, lower, swap(lower, "bucket", plan.nb, distant), count)
    column = lay_column(with_partners(upper, "dp", plan.nd, first), lower)
    for group in more:
        column = jnp.concatenate(with_partners(column, "dp", plan.nd, group), axis=0)
    columns = with_partners(column, "bucket", plan.nb, bits)
    lower = lay_column(with_partners(lower, "dp", plan.nd, first))
    for group in more:
        lower = jnp.concatenate(with_partners(lower, "dp", plan.nd, group), axis=0)
    early, *late = choose(plan, columns, lower)
    others = [swap(x, "dp", plan.nd, 1) for x in (early, *late)]
    return (early, others[0]), (*late, *others[1:])


def scatter_dp(plan, pieces):
    *more, last = groups_of(plan.nd, 1)
    sent = list(zip(pieces[1:], masks_of(last)))
    got = [pieces[0]] + [
        swap(piece, "dp", plan.nd, mask) for piece, mask in sent[1:] + sent[:1]
    ]
    for bits in reversed(more):
        held = tree_sum([x.astype(F32) for x in got])
        size = 1 << len(bits)
        step = held.shape[-3] // size
        parts = [held[..., i * step : (i + 1) * step, :, :] for i in range(size)]
        got = [parts[0]] + [
            swap(part.astype(BF), "dp", plan.nd, mask)
            for part, mask in zip(parts[1:], masks_of(bits))
        ]
    return [x.reshape(*x.shape[:-3], *x.shape[-2:]) for x in got]


def sum_all(plan, x):
    x = [x, swap(x, "dp", plan.nd, 1)]
    for bits in groups_of(plan.nd, 1):
        x = with_partners(add_rows(x), "dp", plan.nd, bits)
    (bits,) = groups_of(plan.nb)
    return with_partners(add_rows(x), "bucket", plan.nb, bits)


def local(
    plan, tokens, cotangent, segment_ids, keep_mask, bucket_patches, master, first_moment, second_moment
):
    seg_row = segment_ids.reshape(1, SEQ)
    keep_row = keep_mask.reshape(1, SEQ)
    pieces_of = 1 << len(groups_of(plan.nd, 1)[-1])
    (b_bits,) = groups_of(plan.nb)

    hat_in, rstd_in, count = ahead(tokens, keep_row)
    early, late = gather_windows(plan, *prepare(plan, master), count)
    wq, vec, head, kept, q, k, v, hat, rstd = project_part(plan, *early, hat_in)
    o, ot, whole, lse, kab, segk = forward(plan, segment_ids, seg_row, keep_row, q, k, v)
    block_output, dh1, do, near, far, tail, _ = middle_part(
        plan, late, tokens, cotangent, o, ot, head, kept, vec, keep_row, bucket_patches
    )
    *stacks, normed, token = stack_part(vec, hat_in, q, k, v, do, whole)
    *pieces, token = add_parts([near, swap(far, "dp", plan.nd, 1)], pieces_of, token)
    rest = scatter_dp(plan, pieces)
    low, gains = backward(
        plan, vec, segment_ids, seg_row, lse, q, do, hat, rstd, segk, [kab, *stacks], token
    )
    da1, near, *far = finish_part(plan, hat_in, normed, wq, tail, low, gains)
    input_grad, *old_rows, squares = input_part(
        plan, hat_in, rstd_in, vec, da1, dh1, master, first_moment, second_moment
    )
    *late_parts, token = add_parts(rest[:2], 1, gains)
    late_parts += rest[2:]
    *pieces, _ = add_parts([near, [swap(half, "dp", plan.nd, 1) for half in far]], pieces_of, token)
    first = scatter_dp(plan, pieces)
    mine, *sent = blend(plan, late_parts, squares, first)
    sent = list(zip(sent, masks_of(b_bits)))
    parts = [mine] + [swap(x, "bucket", plan.nb, mask) for x, mask in sent[::-1]]
    first_rows, second_rows, update_rows, sums = update_part(plan, parts, *old_rows, squares)
    new_first, new_second, token = flatten_part(plan, first_rows, second_rows)
    new_master, norms, trust = apply_part(
        plan, sum_all(plan, sums), old_rows[0], update_rows, token
    )
    return (
        block_output,
        input_grad,
        new_first,
        new_second,
        new_master,
        norms,
        trust.reshape(MATS),
    )


def solution(mesh):
    shards = mesh.shape["bucket"] * mesh.shape["dp"]
    plan = Plan(mesh.shape, PARAMS // shards)
    both = ("bucket", "dp")
    return jax.shard_map(
        functools.partial(local, plan),
        mesh=mesh,
        in_specs=(P(both, None), P(both, None), P(both), P(both), P(), P(both), P(both), P(both)),
        out_specs=(P(both, None), P(both, None), P(both), P(both), P(both), P(), P()),
        check_vma=False,
    )
```

```python
import functools
import math

import jax
import jax.numpy as jnp
from jax import lax
from jax.experimental import pallas as pl
from jax.experimental.pallas import tpu as pltpu
from jax.sharding import PartitionSpec as P

D = 384
HEADS = 6
HD = 64
FF = 1536
SEQ = 1024
STEP = 10
MATS = 10
LANES = 128
PAIRS = HEADS // 2
TILE = 256
TILES = SEQ // TILE
BLOCKS = SEQ // LANES
MIDDLE_BLOCK = 512
FAR_PARTS = 3

norm_epsilon = 1e-06
adam_epsilon = 1e-06
beta_one = 0.9
beta_two = 0.999
learn_rate = 0.5
weight_decay = 0.01
masked_score = -1e30

MATRIX_END = 4 * D * D + 2 * D * FF
BOUNDS = [0, 3 * D * D, 4 * D * D, 4 * D * D + D * FF, MATRIX_END] + [
    MATRIX_END + (j + 1) * D for j in range(6)
]
PARAMS = BOUNDS[-1]
ROW_OUT = BOUNDS[1] // LANES
ROW_UP = BOUNDS[2] // LANES
ROW_DOWN = BOUNDS[3] // LANES
ROW_VEC = BOUNDS[4] // LANES
VEC_ROWS = 6 * D // LANES
EARLY_VEC_ROWS = 4 * D // LANES
ROWS_ALL = PARAMS // LANES

score_scale = HD ** (-0.5) * math.log2(math.e)
grad_scale = HD ** (-0.5)

BF = jnp.bfloat16
F32 = jnp.float32
VMEM = pl.BlockSpec(memory_space=pltpu.VMEM)
SMEM = pl.BlockSpec(memory_space=pltpu.SMEM)


QUICK = pl.CostEstimate(flops=1000, bytes_accessed=1000, transcendentals=0)


def params(limit):
    return pltpu.CompilerParams(vmem_limit_bytes=limit * 1024 * 1024)


def round_up(value, step):
    return -(-value // step) * step


class Plan:
    def __init__(self, mesh_shape, shard):
        self.nb = mesh_shape["bucket"]
        self.nd = mesh_shape["dp"]
        self.n = self.nb * self.nd
        self.shard = shard
        self.start = [k * shard // LANES for k in range(self.n)]
        self.rows = [
            -(-((k + 1) * shard) // LANES) - self.start[k] for k in range(self.n)
        ]
        self.win = round_up(max(self.rows) + 1, 16)
        self.most = max(self.rows)
        self.tail = round_up(self.most + EARLY_VEC_ROWS, 16)
        units = self.tail // 16
        ends = [units * (i + 1) // FAR_PARTS * 16 for i in range(FAR_PARTS)]
        self.far = list(zip([0] + ends[:-1], ends))
        self.upper = self.win * 13 // 16 // 16 * 16
        self.vec_place = ROW_VEC - self.start[-1]
        self.vec_from = self.vec_place // 16 * 16
        self.kept_row = 2 * self.win - self.vec_from
        self.early = self.kept_row + 16

    def device(self):
        return lax.axis_index("bucket") * self.nd + lax.axis_index("dp")


def nn(a, b):
    return lax.dot_general(a, b, (((1,), (0,)), ((), ())), preferred_element_type=F32)


def nt(a, b):
    return lax.dot_general(a, b, (((1,), (1,)), ((), ())), preferred_element_type=F32)


def split_low(x):
    high = x.astype(BF)
    return high, (x - high.astype(F32)).astype(BF)


def rows_at(step):
    if isinstance(step, int):
        return slice(step * TILE, (step + 1) * TILE)
    return pl.ds(pl.multiple_of(step * TILE, TILE), TILE)


def norm_parts(values):
    average = jnp.mean(values, axis=-1, keepdims=True)
    centered = values - average
    variance = jnp.mean(centered * centered, axis=-1, keepdims=True)
    rstd = lax.rsqrt(variance + norm_epsilon)
    return centered * rstd, rstd


def norm_back(hat, rstd, grad):
    mean_grad = jnp.mean(grad, axis=-1, keepdims=True)
    mean_both = jnp.mean(grad * hat, axis=-1, keepdims=True)
    return rstd * (grad - mean_grad - hat * mean_both)


def head_mean_matrix():
    row = lax.broadcasted_iota(jnp.int32, (TILE, TILE), 0)
    col = lax.broadcasted_iota(jnp.int32, (TILE, TILE), 1)
    return jnp.where(row // HD == col // HD, 1.0 / HD, 0.0).astype(BF)


def head_mean_low(low, matrix):
    rest = D - TILE
    return jnp.concatenate(
        [nn(low[:, :TILE], matrix), nn(low[:, TILE:], matrix[:rest, :rest])], axis=1
    )


def head_mean(x, matrix):
    high, rest = split_low(x)
    return head_mean_low(high, matrix) + head_mean_low(rest, matrix)


def flat_to_rows(plan, flat_ref, rows_ref):
    full, rest = divmod(plan.shard, LANES)
    rows_ref[full:, :] = jnp.zeros((plan.win - full, LANES), F32)
    rows_ref[:full, :] = flat_ref[: full * LANES].reshape(full, LANES)
    if rest:
        rows_ref[full : full + 1, :rest] = flat_ref[full * LANES :].reshape(1, rest)
    return rows_ref[...]


def rows_to_flat(plan, rows, flat_ref):
    full, rest = divmod(plan.shard, LANES)
    flat_ref[: full * LANES] = rows[:full].reshape(full * LANES)
    if rest:
        flat_ref[full * LANES :] = rows[full : full + 1, :rest].reshape(rest)


def prepare_kernel(plan, master_ref, upper_ref, lower_ref, rows_ref):
    offset = lax.rem(plan.device() * plan.shard, LANES)
    values = flat_to_rows(plan, master_ref, rows_ref)
    turned = pltpu.roll(values, offset, 1)
    below = pltpu.roll(turned, 1, 0)
    lane = lax.broadcasted_iota(jnp.int32, values.shape, 1)
    window = jnp.where(lane < offset, below, turned).astype(BF)
    upper_ref[...] = window[: plan.upper]
    lower_ref[...] = window[plan.upper :]


def prepare(plan, master):
    return pl.pallas_call(
        functools.partial(prepare_kernel, plan),
        out_shape=(
            jax.ShapeDtypeStruct((plan.upper, LANES), BF),
            jax.ShapeDtypeStruct((plan.win - plan.upper, LANES), BF),
        ),
        in_specs=[VMEM],
        out_specs=(VMEM, VMEM),
        scratch_shapes=[pltpu.VMEM((plan.win, LANES), F32)],
        compiler_params=params(8),
    )(master)


def ahead_kernel(tokens_ref, keep_ref, hat_ref, rstd_ref, count_ref):
    hat, rstd = norm_parts(tokens_ref[...].astype(F32))
    hat_ref[...] = hat
    rstd_ref[...] = jnp.broadcast_to(rstd, rstd_ref.shape)
    row = lax.broadcasted_iota(jnp.int32, count_ref.shape, 0)
    lane = lax.broadcasted_iota(jnp.int32, count_ref.shape, 1)
    count = jnp.sum(keep_ref[...].astype(F32), axis=1, keepdims=True)
    high = jnp.floor(count * (1.0 / 32.0))
    parts = jnp.where(lane == 0, high, jnp.where(lane == 1, count - 32.0 * high, 0.0))
    count_ref[...] = jnp.where(row == 15, parts, 0.0)


def ahead(tokens, keep_row):
    rows = tokens.shape[0]
    return pl.pallas_call(
        ahead_kernel,
        out_shape=(
            jax.ShapeDtypeStruct((rows, D), F32),
            jax.ShapeDtypeStruct((rows, LANES), F32),
            jax.ShapeDtypeStruct((16, LANES), F32),
        ),
        in_specs=[VMEM, VMEM],
        out_specs=(VMEM,) * 3,
        compiler_params=params(12),
        cost_estimate=QUICK,
    )(tokens, keep_row)


def held_window(own_ref, other_ref, rel, at):
    place = jnp.right_shift(rel, 1)
    return jnp.where(
        jnp.bitwise_and(rel, 1) == 0,
        own_ref[place, at].astype(F32),
        other_ref[place, at].astype(F32),
    )


def lay_windows(plan, owners, refs_of, flat, base):
    dp = lax.axis_index("dp")
    for k in owners:
        own_ref, other_ref = refs_of(k)
        window = held_window(own_ref, other_ref, jnp.bitwise_xor(dp, k % plan.nd), slice(0, plan.win))
        first, count = plan.start[k] - base, plan.rows[k]
        shared = k > 0 and (k * plan.shard) % LANES
        if shared:
            before = flat[first : first + 1, :]
        flat[first : first + count, :] = window[:count]
        if shared:
            flat[first : first + 1, :] = before + window[:1]


def take_matrix(target, flat, base, height, width):
    stride = width // LANES
    for j in range(stride):
        target[:, j * LANES : (j + 1) * LANES] = flat[pl.ds(base + j, height, stride=stride), :].astype(BF)


def put_matrix(flat, base, source, height, width):
    stride = width // LANES
    for j in range(stride):
        flat[pl.ds(base + j, height, stride=stride), :] = source[:, j * LANES : (j + 1) * LANES]


def key_chunks(seg_ref, ti):
    first_i, last_i = seg_ref[ti * TILE], seg_ref[ti * TILE + TILE - 1]
    low, high = jnp.int32(0), jnp.int32(0)
    for b in range(BLOCKS):
        low += (seg_ref[b * LANES + LANES - 1] < first_i).astype(jnp.int32)
        high += (seg_ref[b * LANES] <= last_i).astype(jnp.int32)
    count = jnp.right_shift(high - low + 1, 1)
    return jnp.minimum(low, BLOCKS - 2 * count), count


def tile_bias(ti, block, row_seg, key_seg):
    key_place = lax.broadcasted_iota(jnp.int32, (TILE, TILE), 0) + block * LANES
    row_place = lax.broadcasted_iota(jnp.int32, (TILE, TILE), 1) + ti * TILE
    return jnp.where(
        jnp.logical_or(key_seg == row_seg, key_place == row_place), 0.0, masked_score
    )


def keys_at(block):
    return pl.ds(pl.multiple_of(block * LANES, LANES), TILE)


def side_rows(stacked, side):
    return jnp.concatenate(
        [stacked[side * LANES : (side + 1) * LANES], stacked[(2 + side) * LANES : (3 + side) * LANES]],
        axis=0,
    )


def to_column(row):
    return jnp.transpose(jnp.broadcast_to(row, (LANES, row.shape[1])))


def block_heads(pair):
    lane = lax.broadcasted_iota(jnp.int32, pair.shape, 1)
    zero = jnp.zeros_like(pair)
    sides = [jnp.where(lane < HD, pair, zero), jnp.where(lane >= HD, pair, zero)]
    return [side[b * LANES : (b + 1) * LANES] for b in range(2) for side in sides]


def put_blocks(ref, hp, step, pair):
    for i, part in enumerate(block_heads(pair)):
        ref[hp, 2 * step + i // 2, i % 2] = part


def two_blocks(ref, hp, block):
    return ref[hp, pl.ds(block, 2)].reshape(4 * LANES, LANES)


def stack_heads(pair):
    lane = lax.broadcasted_iota(jnp.int32, pair.shape, 1)
    zero = jnp.zeros_like(pair)
    return jnp.concatenate(
        [jnp.where(lane < HD, pair, zero), jnp.where(lane >= HD, pair, zero)], axis=0
    )


def project_kernel(
    plan,
    own_ref,
    other_ref,
    hat_in_ref,
    wq_ref,
    vec_ref,
    head_ref,
    kept_ref,
    q_ref,
    k_ref,
    v_ref,
    hat_ref,
    rstd_ref,
    flat,
):
    dp = lax.axis_index("dp")
    lay_windows(plan, range(plan.nd), lambda k: (own_ref, other_ref), flat, 0)
    take_matrix(wq_ref, flat, 0, D, 3 * D)
    head_ref[...] = flat[ROW_OUT : ROW_OUT + 8, :]
    rel = jnp.bitwise_xor(dp, plan.nd - 1)
    late = held_window(own_ref, other_ref, rel, slice(plan.win, plan.kept_row))
    kept = jnp.zeros((1, LANES), F32)
    for j in range(plan.nd):
        half = other_ref if j & 1 else own_ref
        kept = kept + half[j >> 1, plan.kept_row :].astype(F32)[15:16]
    kept_ref[...] = jnp.broadcast_to(32.0 * kept[:, 0:1] + kept[:, 1:2], kept_ref.shape)
    for t in range(6):
        for j in range(D // LANES):
            at = plan.vec_place - plan.vec_from + 3 * t + j
            vec_ref[t : t + 1, j * LANES : (j + 1) * LANES] = late[at : at + 1]
    matrix = head_mean_matrix()
    gain1, shift1 = vec_ref[0:1, :], vec_ref[1:2, :]
    gain_q, gain_k = vec_ref[2:3, :], vec_ref[3:4, :]

    raw = nn((hat_in_ref[...] * gain1 + shift1).astype(BF), wq_ref[...])

    def head_norm(low_out, part, gain):
        lanes = slice(part * D, (part + 1) * D)
        x = raw[:, lanes]
        centered = x - head_mean(x, matrix)
        rstd = lax.rsqrt(head_mean(centered * centered, matrix) + norm_epsilon)
        normed = centered * rstd
        hat_ref[:, lanes] = normed
        rstd_ref[:, lanes] = rstd
        low_out[...] = (normed * gain).astype(BF)

    head_norm(q_ref, 0, gain_q)
    head_norm(k_ref, 1, gain_k)
    v_ref[...] = raw[:, 2 * D :].astype(BF)


def project_part(plan, own, other, tokens):
    rows = tokens.shape[0]
    low = jax.ShapeDtypeStruct((rows, D), BF)
    return pl.pallas_call(
        functools.partial(project_kernel, plan),
        out_shape=(
            jax.ShapeDtypeStruct((D, 3 * D), BF),
            jax.ShapeDtypeStruct((8, D), F32),
            jax.ShapeDtypeStruct((8, LANES), F32),
            jax.ShapeDtypeStruct((8, LANES), F32),
            low,
            low,
            low,
            jax.ShapeDtypeStruct((rows, 2 * D), F32),
            jax.ShapeDtypeStruct((rows, 2 * D), F32),
        ),
        in_specs=[VMEM] * 3,
        out_specs=(VMEM,) * 9,
        scratch_shapes=[
            pltpu.VMEM((round_up(plan.start[plan.nd - 1] + plan.win, 8), LANES), F32),
        ],
        compiler_params=params(24),
        cost_estimate=QUICK,
    )(own, other, tokens)


def forward_kernel(
    plan,
    seg_smem,
    seg_ref,
    keep_ref,
    q_ref,
    k_ref,
    v_ref,
    o_ref,
    ot_ref,
    whole_ref,
    lse_ref,
    kab,
    segk,
    vt,
    ot,
    rest_t,
    sums,
    expo,
):
    seg_row = seg_ref[...].astype(F32)
    segk[...] = to_column(jnp.where(keep_ref[...] == 1, seg_row, -1.0))

    for step in range(TILES):
        at = rows_at(step)
        for hp in range(PAIRS):
            put_blocks(kab, hp, step, k_ref[at, hp * LANES : (hp + 1) * LANES])
        vt[:, at] = jnp.transpose(v_ref[at, :].astype(F32)).astype(BF)

    def query_tile(ti, carry):
        ot[...] = jnp.zeros_like(ot)
        rest_t[...] = jnp.zeros_like(rest_t)
        sums[...] = jnp.zeros_like(sums)
        row_seg = seg_ref[:, rows_at(ti)].astype(F32)
        first, count = key_chunks(seg_smem, ti)

        def score_chunk(c, inner):
            block = first + 2 * c
            column = segk[keys_at(block), :]
            bias = tile_bias(ti, block, row_seg, jnp.concatenate([column, column], axis=1))
            for hp in range(PAIRS):
                queries = q_ref[rows_at(ti), hp * LANES : (hp + 1) * LANES]
                scores = nt(two_blocks(kab, hp, block), queries)
                for side in range(2):
                    head = 2 * hp + side
                    value = jnp.exp2(side_rows(scores, side) * score_scale + bias)
                    expo[c, head] = value
                    sums[head : head + 1, :] += jnp.sum(value, axis=0, keepdims=True)
            return inner

        lax.fori_loop(0, count, score_chunk, 0)
        lse_ref[ti] = jnp.log2(sums[...])
        sums[...] = 1.0 / sums[...]

        def value_chunk(c, inner):
            keys = keys_at(first + 2 * c)
            for head in range(HEADS):
                prob, rest = split_low(expo[c, head] * sums[head : head + 1, :])
                at = slice(head * HD, (head + 1) * HD)
                ot[at, :] += nn(vt[at, keys], prob)
                rest_t[at, :] += nn(vt[at, keys], rest)
            return inner

        lax.fori_loop(0, count, value_chunk, 0)
        attended = ot[...]
        ot_ref[ti] = attended.astype(BF)
        whole_ref[ti] = attended + rest_t[...]
        o_ref[rows_at(ti), :] = jnp.transpose(attended).astype(BF)
        return carry

    lax.fori_loop(0, TILES, query_tile, 0)


def forward(plan, seg, seg_row, keep_row, q, k, v):
    rows = q.shape[0]
    return pl.pallas_call(
        functools.partial(forward_kernel, plan),
        out_shape=(
            jax.ShapeDtypeStruct((rows, D), BF),
            jax.ShapeDtypeStruct((TILES, D, TILE), BF),
            jax.ShapeDtypeStruct((TILES, D, TILE), F32),
            jax.ShapeDtypeStruct((TILES, 8, TILE), F32),
            jax.ShapeDtypeStruct((PAIRS, BLOCKS, 2, LANES, LANES), BF),
            jax.ShapeDtypeStruct((SEQ, LANES), F32),
        ),
        in_specs=[SMEM] + [VMEM] * 5,
        out_specs=(VMEM,) * 6,
        scratch_shapes=[
            pltpu.VMEM((D, SEQ), BF),
            pltpu.VMEM((D, TILE), F32),
            pltpu.VMEM((D, TILE), F32),
            pltpu.VMEM((8, TILE), F32),
            pltpu.VMEM((TILES, HEADS, TILE, TILE), F32),
        ],
        compiler_params=params(24),
        cost_estimate=QUICK,
    )(seg, seg_row, keep_row, q, k, v)


erfc_step = 0.3275911 * math.sqrt(0.5)
erfc_terms = [0.254829592, -0.284496736, 1.421413741, -1.453152027, 1.061405429]


def normal_parts(u):
    expo = jnp.exp2(u * u * (-0.5 * math.log2(math.e)))
    t = 1.0 / (1.0 + erfc_step * jnp.abs(u))
    poly = 0.5 * erfc_terms[4]
    for term in reversed(erfc_terms[:4]):
        poly = poly * t + 0.5 * term
    below = poly * t * expo
    return jnp.where(u > 0.0, 1.0 - below, below), expo * (1.0 / math.sqrt(2.0 * math.pi))


def middle_kernel(plan, *refs):
    late_refs, rest = refs[: 2 * plan.nb - 2], refs[2 * plan.nb - 2 :]
    middle_body(plan, late_refs, *rest)


def middle_body(
    plan,
    late_refs,
    tokens_ref,
    cot_ref,
    o_ref,
    ot_ref,
    head_ref,
    kept_ref,
    vec_ref,
    keep_ref,
    patches_ref,
    out_ref,
    dh1_ref,
    do_ref,
    near_ref,
    far_ref,
    tail_ref,
    gvec_ref,
    keepc,
    hid,
    dus,
    flat,
    wo_ref,
    wu_ref,
    wd_ref,
):
    bucket = lax.axis_index("bucket")
    base = ROW_OUT
    flat[0:8, :] = head_ref[...]
    dp = lax.axis_index("dp")
    owns, others = late_refs[: plan.nb - 1], late_refs[plan.nb - 1 :]
    lay_windows(
        plan,
        range(plan.nd, plan.n),
        lambda k: (owns[k // plan.nd - 1], others[k // plan.nd - 1]),
        flat,
        base,
    )
    take_matrix(wo_ref, flat, 0, D, D)
    take_matrix(wu_ref, flat, ROW_UP - base, D, FF)
    take_matrix(wd_ref, flat, ROW_DOWN - base, FF, D)
    gain2, shift2 = vec_ref[4:5, :], vec_ref[5:6, :]
    own = patches_ref[bucket].astype(F32)
    total = patches_ref[0].astype(F32)
    for b in range(1, plan.nb):
        total = total + patches_ref[b].astype(F32)
    ones = jnp.ones((1, LANES), F32)
    scale = (plan.nb * own) * ones / (total * ones) * float(SEQ * plan.nd) / kept_ref[0:1, :]
    keepc[...] = to_column(keep_ref[...].astype(F32)) * scale
    gvec_ref[...] = jnp.zeros_like(gvec_ref)

    middle = tokens_ref[...].astype(F32) + nn(o_ref[...], wo_ref[...])
    hat, rstd = norm_parts(middle)
    low = (hat * gain2 + shift2).astype(BF)
    weights = keepc[...]
    seed = cot_ref[...].astype(F32) * jnp.concatenate([weights] * (D // LANES), axis=1)
    seed_low = seed.astype(BF)
    for first in range(0, FF, MIDDLE_BLOCK):
        cols = slice(first, first + MIDDLE_BLOCK)
        u = nn(low, wu_ref[:, cols])
        phi, bell = normal_parts(u)
        hid[:, cols] = (u * phi).astype(BF)
        dus[:, cols] = (nt(seed_low, wd_ref[cols, :]) * (phi + u * bell)).astype(BF)
    out_ref[...] = (middle + nn(hid[...], wd_ref[...])).astype(BF)
    seedt = jnp.transpose(seed).astype(BF)
    lowt = jnp.transpose(low.astype(F32)).astype(BF)
    da2 = nt(dus[...], wu_ref[...])
    gvec_ref[0:1, :] = jnp.sum(da2 * hat, axis=0, keepdims=True)
    gvec_ref[1:2, :] = jnp.sum(da2, axis=0, keepdims=True)
    dh1 = seed + norm_back(hat, rstd, da2 * gain2)
    dh1_ref[...] = dh1
    dh1_low = dh1.astype(BF)
    gout = nn(jnp.concatenate([ot_ref[t] for t in range(TILES)], axis=1), dh1_low)
    do_ref[...] = nt(dh1_low, wo_ref[...]).astype(BF)
    put_matrix(flat, 0, gout, D, D)
    block = 2 * TILE
    for i in range(FF // block):
        part = nn(lowt, dus[:, i * block : (i + 1) * block])
        for j in range(block // LANES):
            flat[pl.ds(ROW_UP - base + i * (block // LANES) + j, D, stride=FF // LANES), :] = part[
                :, j * LANES : (j + 1) * LANES
            ]
        part = jnp.transpose(nn(seedt, hid[:, i * block : (i + 1) * block]))
        for j in range(D // LANES):
            flat[
                pl.ds(ROW_DOWN - base + i * block * (D // LANES) + j, block, stride=D // LANES), :
            ] = part[:, j * LANES : (j + 1) * LANES]
    flat[ROW_VEC - base :, :] = jnp.zeros((flat.shape[0] - ROW_VEC + base, LANES), F32)
    for t in range(2):
        for j in range(D // LANES):
            row = ROW_VEC - base + EARLY_VEC_ROWS + t * (D // LANES) + j
            flat[row : row + 1, :] = gvec_ref[t : t + 1, j * LANES : (j + 1) * LANES]
    tail_ref[...] = flat[0:8, :]
    side = jnp.bitwise_and(dp, 1)
    for k in range(plan.nd, plan.n):
        first = plan.start[k] - base
        quarter = k // plan.nd - 1
        reld = jnp.right_shift(jnp.bitwise_xor(dp, k % plan.nd), 1)
        window = flat[first : first + plan.win, :].astype(BF)

        @pl.when(side == k % 2)
        def _():
            near_ref[quarter, reld] = window

        @pl.when(side != k % 2)
        def _():
            far_ref[quarter, reld] = window


def middle_part(plan, late, tokens, cot, o, ot, head, kept, vec, keep_row, patches):
    rows = tokens.shape[0]
    windows = jax.ShapeDtypeStruct((plan.nb - 1, plan.nd // 2, plan.win, LANES), BF)
    return pl.pallas_call(
        functools.partial(middle_kernel, plan),
        out_shape=(
            jax.ShapeDtypeStruct((rows, D), BF),
            jax.ShapeDtypeStruct((rows, D), F32),
            jax.ShapeDtypeStruct((rows, D), BF),
            windows,
            windows,
            jax.ShapeDtypeStruct((8, LANES), F32),
            jax.ShapeDtypeStruct((8, D), F32),
        ),
        in_specs=[VMEM] * (len(late) + 8) + [SMEM],
        out_specs=(VMEM,) * 7,
        scratch_shapes=[
            pltpu.VMEM((rows, LANES), F32),
            pltpu.VMEM((rows, FF), BF),
            pltpu.VMEM((rows, FF), BF),
            pltpu.VMEM((round_up(plan.start[-1] + plan.win - ROW_OUT, 8), LANES), F32),
            pltpu.VMEM((D, D), BF),
            pltpu.VMEM((D, FF), BF),
            pltpu.VMEM((FF, D), BF),
        ],
        compiler_params=params(36),
        cost_estimate=QUICK,
    )(*late, tokens, cot, o, ot, head, kept, vec, keep_row, patches)


def stack_kernel(
    vec_ref,
    hat_in_ref,
    q_ref,
    k_ref,
    v_ref,
    do_ref,
    whole_ref,
    vab,
    qab,
    dab,
    kt,
    inner_sums,
    normed_ref,
    token_ref,
):
    for step in range(TILES):
        at = rows_at(step)
        grads = do_ref[at, :]
        for hp in range(PAIRS):
            lanes = slice(hp * LANES, (hp + 1) * LANES)
            put_blocks(vab, hp, step, v_ref[at, lanes])
            qab[hp, step] = stack_heads(q_ref[at, lanes])
            dab[hp, step] = stack_heads(grads[:, lanes])
        kt[:, at] = jnp.transpose(k_ref[at, :].astype(F32)).astype(BF)
        both = jnp.transpose(grads.astype(F32)) * whole_ref[step]
        for head in range(HEADS):
            inner_sums[step, head : head + 1, :] = jnp.sum(
                both[head * HD : (head + 1) * HD], axis=0, keepdims=True
            )
        normed = hat_in_ref[at, :] * vec_ref[0:1, :] + vec_ref[1:2, :]
        normed_ref[:, at] = jnp.transpose(normed).astype(BF)
    token_ref[...] = jnp.zeros_like(token_ref)


def stack_part(vec, hat_in, q, k, v, do, whole):
    stacked = jax.ShapeDtypeStruct((PAIRS, TILES, 2 * TILE, LANES), BF)
    return pl.pallas_call(
        stack_kernel,
        out_shape=(
            jax.ShapeDtypeStruct((PAIRS, BLOCKS, 2, LANES, LANES), BF),
            stacked,
            stacked,
            jax.ShapeDtypeStruct((D, SEQ), BF),
            jax.ShapeDtypeStruct((TILES, 8, TILE), F32),
            jax.ShapeDtypeStruct((D, SEQ), BF),
            jax.ShapeDtypeStruct((8, LANES), F32),
        ),
        in_specs=[VMEM] * 7,
        out_specs=(VMEM,) * 7,
        compiler_params=params(16),
        cost_estimate=QUICK,
    )(vec, hat_in, q, k, v, do, whole)


def backward_kernel(
    plan,
    vec_ref,
    seg_smem,
    seg_ref,
    lse_ref,
    q_ref,
    do_ref,
    hat_ref,
    rstd_ref,
    segk,
    kab,
    vab,
    qab,
    dab,
    kt,
    inner_sums,
    token_ref,
    low_ref,
    gains_ref,
    dqt,
    dk,
    dv,
):
    matrix = head_mean_matrix()
    dqt[...] = jnp.zeros_like(dqt)
    dk[...] = jnp.zeros_like(dk)
    dv[...] = jnp.zeros_like(dv)
    gains_ref[...] = jnp.zeros_like(gains_ref)

    def query_tile(ti, carry):
        row_seg = seg_ref[:, rows_at(ti)].astype(F32)
        first, count = key_chunks(seg_smem, ti)

        def key_chunk(c, inner):
            block = first + 2 * c
            keys = keys_at(block)
            column = segk[keys, :]
            bias = tile_bias(ti, block, row_seg, jnp.concatenate([column, column], axis=1))
            raw = []
            for hp in range(PAIRS):
                lanes = slice(hp * LANES, (hp + 1) * LANES)
                raw.append(
                    (
                        nt(two_blocks(kab, hp, block), q_ref[rows_at(ti), lanes]),
                        nt(two_blocks(vab, hp, block), do_ref[rows_at(ti), lanes]),
                    )
                )
            probs, dscores = [], []
            for head in range(HEADS):
                scores, grads = raw[head // 2]
                prob = jnp.exp2(
                    side_rows(scores, head % 2) * score_scale
                    + (bias - lse_ref[ti, head : head + 1, :])
                )
                dscore = prob * (side_rows(grads, head % 2) - inner_sums[ti, head : head + 1, :])
                probs.append(prob.astype(BF))
                dscores.append(dscore.astype(BF))
            for hp in range(PAIRS):
                pair = slice(2 * hp, 2 * hp + 2)
                for head in (2 * hp, 2 * hp + 1):
                    at = slice(head * HD, (head + 1) * HD)
                    dqt[ti, at, :] += nn(kt[at, keys], dscores[head])
                dv[hp, keys] += nn(jnp.concatenate(probs[pair], axis=1), dab[hp, ti])
                dk[hp, keys] += nn(jnp.concatenate(dscores[pair], axis=1), qab[hp, ti])
            return inner

        lax.fori_loop(0, count, key_chunk, 0)
        return carry

    lax.fori_loop(0, TILES, query_tile, 0)

    def finish(step, carry):
        at = rows_at(step)

        def head_norm_back(part, gain, grad):
            lanes = slice(part * D, (part + 1) * D)
            hat = hat_ref[at, lanes]
            both = grad * hat
            gains_ref[part : part + 1, :] += jnp.sum(both, axis=0, keepdims=True)
            scaled = grad * gain
            mean_grad = head_mean_low(scaled.astype(BF), matrix)
            mean_both = head_mean_low((both * gain).astype(BF), matrix)
            back = rstd_ref[at, lanes] * (scaled - mean_grad - hat * mean_both)
            low_ref[at, lanes] = back.astype(BF)

        grad_k = jnp.concatenate([dk[hp, at] for hp in range(PAIRS)], axis=1) * grad_scale
        grad_v = jnp.concatenate([dv[hp, at] for hp in range(PAIRS)], axis=1)
        head_norm_back(0, vec_ref[2:3, :], jnp.transpose(dqt[step]) * grad_scale)
        head_norm_back(1, vec_ref[3:4, :], grad_k)
        low_ref[at, 2 * D :] = grad_v.astype(BF)
        return carry

    lax.fori_loop(0, TILES, finish, 0)


def backward(plan, vec, seg, seg_row, lse, q, do, hat, rstd, segk, stacks, token):
    rows = q.shape[0]
    return pl.pallas_call(
        functools.partial(backward_kernel, plan),
        out_shape=(
            jax.ShapeDtypeStruct((rows, 3 * D), BF),
            jax.ShapeDtypeStruct((8, D), F32),
        ),
        in_specs=[VMEM, SMEM] + [VMEM] * 14,
        out_specs=(VMEM, VMEM),
        scratch_shapes=[
            pltpu.VMEM((TILES, D, TILE), F32),
            pltpu.VMEM((PAIRS, SEQ, LANES), F32),
            pltpu.VMEM((PAIRS, SEQ, LANES), F32),
        ],
        compiler_params=params(26),
        cost_estimate=QUICK,
    )(vec, seg, seg_row, lse, q, do, hat, rstd, segk, *stacks, token)


def finish_kernel(
    plan,
    hat_ref,
    normed_ref,
    wq_ref,
    tail_ref,
    low_ref,
    gqk_ref,
    da1_ref,
    near_ref,
    *refs,
):
    *far_refs, gains, flat = refs
    hat = hat_ref[...]
    for i in range(3):
        part = nn(normed_ref[...], low_ref[:, i * D : (i + 1) * D])
        for j in range(D // LANES):
            flat[pl.ds(i * (D // LANES) + j, D, stride=3 * D // LANES), :] = part[
                :, j * LANES : (j + 1) * LANES
            ]
    da1 = nt(low_ref[...], wq_ref[...])
    da1_ref[...] = da1
    gains[...] = jnp.zeros_like(gains)
    gains[0:1, :] = jnp.sum(da1 * hat, axis=0, keepdims=True)
    gains[1:2, :] = jnp.sum(da1, axis=0, keepdims=True)
    gains[2:4, :] = gqk_ref[0:2, :]
    flat[ROW_OUT : ROW_OUT + 8, :] = tail_ref[...]
    dp = lax.axis_index("dp")
    side = jnp.bitwise_and(dp, 1)
    vector_rows = []
    for t in range(4):
        for j in range(D // LANES):
            vector_rows.append(gains[t : t + 1, j * LANES : (j + 1) * LANES])
    spare = plan.tail - plan.most - EARLY_VEC_ROWS
    if spare:
        vector_rows.append(jnp.zeros((spare, LANES), F32))
    for k in range(plan.nd):
        first = plan.start[k]
        reld = jnp.right_shift(jnp.bitwise_xor(dp, k), 1)
        window = flat[first : first + plan.tail, :]
        if k == plan.nd - 1:
            window = jnp.concatenate([window[: plan.most], *vector_rows], axis=0)
        window = window.astype(BF)

        @pl.when(side == k % 2)
        def _():
            near_ref[reld] = window

        @pl.when(side != k % 2)
        def _():
            for (low, high), far_ref in zip(plan.far, far_refs):
                far_ref[reld] = window[low:high]


def finish_part(plan, hat, normed, wq, tail, low, gains):
    rows = hat.shape[0]
    windows = jax.ShapeDtypeStruct((plan.nd // 2, plan.tail, LANES), BF)
    parts = tuple(
        jax.ShapeDtypeStruct((plan.nd // 2, high - low, LANES), BF) for low, high in plan.far
    )
    return pl.pallas_call(
        functools.partial(finish_kernel, plan),
        out_shape=(jax.ShapeDtypeStruct((rows, D), F32), windows) + parts,
        in_specs=[VMEM] * 6,
        out_specs=(VMEM,) * (2 + FAR_PARTS),
        scratch_shapes=[
            pltpu.VMEM((8, D), F32),
            pltpu.VMEM((round_up(plan.start[plan.nd - 1] + plan.tail, 8), LANES), F32),
        ],
        compiler_params=params(28),
        cost_estimate=QUICK,
    )(hat, normed, wq, tail, low, gains)


def input_kernel(
    plan,
    hat_ref,
    rstd_ref,
    vec_ref,
    da1_ref,
    dh1_ref,
    master_ref,
    moment_ref,
    second_ref,
    grad_ref,
    master_rows,
    moment_rows,
    second_rows,
    squares_ref,
):
    back = norm_back(hat_ref[...], rstd_ref[:, 0:1], da1_ref[...] * vec_ref[0:1, :])
    grad_ref[...] = dh1_ref[...] + back
    master = flat_to_rows(plan, master_ref, master_rows)
    flat_to_rows(plan, moment_ref, moment_rows)
    flat_to_rows(plan, second_ref, second_rows)
    _, index = flat_place(plan, master.shape)
    squares_ref[...] = jnp.broadcast_to(tensor_sums(master * master, index), squares_ref.shape)


def input_part(plan, hat, rstd, vec, da1, dh1, master, moment, second):
    rows = jax.ShapeDtypeStruct((plan.win, LANES), F32)
    return pl.pallas_call(
        functools.partial(input_kernel, plan),
        out_shape=(
            jax.ShapeDtypeStruct(dh1.shape, F32),
            rows,
            rows,
            rows,
            jax.ShapeDtypeStruct((8, LANES), F32),
        ),
        in_specs=[VMEM] * 8,
        out_specs=(VMEM,) * 5,
        compiler_params=params(16),
        cost_estimate=QUICK,
    )(hat, rstd, vec, da1, dh1, master, moment, second)


def flat_place(plan, shape):
    row = lax.broadcasted_iota(jnp.int32, shape, 0)
    lane = lax.broadcasted_iota(jnp.int32, shape, 1)
    place = row * LANES + lane
    return place, plan.device() * plan.shard + place


def tensor_sums(squares, index):
    lanes = lax.broadcasted_iota(jnp.int32, (1, LANES), 1)
    row = jnp.zeros((1, LANES), F32)
    for t in range(MATS):
        mine = jnp.logical_and(index >= BOUNDS[t], index < BOUNDS[t + 1])
        part = jnp.sum(jnp.where(mine, squares, 0.0), axis=0, keepdims=True)
        row = jnp.where(lanes == t, jnp.sum(part, axis=1, keepdims=True), row)
    return row


def update_kernel(
    plan,
    own_ref,
    got0_ref,
    got1_ref,
    got2_ref,
    master_ref,
    moment_ref,
    second_ref,
    squares_ref,
    new_moment_ref,
    new_second_ref,
    update_ref,
    sums_ref,
    window,
):
    bucket = lax.axis_index("bucket")
    dp = lax.axis_index("dp")
    total = tree_sum([ref[...].astype(F32) for ref in (own_ref, got0_ref, got1_ref, got2_ref)])
    window[...] = total[: plan.win]

    @pl.when(jnp.logical_and(bucket == plan.nb - 1, dp == plan.nd - 1))
    def _():
        window[plan.vec_place : plan.vec_place + EARLY_VEC_ROWS, :] = total[
            plan.most : plan.most + EARLY_VEC_ROWS
        ]

    offset = lax.rem(plan.device() * plan.shard, LANES)
    back = lax.rem(LANES - offset, LANES)
    turned = pltpu.roll(window[...], back, 1)
    above = pltpu.roll(turned, plan.win - 1, 0)
    lane = lax.broadcasted_iota(jnp.int32, turned.shape, 1)
    place, index = flat_place(plan, turned.shape)
    inside = place < plan.shard
    grad = jnp.where(inside, jnp.where(lane + offset < LANES, turned, above), 0.0)
    master = master_ref[...]
    moment = beta_one * moment_ref[...] + (1.0 - beta_one) * grad
    second = beta_two * second_ref[...] + (1.0 - beta_two) * grad * grad
    first_hat = moment / (1.0 - beta_one**STEP)
    second_hat = second / (1.0 - beta_two**STEP)
    decay = jnp.where(index < BOUNDS[4], weight_decay, 0.0)
    update = first_hat / (jnp.sqrt(second_hat) + adam_epsilon) + decay * master
    update = jnp.where(inside, update, 0.0)
    new_moment_ref[...] = moment
    new_second_ref[...] = second
    update_ref[...] = update
    rows = [squares_ref[0:1, :], tensor_sums(update * update, index), jnp.zeros((6, LANES), F32)]
    sums_ref[...] = jnp.concatenate(rows, axis=0)


def update_part(plan, parts, master, moment, second, squares):
    rows = jax.ShapeDtypeStruct((plan.win, LANES), F32)
    return pl.pallas_call(
        functools.partial(update_kernel, plan),
        out_shape=(rows, rows, rows, jax.ShapeDtypeStruct((8, LANES), F32)),
        in_specs=[VMEM] * 8,
        out_specs=(VMEM,) * 4,
        scratch_shapes=[pltpu.VMEM((plan.win, LANES), F32)],
        compiler_params=params(12),
    )(*parts, master, moment, second, squares)


def flatten_kernel(plan, moment_ref, second_ref, new_moment_ref, new_second_ref, token_ref):
    rows_to_flat(plan, moment_ref[...], new_moment_ref)
    rows_to_flat(plan, second_ref[...], new_second_ref)
    token_ref[...] = jnp.zeros_like(token_ref)


def flatten_part(plan, moment, second):
    flat = jax.ShapeDtypeStruct((plan.shard,), F32)
    return pl.pallas_call(
        functools.partial(flatten_kernel, plan),
        out_shape=(flat, flat, jax.ShapeDtypeStruct((8, LANES), F32)),
        in_specs=[VMEM] * 2,
        out_specs=(VMEM,) * 3,
        compiler_params=params(8),
        cost_estimate=QUICK,
    )(moment, second)


def apply_kernel(plan, *refs):
    *sums_refs, master_ref, update_ref, _, new_ref, norms_ref, trust_ref = refs
    roots = jnp.sqrt(tree_sum([ref[...] for ref in sums_refs]))
    trust = roots[0:1, :] / (roots[1:2, :] + adam_epsilon)
    norms_ref[...] = roots[0:2, :MATS]
    trust_ref[...] = trust[:, :MATS]
    master = master_ref[...]
    _, index = flat_place(plan, master.shape)
    factors = jnp.broadcast_to(trust[:, 0:1], master.shape)
    for t in range(1, MATS):
        factors = jnp.where(index >= BOUNDS[t], trust[:, t : t + 1], factors)
    rows_to_flat(plan, master - learn_rate * factors * update_ref[...], new_ref)


def apply_part(plan, sums, master, update_rows, token):
    return pl.pallas_call(
        functools.partial(apply_kernel, plan),
        out_shape=(
            jax.ShapeDtypeStruct((plan.shard,), F32),
            jax.ShapeDtypeStruct((2, MATS), F32),
            jax.ShapeDtypeStruct((1, MATS), F32),
        ),
        in_specs=[VMEM] * (len(sums) + 3),
        out_specs=(VMEM,) * 3,
        compiler_params=params(8),
    )(*sums, master, update_rows, token)


def lay_column_kernel(count, *refs):
    for i, part in enumerate(refs[:count]):
        refs[-1][i] = part[...]


def lay_column(parts, *after):
    return pl.pallas_call(
        functools.partial(lay_column_kernel, len(parts)),
        out_shape=jax.ShapeDtypeStruct((len(parts), *parts[0].shape), parts[0].dtype),
        in_specs=[VMEM] * (len(parts) + len(after)),
        out_specs=VMEM,
        compiler_params=params(4),
    )(*parts, *after)


def lay_lower_kernel(plan, mine_ref, got_ref, count_ref, out_ref):
    half = mine_ref.shape[0]
    out_ref[:half] = mine_ref[...]
    out_ref[half:] = got_ref[...]
    last = mine_ref[0, -16:, :].astype(F32)
    out_ref[0, plan.win - plan.upper - 16 :, :] = (last + count_ref[...]).astype(BF)


def lay_lower(plan, mine, got, count):
    half, height, _ = mine.shape
    return pl.pallas_call(
        functools.partial(lay_lower_kernel, plan),
        out_shape=jax.ShapeDtypeStruct((2 * half, height, LANES), BF),
        in_specs=[VMEM] * 3,
        out_specs=VMEM,
        compiler_params=params(4),
    )(mine, got, count)


def choose_kernel(plan, *refs):
    columns, (lower_ref, early_ref), late_refs = (
        refs[: plan.nb],
        refs[plan.nb : plan.nb + 2],
        refs[plan.nb + 2 :],
    )
    bucket = lax.axis_index("bucket")
    early_ref[:, plan.kept_row :] = lower_ref[:, 0, plan.win - plan.upper - 16 :]
    for i, part in enumerate(columns):
        for owner, out_ref in enumerate((early_ref, *late_refs)):

            @pl.when(jnp.bitwise_xor(bucket, i) == owner)
            def _():
                out_ref[:, : plan.upper] = part[...]
                out_ref[:, plan.upper : plan.win] = lower_ref[:, i]

    early_ref[:, plan.win : plan.kept_row] = late_refs[-1][:, plan.vec_from :]


def choose(plan, columns, lower):
    step = columns[0].shape[0]
    late = jax.ShapeDtypeStruct((step, plan.win, LANES), BF)
    return pl.pallas_call(
        functools.partial(choose_kernel, plan),
        out_shape=(jax.ShapeDtypeStruct((step, plan.early, LANES), BF),) + (late,) * (plan.nb - 1),
        in_specs=[VMEM] * (len(columns) + 1),
        out_specs=(VMEM,) * plan.nb,
        compiler_params=params(10),
    )(*columns, lower)


def add_parts_kernel(halves, *refs):
    refs = list(refs)
    parts = [[refs.pop(0) for _ in range(count)] for count in halves]
    for i, out in enumerate(refs[1:-1]):
        step = out.shape[-3]
        at = slice(i * step, (i + 1) * step)
        at = (slice(None), at) if len(out.shape) == 4 else at
        values = [
            jnp.concatenate([half[at].astype(F32) for half in part], axis=-2) for part in parts
        ]
        out[...] = tree_sum(values).astype(out.dtype)
    refs[-1][...] = jnp.zeros_like(refs[-1])


def add_parts(parts, pieces, token):
    *lead, total, height, width = parts[0].shape
    parts = [part if isinstance(part, list) else [part] for part in parts]
    halves = [len(part) for part in parts]
    parts = [half for part in parts for half in part]
    return pl.pallas_call(
        functools.partial(add_parts_kernel, halves),
        out_shape=tuple(
            jax.ShapeDtypeStruct((*lead, total // pieces, height, width), BF if i else F32)
            for i in range(pieces)
        )
        + (jax.ShapeDtypeStruct((8, LANES), F32),),
        in_specs=[VMEM] * (len(parts) + 1),
        out_specs=(VMEM,) * (pieces + 1),
        compiler_params=params(14),
    )(*parts, token)


def blend_kernel(plan, late_count, *refs):
    late, parts, outs = refs[:late_count], refs[late_count + 1 : -plan.nb], refs[-plan.nb :]
    bucket = lax.axis_index("bucket")
    first = tree_sum([part[...].astype(F32) for part in parts])
    for i, out in enumerate(outs):
        owner = jnp.bitwise_xor(bucket, i)
        quarter = jnp.maximum(owner - 1, 0)
        window = late[0][quarter]
        if late_count > 1:
            window = window + tree_sum([ref[quarter].astype(F32) for ref in late[1:]])
        if plan.tail > plan.win:
            empty = jnp.zeros((plan.tail - plan.win, LANES), F32)
            window = jnp.concatenate([window, empty], axis=0)
        row = lax.broadcasted_iota(jnp.int32, first.shape, 0)
        takes_first = jnp.logical_or(row >= plan.most, owner == 0)
        out[...] = jnp.where(takes_first, first, window).astype(out.dtype)


def blend(plan, late, token, parts):
    return pl.pallas_call(
        functools.partial(blend_kernel, plan, len(late)),
        out_shape=tuple(
            jax.ShapeDtypeStruct((plan.tail, LANES), BF if i else F32) for i in range(plan.nb)
        ),
        in_specs=[VMEM] * (len(late) + 1 + len(parts)),
        out_specs=(VMEM,) * plan.nb,
        compiler_params=params(10),
    )(*late, token, *parts)


def add_rows_kernel(*refs):
    refs[-1][...] = tree_sum([ref[...] for ref in refs[:-1]])


def add_rows(parts):
    return pl.pallas_call(
        add_rows_kernel,
        out_shape=jax.ShapeDtypeStruct(parts[0].shape, F32),
        in_specs=[VMEM] * len(parts),
        out_specs=VMEM,
        compiler_params=params(4),
    )(*parts)


def groups_of(size, skip=0):
    bits = list(range(skip, size.bit_length() - 1))
    return [bits[i : i + 2] for i in range(0, len(bits), 2)]


def masks_of(bits):
    masks = [1 << bits[0]]
    if len(bits) == 2:
        masks += [1 << bits[1], (1 << bits[0]) | (1 << bits[1])]
    return masks


def swap(x, axis, size, mask):
    return lax.ppermute(x, axis, [(i, i ^ mask) for i in range(size)])


def tree_sum(parts):
    if len(parts) == 1:
        return parts[0]
    half = len(parts) // 2
    return tree_sum(parts[:half]) + tree_sum(parts[half:])


def with_partners(x, axis, size, bits):
    return [x] + [swap(x, axis, size, mask) for mask in masks_of(bits)]


def gather_windows(plan, upper, lower, count):
    first, *more = groups_of(plan.nd, 1)
    (bits,) = groups_of(plan.nb)
    near, distant = masks_of(bits)[:2]
    lower = lay_column([lower, swap(lower, "bucket", plan.nb, near)])
    lower = lay_lower(plan, lower, swap(lower, "bucket", plan.nb, distant), count)
    column = lay_column(with_partners(upper, "dp", plan.nd, first), lower)
    for group in more:
        column = jnp.concatenate(with_partners(column, "dp", plan.nd, group), axis=0)
    columns = with_partners(column, "bucket", plan.nb, bits)
    lower = lay_column(with_partners(lower, "dp", plan.nd, first))
    for group in more:
        lower = jnp.concatenate(with_partners(lower, "dp", plan.nd, group), axis=0)
    early, *late = choose(plan, columns, lower)
    others = [swap(x, "dp", plan.nd, 1) for x in (early, *late)]
    return (early, others[0]), (*late, *others[1:])


def scatter_dp(plan, pieces):
    *more, last = groups_of(plan.nd, 1)
    sent = list(zip(pieces[1:], masks_of(last)))
    got = [pieces[0]] + [
        swap(piece, "dp", plan.nd, mask) for piece, mask in sent[1:] + sent[:1]
    ]
    for bits in reversed(more):
        held = tree_sum([x.astype(F32) for x in got])
        size = 1 << len(bits)
        step = held.shape[-3] // size
        parts = [held[..., i * step : (i + 1) * step, :, :] for i in range(size)]
        got = [parts[0]] + [
            swap(part.astype(BF), "dp", plan.nd, mask)
            for part, mask in zip(parts[1:], masks_of(bits))
        ]
    return [x.reshape(*x.shape[:-3], *x.shape[-2:]) for x in got]


def sum_all(plan, x):
    x = [x, swap(x, "dp", plan.nd, 1)]
    for bits in groups_of(plan.nd, 1):
        x = with_partners(add_rows(x), "dp", plan.nd, bits)
    (bits,) = groups_of(plan.nb)
    return with_partners(add_rows(x), "bucket", plan.nb, bits)


def local(
    plan, tokens, cotangent, segment_ids, keep_mask, bucket_patches, master, first_moment, second_moment
):
    seg_row = segment_ids.reshape(1, SEQ)
    keep_row = keep_mask.reshape(1, SEQ)
    pieces_of = 1 << len(groups_of(plan.nd, 1)[-1])
    (b_bits,) = groups_of(plan.nb)

    hat_in, rstd_in, count = ahead(tokens, keep_row)
    early, late = gather_windows(plan, *prepare(plan, master), count)
    wq, vec, head, kept, q, k, v, hat, rstd = project_part(plan, *early, hat_in)
    o, ot, whole, lse, kab, segk = forward(plan, segment_ids, seg_row, keep_row, q, k, v)
    block_output, dh1, do, near, far, tail, _ = middle_part(
        plan, late, tokens, cotangent, o, ot, head, kept, vec, keep_row, bucket_patches
    )
    *stacks, normed, token = stack_part(vec, hat_in, q, k, v, do, whole)
    *pieces, token = add_parts([near, swap(far, "dp", plan.nd, 1)], pieces_of, token)
    rest = scatter_dp(plan, pieces)
    low, gains = backward(
        plan, vec, segment_ids, seg_row, lse, q, do, hat, rstd, segk, [kab, *stacks], token
    )
    da1, near, *far = finish_part(plan, hat_in, normed, wq, tail, low, gains)
    input_grad, *old_rows, squares = input_part(
        plan, hat_in, rstd_in, vec, da1, dh1, master, first_moment, second_moment
    )
    *late_parts, token = add_parts(rest[:2], 1, gains)
    late_parts += rest[2:]
    *pieces, _ = add_parts([near, [swap(half, "dp", plan.nd, 1) for half in far]], pieces_of, token)
    first = scatter_dp(plan, pieces)
    mine, *sent = blend(plan, late_parts, squares, first)
    sent = list(zip(sent, masks_of(b_bits)))
    parts = [mine] + [swap(x, "bucket", plan.nb, mask) for x, mask in sent[::-1]]
    first_rows, second_rows, update_rows, sums = update_part(plan, parts, *old_rows, squares)
    new_first, new_second, token = flatten_part(plan, first_rows, second_rows)
    new_master, norms, trust = apply_part(
        plan, sum_all(plan, sums), old_rows[0], update_rows, token
    )
    return (
        block_output,
        input_grad,
        new_first,
        new_second,
        new_master,
        norms,
        trust.reshape(MATS),
    )


def solution(mesh):
    shards = mesh.shape["bucket"] * mesh.shape["dp"]
    plan = Plan(mesh.shape, PARAMS // shards)
    both = ("bucket", "dp")
    return jax.shard_map(
        functools.partial(local, plan),
        mesh=mesh,
        in_specs=(P(both, None), P(both, None), P(both), P(both), P(), P(both), P(both), P(both)),
        out_specs=(P(both, None), P(both, None), P(both), P(both), P(both), P(), P()),
        check_vma=False,
    )
```
